32 devices in a mesh: grp: 2 (over core), seq: 16 (over z, y, x).
Axes of the slice: x: 2, y: 2, z: 4, core: 2. Of those that a mesh axis runs over, the one named last changes fastest.
Arguments:
- tokens: bfloat16 [4096, 1152], P(('grp', 'seq')), may hold values from -6 to 6
- routes: int32 [4096], P(('grp', 'seq')), may hold values from 0 to 1
- lengths: int32 [2, 2], P('grp'), may hold values from 512 to 1536, as said below
- grad_out: float32 [4096, 1152], P(('grp', 'seq')), may hold values from -6 to 6
- norm_gains: float32 [2, 1152], replicated, may hold values from 0.1 to 1.9
- router: bfloat16 [1152, 2], replicated, may hold values from -0.1875 to 0.1875
- in_weight: bfloat16 [2, 2304, 1152], P(None, ('grp', 'seq')), may hold values from -0.1875 to 0.1875
- conv_weight: bfloat16 [2304, 4], P(('grp', 'seq')), may hold values from -3 to 3
- x_weight: bfloat16 [2304, 104], P(('grp', 'seq')), may hold values from -0.125 to 0.125
- dt_weight: bfloat16 [2304, 72], P(('grp', 'seq')), may hold values from -0.75 to 0.75
- dt_bias: bfloat16 [2304], P(('grp', 'seq')), may hold values from -6 to -4
- a_log: bfloat16 [2304, 16], P(('grp', 'seq')), may hold values from -6 to 2
- skip_gain: bfloat16 [2304], P(('grp', 'seq')), may hold values from 0.5 to 1.5
- out_weight: bfloat16 [2304, 1152], P(('grp', 'seq')), may hold values from -0.375 to 0.375
- expert_in: bfloat16 [2, 3072, 1152], P(None, ('grp', 'seq')), may hold values from -0.1875 to 0.1875
- expert_out: bfloat16 [2, 3072, 1152], P(None, ('grp', 'seq')), may hold values from -0.21875 to 0.21875
Outputs:
- mixed_out: bfloat16 [4096, 1152], P(('grp', 'seq'))
- grad_tokens: float32 [4096, 1152], P(('grp', 'seq'))
- grad_gains: float32 [2, 1152], replicated
- grad_router: float32 [1152, 2], replicated
- grad_in_weight: float32 [2, 2304, 1152], P(None, ('grp', 'seq'))
- grad_conv_weight: float32 [2304, 4], P(('grp', 'seq'))
- grad_x_weight: float32 [2304, 104], P(('grp', 'seq'))
- grad_dt_weight: float32 [2304, 72], P(('grp', 'seq'))
- grad_dt_bias: float32 [2304], P(('grp', 'seq'))
- grad_a_log: float32 [2304, 16], P(('grp', 'seq'))
- grad_skip: float32 [2304], P(('grp', 'seq'))
- grad_out_weight: float32 [2304, 1152], P(('grp', 'seq'))
- grad_expert_in: float32 [2, 3072, 1152], P(None, ('grp', 'seq'))
- grad_expert_out: float32 [2, 3072, 1152], P(None, ('grp', 'seq'))
The draws below stay inside these ranges and needn't reach their ends.
Inputs may be any that keep to these rules, and one draw needn't show every extreme that they name: lengths[g, 0] + lengths[g, 1] = 2048 for every group.
All inputs are finite; a program needn't handle non-finite values.
Results may differ from the reference program's by a relative error of at most 0.012.
The reference program's roundings to bfloat16 on the way count: a program that leaves them out, or rounds other values in their place, can miss the bound.
Values may be sent and summed in bfloat16 or wider, within the bound.
A program may use at most 448 MiB of HBM per device.

```python
import math
from functools import partial
import jax
import jax.numpy as jnp
from jax import lax

D = 1152
DI = 2304
N = 16
R = 72
FF = 3072
CONV = 4
EXPERTS = 2
GROUPS = 2
TOKENS_GRP = 2048
TOKENS = 4096


def draw_lengths(key, part):
    key = jax.random.fold_in(key, 11)
    key_first, key_pick, key_side = jax.random.split(key, 3)
    quarter = TOKENS_GRP // 4
    first_len = quarter + jax.random.randint(key_first, (GROUPS,), 0, 2 * quarter + 1)
    picked = jax.random.randint(key_pick, (), 0, GROUPS)
    side_bit = jax.random.randint(key_side, (), 0, 2)
    edge_len = jnp.where(side_bit == 0, quarter, TOKENS_GRP - quarter)
    first_len = jnp.where(jnp.arange(GROUPS) == picked, edge_len, first_len)
    return jnp.stack([first_len, TOKENS_GRP - first_len], 1).astype(jnp.int32)


def draw_a_log(key, part):
    key = jax.random.fold_in(key, 23)
    key_kind, key_slow, key_fast = jax.random.split(key, 3)
    fast_flag = jax.random.randint(key_kind, (DI, 1), 0, 2)
    slow_vals = jax.random.uniform(key_slow, (DI, N), jnp.float32, -6.0, -4.0)
    fast_vals = jax.random.uniform(key_fast, (DI, N), jnp.float32, 1.0, 2.0)
    return jnp.where(fast_flag == 1, fast_vals, slow_vals).astype(jnp.bfloat16)


def plant(values, key, low, high):
    shape = values.shape
    spot = [jax.random.randint(jax.random.fold_in(key, axis), (), 0, shape[axis]) for axis in range(len(shape))]
    values = values.at[tuple(spot)].set(low)
    longest = shape.index(max(shape))
    spot[longest] = (spot[longest] + 1) % shape[longest]
    return values.at[tuple(spot)].set(high)


def steps_of(rng, shape, cuts, smallest, largest):
    def one(axis_at, shards_of):
        heights = jax.random.uniform(jax.random.fold_in(jax.random.fold_in(rng, 6), axis_at), (shards_of,), jnp.float32, smallest / len(cuts), largest / len(cuts))
        return jnp.repeat(jnp.exp(heights), shape[axis_at] // shards_of).reshape((-1,) + (1,) * (len(shape) - axis_at - 1))

    gain = one(*cuts[0])
    for cut in cuts[1:]:
        gain = gain * one(*cut)
    return gain


def scatter_about(own_key, extent, width, reach, cuts=(), kind=jnp.bfloat16):
    entries = jax.random.normal(own_key, extent, jnp.float32) * width
    if len(cuts) > 0:
        entries = steps_of(own_key, extent, cuts, -0.22, 0.18) * entries
    return jnp.clip(entries, min=-reach, max=reach).astype(kind)


def setup_inputs(seed: int = 0) -> dict:
    keys = jax.random.split(jax.random.key(seed), 17)
    tokens = scatter_about(keys[0], (TOKENS, D), 1.0, 6.0, ((0, 32),))
    routes = plant(jax.random.randint(keys[1], (TOKENS,), 0, EXPERTS), jax.random.fold_in(keys[1], 1), 0, EXPERTS - 1).astype(jnp.int32)
    lengths = draw_lengths(jax.random.fold_in(keys[16], 71), 0)
    grad_out = scatter_about(keys[3], (TOKENS, D), 1.0, 6.0, ((0, 32),), jnp.float32)
    norm_gains = jnp.clip(1.0 + 0.18 * jax.random.normal(keys[4], (2, D), jnp.float32), 0.1, 1.9)
    router = scatter_about(keys[5], (D, EXPERTS), D ** -0.5, 0.1875)
    in_weight = scatter_about(keys[6], (2, DI, D), D ** -0.5, 0.1875, ((1, 32),))
    conv_weight = scatter_about(keys[7], (DI, CONV), CONV ** -0.5, 3.0, ((0, 32),))
    x_weight = scatter_about(keys[8], (DI, R + 2 * N), DI ** -0.5, 0.125, ((0, 32),))
    dt_weight = scatter_about(keys[9], (DI, R), R ** -0.5, 0.75, ((0, 32),))
    dt_bias = jnp.clip(-6.0 + 2.0 * jax.random.uniform(keys[10], (DI,), jnp.float32) ** steps_of(keys[10], (DI,), ((0, 32),), -0.2, 0.2), -6.0, -4.0).astype(jnp.bfloat16)
    a_log = draw_a_log(jax.random.fold_in(keys[16], 71), 0)
    skip_gain = jnp.clip(0.5 + 1.0 * jax.random.uniform(keys[12], (DI,), jnp.float32) ** steps_of(keys[12], (DI,), ((0, 32),), -0.2, 0.2), 0.5, 1.5).astype(jnp.bfloat16)
    out_weight = scatter_about(keys[13], (DI, D), (DI // 8) ** -0.5, 0.375, ((0, 32),))
    expert_in = scatter_about(keys[14], (EXPERTS, FF, D), D ** -0.5, 0.1875, ((1, 32),))
    expert_out = scatter_about(keys[15], (EXPERTS, FF, D), (FF // 4) ** -0.5, 0.21875, ((1, 32),))
    return dict(tokens=tokens, routes=routes, lengths=lengths, grad_out=grad_out, norm_gains=norm_gains, router=router, in_weight=in_weight, conv_weight=conv_weight, x_weight=x_weight, dt_weight=dt_weight, dt_bias=dt_bias, a_log=a_log, skip_gain=skip_gain, out_weight=out_weight, expert_in=expert_in, expert_out=expert_out)


eps_norm = 1e-05
highest = lax.Precision.HIGHEST

@jax.custom_vjp
def low(v):
    return lax.optimization_barrier(v.astype(jnp.bfloat16)).astype(jnp.float32)

@jax.custom_vjp
def low_back(v):
    return v

def low_keep(v):
    return (low(v), None)

def low_pass(kept, grad):
    return (grad,)

def back_keep(v):
    return (v, None)

def back_low(kept, grad):
    return (low(grad),)
low.defvjp(low_keep, low_pass)
low_back.defvjp(back_keep, back_low)

def norm_rows(values, gain_row):
    return values * lax.rsqrt(lax.optimization_barrier(jnp.mean(values * values, -1, keepdims=True)) + eps_norm) * gain_row

def product(first_op, second_op):
    return jnp.dot(first_op, second_op, precision=highest)

def layer_rows(weights, carry_in, pieces):
    norm_gains, router, in_weight, conv_weight, x_weight, dt_weight, dt_bias, a_log, skip_gain, out_weight, expert_in, expert_out = weights
    history, state_now = carry_in
    row_input, route_rows, offset_rows = pieces
    inner_width = conv_weight.shape[0]
    tap_count = conv_weight.shape[1]
    dt_rank = dt_weight.shape[1]
    states = a_log.shape[1]
    expert_count = expert_in.shape[0]
    row_count = row_input.shape[0]
    normed = low(norm_rows(row_input, norm_gains[0]))
    conv_input = low(low_back(product(normed, in_weight[0].T)))
    z_gate = low_back(product(normed, in_weight[1].T))
    window = jnp.concatenate([history, conv_input], 0)
    conv_sum = jnp.zeros((row_count, inner_width), jnp.float32)
    for k in range(tap_count):
        valid_rows = (offset_rows >= tap_count - 1 - k).astype(jnp.float32)[:, None]
        conv_sum = conv_sum + conv_weight[:, k] * window[k:k + row_count] * valid_rows
    mixed = low(jax.nn.silu(conv_sum))
    coef_rows = low_back(product(mixed, x_weight))
    dt_low = low(coef_rows[:, :dt_rank])
    in_coef = coef_rows[:, dt_rank:dt_rank + states]
    out_coef = coef_rows[:, dt_rank + states:]
    dt_pre = low_back(product(dt_low, dt_weight.T))
    step_size = jax.nn.softplus(dt_pre + dt_bias)
    decay_rate = -jnp.exp(a_log).T
    keep_rows = (offset_rows != 0).astype(jnp.float32)

    def advance(hidden_state, row):
        delta_row, in_row, out_row, mixed_row, keep_flag = row
        hidden_state = jnp.exp(delta_row[None, :] * decay_rate) * keep_flag * hidden_state + in_row[:, None] * (delta_row * mixed_row)[None, :]
        return (hidden_state, lax.optimization_barrier(jnp.sum(out_row[:, None] * hidden_state, 0)))
    state_now, y_state = lax.scan(advance, state_now, (step_size, in_coef, out_coef, mixed, keep_rows))
    y_value = y_state + skip_gain * mixed
    gated = low(y_value * jax.nn.silu(z_gate))
    branch = low_back(product(gated, out_weight))
    resid = row_input + branch
    second = low(norm_rows(resid, norm_gains[1]))
    logits = low_back(product(second, router))
    soft_probs = jax.nn.softmax(logits, -1)
    chosen = (route_rows[:, None] == jnp.arange(expert_count, dtype=jnp.int32)[None, :]).astype(jnp.float32)
    gate_prob = lax.optimization_barrier(jnp.sum(soft_probs * chosen, -1))
    combined = resid
    for e in range(expert_count):
        pre_act = low_back(product(second, expert_in[e].T))
        activated = low(jax.nn.gelu(pre_act, approximate=False))
        expert_y = low_back(product(activated, expert_out[e]))
        combined = combined + chosen[:, e:e + 1] * gate_prob[:, None] * expert_y
    return ((window[row_count:], state_now), combined)

def forward(token_rows, weights, routes, lengths):
    inner_width = weights[3].shape[0]
    tap_count = weights[3].shape[1]
    states = weights[7].shape[1]
    block = math.gcd(TOKENS_GRP, 1024)
    step_fn = jax.checkpoint(partial(layer_rows, weights))
    outputs = []
    place = jnp.arange(TOKENS_GRP, dtype=jnp.int32)
    for group in range(GROUPS):
        first_len = lengths[group, 0].astype(jnp.int32)
        offset = jnp.where(place < first_len, place, place - first_len).astype(jnp.int32)
        first_row = group * TOKENS_GRP
        group_rows = token_rows[first_row:first_row + TOKENS_GRP]
        group_routes = routes[first_row:first_row + TOKENS_GRP]
        start_carry = (jnp.zeros((tap_count - 1, inner_width), jnp.float32), jnp.zeros((states, inner_width), jnp.float32))
        pieces = (group_rows.reshape(-1, block, D), group_routes.reshape(-1, block), offset.reshape(-1, block))
        _, group_out = lax.scan(step_fn, start_carry, pieces)
        outputs.append(group_out.reshape(TOKENS_GRP, D))
    return jnp.concatenate(outputs, 0)

def reference(tokens, routes, lengths, grad_out, norm_gains, router, in_weight, conv_weight, x_weight, dt_weight, dt_bias, a_log, skip_gain, out_weight, expert_in, expert_out):
    weights = tuple((w.astype(jnp.float32) for w in (norm_gains, router, in_weight, conv_weight, x_weight, dt_weight, dt_bias, a_log, skip_gain, out_weight, expert_in, expert_out)))
    token_rows = tokens.astype(jnp.float32)

    def run(rows_in, *weight_list):
        return forward(rows_in, weight_list, routes, lengths)
    result, pull = jax.vjp(run, token_rows, *weights)
    grads = pull(grad_out.astype(jnp.float32))
    return (result.astype(jnp.bfloat16), grads[0], grads[1], grads[2], grads[3], grads[4], grads[5], grads[6], grads[7], grads[8], grads[9], grads[10], grads[11], grads[12])
```

```python
import functools
import math

import jax
import jax.numpy as jnp
from jax import lax
from jax.experimental import pallas as pl
from jax.experimental.pallas import tpu as pltpu
from jax.sharding import PartitionSpec as P

eps_norm = 1e-05
split = 4
lanes = 128
subs = 8
log2e = 1.4426950408889634


def spread(coef_ref, first, spread_ref, steps, states):
    def one(s, _):
        rows = coef_ref[pl.ds(s, subs, stride=steps), :]
        for n in range(states):
            spread_ref[s, n] = jnp.broadcast_to(rows[:, first + n : first + n + 1], (subs, lanes))
        return 0

    lax.fori_loop(0, steps, one, 0, unroll=8)


def chain_rows(grow, state, reverse):
    row = lax.broadcasted_iota(jnp.int32, (subs, lanes), 0)
    shift = 1
    while shift < subs:
        turn = subs - shift if reverse else shift
        has = row < subs - shift if reverse else row >= shift
        near_grow = jnp.where(has, pltpu.roll(grow, turn, 0), 1.0)
        near_state = jnp.where(has, pltpu.roll(state, turn, 0), 0.0)
        state = state + grow * near_state
        grow = grow * near_grow
        shift *= 2
    return grow, state


def ends_kernel(
    first, reverse, states, steps, peers,
    delta_ref, reset_ref, drive_ref, coef_ref, rate_ref,
    grow_ref, state_ref, enter_ref,
    spread_ref, send_ref, arrive_ref, send_sem, arrive_sem,
):
    tile = pl.program_id(0)
    tiles = pl.num_programs(0)
    place = lax.axis_index("seq")
    high, low, core = place // split, place % split, lax.axis_index("grp")

    def other(k):
        return (core, lax.rem(high + (peers + 1 - k if reverse else k), peers + 1) * split + low)

    def copy_to(k, j):
        return pltpu.make_async_remote_copy(
            src_ref=send_ref.at[j],
            dst_ref=arrive_ref.at[k - 1, j],
            send_sem=send_sem.at[k - 1, j],
            recv_sem=arrive_sem.at[k - 1, j],
            device_id=other(k),
            device_id_type=pl.DeviceIdType.MESH,
        )

    @pl.when(tile == 0)
    def _():
        if peers:
            barrier = pltpu.get_barrier_semaphore()
            for k in range(1, peers + 1):
                pl.semaphore_signal(
                    barrier, inc=1, device_id=other(k), device_id_type=pl.DeviceIdType.MESH
                )
        spread(coef_ref, first, spread_ref, steps, states)

    rates = [jnp.broadcast_to(rate_ref[n : n + 1, :], (subs, lanes)) for n in range(states)]

    def one(turn, carry):
        s = steps - 1 - turn if reverse else turn
        total, held = carry
        step = delta_ref[pl.ds(s, subs, stride=steps), :] + reset_ref[pl.ds(s, subs, stride=steps), :]
        drive = drive_ref[pl.ds(s, subs, stride=steps), :]
        after = []
        for n in range(states):
            factor = jnp.exp2(step * rates[n])
            if reverse:
                after.append(factor * (held[n] + spread_ref[s, n] * drive))
            else:
                after.append(factor * held[n] + spread_ref[s, n] * drive)
        return total + step, tuple(after)

    zero = jnp.zeros((subs, lanes), jnp.float32)
    total, held = lax.fori_loop(0, steps, one, (zero, (zero,) * states), unroll=2)
    last = 0 if reverse else subs - 1
    for n in range(states):
        grow, state = chain_rows(jnp.exp2(total * rates[n]), held[n], reverse)
        grow_ref[n] = grow
        state_ref[n] = state
        if peers:
            send_ref[tile, n : n + 1] = grow[last : last + 1]
            send_ref[tile, states + n : states + n + 1] = state[last : last + 1]
    if not peers:
        enter_ref[...] = jnp.zeros_like(enter_ref)
        return

    @pl.when(tile == 0)
    def _():
        pl.semaphore_wait(pltpu.get_barrier_semaphore(), peers)

    for k in range(1, peers + 1):
        copy_to(k, tile).start()

    @pl.when(tile == tiles - 1)
    def _():
        for j in range(enter_ref.shape[1] // lanes):
            total = jnp.zeros((states, lanes), jnp.float32)
            for k in range(peers, 0, -1):
                copy_to(k, j).wait()
                piece = arrive_ref[k - 1, j]
                has = high + k <= peers if reverse else high >= k
                total = jnp.where(has, piece[states:] + piece[:states] * total, 0.0)
            enter_ref[:, j * lanes : (j + 1) * lanes] = total


def scan_ends(delta, reset, drive, coef, rate, first, reverse, peers):
    row_count, width = delta.shape
    states = rate.shape[0]
    steps = row_count // subs
    tiles = width // lanes
    column = pl.BlockSpec((row_count, lanes), lambda j: (0, j))
    whole = pl.BlockSpec((row_count, lanes), lambda j: (0, 0))
    ends = pl.BlockSpec((states, subs, lanes), lambda j: (0, 0, j))
    params = dict(vmem_limit_bytes=48 << 20)
    if peers:
        params.update(collective_id=2 if reverse else 1, has_side_effects=True)
    slots = max(peers, 1)
    return pl.pallas_call(
        functools.partial(ends_kernel, first, reverse, states, steps, peers),
        grid=(tiles,),
        in_specs=[column, whole, column, whole, pl.BlockSpec((states, lanes), lambda j: (0, j))],
        out_specs=[ends, ends, pl.BlockSpec((states, width), lambda j: (0, 0))],
        out_shape=[jax.ShapeDtypeStruct((states, subs, width), jnp.float32)] * 2
        + [jax.ShapeDtypeStruct((states, width), jnp.float32)],
        scratch_shapes=[
            pltpu.VMEM((steps, states, subs, lanes), jnp.float32),
            pltpu.VMEM((tiles, 2 * states, lanes), jnp.float32),
            pltpu.VMEM((slots, tiles, 2 * states, lanes), jnp.float32),
            pltpu.SemaphoreType.DMA((slots, tiles)),
            pltpu.SemaphoreType.DMA((slots, tiles)),
        ],
        compiler_params=pltpu.CompilerParams(**params),
        cost_estimate=pl.CostEstimate(flops=1000, bytes_accessed=1000, transcendentals=0),
    )(delta, reset, drive, coef, rate)


def forward_kernel(first_in, first_out, states, steps, delta_ref, reset_ref, drive_ref, coef_ref, rate_ref, grow_ref, state_ref, enter_ref, y_ref, start_ref, hist_ref, in_ref, out_ref):
    @pl.when(pl.program_id(0) == 0)
    def _():
        spread(coef_ref, first_in, in_ref, steps, states)
        spread(coef_ref, first_out, out_ref, steps, states)

    rates = [jnp.broadcast_to(rate_ref[n : n + 1, :], (subs, lanes)) for n in range(states)]
    row = lax.broadcasted_iota(jnp.int32, (subs, lanes), 0)
    held = []
    for n in range(states):
        near_grow = jnp.where(row >= 1, pltpu.roll(grow_ref[n], 1, 0), 1.0)
        near_state = jnp.where(row >= 1, pltpu.roll(state_ref[n], 1, 0), 0.0)
        start = near_state + near_grow * jnp.broadcast_to(enter_ref[n : n + 1, :], (subs, lanes))
        start_ref[n] = start
        held.append(start)

    def one(s, held):
        step = delta_ref[pl.ds(s, subs, stride=steps), :] + reset_ref[pl.ds(s, subs, stride=steps), :]
        drive = drive_ref[pl.ds(s, subs, stride=steps), :]
        after = []
        y = jnp.zeros((subs, lanes), jnp.float32)
        for n in range(states):
            now = jnp.exp2(step * rates[n]) * held[n] + in_ref[s, n] * drive
            hist_ref[0, s, n] = now
            y = y + out_ref[s, n] * now
            after.append(now)
        y_ref[pl.ds(s, subs, stride=steps), :] = y
        return tuple(after)

    lax.fori_loop(0, steps, one, tuple(held), unroll=2)


def scan_forward(delta, reset, drive, coef, rate, grow, state, enter, first_in, first_out):
    row_count, width = delta.shape
    states = rate.shape[0]
    steps = row_count // subs
    tiles = width // lanes
    column = pl.BlockSpec((row_count, lanes), lambda j: (0, j))
    whole = pl.BlockSpec((row_count, lanes), lambda j: (0, 0))
    ends = pl.BlockSpec((states, subs, lanes), lambda j: (0, 0, j))
    per_state = pl.BlockSpec((states, lanes), lambda j: (0, j))
    return pl.pallas_call(
        functools.partial(forward_kernel, first_in, first_out, states, steps),
        grid=(tiles,),
        in_specs=[column, whole, column, whole, per_state, ends, ends, per_state],
        out_specs=[column, ends, pl.BlockSpec((1, steps, states, subs, lanes), lambda j: (j, 0, 0, 0, 0))],
        out_shape=[
            jax.ShapeDtypeStruct((row_count, width), jnp.float32),
            jax.ShapeDtypeStruct((states, subs, width), jnp.float32),
            jax.ShapeDtypeStruct((tiles, steps, states, subs, lanes), jnp.float32),
        ],
        scratch_shapes=[pltpu.VMEM((steps, states, subs, lanes), jnp.float32)] * 2,
        compiler_params=pltpu.CompilerParams(vmem_limit_bytes=48 << 20),
        cost_estimate=pl.CostEstimate(flops=1000, bytes_accessed=1000, transcendentals=0),
    )(delta, reset, drive, coef, rate, grow, state, enter)


def backward_kernel(first_in, first_out, states, steps, delta_ref, reset_ref, drive_ref, dy_ref, coef_ref, rate_ref, start_ref, hist_ref, grow_ref, state_ref, enter_ref, q_ref, r_ref, rsum_ref, din_ref, dout_ref, in_ref, out_ref, ain_ref, aout_ref):
    tile = pl.program_id(0)

    @pl.when(tile == 0)
    def _():
        spread(coef_ref, first_in, in_ref, steps, states)
        spread(coef_ref, first_out, out_ref, steps, states)
        ain_ref[...] = jnp.zeros_like(ain_ref)
        aout_ref[...] = jnp.zeros_like(aout_ref)

    row = lax.broadcasted_iota(jnp.int32, (subs, lanes), 0)
    rates = [jnp.broadcast_to(rate_ref[n : n + 1, :], (subs, lanes)) for n in range(states)]
    later = []
    for n in range(states):
        near_grow = jnp.where(row < subs - 1, pltpu.roll(grow_ref[n], subs - 1, 0), 1.0)
        near_state = jnp.where(row < subs - 1, pltpu.roll(state_ref[n], subs - 1, 0), 0.0)
        later.append(near_state + near_grow * jnp.broadcast_to(enter_ref[n : n + 1, :], (subs, lanes)))

    def at(s, load_before, carry):
        later, sums = carry
        delta = delta_ref[pl.ds(s, subs, stride=steps), :]
        step = delta + reset_ref[pl.ds(s, subs, stride=steps), :]
        drive = drive_ref[pl.ds(s, subs, stride=steps), :]
        dy = dy_ref[pl.ds(s, subs, stride=steps), :]
        q = jnp.zeros((subs, lanes), jnp.float32)
        r = jnp.zeros((subs, lanes), jnp.float32)
        after, sums_after = [], []
        for n in range(states):
            d_state = out_ref[s, n] * dy + later[n]
            back = jnp.exp2(step * rates[n]) * d_state
            scaled = back * load_before(n)
            sums_after.append(sums[n] + scaled * delta)
            q = q + scaled * rates[n]
            r = r + d_state * in_ref[s, n]
            ain_ref[s, n] += d_state * drive
            aout_ref[s, n] += hist_ref[0, s, n] * dy
            after.append(back)
        q_ref[pl.ds(s, subs, stride=steps), :] = q * (1.0 / log2e)
        r_ref[pl.ds(s, subs, stride=steps), :] = r
        return tuple(after), tuple(sums_after)

    zero = jnp.zeros((subs, lanes), jnp.float32)

    def one(turn, carry):
        s = steps - 1 - turn
        return at(s, lambda n: hist_ref[0, s - 1, n], carry)

    carry = lax.fori_loop(0, steps - 1, one, (tuple(later), (zero,) * states))
    _, sums = at(0, lambda n: start_ref[n], carry)
    for n in range(states):
        rsum_ref[n : n + 1, :] = jnp.sum(sums[n] * rates[n], 0, keepdims=True) * (1.0 / log2e)

    @pl.when(tile == pl.num_programs(0) - 1)
    def _():
        ones = jnp.ones((subs, lanes), jnp.bfloat16)

        def fold(ref, s):
            values = ref[s].reshape(states * subs, lanes)
            high = values.astype(jnp.bfloat16)
            low = (values - high.astype(jnp.float32)).astype(jnp.bfloat16)
            dims = (((1,), (1,)), ((), ()))
            return lax.dot_general(ones, high, dims, preferred_element_type=jnp.float32) + lax.dot_general(ones, low, dims, preferred_element_type=jnp.float32)

        def both(s, _):
            din_ref[pl.ds(s, 1), :] = fold(ain_ref, s)[:1]
            dout_ref[pl.ds(s, 1), :] = fold(aout_ref, s)[:1]
            return 0

        lax.fori_loop(0, steps, both, 0)


def scan_backward(delta, reset, drive, dy, coef, rate, start, hist, grow, state, enter, first_in, first_out):
    row_count, width = delta.shape
    states = rate.shape[0]
    steps = row_count // subs
    tiles = width // lanes
    column = pl.BlockSpec((row_count, lanes), lambda j: (0, j))
    whole = pl.BlockSpec((row_count, lanes), lambda j: (0, 0))
    ends = pl.BlockSpec((states, subs, lanes), lambda j: (0, 0, j))
    per_state = pl.BlockSpec((states, lanes), lambda j: (0, j))
    folded = pl.BlockSpec((steps, states * subs), lambda j: (0, 0))
    q, r, rsum, din, dout = pl.pallas_call(
        functools.partial(backward_kernel, first_in, first_out, states, steps),
        grid=(tiles,),
        in_specs=[column, whole, column, column, whole, per_state, ends, pl.BlockSpec((1, steps, states, subs, lanes), lambda j: (j, 0, 0, 0, 0)), ends, ends, per_state],
        out_specs=[column, column, per_state, folded, folded],
        out_shape=[
            jax.ShapeDtypeStruct((row_count, width), jnp.float32),
            jax.ShapeDtypeStruct((row_count, width), jnp.float32),
            jax.ShapeDtypeStruct((states, width), jnp.float32),
            jax.ShapeDtypeStruct((steps, states * subs), jnp.float32),
            jax.ShapeDtypeStruct((steps, states * subs), jnp.float32),
        ],
        scratch_shapes=[pltpu.VMEM((steps, states, subs, lanes), jnp.float32)] * 4,
        compiler_params=pltpu.CompilerParams(vmem_limit_bytes=56 << 20),
        cost_estimate=pl.CostEstimate(flops=1000, bytes_accessed=1000, transcendentals=0),
    )(delta, reset, drive, dy, coef, rate, start, hist, grow, state, enter)

    def unfold(folded_rows):
        return folded_rows.reshape(steps, states, subs).transpose(2, 0, 1).reshape(row_count, states)

    return q, r, rsum, unfold(din), unfold(dout)


def experts_kernel(
    expert_count, second_ref, routed_ref, route_ref, *refs
):
    weights_in, weights_out = refs[:expert_count], refs[expert_count : 2 * expert_count]
    sums_ref, grads_ref, y_ref, d_ref = refs[2 * expert_count :]
    step = pl.program_id(0)
    blocks, hidden, model_width = weights_in[0].shape
    rows = blocks * hidden

    @pl.when(step == 0)
    def _():
        y_ref[...] = jnp.zeros_like(y_ref)
        d_ref[...] = jnp.zeros_like(d_ref)

    up = jnp.concatenate([w[...].reshape(rows, model_width) for w in weights_in], 0)
    down = jnp.concatenate([w[...].reshape(rows, model_width) for w in weights_out], 0)
    second, routed = second_ref[...], routed_ref[...]
    pre = matmul_nt(second, up)
    column = lax.broadcasted_iota(jnp.int32, (1, expert_count * rows), 1)
    owner = jnp.zeros_like(column)
    for e in range(1, expert_count):
        owner = owner + (column >= e * rows).astype(jnp.int32)
    picked = route_ref[:, :1] == owner.astype(jnp.float32)
    half = 0.5 + 0.5 * lax.erf(pre * (0.5**0.5))
    bell = jnp.exp(-0.5 * pre * pre) * (1.0 / (2.0 * math.pi) ** 0.5)
    act = low_bits(jnp.where(picked, pre * half, 0.0))
    d_pre = low_bits(jnp.where(picked, matmul_nt(routed, down) * (half + pre * bell), 0.0))
    y_ref[...] += matmul(act, down)
    d_ref[...] += matmul(d_pre, up)
    grad_up = low_bits(matmul_tn(d_pre, second))
    grad_down = low_bits(matmul_tn(act, routed))
    for e in range(expert_count):
        for b in range(blocks):
            at = e * rows + b * hidden
            grads_ref[b, e * hidden : (e + 1) * hidden] = grad_up[at : at + hidden]
            to = (expert_count + e) * hidden
            grads_ref[b, to : to + hidden] = grad_down[at : at + hidden]

    @pl.when(step == pl.num_programs(0) - 1)
    def _():
        sums_ref[:, :model_width] = low_bits(y_ref[...])
        sums_ref[:, model_width:] = low_bits(d_ref[...])


def run_experts(second, routed, route_lanes, parts, hidden):
    row_count, model_width = second.shape
    expert_count = len(parts) // 2
    block_count = parts[0][0].shape[0]
    blocks = 2
    fixed = pl.BlockSpec((row_count, model_width), lambda i: (0, 0))

    def spec(first):
        return pl.BlockSpec((blocks, hidden, model_width), lambda i: (i, first // hidden, 0))

    return pl.pallas_call(
        functools.partial(experts_kernel, expert_count),
        grid=(block_count // blocks,),
        in_specs=[fixed, fixed, pl.BlockSpec((row_count, lanes), lambda i: (0, 0))]
        + [spec(first) for _, first in parts],
        out_specs=[
            pl.BlockSpec((row_count, 2 * model_width), lambda i: (0, 0)),
            pl.BlockSpec((blocks, 2 * expert_count * hidden, model_width), lambda i: (i, 0, 0)),
        ],
        out_shape=[
            jax.ShapeDtypeStruct((row_count, 2 * model_width), jnp.bfloat16),
            jax.ShapeDtypeStruct(
                (block_count, 2 * expert_count * hidden, model_width), jnp.bfloat16
            ),
        ],
        scratch_shapes=[pltpu.VMEM((row_count, model_width), jnp.float32)] * 2,
        compiler_params=pltpu.CompilerParams(vmem_limit_bytes=56 << 20),
        cost_estimate=pl.CostEstimate(flops=1000, bytes_accessed=1000, transcendentals=0),
    )(second, routed, route_lanes, *[w for w, _ in parts])


def norm_rows(values, gain_row):
    return values * lax.rsqrt(jnp.mean(values * values, -1, keepdims=True) + eps_norm) * gain_row


def matmul(first_op, second_op):
    return jnp.dot(first_op, second_op, preferred_element_type=jnp.float32)


def matmul_nt(first_op, second_op):
    return lax.dot_general(
        first_op, second_op, (((1,), (1,)), ((), ())), preferred_element_type=jnp.float32
    )


def matmul_tn(first_op, second_op):
    return lax.dot_general(
        first_op, second_op, (((0,), (0,)), ((), ())), preferred_element_type=jnp.float32
    )


def low_bits(value):
    return value.astype(jnp.bfloat16)


def swap_low(value, k):
    count = lax.axis_size("seq")
    return lax.ppermute(value, "seq", [(s, s ^ k) for s in range(count)])


def turn_high(value, k):
    count = lax.axis_size("seq")
    return lax.ppermute(value, "seq", [(s, (s + split * k) % count) for s in range(count)])


def from_high(value, k):
    count = lax.axis_size("seq")
    pairs = [(s, s + split * k) for s in range(count) if 0 <= s + split * k < count]
    return lax.ppermute(value, "seq", pairs)


def swap_core(value):
    return lax.ppermute(value, "grp", [(0, 1), (1, 0)])


def high_groups():
    count = lax.axis_size("seq")
    return [[h * split + l for h in range(count // split)] for l in range(split)]


def gather_low(value):
    low = lax.axis_index("seq") % split
    first_bit, second_bit = low % 2 == 1, low // 2 == 1
    own, one, two, three = [value] + [swap_low(value, k) for k in range(1, split)]
    a, b = jnp.where(first_bit, one, own), jnp.where(first_bit, own, one)
    c, d = jnp.where(first_bit, three, two), jnp.where(first_bit, two, three)
    pieces = [
        jnp.where(second_bit, c, a),
        jnp.where(second_bit, d, b),
        jnp.where(second_bit, a, c),
        jnp.where(second_bit, b, d),
    ]
    return jnp.concatenate(pieces, 0)


def scatter_low(partial):
    low = lax.axis_index("seq") % split
    rows = partial.shape[0] // split

    def block(at):
        return lax.dynamic_slice_in_dim(partial, at * rows, rows, 0)

    arrived = [swap_low(low_bits(block(low ^ k)), k) for k in range(1, split)]
    return sum(a.astype(jnp.float32) for a in [block(low)] + arrived)


def sum_low(partial):
    low_partial = low_bits(partial)
    arrived = [swap_low(low_partial, k) for k in range(1, split)]
    return partial + sum(a.astype(jnp.float32) for a in arrived)


def gather_high(value):
    high_count = lax.axis_size("seq") // split
    if high_count > 4:
        return lax.all_gather(value, "seq", axis_index_groups=high_groups())
    high = lax.axis_index("seq") // split
    turned = [turn_high(value, k) for k in range(1, high_count)]
    line = turned[::-1] + [value] + turned[::-1]
    return lax.dynamic_slice_in_dim(jnp.stack(line), high_count - 1 - high, high_count, 0)


def gather_core(own):
    full = jnp.stack([own, swap_core(own)])
    return full.reshape((-1,) + own.shape[1:])


def after(value, *others):
    return lax.optimization_barrier((value,) + others)[0]


def pad_rows(value, rows):
    return jnp.pad(value, ((0, rows - value.shape[0]), (0, 0)))


def fold_core(partial, rows):
    high_count = lax.axis_size("seq") // split
    blocks = partial.reshape(2, high_count, rows, partial.shape[-1])
    arrived = swap_core(low_bits(blocks[1]))
    return low_bits(blocks[0].astype(jnp.float32) + arrived.astype(jnp.float32))


def fold_high(mine):
    high_count = lax.axis_size("seq") // split
    if high_count > 4:
        return lax.psum_scatter(
            mine.astype(jnp.float32), "seq", scatter_dimension=0, axis_index_groups=high_groups()
        )
    high = lax.axis_index("seq") // split

    def block(at):
        return lax.dynamic_index_in_dim(mine, at % high_count, 0, False)

    arrived = [turn_high(block(high + k), k) for k in range(1, high_count)]
    return sum(a.astype(jnp.float32) for a in [block(high)] + arrived)


def sum_all(partial):
    high_count = lax.axis_size("seq") // split
    total = partial + swap_core(partial)
    step = 1
    while step < high_count * split:
        total = total + swap_low(total, step)
        step *= 2
    return total


def entering_state(grow, state, reverse):
    high_count = lax.axis_size("seq") // split
    packed = jnp.concatenate([grow, state], 0)
    states = grow.shape[0]
    if high_count > 4:
        high = lax.axis_index("seq") // split
        every = lax.all_gather(packed, "seq", axis_index_groups=high_groups())

        def one(turn, total):
            source = high_count - 1 - turn if reverse else turn
            piece = lax.dynamic_index_in_dim(every, source, 0, False)
            return piece[states:] + piece[:states] * total

        ahead = high_count - 1 - high if reverse else high
        return lax.fori_loop(0, ahead, one, jnp.zeros_like(state))
    total = jnp.zeros_like(state)
    near = [from_high(packed, -k if reverse else k) for k in range(1, high_count)]
    for piece in near[::-1]:
        total = piece[states:] + piece[:states] * total
    return total


def shards(
    tokens,
    routes,
    lengths,
    grad_out,
    norm_gains,
    router,
    in_weight,
    conv_weight,
    x_weight,
    dt_weight,
    dt_bias,
    a_log,
    skip_gain,
    out_weight,
    expert_in,
    expert_out,
):
    channels, tap_count = conv_weight.shape
    dt_rank = dt_weight.shape[1]
    states = a_log.shape[1]
    expert_count, hidden, model_width = expert_in.shape
    own_rows = tokens.shape[0]
    row_count = own_rows * split
    high_count = lax.axis_size("seq") // split
    low = lax.axis_index("seq") % split
    high = lax.axis_index("seq") // split
    coef_count = dt_rank + 2 * states
    channel_rows = -(-channels // 16) * 16
    width = 2 * high_count * channel_rows
    hidden_rows = expert_count * hidden
    small_width = -(-(coef_count + dt_rank + tap_count + 2 + states) // lanes) * lanes

    small = jnp.concatenate(
        [x_weight, dt_weight, conv_weight, dt_bias[:, None], a_log, skip_gain[:, None]], 1
    )
    small = jnp.pad(small, ((0, 0), (0, small_width - small.shape[1])))
    inputs = tokens.astype(jnp.float32)
    edge = 16
    halo = from_high(tokens[own_rows - edge :], 1).astype(jnp.float32)
    normed_own = low_bits(norm_rows(jnp.concatenate([inputs, halo], 0), norm_gains[0]))
    payload = pad_rows(jnp.concatenate([in_weight[0], small], 1), channel_rows)
    first_full = gather_core(gather_high(payload)).reshape(width, -1)
    normed = gather_low(normed_own).reshape(split, own_rows + edge, model_width)
    normed_edge = normed[split - 1, own_rows:]
    normed = normed[:, :own_rows].reshape(row_count, model_width)
    first_in, small_full = first_full[:, :model_width], first_full[:, model_width:]
    x_full = small_full[:, :coef_count]
    at = coef_count
    dt_full = small_full[:, at : at + dt_rank]
    at = at + dt_rank
    conv_taps = small_full[:, at : at + tap_count].astype(jnp.float32)
    at = at + tap_count
    bias_vals = small_full[:, at].astype(jnp.float32)
    at = at + 1
    decay_rate = -jnp.exp(small_full[:, at : at + states].astype(jnp.float32)).T
    at = at + states
    skip_vals = small_full[:, at].astype(jnp.float32)
    rate = decay_rate * log2e

    early_part = jnp.concatenate(
        [
            pad_rows(in_weight[1], channel_rows),
            pad_rows(out_weight, channel_rows),
            expert_in[0],
        ],
        0,
    )
    early_part = gather_high(after(early_part, first_full))
    routed_part = jnp.concatenate(
        [grad_out, routes[:, None].astype(jnp.float32) * jnp.ones((1, lanes), jnp.float32)], 1
    )
    routed_part = gather_low(after(low_bits(routed_part), normed))
    grad_rows = routed_part[:, :model_width]
    routes_all = routed_part[:, model_width : model_width + 1].astype(jnp.int32)
    late_part = jnp.concatenate(
        [expert_in[1:].reshape(-1, model_width), expert_out.reshape(-1, model_width)], 0
    )

    place = high * row_count + jnp.arange(row_count, dtype=jnp.int32)
    first_len = lengths[0, 0]
    offset = jnp.where(place < first_len, place, place - first_len)
    reset = jnp.where(offset[:, None] == 0, 1e30, 0.0) * jnp.ones((1, lanes), jnp.float32)
    valid_rows = [
        (offset >= tap_count - 1 - k).astype(jnp.float32)[:, None] for k in range(tap_count)
    ]

    all_input = low_bits(matmul_nt(jnp.concatenate([normed_edge, normed], 0), first_in))
    conv_input = all_input[edge:]
    window = all_input[edge - (tap_count - 1) :].astype(jnp.float32)
    conv_sum = sum(
        conv_taps[:, k] * window[k : k + row_count] * valid_rows[k] for k in range(tap_count)
    )
    mixed_in = low_bits(jax.nn.silu(conv_sum))
    mixed_val = mixed_in.astype(jnp.float32)
    coef_pad = jnp.pad(x_full, ((0, 0), (0, lanes - coef_count)))
    coef_rows = sum_low(matmul(mixed_in, coef_pad))
    dt_low = low_bits(coef_rows[:, :dt_rank])
    dt_pre = matmul_nt(dt_low, dt_full) + bias_vals
    step_size = jax.nn.softplus(dt_pre)
    drive = step_size * mixed_val
    first_b, first_c = dt_rank, dt_rank + states
    peers = high_count - 1 if high_count <= 4 else 0
    grow, state, enter = scan_ends(
        step_size, reset, drive, coef_rows, rate, first_b, False, peers
    )
    slice_grow = grow[:, subs - 1]
    if not peers:
        enter = entering_state(slice_grow, state[:, subs - 1], False)
    enter, early_part, late_part = lax.optimization_barrier((enter, early_part, late_part))
    early_full = gather_core(early_part)
    late_part = gather_high(late_part)
    y_scan, start, hist = scan_forward(
        step_size, reset, drive, coef_rows, rate, grow, state, enter, first_b, first_c
    )
    y_scan, early_full = lax.optimization_barrier((y_scan, early_full))
    second_in = early_full[:, :channel_rows].reshape(width, model_width)
    out_full = early_full[:, channel_rows : 2 * channel_rows].reshape(width, model_width)
    z_gate = matmul_nt(normed, second_in)
    y_value = y_scan + skip_vals * mixed_val
    gate_z = jax.nn.silu(z_gate)
    gated = low_bits(y_value * gate_z)
    resid = inputs + scatter_low(matmul(gated, out_full))

    resid, late_part = lax.optimization_barrier((resid, late_part))
    late_full = gather_core(late_part)
    second_own = low_bits(norm_rows(resid, norm_gains[1]))
    second = gather_low(second_own)

    def gate_of(rows, row_routes):
        logits = matmul(rows, router)
        chosen = row_routes == jnp.arange(expert_count, dtype=jnp.int32)[None, :]
        chosen = chosen.astype(jnp.float32)
        probs = jax.nn.softmax(logits, -1)
        return logits, chosen, jnp.sum(probs * chosen, -1, keepdims=True)

    gate_rows = gate_of(second, routes_all)[2]
    routed = low_bits(gate_rows * grad_rows.astype(jnp.float32))
    parts = [(early_full[:, 2 * channel_rows :], 0)]
    parts += [(late_full, e * hidden) for e in range(2 * expert_count - 1)]
    step_rows = hidden
    if hidden % 16:
        step_rows = 2 * high_count * hidden // 4
        parts = [
            (w[:, a : a + hidden].reshape(4, step_rows, model_width), 0) for w, a in parts
        ]
    sums, hidden_grads = run_experts(
        second, routed, routed_part[:, model_width:].astype(jnp.float32), parts, step_rows
    )
    if hidden % 16:
        pieces = hidden_grads.reshape(4, 2 * expert_count, -1, hidden, model_width)
        hidden_grads = pieces.swapaxes(1, 2).reshape(-1, 2 * hidden_rows, model_width)
    hidden_mine = fold_core(hidden_grads, 2 * hidden_rows)
    sums = scatter_low(sums)
    expert_y, d_second = sums[:, :model_width], sums[:, model_width:]
    d_second, hidden_mine = lax.optimization_barrier((d_second, hidden_mine))
    cut = hidden_rows * 2 // 3
    hidden_early = fold_high(hidden_mine[:, :cut])
    hidden_mine = hidden_mine[:, cut:]
    logits, chosen, gate_own = gate_of(second_own, routes[:, None])
    mixed_out = low_bits(resid + gate_own * expert_y)
    d_gate = jnp.sum(expert_y * grad_out, -1, keepdims=True)
    _, soft_pull = jax.vjp(lambda v: jax.nn.softmax(v, -1), logits)
    d_logits = low_bits(soft_pull(chosen * d_gate)[0])
    grad_router = matmul_tn(d_logits, second_own)
    d_second = d_second + matmul_nt(d_logits, router)
    _, norm_pull_two = jax.vjp(norm_rows, resid, norm_gains[1])
    d_resid_norm, d_gain_two = norm_pull_two(d_second)
    d_resid = grad_out + d_resid_norm

    g_branch = gather_low(low_bits(d_resid))
    d_gated = matmul_nt(g_branch, out_full)
    d_y = d_gated * gate_z
    _, silu_pull = jax.vjp(jax.nn.silu, z_gate)
    d_z = silu_pull(d_gated * y_value)[0]
    gate_grads = jnp.concatenate(
        [matmul_tn(low_bits(d_z), normed), matmul_tn(gated, g_branch)], 1
    )
    gate_mine = fold_core(gate_grads, channel_rows)
    back_grow, back_state, back_enter = scan_ends(
        step_size, reset, d_y, coef_rows, rate, first_c, True, peers
    )
    if not peers:
        back_enter = entering_state(slice_grow, back_state[:, 0], True)
    back_enter, hidden_mine = lax.optimization_barrier((back_enter, hidden_mine))
    hidden_late = fold_high(hidden_mine)
    scaled_sum, in_sum, rate_sum, d_in_coef, d_out_coef = scan_backward(
        step_size,
        reset,
        drive,
        d_y,
        coef_rows,
        rate,
        start,
        hist,
        back_grow,
        back_state,
        back_enter,
        first_b,
        first_c,
    )
    d_step = scaled_sum + in_sum * mixed_val
    d_mixed = skip_vals * d_y + in_sum * step_size
    grad_skip = jnp.sum(d_y * mixed_val, 0)
    d_dt = d_step * jax.nn.sigmoid(dt_pre)
    grad_bias = jnp.sum(d_dt, 0)
    g_dt = low_bits(d_dt)
    grad_dt = matmul_tn(g_dt, dt_low)
    part_coef = jnp.concatenate([matmul(g_dt, dt_full), d_in_coef, d_out_coef], 1)
    part_coef = jnp.pad(part_coef, ((0, 0), (0, lanes - coef_count)))
    g_coef = low_bits(sum_low(part_coef)[:, :coef_count])
    grad_x = matmul_tn(mixed_in, g_coef)
    d_mixed = d_mixed + matmul_nt(g_coef, x_full)
    _, conv_pull = jax.vjp(jax.nn.silu, conv_sum)
    d_conv = conv_pull(d_mixed)[0]
    grad_conv = jnp.stack(
        [jnp.sum(d_conv * valid_rows[k] * window[k : k + row_count], 0) for k in range(tap_count)],
        1,
    )
    d_window = sum(
        jnp.pad(conv_taps[:, k] * d_conv * valid_rows[k], ((k, tap_count - 1 - k), (0, 0)))
        for k in range(tap_count)
    )
    from_next = from_high(d_window[: tap_count - 1], -1)
    d_input = d_window[tap_count - 1 :] + jnp.pad(
        from_next, ((row_count - (tap_count - 1), 0), (0, 0))
    )
    g_in = low_bits(d_input)
    g_in, hidden_late, gate_mine = lax.optimization_barrier((g_in, hidden_late, gate_mine))
    hidden_own = jnp.concatenate([hidden_early, hidden_late], 0)
    gate_own_grads = fold_high(gate_mine)
    g_z = low_bits(d_z)
    d_normed = scatter_low(matmul(g_in, first_in) + matmul(g_z, second_in))
    _, norm_pull_one = jax.vjp(norm_rows, inputs, norm_gains[0])
    d_inputs, d_gain_one = norm_pull_one(d_normed)
    grad_tokens = d_resid + d_inputs

    rest = jnp.concatenate(
        [grad_x, grad_dt, grad_conv, grad_bias[:, None], rate_sum.T, grad_skip[:, None]], 1
    )
    rest = jnp.pad(rest, ((0, 0), (0, small_width - rest.shape[1])))
    first_own = fold_high(
        fold_core(jnp.concatenate([matmul_tn(g_in, normed), rest], 1), channel_rows)
    )[:channels]
    rest_own = first_own[:, model_width:]
    gate_own_grads = gate_own_grads[:channels]
    sums = sum_all(jnp.concatenate([jnp.stack([d_gain_one, d_gain_two]), grad_router], 0))
    ends = [0]
    for count in (coef_count, dt_rank, tap_count, 1, states, 1):
        ends.append(ends[-1] + count)
    grad_x, grad_dt, grad_conv, grad_bias, grad_alog, grad_skip = (
        rest_own[:, a:b] for a, b in zip(ends[:-1], ends[1:], strict=True)
    )
    return (
        mixed_out,
        grad_tokens,
        sums[:2],
        sums[2:].T,
        jnp.stack([first_own[:, :model_width], gate_own_grads[:, :model_width]]),
        grad_conv,
        grad_x,
        grad_dt,
        grad_bias[:, 0],
        grad_alog,
        grad_skip[:, 0],
        gate_own_grads[:, model_width:],
        hidden_own[:hidden_rows].reshape(expert_count, hidden, model_width),
        hidden_own[hidden_rows:].reshape(expert_count, hidden, model_width),
    )


def solution(mesh):
    both = ("grp", "seq")
    in_specs = (
        P(both, None),
        P(both),
        P("grp", None),
        P(both, None),
        P(),
        P(),
        P(None, both, None),
        P(both, None),
        P(both, None),
        P(both, None),
        P(both),
        P(both, None),
        P(both),
        P(both, None),
        P(None, both, None),
        P(None, both, None),
    )
    out_specs = (
        P(both, None),
        P(both, None),
        P(),
        P(),
        P(None, both, None),
        P(both, None),
        P(both, None),
        P(both, None),
        P(both),
        P(both, None),
        P(both),
        P(both, None),
        P(None, both, None),
        P(None, both, None),
    )
    return jax.shard_map(shards, mesh=mesh, in_specs=in_specs, out_specs=out_specs, check_vma=False)
```

```python
import functools
import math

import jax
import jax.numpy as jnp
from jax import lax
from jax.experimental import pallas as pl
from jax.experimental.pallas import tpu as pltpu
from jax.sharding import PartitionSpec as P

eps_norm = 1e-05
split = 4
lanes = 128
subs = 8
log2e = 1.4426950408889634


def spread(coef_ref, first, spread_ref, steps, states):
    def one(s, _):
        rows = coef_ref[pl.ds(s, subs, stride=steps), :]
        for n in range(states):
            spread_ref[s, n] = jnp.broadcast_to(rows[:, first + n : first + n + 1], (subs, lanes))
        return 0

    lax.fori_loop(0, steps, one, 0, unroll=8)


def chain_rows(grow, state, reverse):
    row = lax.broadcasted_iota(jnp.int32, (subs, lanes), 0)
    shift = 1
    while shift < subs:
        turn = subs - shift if reverse else shift
        has = row < subs - shift if reverse else row >= shift
        near_grow = jnp.where(has, pltpu.roll(grow, turn, 0), 1.0)
        near_state = jnp.where(has, pltpu.roll(state, turn, 0), 0.0)
        state = state + grow * near_state
        grow = grow * near_grow
        shift *= 2
    return grow, state


def ends_kernel(
    first, reverse, states, steps, peers,
    delta_ref, reset_ref, drive_ref, coef_ref, rate_ref,
    grow_ref, state_ref, enter_ref,
    spread_ref, send_ref, arrive_ref, send_sem, arrive_sem,
):
    tile = pl.program_id(0)
    tiles = pl.num_programs(0)
    place = lax.axis_index("seq")
    high, low, core = place // split, place % split, lax.axis_index("grp")

    def other(k):
        return (core, lax.rem(high + (peers + 1 - k if reverse else k), peers + 1) * split + low)

    def copy_to(k, j):
        return pltpu.make_async_remote_copy(
            src_ref=send_ref.at[j],
            dst_ref=arrive_ref.at[k - 1, j],
            send_sem=send_sem.at[k - 1, j],
            recv_sem=arrive_sem.at[k - 1, j],
            device_id=other(k),
            device_id_type=pl.DeviceIdType.MESH,
        )

    @pl.when(tile == 0)
    def _():
        if peers:
            barrier = pltpu.get_barrier_semaphore()
            for k in range(1, peers + 1):
                pl.semaphore_signal(
                    barrier, inc=1, device_id=other(k), device_id_type=pl.DeviceIdType.MESH
                )
        spread(coef_ref, first, spread_ref, steps, states)

    rates = [jnp.broadcast_to(rate_ref[n : n + 1, :], (subs, lanes)) for n in range(states)]

    def one(turn, carry):
        s = steps - 1 - turn if reverse else turn
        total, held = carry
        step = delta_ref[pl.ds(s, subs, stride=steps), :] + reset_ref[pl.ds(s, subs, stride=steps), :]
        drive = drive_ref[pl.ds(s, subs, stride=steps), :]
        after = []
        for n in range(states):
            factor = jnp.exp2(step * rates[n])
            if reverse:
                after.append(factor * (held[n] + spread_ref[s, n] * drive))
            else:
                after.append(factor * held[n] + spread_ref[s, n] * drive)
        return total + step, tuple(after)

    zero = jnp.zeros((subs, lanes), jnp.float32)
    total, held = lax.fori_loop(0, steps, one, (zero, (zero,) * states), unroll=2)
    last = 0 if reverse else subs - 1
    for n in range(states):
        grow, state = chain_rows(jnp.exp2(total * rates[n]), held[n], reverse)
        grow_ref[n] = grow
        state_ref[n] = state
        if peers:
            send_ref[tile, n : n + 1] = grow[last : last + 1]
            send_ref[tile, states + n : states + n + 1] = state[last : last + 1]
    if not peers:
        enter_ref[...] = jnp.zeros_like(enter_ref)
        return

    @pl.when(tile == 0)
    def _():
        pl.semaphore_wait(pltpu.get_barrier_semaphore(), peers)

    for k in range(1, peers + 1):
        copy_to(k, tile).start()

    @pl.when(tile == tiles - 1)
    def _():
        for j in range(enter_ref.shape[1] // lanes):
            total = jnp.zeros((states, lanes), jnp.float32)
            for k in range(peers, 0, -1):
                copy_to(k, j).wait()
                piece = arrive_ref[k - 1, j]
                has = high + k <= peers if reverse else high >= k
                total = jnp.where(has, piece[states:] + piece[:states] * total, 0.0)
            enter_ref[:, j * lanes : (j + 1) * lanes] = total


def scan_ends(delta, reset, drive, coef, rate, first, reverse, peers):
    row_count, width = delta.shape
    states = rate.shape[0]
    steps = row_count // subs
    tiles = width // lanes
    column = pl.BlockSpec((row_count, lanes), lambda j: (0, j))
    whole = pl.BlockSpec((row_count, lanes), lambda j: (0, 0))
    ends = pl.BlockSpec((states, subs, lanes), lambda j: (0, 0, j))
    params = dict(vmem_limit_bytes=48 << 20)
    if peers:
        params.update(collective_id=2 if reverse else 1, has_side_effects=True)
    slots = max(peers, 1)
    return pl.pallas_call(
        functools.partial(ends_kernel, first, reverse, states, steps, peers),
        grid=(tiles,),
        in_specs=[column, whole, column, whole, pl.BlockSpec((states, lanes), lambda j: (0, j))],
        out_specs=[ends, ends, pl.BlockSpec((states, width), lambda j: (0, 0))],
        out_shape=[jax.ShapeDtypeStruct((states, subs, width), jnp.float32)] * 2
        + [jax.ShapeDtypeStruct((states, width), jnp.float32)],
        scratch_shapes=[
            pltpu.VMEM((steps, states, subs, lanes), jnp.float32),
            pltpu.VMEM((tiles, 2 * states, lanes), jnp.float32),
            pltpu.VMEM((slots, tiles, 2 * states, lanes), jnp.float32),
            pltpu.SemaphoreType.DMA((slots, tiles)),
            pltpu.SemaphoreType.DMA((slots, tiles)),
        ],
        compiler_params=pltpu.CompilerParams(**params),
        cost_estimate=pl.CostEstimate(flops=1000, bytes_accessed=1000, transcendentals=0),
    )(delta, reset, drive, coef, rate)


def forward_kernel(first_in, first_out, states, steps, delta_ref, reset_ref, drive_ref, coef_ref, rate_ref, grow_ref, state_ref, enter_ref, y_ref, start_ref, hist_ref, in_ref, out_ref):
    @pl.when(pl.program_id(0) == 0)
    def _():
        spread(coef_ref, first_in, in_ref, steps, states)
        spread(coef_ref, first_out, out_ref, steps, states)

    rates = [jnp.broadcast_to(rate_ref[n : n + 1, :], (subs, lanes)) for n in range(states)]
    row = lax.broadcasted_iota(jnp.int32, (subs, lanes), 0)
    held = []
    for n in range(states):
        near_grow = jnp.where(row >= 1, pltpu.roll(grow_ref[n], 1, 0), 1.0)
        near_state = jnp.where(row >= 1, pltpu.roll(state_ref[n], 1, 0), 0.0)
        start = near_state + near_grow * jnp.broadcast_to(enter_ref[n : n + 1, :], (subs, lanes))
        start_ref[n] = start
        held.append(start)

    def one(s, held):
        step = delta_ref[pl.ds(s, subs, stride=steps), :] + reset_ref[pl.ds(s, subs, stride=steps), :]
        drive = drive_ref[pl.ds(s, subs, stride=steps), :]
        after = []
        y = jnp.zeros((subs, lanes), jnp.float32)
        for n in range(states):
            now = jnp.exp2(step * rates[n]) * held[n] + in_ref[s, n] * drive
            hist_ref[0, s, n] = now
            y = y + out_ref[s, n] * now
            after.append(now)
        y_ref[pl.ds(s, subs, stride=steps), :] = y
        return tuple(after)

    lax.fori_loop(0, steps, one, tuple(held), unroll=2)


def scan_forward(delta, reset, drive, coef, rate, grow, state, enter, first_in, first_out):
    row_count, width = delta.shape
    states = rate.shape[0]
    steps = row_count // subs
    tiles = width // lanes
    column = pl.BlockSpec((row_count, lanes), lambda j: (0, j))
    whole = pl.BlockSpec((row_count, lanes), lambda j: (0, 0))
    ends = pl.BlockSpec((states, subs, lanes), lambda j: (0, 0, j))
    per_state = pl.BlockSpec((states, lanes), lambda j: (0, j))
    return pl.pallas_call(
        functools.partial(forward_kernel, first_in, first_out, states, steps),
        grid=(tiles,),
        in_specs=[column, whole, column, whole, per_state, ends, ends, per_state],
        out_specs=[column, ends, pl.BlockSpec((1, steps, states, subs, lanes), lambda j: (j, 0, 0, 0, 0))],
        out_shape=[
            jax.ShapeDtypeStruct((row_count, width), jnp.float32),
            jax.ShapeDtypeStruct((states, subs, width), jnp.float32),
            jax.ShapeDtypeStruct((tiles, steps, states, subs, lanes), jnp.float32),
        ],
        scratch_shapes=[pltpu.VMEM((steps, states, subs, lanes), jnp.float32)] * 2,
        compiler_params=pltpu.CompilerParams(vmem_limit_bytes=48 << 20),
        cost_estimate=pl.CostEstimate(flops=1000, bytes_accessed=1000, transcendentals=0),
    )(delta, reset, drive, coef, rate, grow, state, enter)


def backward_kernel(first_in, first_out, states, steps, delta_ref, reset_ref, drive_ref, dy_ref, coef_ref, rate_ref, start_ref, hist_ref, grow_ref, state_ref, enter_ref, q_ref, r_ref, rsum_ref, din_ref, dout_ref, in_ref, out_ref, ain_ref, aout_ref):
    tile = pl.program_id(0)

    @pl.when(tile == 0)
    def _():
        spread(coef_ref, first_in, in_ref, steps, states)
        spread(coef_ref, first_out, out_ref, steps, states)
        ain_ref[...] = jnp.zeros_like(ain_ref)
        aout_ref[...] = jnp.zeros_like(aout_ref)

    row = lax.broadcasted_iota(jnp.int32, (subs, lanes), 0)
    rates = [jnp.broadcast_to(rate_ref[n : n + 1, :], (subs, lanes)) for n in range(states)]
    later = []
    for n in range(states):
        near_grow = jnp.where(row < subs - 1, pltpu.roll(grow_ref[n], subs - 1, 0), 1.0)
        near_state = jnp.where(row < subs - 1, pltpu.roll(state_ref[n], subs - 1, 0), 0.0)
        later.append(near_state + near_grow * jnp.broadcast_to(enter_ref[n : n + 1, :], (subs, lanes)))

    def at(s, load_before, carry):
        later, sums = carry
        delta = delta_ref[pl.ds(s, subs, stride=steps), :]
        step = delta + reset_ref[pl.ds(s, subs, stride=steps), :]
        drive = drive_ref[pl.ds(s, subs, stride=steps), :]
        dy = dy_ref[pl.ds(s, subs, stride=steps), :]
        q = jnp.zeros((subs, lanes), jnp.float32)
        r = jnp.zeros((subs, lanes), jnp.float32)
        after, sums_after = [], []
        for n in range(states):
            d_state = out_ref[s, n] * dy + later[n]
            back = jnp.exp2(step * rates[n]) * d_state
            scaled = back * load_before(n)
            sums_after.append(sums[n] + scaled * delta)
            q = q + scaled * rates[n]
            r = r + d_state * in_ref[s, n]
            ain_ref[s, n] += d_state * drive
            aout_ref[s, n] += hist_ref[0, s, n] * dy
            after.append(back)
        q_ref[pl.ds(s, subs, stride=steps), :] = q * (1.0 / log2e)
        r_ref[pl.ds(s, subs, stride=steps), :] = r
        return tuple(after), tuple(sums_after)

    zero = jnp.zeros((subs, lanes), jnp.float32)

    def one(turn, carry):
        s = steps - 1 - turn
        return at(s, lambda n: hist_ref[0, s - 1, n], carry)

    carry = lax.fori_loop(0, steps - 1, one, (tuple(later), (zero,) * states))
    _, sums = at(0, lambda n: start_ref[n], carry)
    for n in range(states):
        rsum_ref[n : n + 1, :] = jnp.sum(sums[n] * rates[n], 0, keepdims=True) * (1.0 / log2e)

    @pl.when(tile == pl.num_programs(0) - 1)
    def _():
        ones = jnp.ones((subs, lanes), jnp.bfloat16)

        def fold(ref, s):
            values = ref[s].reshape(states * subs, lanes)
            high = values.astype(jnp.bfloat16)
            low = (values - high.astype(jnp.float32)).astype(jnp.bfloat16)
            dims = (((1,), (1,)), ((), ()))
            return lax.dot_general(ones, high, dims, preferred_element_type=jnp.float32) + lax.dot_general(ones, low, dims, preferred_element_type=jnp.float32)

        def both(s, _):
            din_ref[pl.ds(s, 1), :] = fold(ain_ref, s)[:1]
            dout_ref[pl.ds(s, 1), :] = fold(aout_ref, s)[:1]
            return 0

        lax.fori_loop(0, steps, both, 0)


def scan_backward(delta, reset, drive, dy, coef, rate, start, hist, grow, state, enter, first_in, first_out):
    row_count, width = delta.shape
    states = rate.shape[0]
    steps = row_count // subs
    tiles = width // lanes
    column = pl.BlockSpec((row_count, lanes), lambda j: (0, j))
    whole = pl.BlockSpec((row_count, lanes), lambda j: (0, 0))
    ends = pl.BlockSpec((states, subs, lanes), lambda j: (0, 0, j))
    per_state = pl.BlockSpec((states, lanes), lambda j: (0, j))
    folded = pl.BlockSpec((steps, states * subs), lambda j: (0, 0))
    q, r, rsum, din, dout = pl.pallas_call(
        functools.partial(backward_kernel, first_in, first_out, states, steps),
        grid=(tiles,),
        in_specs=[column, whole, column, column, whole, per_state, ends, pl.BlockSpec((1, steps, states, subs, lanes), lambda j: (j, 0, 0, 0, 0)), ends, ends, per_state],
        out_specs=[column, column, per_state, folded, folded],
        out_shape=[
            jax.ShapeDtypeStruct((row_count, width), jnp.float32),
            jax.ShapeDtypeStruct((row_count, width), jnp.float32),
            jax.ShapeDtypeStruct((states, width), jnp.float32),
            jax.ShapeDtypeStruct((steps, states * subs), jnp.float32),
            jax.ShapeDtypeStruct((steps, states * subs), jnp.float32),
        ],
        scratch_shapes=[pltpu.VMEM((steps, states, subs, lanes), jnp.float32)] * 4,
        compiler_params=pltpu.CompilerParams(vmem_limit_bytes=56 << 20),
        cost_estimate=pl.CostEstimate(flops=1000, bytes_accessed=1000, transcendentals=0),
    )(delta, reset, drive, dy, coef, rate, start, hist, grow, state, enter)

    def unfold(folded_rows):
        return folded_rows.reshape(steps, states, subs).transpose(2, 0, 1).reshape(row_count, states)

    return q, r, rsum, unfold(din), unfold(dout)


def experts_kernel(
    expert_count, second_ref, routed_ref, route_ref, *refs
):
    weights_in, weights_out = refs[:expert_count], refs[expert_count : 2 * expert_count]
    sums_ref, grads_ref, y_ref, d_ref = refs[2 * expert_count :]
    step = pl.program_id(0)
    blocks, hidden, model_width = weights_in[0].shape
    rows = blocks * hidden

    @pl.when(step == 0)
    def _():
        y_ref[...] = jnp.zeros_like(y_ref)
        d_ref[...] = jnp.zeros_like(d_ref)

    up = jnp.concatenate([w[...].reshape(rows, model_width) for w in weights_in], 0)
    down = jnp.concatenate([w[...].reshape(rows, model_width) for w in weights_out], 0)
    second, routed = second_ref[...], routed_ref[...]
    pre = matmul_nt(second, up)
    column = lax.broadcasted_iota(jnp.int32, (1, expert_count * rows), 1)
    owner = jnp.zeros_like(column)
    for e in range(1, expert_count):
        owner = owner + (column >= e * rows).astype(jnp.int32)
    picked = route_ref[:, :1] == owner.astype(jnp.float32)
    half = 0.5 + 0.5 * lax.erf(pre * (0.5**0.5))
    bell = jnp.exp(-0.5 * pre * pre) * (1.0 / (2.0 * math.pi) ** 0.5)
    act = low_bits(jnp.where(picked, pre * half, 0.0))
    d_pre = low_bits(jnp.where(picked, matmul_nt(routed, down) * (half + pre * bell), 0.0))
    y_ref[...] += matmul(act, down)
    d_ref[...] += matmul(d_pre, up)
    grad_up = low_bits(matmul_tn(d_pre, second))
    grad_down = low_bits(matmul_tn(act, routed))
    for e in range(expert_count):
        for b in range(blocks):
            at = e * rows + b * hidden
            grads_ref[b, e * hidden : (e + 1) * hidden] = grad_up[at : at + hidden]
            to = (expert_count + e) * hidden
            grads_ref[b, to : to + hidden] = grad_down[at : at + hidden]

    @pl.when(step == pl.num_programs(0) - 1)
    def _():
        sums_ref[:, :model_width] = low_bits(y_ref[...])
        sums_ref[:, model_width:] = low_bits(d_ref[...])


def run_experts(second, routed, route_lanes, parts, hidden):
    row_count, model_width = second.shape
    expert_count = len(parts) // 2
    block_count = parts[0][0].shape[0]
    blocks = 2
    fixed = pl.BlockSpec((row_count, model_width), lambda i: (0, 0))

    def spec(first):
        return pl.BlockSpec((blocks, hidden, model_width), lambda i: (i, first // hidden, 0))

    return pl.pallas_call(
        functools.partial(experts_kernel, expert_count),
        grid=(block_count // blocks,),
        in_specs=[fixed, fixed, pl.BlockSpec((row_count, lanes), lambda i: (0, 0))]
        + [spec(first) for _, first in parts],
        out_specs=[
            pl.BlockSpec((row_count, 2 * model_width), lambda i: (0, 0)),
            pl.BlockSpec((blocks, 2 * expert_count * hidden, model_width), lambda i: (i, 0, 0)),
        ],
        out_shape=[
            jax.ShapeDtypeStruct((row_count, 2 * model_width), jnp.bfloat16),
            jax.ShapeDtypeStruct(
                (block_count, 2 * expert_count * hidden, model_width), jnp.bfloat16
            ),
        ],
        scratch_shapes=[pltpu.VMEM((row_count, model_width), jnp.float32)] * 2,
        compiler_params=pltpu.CompilerParams(vmem_limit_bytes=56 << 20),
        cost_estimate=pl.CostEstimate(flops=1000, bytes_accessed=1000, transcendentals=0),
    )(second, routed, route_lanes, *[w for w, _ in parts])


def kernel_place():
    place = lax.axis_index("seq")
    return lax.axis_index("grp"), place // split, place % split


def remote(src, dst, send_sem, arrive_sem, core, high, low):
    return pltpu.make_async_remote_copy(
        src_ref=src,
        dst_ref=dst,
        send_sem=send_sem,
        recv_sem=arrive_sem,
        device_id=(core, high * split + low),
        device_id_type=pl.DeviceIdType.MESH,
    )


def greet_all():
    core, high, low = kernel_place()
    barrier = pltpu.get_barrier_semaphore()
    others = [(core, lax.rem(high + k, split), low) for k in range(1, split)]
    others += [(core, high, lax.rem(low + k, split)) for k in range(1, split)]
    others += [(1 - core, high, low)]
    for c, h, l in others:
        pl.semaphore_signal(
            barrier, inc=1, device_id=(c, h * split + l), device_id_type=pl.DeviceIdType.MESH
        )
    return len(others)


def plane_copies(src_of, dst, sems, slot_by_sender):
    core, high, low = kernel_place()
    copies = []
    for k in range(1, split):
        to = lax.rem(low + k, split)
        slot = low if slot_by_sender else k - 1
        copies.append(
            remote(src_of(to, k), dst.at[slot], sems.at[0, k - 1], sems.at[1, k - 1], core, high, to)
        )
    return copies


def line_copies(src, dst_of, sems):
    core, high, low = kernel_place()
    return [
        remote(
            src, dst_of(high), sems.at[0, k - 1], sems.at[1, k - 1], core, lax.rem(high + k, split), low
        )
        for k in range(1, split)
    ]


def line_arrived(src, dst_of, sems, k):
    core, high, low = kernel_place()
    at = lax.rem(high + split - k, split)
    remote(src, dst_of(at), sems.at[0, k - 1], sems.at[1, k - 1], core, high, low).wait_recv()


def core_copy(dst_of, sems, k):
    core, high, low = kernel_place()
    at = lax.rem(high + split - k, split)
    return remote(dst_of(at), dst_of(split + at), sems.at[0, k], sems.at[1, k], 1 - core, high, low)


def softplus_of(value):
    return jnp.maximum(value, 0.0) + jnp.log1p(jnp.exp(-jnp.abs(value)))


def sigmoid_of(value):
    return 1.0 / (1.0 + jnp.exp(-value))


def row_loop(count, size, body):
    def one(i, _):
        body(pl.multiple_of(i * size, size))
        return 0

    lax.fori_loop(0, count // size, one, 0)


def scan_one_way(j, first_sub, reverse, states, steps, step_ref, reset_ref, drive_ref, spread_ref, rates):
    def one(turn, carry):
        s = steps - 1 - turn if reverse else turn
        total, held = carry
        step = step_ref[j, pl.ds(s, subs, stride=steps), :] + reset_ref[pl.ds(s, subs, stride=steps), :]
        drive = drive_ref[j, pl.ds(s, subs, stride=steps), :]
        after_step = []
        for n in range(states):
            factor = jnp.exp2(step * rates[n])
            if reverse:
                after_step.append(factor * (held[n] + spread_ref[s, n] * drive))
            else:
                after_step.append(factor * held[n] + spread_ref[s, n] * drive)
        return total + step, tuple(after_step)

    zero = jnp.zeros((subs, lanes), jnp.float32)
    total, held = lax.fori_loop(0, steps, one, (zero, (zero,) * states), unroll=2)
    return [chain_rows(jnp.exp2(total * rates[n]), held[n], reverse) for n in range(states)]


def chain_enter(arrive_ref, j, states, reverse):
    _, high, _ = kernel_place()
    total = jnp.zeros((states, lanes), jnp.float32)
    for k in range(split - 1, 0, -1):
        piece = arrive_ref[k - 1, j]
        has = high + k < split if reverse else high >= k
        total = jnp.where(has, piece[states:] + piece[:states] * total, 0.0)
    return total


def tile_rates(rows_ref, j, states):
    decay = -jnp.exp(rows_ref[j, alog_row : alog_row + states, :])
    return decay


def ends_copies(send_ref, arrive_ref, sems, j, reverse):
    core, high, low = kernel_place()
    copies = []
    for k in range(1, split):
        to = lax.rem(high + split - k, split) if reverse else lax.rem(high + k, split)
        copies.append(
            remote(
                send_ref.at[j],
                arrive_ref.at[k - 1, j],
                sems.at[0, k - 1, j],
                sems.at[1, k - 1, j],
                core,
                to,
                low,
            )
        )
    return copies


alog_row = 8
bias_row = 4
skip_row = 5
early_hidden = 96


def mixer_kernel(
    dt_rank, states, tap_count,
    tokens_ref, gains_ref, lengths_ref, a_ref, b_ref, c_ref, g_ref,
    first_ref, gate_ref, hidden_ref, normed_ref, edge_ref, routed_ref, input_ref, coef_ref,
    step_ref, z_ref, y_ref, gated_ref, start_ref, resid_ref, second_ref, rows_ref,
    in_ref, out_ref, drive_ref, reset_ref, mixed_ref, partial_ref, arrive_ref, coef_send_ref,
    coef_arrive_ref, send_ref, ends_ref, grow_ref, state_ref,
    a_sems, b_sems, c_sems, d_sems, a_core, b_core, c_core, d_core, token_sems, route_sems,
    second_sems, coef_sems, sum_sems, edge_send, edge_arrive, ends_sems, local_sems,
):
    core, high, low = kernel_place()
    own_rows, model_width = tokens_ref.shape
    row_count = own_rows * split
    steps = row_count // subs
    tiles = step_ref.shape[0]
    width = tiles * lanes
    edge = edge_ref.shape[0]
    first_b, first_c = dt_rank, dt_rank + states
    greeted = greet_all()

    def edge_copy(l):
        return remote(
            normed_ref.at[low, pl.ds(own_rows - edge, edge)],
            edge_ref,
            edge_send.at[l],
            edge_arrive,
            core,
            lax.rem(high + 1, split),
            l,
        )

    barrier = pltpu.get_barrier_semaphore()
    for k in range(1, split):
        pl.semaphore_signal(
            barrier,
            inc=1,
            device_id=(core, lax.rem(high + split - 1, split) * split + lax.rem(low + k, split)),
            device_id_type=pl.DeviceIdType.MESH,
        )
    greeted += split - 1
    tokens = tokens_ref[...].astype(jnp.float32)
    normed_ref[low] = low_bits(norm_rows(tokens, gains_ref[0:1, :]))
    local = [
        pltpu.make_async_copy(a_ref, first_ref.at[high], local_sems.at[0]),
        pltpu.make_async_copy(b_ref, gate_ref.at[high], local_sems.at[1]),
        pltpu.make_async_copy(c_ref, hidden_ref.at[high], local_sems.at[2]),
        pltpu.make_async_copy(g_ref, routed_ref.at[low], local_sems.at[3]),
    ]
    for copy in local:
        copy.start()
    pl.semaphore_wait(barrier, greeted)

    @pl.when((low == split - 1) & (high < split - 1))
    def _():
        for l in range(split):
            edge_copy(l).start()

    hidden_count = c_ref.shape[0]
    c_src = c_ref.at[pl.ds(0, early_hidden)]
    d_src = c_ref.at[pl.ds(early_hidden, hidden_count - early_hidden)]

    def a_dst(at):
        return first_ref.at[at]

    def b_dst(at):
        return gate_ref.at[at]

    def c_dst(at):
        return hidden_ref.at[at, pl.ds(0, early_hidden)]

    def d_dst(at):
        return hidden_ref.at[at, pl.ds(early_hidden, hidden_count - early_hidden)]

    token_copies = plane_copies(lambda to, k: normed_ref.at[low], normed_ref, token_sems, True)
    a_copies = line_copies(a_ref, a_dst, a_sems)
    b_copies = line_copies(b_ref, b_dst, b_sems)
    c_copies = line_copies(c_src, c_dst, c_sems)
    d_copies = line_copies(d_src, d_dst, d_sems)
    route_copies = plane_copies(lambda to, k: g_ref, routed_ref, route_sems, True)
    for copy in token_copies + a_copies + b_copies + c_copies + route_copies:
        copy.start()
    for copy in local:
        copy.wait()
    core_copies = [core_copy(a_dst, a_core, 0), core_copy(b_dst, b_core, 0)]
    core_copies += [core_copy(c_dst, c_core, 0), core_copy(d_dst, d_core, 0)]
    for copy in core_copies:
        copy.start()

    first_len = lengths_ref[0, 0]

    def offsets(at, rows):
        place = high * row_count + at + lax.broadcasted_iota(jnp.int32, (rows, lanes), 0)
        return jnp.where(place < first_len, place, place - first_len)

    def fill_reset(at):
        reset_ref[pl.ds(at, 64), :] = jnp.where(offsets(at, 64) == 0, 1e30, 0.0)

    row_loop(row_count, 64, fill_reset)

    @pl.when(high == 0)
    def _():
        edge_ref[...] = jnp.zeros_like(edge_ref)

    for k in range(1, split):
        line_arrived(a_ref, a_dst, a_sems, k)
        copy = core_copy(a_dst, a_core, k)
        copy.start()
        core_copies.append(copy)
    for copy in token_copies:
        copy.wait()

    @pl.when(high > 0)
    def _():
        edge_copy(0).wait_recv()

    @pl.when((low == split - 1) & (high < split - 1))
    def _():
        for l in range(split):
            edge_copy(l).wait_send()

    for k in range(split):
        core_copy(a_dst, a_core, k).wait_recv()

    weights = first_ref[:, :, :model_width].reshape(width, model_width)
    input_ref[:edge, :] = low_bits(matmul_nt(edge_ref[...], weights)).astype(jnp.float32)
    for l in range(split):
        block = low_bits(matmul_nt(normed_ref[l], weights)).astype(jnp.float32)
        input_ref[edge + l * own_rows : edge + (l + 1) * own_rows, :] = block
    small = first_ref[:, :, model_width + 2 * lanes :].reshape(width, lanes).astype(jnp.float32)
    for j in range(tiles):
        rows_ref[j] = small[j * lanes : (j + 1) * lanes].T

    def convolve(at):
        offset = offsets(at, 32)
        for j in range(tiles):
            span = input_ref[pl.ds(at, 32 + edge), j * lanes : (j + 1) * lanes]
            conv_sum = jnp.zeros((32, lanes), jnp.float32)
            for k in range(tap_count):
                shift = edge - (tap_count - 1) + k
                term = rows_ref[j, k : k + 1, :] * span[shift : shift + 32]
                conv_sum = conv_sum + jnp.where(offset >= tap_count - 1 - k, term, 0.0)
            mixed_ref[pl.ds(at, 32), j * lanes : (j + 1) * lanes] = low_bits(
                conv_sum * sigmoid_of(conv_sum)
            )

    row_loop(row_count, 32, convolve)

    x_full = first_ref[:, :, model_width : model_width + lanes].reshape(width, lanes)
    part = matmul(mixed_ref[...], x_full)
    coef_ref[...] = part
    coef_send_ref[...] = low_bits(part)
    coef_copies = plane_copies(lambda to, k: coef_send_ref, coef_arrive_ref, coef_sems, False)
    for copy in coef_copies:
        copy.start()
    for copy in coef_copies:
        copy.wait()
    total = coef_ref[...]
    for k in range(1, split):
        total = total + coef_arrive_ref[k - 1].astype(jnp.float32)
    coef_ref[...] = total
    dt_full = first_ref[:, :, model_width + lanes : model_width + 2 * lanes].reshape(width, lanes)

    def step_sizes(at):
        pre = matmul_nt(low_bits(coef_ref[pl.ds(at, 128), :]), dt_full)
        for j in range(tiles):
            cols = slice(j * lanes, (j + 1) * lanes)
            step = softplus_of(pre[:, cols] + rows_ref[j, bias_row : bias_row + 1, :])
            step_ref[j, pl.ds(at, 128), :] = step
            drive_ref[j, pl.ds(at, 128), :] = step * mixed_ref[pl.ds(at, 128), cols].astype(
                jnp.float32
            )

    row_loop(row_count, 128, step_sizes)
    spread(coef_ref, first_b, in_ref, steps, states)

    def rates_of(j):
        values = -jnp.exp(rows_ref[j, alog_row : alog_row + states, :]) * log2e
        return [jnp.broadcast_to(values[n : n + 1, :], (subs, lanes)) for n in range(states)]

    def ends_of(j, _):
        found = scan_one_way(
            j, None, False, states, steps, step_ref, reset_ref, drive_ref, in_ref, rates_of(j)
        )
        for n, (grow, state) in enumerate(found):
            grow_ref[j, n] = grow
            state_ref[j, n] = state
            send_ref[j, n : n + 1] = grow[subs - 1 :]
            send_ref[j, states + n : states + n + 1] = state[subs - 1 :]
        for copy in ends_copies(send_ref, ends_ref, ends_sems, j, False):
            copy.start()
        return 0

    lax.fori_loop(0, tiles, ends_of, 0)
    for copy in d_copies:
        copy.start()
    spread(coef_ref, first_c, out_ref, steps, states)
    for k in range(1, split):
        line_arrived(b_ref, b_dst, b_sems, k)
        copy = core_copy(b_dst, b_core, k)
        copy.start()
        core_copies.append(copy)
    row = lax.broadcasted_iota(jnp.int32, (subs, lanes), 0)

    def forward_of(j, _):
        for copy in ends_copies(send_ref, ends_ref, ends_sems, j, False):
            copy.wait()
        enter = chain_enter(ends_ref, j, states, False)
        rates = rates_of(j)
        held = []
        for n in range(states):
            near_grow = jnp.where(row >= 1, pltpu.roll(grow_ref[j, n], 1, 0), 1.0)
            near_state = jnp.where(row >= 1, pltpu.roll(state_ref[j, n], 1, 0), 0.0)
            start = near_state + near_grow * jnp.broadcast_to(enter[n : n + 1, :], (subs, lanes))
            start_ref[j, n] = start
            held.append(start)

        def one(s, held):
            step = step_ref[j, pl.ds(s, subs, stride=steps), :]
            step = step + reset_ref[pl.ds(s, subs, stride=steps), :]
            drive = drive_ref[j, pl.ds(s, subs, stride=steps), :]
            now_all = []
            y = jnp.zeros((subs, lanes), jnp.float32)
            for n in range(states):
                now = jnp.exp2(step * rates[n]) * held[n] + in_ref[s, n] * drive
                y = y + out_ref[s, n] * now
                now_all.append(now)
            y_ref[j, pl.ds(s, subs, stride=steps), :] = y
            return tuple(now_all)

        lax.fori_loop(0, steps, one, tuple(held), unroll=2)
        return 0

    lax.fori_loop(0, tiles, forward_of, 0)

    for k in range(split):
        core_copy(b_dst, b_core, k).wait_recv()
    channel_rows = width // (2 * split)
    second_in = gate_ref[:, :channel_rows].reshape(width, model_width)
    for l in range(split):
        z_block = matmul_nt(normed_ref[l], second_in)
        rows = slice(l * own_rows, (l + 1) * own_rows)
        for j in range(tiles):
            z_ref[j, rows, :] = z_block[:, j * lanes : (j + 1) * lanes]

    def gate(at):
        for j in range(tiles):
            cols = slice(j * lanes, (j + 1) * lanes)
            mixed = mixed_ref[pl.ds(at, 32), cols].astype(jnp.float32)
            y = y_ref[j, pl.ds(at, 32), :] + rows_ref[j, skip_row : skip_row + 1, :] * mixed
            y_ref[j, pl.ds(at, 32), :] = y
            z = z_ref[j, pl.ds(at, 32), :]
            gated_ref[pl.ds(at, 32), cols] = low_bits(y * z * sigmoid_of(z))

    row_loop(row_count, 32, gate)
    out_full = gate_ref[:, channel_rows:].reshape(width, model_width)

    def out_block(l):
        at = pl.multiple_of(l * own_rows, own_rows)
        return matmul(gated_ref[pl.ds(at, own_rows), :], out_full)

    sum_copies = plane_copies(lambda to, k: partial_ref.at[k - 1], arrive_ref, sum_sems, False)
    for k in range(1, split):
        partial_ref[k - 1] = low_bits(out_block(lax.rem(low + k, split)))
        sum_copies[k - 1].start()
    resid = tokens_ref[...].astype(jnp.float32) + out_block(low)
    for k in range(1, split):
        line_arrived(c_src, c_dst, c_sems, k)
        copy = core_copy(c_dst, c_core, k)
        copy.start()
        core_copies.append(copy)
    for k in range(1, split):
        sum_copies[k - 1].wait()
        resid = resid + arrive_ref[k - 1].astype(jnp.float32)
    resid_ref[...] = resid
    second_ref[low] = low_bits(norm_rows(resid, gains_ref[1:2, :]))
    second_copies = plane_copies(lambda to, k: second_ref.at[low], second_ref, second_sems, True)
    for copy in second_copies:
        copy.start()
    for k in range(1, split):
        line_arrived(d_src, d_dst, d_sems, k)
        copy = core_copy(d_dst, d_core, k)
        copy.start()
        core_copies.append(copy)
    for copy in second_copies + route_copies:
        copy.wait()
    for copy in a_copies + b_copies + c_copies + d_copies + core_copies:
        copy.wait_send()
    for dst_of, sems in ((c_dst, c_core), (d_dst, d_core)):
        for k in range(split):
            core_copy(dst_of, sems, k).wait_recv()


def run_mixer(tokens, gains, lengths, a_part, b_part, c_part, g_part, dt_rank, states, tap_count):
    own_rows, model_width = tokens.shape
    row_count = own_rows * split
    steps = row_count // subs
    blocks = 2 * split
    width = blocks * a_part.shape[0]
    tiles = width // lanes
    vmem = pl.BlockSpec(memory_space=pltpu.VMEM)
    anywhere = pl.BlockSpec(memory_space=pl.ANY)
    f32, bf16 = jnp.float32, jnp.bfloat16
    tiled = (tiles, row_count, lanes)
    outs = [
        ((blocks,) + a_part.shape, bf16),
        ((blocks,) + b_part.shape, bf16),
        ((blocks,) + c_part.shape, bf16),
        ((split, own_rows, model_width), bf16),
        ((16, model_width), bf16),
        ((split,) + g_part.shape, bf16),
        ((row_count + 16, width), f32),
        ((row_count, lanes), f32),
        (tiled, f32),
        (tiled, f32),
        (tiled, f32),
        ((row_count, width), bf16),
        ((tiles, states, subs, lanes), f32),
        ((own_rows, model_width), f32),
        ((split, own_rows, model_width), bf16),
        ((tiles, lanes, lanes), f32),
    ]
    spreads = pltpu.VMEM((steps, states, subs, lanes), f32)
    dma = pltpu.SemaphoreType.DMA
    others = split - 1
    return pl.pallas_call(
        functools.partial(mixer_kernel, dt_rank, states, tap_count),
        in_specs=[vmem, vmem, pl.BlockSpec(memory_space=pltpu.SMEM), vmem, vmem, anywhere, vmem],
        out_specs=[anywhere if i == 2 else vmem for i in range(len(outs))],
        out_shape=[jax.ShapeDtypeStruct(shape, kind) for shape, kind in outs],
        scratch_shapes=[
            spreads,
            spreads,
            pltpu.VMEM(tiled, f32),
            pltpu.VMEM((row_count, lanes), f32),
            pltpu.VMEM((row_count, width), bf16),
            pltpu.VMEM((others, own_rows, model_width), bf16),
            pltpu.VMEM((others, own_rows, model_width), bf16),
            pltpu.VMEM((row_count, lanes), bf16),
            pltpu.VMEM((others, row_count, lanes), bf16),
            pltpu.VMEM((tiles, 2 * states, lanes), f32),
            pltpu.VMEM((others, tiles, 2 * states, lanes), f32),
            pltpu.VMEM((tiles, states, subs, lanes), f32),
            pltpu.VMEM((tiles, states, subs, lanes), f32),
        ]
        + [dma((2, others))] * 4
        + [dma((2, split))] * 4
        + [dma((2, others))] * 5
        + [dma((split,)), dma, dma((2, others, tiles)), dma((4,))],
        compiler_params=pltpu.CompilerParams(
            collective_id=3, has_side_effects=True, vmem_limit_bytes=60 << 20
        ),
        cost_estimate=pl.CostEstimate(flops=1000, bytes_accessed=1000, transcendentals=0),
    )(tokens, gains, lengths, a_part, b_part, c_part, g_part)


def norm_back(values, gain_row, grads):
    scale = lax.rsqrt(jnp.mean(values * values, -1, keepdims=True) + eps_norm)
    unit = values * scale
    inner = grads * gain_row
    return scale * (inner - unit * jnp.mean(inner * unit, -1, keepdims=True)), grads * unit


def route_probs(rows, router, route_lanes, expert_count):
    logits = matmul(rows, router)
    lane = lax.broadcasted_iota(jnp.int32, logits.shape, 1)
    logits = jnp.where(lane < expert_count, logits, -1e30)
    powers = jnp.exp(logits - jnp.max(logits, -1, keepdims=True))
    probs = powers / jnp.sum(powers, -1, keepdims=True)
    chosen = jnp.where(lane.astype(jnp.float32) == route_lanes, 1.0, 0.0)
    return probs, chosen, jnp.sum(probs * chosen, -1, keepdims=True)


def scatter_copies(src_of, arrive_ref, sems):
    core, high, low = kernel_place()
    copies = []
    for k in range(1, split):
        to = lax.rem(high + k, split)
        copies.append(
            remote(
                src_of(to), arrive_ref.at[k - 1], sems.at[0, k - 1], sems.at[1, k - 1], core, to, low
            )
        )
    return copies


def half_copy(src, dst, sems, h):
    core, high, low = kernel_place()
    return remote(src, dst, sems.at[0, h], sems.at[1, h], 1 - core, high, low)


def fill_offsets(reset_ref, lengths_ref, row_count):
    _, high, _ = kernel_place()
    first_len = lengths_ref[0, 0]

    def fill(at):
        place = high * row_count + at + lax.broadcasted_iota(jnp.int32, (64, lanes), 0)
        reset_ref[pl.ds(at, 64), :] = jnp.where((place == 0) | (place == first_len), 1e30, 0.0)

    row_loop(row_count, 64, fill)


def turn_kernel(
    dt_rank, states, expert_count, cut,
    second_ref, routed_ref, hidden_ref, router_ref, resid_ref, grad_ref, gains_ref, lengths_ref,
    gate_ref, normed_ref, coef_ref, step_ref, z_ref, y_ref, gated_ref, rows_ref,
    mixed_out_ref, d_resid_ref, small_ref, dy_ref, gz_ref, later_ref, mine_ref, early_ref,
    gate_mine_ref,
    grads_ref, half_ref, y_sum_ref, d_sum_ref, dg_sum_ref, gates_ref, scaled_ref, act_ref, pre_ref,
    part_ref, arrive_ref, y_part_ref, y_arrive_ref, branch_ref, out_ref, reset_ref, send_ref,
    ends_ref, early_arrive_ref, gate_half_ref,
    half_sems, sum_sems, y_sems, branch_sems, early_sems, ends_sems, gate_half_sems,
):
    core, high, low = kernel_place()
    _, own_rows, model_width = second_ref.shape
    row_count = own_rows * split
    steps = row_count // subs
    tiles = step_ref.shape[0]
    width = tiles * lanes
    hidden = hidden_ref.shape[1] // (2 * expert_count)
    channel_rows = width // (2 * split)
    greeted = greet_all()
    router = router_ref[...]

    for l in range(split):
        rows = slice(l * own_rows, (l + 1) * own_rows)
        route_lanes = routed_ref[l, :, model_width:].astype(jnp.float32)
        _, _, gate = route_probs(second_ref[l], router, route_lanes, expert_count)
        gates_ref[rows, :] = jnp.broadcast_to(gate, (own_rows, lanes))
        scaled_ref[rows, :] = low_bits(gate * routed_ref[l, :, :model_width].astype(jnp.float32))
    y_sum_ref[...] = jnp.zeros_like(y_sum_ref)
    d_sum_ref[...] = jnp.zeros_like(d_sum_ref)
    dg_sum_ref[...] = jnp.zeros_like(dg_sum_ref)
    per_step = 2
    span = per_step * hidden
    column = lax.broadcasted_iota(jnp.int32, (1, expert_count * span), 1)
    owner = jnp.zeros_like(column)
    for e in range(1, expert_count):
        owner = owner + (column >= e * span).astype(jnp.int32)
    owner = owner.astype(jnp.float32)

    def blocks_of(first):
        def rows_of(part):
            at = part * hidden
            return hidden_ref[pl.ds(first, per_step), at : at + hidden].reshape(span, model_width)

        up = jnp.concatenate([rows_of(e) for e in range(expert_count)], 0)
        down = jnp.concatenate([rows_of(expert_count + e) for e in range(expert_count)], 0)

        def token_block(l, _):
            at = pl.multiple_of(l * own_rows, own_rows)
            rows = pl.ds(at, own_rows)
            pre = matmul_nt(second_ref[l], up)
            picked = routed_ref[l, :, model_width : model_width + 1].astype(jnp.float32) == owner
            half = 0.5 + 0.5 * lax.erf(pre * (0.5**0.5))
            bell = jnp.exp(-0.5 * pre * pre) * (1.0 / (2.0 * math.pi) ** 0.5)
            act = low_bits(jnp.where(picked, pre * half, 0.0))
            d_raw = matmul_nt(routed_ref[l, :, :model_width], down)
            weighted = act.astype(jnp.float32) * d_raw
            dg_sum_ref[rows, :] += sum(
                weighted[:, c : c + lanes] for c in range(0, expert_count * span, lanes)
            )
            d_pre = jnp.where(picked, gates_ref[rows, :1] * d_raw * (half + pre * bell), 0.0)
            d_pre = low_bits(d_pre)
            y_sum_ref[rows, :] += matmul(act, down)
            d_sum_ref[rows, :] += matmul(d_pre, up)
            act_ref[rows, :] = act
            pre_ref[rows, :] = d_pre
            return 0

        lax.fori_loop(0, split, token_block, 0)
        second = second_ref[...].reshape(row_count, model_width)
        for e in range(expert_count):
            cols = slice(e * span, (e + 1) * span)
            up_grad = low_bits(matmul_tn(pre_ref[:, cols], second))
            down_grad = low_bits(matmul_tn(act_ref[:, cols], scaled_ref[...]))
            for b in range(per_step):
                piece = slice(b * hidden, (b + 1) * hidden)
                grads_ref[first + b, e * hidden : (e + 1) * hidden] = up_grad[piece]
                to = (expert_count + e) * hidden
                grads_ref[first + b, to : to + hidden] = down_grad[piece]

    lax.fori_loop(0, split // per_step, lambda i, _: (blocks_of(split + per_step * i), 0)[1], 0)
    pl.semaphore_wait(pltpu.get_barrier_semaphore(), greeted)
    half_copies = [
        half_copy(grads_ref.at[split + h], half_ref.at[h], half_sems, h) for h in range(split)
    ]
    for copy in half_copies:
        copy.start()
    lax.fori_loop(0, split // per_step, lambda i, _: (blocks_of(per_step * i), 0)[1], 0)

    sum_copies = plane_copies(lambda to, k: part_ref.at[k - 1], arrive_ref, sum_sems, False)
    y_copies = plane_copies(lambda to, k: y_part_ref.at[k - 1], y_arrive_ref, y_sems, False)
    for k in range(1, split):
        to = pl.ds(pl.multiple_of(lax.rem(low + k, split) * own_rows, own_rows), own_rows)
        part_ref[k - 1, :, :model_width] = low_bits(d_sum_ref[to, :])
        part_ref[k - 1, :, model_width:] = low_bits(dg_sum_ref[to, :])
        sum_copies[k - 1].start()
        y_part_ref[k - 1] = low_bits(y_sum_ref[to, :])

    for h in range(split):
        half_copies[h].wait()

    def add_half(h, _):
        mine_ref[h] = low_bits(
            grads_ref[h].astype(jnp.float32) + half_ref[h].astype(jnp.float32)
        )
        return 0

    lax.fori_loop(0, split, add_half, 0)
    early_copies = scatter_copies(
        lambda to: mine_ref.at[to, pl.ds(0, cut)], early_arrive_ref, early_sems
    )
    for copy in early_copies:
        copy.start()
    own = pl.ds(pl.multiple_of(low * own_rows, own_rows), own_rows)
    d_second, dg_lanes = d_sum_ref[own, :], dg_sum_ref[own, :]
    for k in range(1, split):
        sum_copies[k - 1].wait()
        d_second = d_second + arrive_ref[k - 1, :, :model_width].astype(jnp.float32)
        dg_lanes = dg_lanes + arrive_ref[k - 1, :, model_width:].astype(jnp.float32)
    d_gate = jnp.sum(dg_lanes, -1, keepdims=True)
    second_own = second_ref[low]
    route_lanes = routed_ref[low, :, model_width:].astype(jnp.float32)
    probs, chosen, gate = route_probs(second_own, router, route_lanes, expert_count)
    d_logits = low_bits(probs * (d_gate * (chosen - gate)))
    d_second = d_second + matmul_nt(d_logits, router)
    d_rows, d_gain = norm_back(resid_ref[...], gains_ref[1:2, :], d_second)
    d_resid = grad_ref[...] + d_rows
    d_resid_ref[...] = d_resid
    branch_ref[low] = low_bits(d_resid)
    branch_copies = plane_copies(lambda to, k: branch_ref.at[low], branch_ref, branch_sems, True)
    for copy in branch_copies + y_copies:
        copy.start()
    small_ref[...] = jnp.zeros_like(small_ref)
    small_ref[1:2, :] = jnp.sum(d_gain, 0, keepdims=True)
    small_ref[2 : 2 + expert_count, :] = matmul_tn(d_logits, second_own)[:expert_count]

    fill_offsets(reset_ref, lengths_ref, row_count)
    spread(coef_ref, dt_rank + states, out_ref, steps, states)
    out_full = gate_ref[:, channel_rows:].reshape(width, model_width)
    for copy in branch_copies:
        copy.wait()
    for l in range(split):
        d_gated = matmul_nt(branch_ref[l], out_full)
        rows = slice(l * own_rows, (l + 1) * own_rows)
        for j in range(tiles):
            cols = slice(j * lanes, (j + 1) * lanes)
            z = z_ref[j, rows, :]
            sig = sigmoid_of(z)
            d_tile = d_gated[:, cols]
            dy_ref[j, rows, :] = d_tile * (z * sig)
            d_z = d_tile * y_ref[j, rows, :] * (sig * (1.0 + z * (1.0 - sig)))
            gz_ref[rows, cols] = low_bits(d_z)

    def rates_of(j):
        values = -jnp.exp(rows_ref[j, alog_row : alog_row + states, :]) * log2e
        return [jnp.broadcast_to(values[n : n + 1, :], (subs, lanes)) for n in range(states)]

    def ends_of(j, _):
        found = scan_one_way(
            j, None, True, states, steps, step_ref, reset_ref, dy_ref, out_ref, rates_of(j)
        )
        row = lax.broadcasted_iota(jnp.int32, (subs, lanes), 0)
        for n, (grow, state) in enumerate(found):
            send_ref[j, n : n + 1] = grow[:1]
            send_ref[j, states + n : states + n + 1] = state[:1]
            has = row < subs - 1
            later_ref[0, j, n] = jnp.where(has, pltpu.roll(grow, subs - 1, 0), 1.0)
            later_ref[1, j, n] = jnp.where(has, pltpu.roll(state, subs - 1, 0), 0.0)
        for copy in ends_copies(send_ref, ends_ref, ends_sems, j, True):
            copy.start()
        return 0

    lax.fori_loop(0, tiles, ends_of, 0)

    normed = normed_ref[...].reshape(row_count, model_width)
    branch = branch_ref[...].reshape(row_count, model_width)
    for part, (first_op, second_op) in enumerate(((gz_ref, normed), (gated_ref, branch))):
        half_width = width // 2
        for at in (half_width, 0):
            grad = low_bits(matmul_tn(first_op[:, at : at + half_width], second_op))
            for b in range(split):
                piece = grad[b * channel_rows : (b + 1) * channel_rows]
                to = part * channel_rows
                grads_ref[at // channel_rows + b, to : to + channel_rows] = piece
    gate_rows = 2 * channel_rows
    gate_copies = [
        half_copy(
            grads_ref.at[split + h, pl.ds(0, gate_rows)], gate_half_ref.at[h], gate_half_sems, h
        )
        for h in range(split)
    ]
    for copy in gate_copies:
        copy.start()

    def settle(j, _):
        for copy in ends_copies(send_ref, ends_ref, ends_sems, j, True):
            copy.wait()
        enter = chain_enter(ends_ref, j, states, True)
        for n in range(states):
            entered = jnp.broadcast_to(enter[n : n + 1, :], (subs, lanes))
            later_ref[1, j, n] += later_ref[0, j, n] * entered
        return 0

    lax.fori_loop(0, tiles, settle, 0)
    y = y_sum_ref[own, :]
    for k in range(1, split):
        y_copies[k - 1].wait()
        y = y + y_arrive_ref[k - 1].astype(jnp.float32)
    mixed_out_ref[...] = low_bits(resid_ref[...] + gates_ref[own, :1] * y)
    for h in range(split):
        gate_copies[h].wait()

        def add_gate(at, h=h):
            rows = pl.ds(at, 16)
            total = grads_ref[h, rows].astype(jnp.float32) + gate_half_ref[h, rows].astype(jnp.float32)
            gate_mine_ref[h, rows] = low_bits(total)

        row_loop(gate_rows, 16, add_gate)
    early = mine_ref[high, :cut].astype(jnp.float32)
    for k in range(1, split):
        early_copies[k - 1].wait()
        early = early + early_arrive_ref[k - 1].astype(jnp.float32)
    early_ref[...] = early


def run_turn(
    second, routed, hidden_full, router_lanes, resid, grad_out, gains, lengths, gate_full, normed,
    coef, step, z, y, gated, rows, dt_rank, states, expert_count, cut,
):
    _, own_rows, model_width = second.shape
    row_count = own_rows * split
    steps = row_count // subs
    tiles = step.shape[0]
    width = tiles * lanes
    hidden_rows = hidden_full.shape[1]
    gate_rows = gate_full.shape[1]
    others = split - 1
    vmem = pl.BlockSpec(memory_space=pltpu.VMEM)
    f32, bf16 = jnp.float32, jnp.bfloat16
    dma = pltpu.SemaphoreType.DMA
    outs = [
        ((own_rows, model_width), bf16),
        ((own_rows, model_width), f32),
        ((8, model_width), f32),
        ((tiles, row_count, lanes), f32),
        ((row_count, width), bf16),
        ((2, tiles, states, subs, lanes), f32),
        ((split, hidden_rows, model_width), bf16),
        ((cut, model_width), f32),
        ((split, gate_rows, model_width), bf16),
    ]
    span = 2 * hidden_rows // 2
    return pl.pallas_call(
        functools.partial(turn_kernel, dt_rank, states, expert_count, cut),
        in_specs=[pl.BlockSpec(memory_space=pltpu.SMEM) if i == 7 else vmem for i in range(16)],
        out_specs=[vmem] * len(outs),
        out_shape=[jax.ShapeDtypeStruct(shape, kind) for shape, kind in outs],
        scratch_shapes=[
            pltpu.VMEM((2 * split, hidden_rows, model_width), bf16),
            pltpu.VMEM((split, hidden_rows, model_width), bf16),
            pltpu.VMEM((row_count, model_width), f32),
            pltpu.VMEM((row_count, model_width), f32),
            pltpu.VMEM((row_count, lanes), f32),
            pltpu.VMEM((row_count, lanes), f32),
            pltpu.VMEM((row_count, model_width), bf16),
            pltpu.VMEM((row_count, span), bf16),
            pltpu.VMEM((row_count, span), bf16),
            pltpu.VMEM((others, own_rows, model_width + lanes), bf16),
            pltpu.VMEM((others, own_rows, model_width + lanes), bf16),
            pltpu.VMEM((others, own_rows, model_width), bf16),
            pltpu.VMEM((others, own_rows, model_width), bf16),
            pltpu.VMEM((split, own_rows, model_width), bf16),
            pltpu.VMEM((steps, states, subs, lanes), f32),
            pltpu.VMEM((row_count, lanes), f32),
            pltpu.VMEM((tiles, 2 * states, lanes), f32),
            pltpu.VMEM((others, tiles, 2 * states, lanes), f32),
            pltpu.VMEM((others, cut, model_width), bf16),
            pltpu.VMEM((split, gate_rows, model_width), bf16),
            dma((2, split)),
            dma((2, others)),
            dma((2, others)),
            dma((2, others)),
            dma((2, others)),
            dma((2, others, tiles)),
            dma((2, split)),
        ],
        compiler_params=pltpu.CompilerParams(
            collective_id=4, has_side_effects=True, vmem_limit_bytes=62 << 20
        ),
        cost_estimate=pl.CostEstimate(flops=1000, bytes_accessed=1000, transcendentals=0),
    )(
        second, routed, hidden_full, router_lanes, resid, grad_out, gains, lengths, gate_full, normed,
        coef, step, z, y, gated, rows,
    )


def back_kernel(
    dt_rank, states, tap_count, cut,
    dy_ref, gz_ref, later_ref, mine_ref, gate_mine_ref, first_ref, gate_ref, normed_ref, input_ref,
    coef_ref, step_ref, start_ref, rows_ref, d_resid_ref, tokens_ref, gains_ref, small_ref,
    lengths_ref,
    grad_tokens_ref, total_ref, late_ref, gate_own_ref, first_own_ref,
    in_ref, out_ref, hist_ref, acc_in_ref, acc_out_ref, mixed_ref, conv_ref, q_ref, r_ref, reset_ref,
    gdt_ref, gin_ref, dconv_ref, halo_ref, part_ref, arrive_ref, fold_ref, coef_send_ref,
    coef_arrive_ref, gcoef_ref, misc_ref, select_ref, payload_ref, half_ref, mine_first_ref,
    late_arrive_ref, gate_arrive_ref, first_arrive_ref, core_slots, plane_slots, line_slots,
    late_sems, gate_sems, first_sems, half_sems, halo_sems, coef_sems, sum_sems, core_sems,
    plane_sems, line_sems, local_sems,
):
    core, high, low = kernel_place()
    _, own_rows, model_width = normed_ref.shape
    row_count = own_rows * split
    steps = row_count // subs
    tiles = step_ref.shape[0]
    width = tiles * lanes
    channel_rows = width // (2 * split)
    edge = input_ref.shape[0] - row_count
    late_rows = late_ref.shape[0]
    greeted = greet_all()
    first_len = lengths_ref[0, 0]

    def offsets(at, rows):
        place = high * row_count + at + lax.broadcasted_iota(jnp.int32, (rows, lanes), 0)
        return jnp.where(place < first_len, place, place - first_len)

    fill_offsets(reset_ref, lengths_ref, row_count)
    pl.semaphore_wait(pltpu.get_barrier_semaphore(), greeted)
    late_copies = scatter_copies(
        lambda to: mine_ref.at[to, pl.ds(cut, late_rows)], late_arrive_ref, late_sems
    )
    gate_copies = scatter_copies(lambda to: gate_mine_ref.at[to], gate_arrive_ref, gate_sems)
    local = [
        pltpu.make_async_copy(
            mine_ref.at[high, pl.ds(cut, late_rows)], late_arrive_ref.at[split - 1], local_sems.at[0]
        ),
        pltpu.make_async_copy(
            gate_mine_ref.at[high], gate_arrive_ref.at[split - 1], local_sems.at[1]
        ),
    ]
    for copy in local + late_copies:
        copy.start()

    def convolve(at):
        offset = offsets(at, 32)
        for j in range(tiles):
            span = input_ref[pl.ds(at, 32 + edge), j * lanes : (j + 1) * lanes]
            conv_sum = jnp.zeros((32, lanes), jnp.float32)
            for k in range(tap_count):
                shift = edge - (tap_count - 1) + k
                term = rows_ref[j, k : k + 1, :] * span[shift : shift + 32]
                conv_sum = conv_sum + jnp.where(offset >= tap_count - 1 - k, term, 0.0)
            conv_ref[j, pl.ds(at, 32), :] = conv_sum
            mixed = low_bits(conv_sum * sigmoid_of(conv_sum)).astype(jnp.float32)
            mixed_ref[j, pl.ds(at, 32), :] = mixed

    row_loop(row_count, 32, convolve)
    spread(coef_ref, dt_rank, in_ref, steps, states)
    spread(coef_ref, dt_rank + states, out_ref, steps, states)
    acc_in_ref[...] = jnp.zeros_like(acc_in_ref)
    acc_out_ref[...] = jnp.zeros_like(acc_out_ref)
    misc_ref[...] = jnp.zeros_like(misc_ref)

    def back_of(j, _):
        values = -jnp.exp(rows_ref[j, alog_row : alog_row + states, :]) * log2e
        rates = [jnp.broadcast_to(values[n : n + 1, :], (subs, lanes)) for n in range(states)]

        def forward(s, held):
            step = step_ref[j, pl.ds(s, subs, stride=steps), :]
            drive = step * mixed_ref[j, pl.ds(s, subs, stride=steps), :]
            step = step + reset_ref[pl.ds(s, subs, stride=steps), :]
            now_all = []
            for n in range(states):
                now = jnp.exp2(step * rates[n]) * held[n] + in_ref[s, n] * drive
                hist_ref[s + 1, n] = now
                now_all.append(now)
            return tuple(now_all)

        held = []
        for n in range(states):
            hist_ref[0, n] = start_ref[j, n]
            held.append(start_ref[j, n])
        lax.fori_loop(0, steps, forward, tuple(held), unroll=2)

        def backward(turn, carry):
            s = steps - 1 - turn
            later, sums = carry
            delta = step_ref[j, pl.ds(s, subs, stride=steps), :]
            drive = delta * mixed_ref[j, pl.ds(s, subs, stride=steps), :]
            step = delta + reset_ref[pl.ds(s, subs, stride=steps), :]
            dy = dy_ref[j, pl.ds(s, subs, stride=steps), :]
            rows = pl.ds(pl.multiple_of(s * subs, subs), subs)
            q = jnp.zeros((subs, lanes), jnp.float32)
            r = jnp.zeros((subs, lanes), jnp.float32)
            later_next, sums_next = [], []
            for n in range(states):
                cols = slice(n * lanes, (n + 1) * lanes)
                d_state = out_ref[s, n] * dy + later[n]
                back = jnp.exp2(step * rates[n]) * d_state
                scaled = back * hist_ref[s, n]
                sums_next.append(sums[n] + scaled * delta)
                q = q + scaled * rates[n]
                r = r + d_state * in_ref[s, n]
                acc_in_ref[rows, cols] += d_state * drive
                acc_out_ref[rows, cols] += hist_ref[s + 1, n] * dy
                later_next.append(back)
            q_ref[j, pl.ds(s, subs, stride=steps), :] = q * (1.0 / log2e)
            r_ref[j, pl.ds(s, subs, stride=steps), :] = r
            return tuple(later_next), tuple(sums_next)

        zero = jnp.zeros((subs, lanes), jnp.float32)
        later = tuple(later_ref[1, j, n] for n in range(states))
        _, sums = lax.fori_loop(0, steps, backward, (later, (zero,) * states))
        for n in range(states):
            total = jnp.sum(sums[n] * rates[n], 0, keepdims=True) * (1.0 / log2e)
            misc_ref[j, alog_row + n : alog_row + n + 1, :] = total
        return 0

    lax.fori_loop(0, tiles, back_of, 0)

    source = lax.broadcasted_iota(jnp.int32, select_ref.shape, 0) // lanes
    target = lax.broadcasted_iota(jnp.int32, select_ref.shape, 1)

    def fold(acc_ref, first, fresh):
        select_ref[...] = jnp.where(target == first + source, 1.0, 0.0).astype(jnp.bfloat16)

        def one(at):
            values = acc_ref[pl.ds(at, 128), :]
            coarse = low_bits(values)
            fine = low_bits(values - coarse.astype(jnp.float32))
            found = matmul(coarse, select_ref[...]) + matmul(fine, select_ref[...])
            for i in range(128 // subs):
                rows = pl.ds(at // subs + i, subs, stride=steps)
                piece = found[i * subs : (i + 1) * subs]
                fold_ref[rows, :] = piece if fresh else fold_ref[rows, :] + piece

        row_loop(row_count, 128, one)

    fold(acc_in_ref, dt_rank, True)
    fold(acc_out_ref, dt_rank + states, False)
    dt_full = first_ref[:, :, model_width + lanes : model_width + 2 * lanes].reshape(width, lanes)

    def step_grads(at):
        rows = pl.ds(at, 128)
        pre = matmul_nt(low_bits(coef_ref[rows, :]), dt_full)
        for j in range(tiles):
            cols = slice(j * lanes, (j + 1) * lanes)
            mixed = mixed_ref[j, rows, :]
            d_step = q_ref[j, rows, :] + r_ref[j, rows, :] * mixed
            d_dt = d_step * sigmoid_of(pre[:, cols] + rows_ref[j, bias_row : bias_row + 1, :])
            gdt_ref[rows, cols] = low_bits(d_dt)
            misc_ref[j, bias_row : bias_row + 1, :] += jnp.sum(d_dt, 0, keepdims=True)
            misc_ref[j, skip_row : skip_row + 1, :] += jnp.sum(
                dy_ref[j, rows, :] * mixed, 0, keepdims=True
            )
        part = fold_ref[rows, :] + matmul(gdt_ref[rows, :], dt_full)
        fold_ref[rows, :] = part
        coef_send_ref[rows, :] = low_bits(part)

    row_loop(row_count, 128, step_grads)
    coef_copies = plane_copies(lambda to, k: coef_send_ref, coef_arrive_ref, coef_sems, False)
    for copy in coef_copies:
        copy.start()
    low_coef = low_bits(coef_ref[...])
    for j in range(tiles):
        rows = slice(j * lanes, (j + 1) * lanes)
        payload_ref[rows, model_width + lanes : model_width + 2 * lanes] = low_bits(
            matmul_tn(gdt_ref[:, rows], low_coef)
        )
    for copy in coef_copies:
        copy.wait()
    total = fold_ref[...]
    for k in range(1, split):
        total = total + coef_arrive_ref[k - 1].astype(jnp.float32)
    gcoef_ref[...] = low_bits(total)
    x_full = first_ref[:, :, model_width : model_width + lanes].reshape(width, lanes)

    def conv_grads(at):
        rows = pl.ds(at, 128)
        from_coef = matmul_nt(gcoef_ref[rows, :], x_full)
        for j in range(tiles):
            cols = slice(j * lanes, (j + 1) * lanes)
            d_mixed = rows_ref[j, skip_row : skip_row + 1, :] * dy_ref[j, rows, :]
            d_mixed = d_mixed + r_ref[j, rows, :] * step_ref[j, rows, :] + from_coef[:, cols]
            conv = conv_ref[j, rows, :]
            sig = sigmoid_of(conv)
            dconv_ref[rows, cols] = d_mixed * (sig * (1.0 + conv * (1.0 - sig)))

    row_loop(row_count, 128, conv_grads)

    def halo_copy():
        return remote(
            dconv_ref.at[pl.ds(0, subs)], halo_ref, halo_sems.at[0], halo_sems.at[1],
            core, lax.rem(high + split - 1, split), low,
        )

    @pl.when(high > 0)
    def _():
        halo_copy().start()

    for copy in gate_copies:
        copy.start()

    def tap_grads(at):
        offset = offsets(at, 32)
        for j in range(tiles):
            cols = slice(j * lanes, (j + 1) * lanes)
            span = input_ref[pl.ds(at, 32 + edge), cols]
            d_conv = dconv_ref[pl.ds(at, 32), cols]
            for k in range(tap_count):
                shift = edge - (tap_count - 1) + k
                term = jnp.where(offset >= tap_count - 1 - k, d_conv * span[shift : shift + 32], 0.0)
                misc_ref[j, k : k + 1, :] += jnp.sum(term, 0, keepdims=True)

    row_loop(row_count, 32, tap_grads)

    @pl.when(high < split - 1)
    def _():
        halo_copy().wait_recv()
        dconv_ref[row_count:, :] = halo_ref[...]

    @pl.when(high == split - 1)
    def _():
        dconv_ref[row_count:, :] = jnp.zeros_like(halo_ref)

    def input_grads(at):
        masks = [offsets(at + m, 32) >= m for m in range(tap_count)]
        for j in range(tiles):
            cols = slice(j * lanes, (j + 1) * lanes)
            span = dconv_ref[pl.ds(at, 32 + subs), cols]
            d_input = jnp.zeros((32, lanes), jnp.float32)
            for m in range(tap_count):
                k = tap_count - 1 - m
                term = rows_ref[j, k : k + 1, :] * span[m : m + 32]
                d_input = d_input + jnp.where(masks[m], term, 0.0)
            gin_ref[pl.ds(at, 32), cols] = low_bits(d_input)

    row_loop(row_count, 32, input_grads)

    first_in = first_ref[:, :, :model_width].reshape(width, model_width)
    second_in = gate_ref[:, :channel_rows].reshape(width, model_width)

    def normed_block(l):
        rows = pl.ds(pl.multiple_of(l * own_rows, own_rows), own_rows)
        return matmul(gin_ref[rows, :], first_in) + matmul(gz_ref[rows, :], second_in)

    sum_copies = plane_copies(lambda to, k: part_ref.at[k - 1], arrive_ref, sum_sems, False)
    for k in range(1, split):
        part_ref[k - 1] = low_bits(normed_block(lax.rem(low + k, split)))
        sum_copies[k - 1].start()

    normed = normed_ref[...].reshape(row_count, model_width)
    for j in range(tiles):
        rows = slice(j * lanes, (j + 1) * lanes)
        payload_ref[rows, model_width : model_width + lanes] = low_bits(
            matmul_tn(low_bits(mixed_ref[j]), gcoef_ref[...])
        )
        payload_ref[rows, model_width + 2 * lanes :] = low_bits(misc_ref[j].T)
    half_width = width // 2
    for at in (half_width, 0):
        payload_ref[at : at + half_width, :model_width] = low_bits(
            matmul_tn(gin_ref[:, at : at + half_width], normed)
        )
        if at:
            half = remote(
                payload_ref.at[pl.ds(half_width, half_width)], half_ref, half_sems.at[0],
                half_sems.at[1], 1 - core, high, low,
            )
            half.start()
    d_normed = normed_block(low)
    for k in range(1, split):
        sum_copies[k - 1].wait()
        d_normed = d_normed + arrive_ref[k - 1].astype(jnp.float32)
    tokens = tokens_ref[...].astype(jnp.float32)
    d_rows, d_gain = norm_back(tokens, gains_ref[0:1, :], d_normed)
    grad_tokens_ref[...] = d_resid_ref[...] + d_rows

    core_slots[core] = small_ref[...]
    core_slots[core, 0:1, :] = jnp.sum(d_gain, 0, keepdims=True)
    hop = remote(
        core_slots.at[core], core_slots.at[core], core_sems.at[0], core_sems.at[1], 1 - core, high, low
    )
    hop.start()
    half.wait()

    def add_half(at):
        rows = pl.ds(at, 64)
        both = payload_ref[rows, :].astype(jnp.float32) + half_ref[rows, :].astype(jnp.float32)
        mine_first_ref[rows, :] = low_bits(both)

    row_loop(half_width, 64, add_half)
    hop.wait()
    plane_slots[low] = core_slots[0] + core_slots[1]
    plane = plane_copies(lambda to, k: plane_slots.at[low], plane_slots, plane_sems, True)
    for copy in plane:
        copy.start()
    for copy in plane:
        copy.wait()
    line_slots[high] = (plane_slots[0] + plane_slots[1]) + (plane_slots[2] + plane_slots[3])
    line = line_copies(line_slots.at[high], lambda at: line_slots.at[at], line_sems)
    for copy in line:
        copy.start()
    first_copies = scatter_copies(
        lambda to: mine_first_ref.at[pl.ds(pl.multiple_of(to * channel_rows, 16), channel_rows)],
        first_arrive_ref,
        first_sems,
    )
    for copy in first_copies:
        copy.start()

    for copy in local:
        copy.wait()
    finish(late_copies, late_arrive_ref, late_ref)
    finish(gate_copies, gate_arrive_ref, gate_own_ref)
    for k in range(1, split):
        line_arrived(line_slots.at[high], lambda at: line_slots.at[at], line_sems, k)
    for copy in line:
        copy.wait_send()
    total_ref[...] = (line_slots[0] + line_slots[1]) + (line_slots[2] + line_slots[3])
    own = pl.ds(pl.multiple_of(high * channel_rows, 16), channel_rows)
    first_arrive_ref[split - 1] = mine_first_ref[own, :]
    finish(first_copies, first_arrive_ref, first_own_ref)

    @pl.when(high > 0)
    def _():
        halo_copy().wait_send()


def finish(copies, arrive_ref, out_ref):
    for copy in copies:
        copy.wait()

    def one(at):
        rows = pl.ds(at, 16)
        total = arrive_ref[split - 1, rows].astype(jnp.float32)
        for k in range(split - 1):
            total = total + arrive_ref[k, rows].astype(jnp.float32)
        out_ref[rows, :] = total

    row_loop(out_ref.shape[0], 16, one)


def run_back(
    dy, gz, later, mine, gate_mine, first_full, gate_full, normed, input_all, coef, step, start, rows,
    d_resid, tokens, gains, small, lengths, dt_rank, states, tap_count, cut,
):
    _, own_rows, model_width = normed.shape
    row_count = own_rows * split
    steps = row_count // subs
    tiles = step.shape[0]
    width = tiles * lanes
    channel_rows = width // (2 * split)
    others = split - 1
    late_rows = mine.shape[1] - cut
    gate_rows = gate_mine.shape[1]
    first_columns = first_full.shape[2]
    vmem = pl.BlockSpec(memory_space=pltpu.VMEM)
    anywhere = pl.BlockSpec(memory_space=pl.ANY)
    specs = [anywhere if i in (3, 4) else vmem for i in range(17)]
    specs.append(pl.BlockSpec(memory_space=pltpu.SMEM))
    f32, bf16 = jnp.float32, jnp.bfloat16
    dma = pltpu.SemaphoreType.DMA
    outs = [
        (own_rows, model_width),
        (8, model_width),
        (late_rows, model_width),
        (gate_rows, model_width),
        (channel_rows, first_columns),
    ]
    tiled = pltpu.VMEM((tiles, row_count, lanes), f32)
    spreads = pltpu.VMEM((steps, states, subs, lanes), f32)
    summed = pltpu.VMEM((row_count, states * lanes), f32)
    return pl.pallas_call(
        functools.partial(back_kernel, dt_rank, states, tap_count, cut),
        in_specs=specs,
        out_specs=[vmem] * len(outs),
        out_shape=[jax.ShapeDtypeStruct(shape, f32) for shape in outs],
        scratch_shapes=[
            spreads,
            spreads,
            pltpu.VMEM((steps + 1, states, subs, lanes), f32),
            summed,
            summed,
            tiled,
            tiled,
            tiled,
            tiled,
            pltpu.VMEM((row_count, lanes), f32),
            pltpu.VMEM((row_count, width), bf16),
            pltpu.VMEM((row_count, width), bf16),
            pltpu.VMEM((row_count + subs, width), f32),
            pltpu.VMEM((subs, width), f32),
            pltpu.VMEM((others, own_rows, model_width), bf16),
            pltpu.VMEM((others, own_rows, model_width), bf16),
            pltpu.VMEM((row_count, lanes), f32),
            pltpu.VMEM((row_count, lanes), bf16),
            pltpu.VMEM((others, row_count, lanes), bf16),
            pltpu.VMEM((row_count, lanes), bf16),
            pltpu.VMEM((tiles, lanes, lanes), f32),
            pltpu.VMEM((states * lanes, lanes), bf16),
            pltpu.VMEM((width, first_columns), bf16),
            pltpu.VMEM((width // 2, first_columns), bf16),
            pltpu.VMEM((width // 2, first_columns), bf16),
            pltpu.VMEM((split, late_rows, model_width), bf16),
            pltpu.VMEM((split, gate_rows, model_width), bf16),
            pltpu.VMEM((split, channel_rows, first_columns), bf16),
            pltpu.VMEM((2, 8, model_width), f32),
            pltpu.VMEM((split, 8, model_width), f32),
            pltpu.VMEM((split, 8, model_width), f32),
        ]
        + [dma((2, others))] * 3
        + [dma((2,)), dma((2,)), dma((2, others)), dma((2, others)), dma((2,))]
        + [dma((2, others)), dma((2, others)), dma((2,))],
        compiler_params=pltpu.CompilerParams(
            collective_id=5, has_side_effects=True, vmem_limit_bytes=62 << 20
        ),
        cost_estimate=pl.CostEstimate(flops=1000, bytes_accessed=1000, transcendentals=0),
    )(
        dy, gz, later, mine, gate_mine, first_full, gate_full, normed, input_all, coef, step, start,
        rows, d_resid, tokens, gains, small, lengths,
    )


def norm_rows(values, gain_row):
    return values * lax.rsqrt(jnp.mean(values * values, -1, keepdims=True) + eps_norm) * gain_row


def matmul(first_op, second_op):
    return jnp.dot(first_op, second_op, preferred_element_type=jnp.float32)


def matmul_nt(first_op, second_op):
    return lax.dot_general(
        first_op, second_op, (((1,), (1,)), ((), ())), preferred_element_type=jnp.float32
    )


def matmul_tn(first_op, second_op):
    return lax.dot_general(
        first_op, second_op, (((0,), (0,)), ((), ())), preferred_element_type=jnp.float32
    )


def low_bits(value):
    return value.astype(jnp.bfloat16)


def swap_low(value, k):
    count = lax.axis_size("seq")
    return lax.ppermute(value, "seq", [(s, s ^ k) for s in range(count)])


def turn_high(value, k):
    count = lax.axis_size("seq")
    return lax.ppermute(value, "seq", [(s, (s + split * k) % count) for s in range(count)])


def from_high(value, k):
    count = lax.axis_size("seq")
    pairs = [(s, s + split * k) for s in range(count) if 0 <= s + split * k < count]
    return lax.ppermute(value, "seq", pairs)


def swap_core(value):
    return lax.ppermute(value, "grp", [(0, 1), (1, 0)])


def high_groups():
    count = lax.axis_size("seq")
    return [[h * split + l for h in range(count // split)] for l in range(split)]


def gather_low(value):
    low = lax.axis_index("seq") % split
    first_bit, second_bit = low % 2 == 1, low // 2 == 1
    own, one, two, three = [value] + [swap_low(value, k) for k in range(1, split)]
    a, b = jnp.where(first_bit, one, own), jnp.where(first_bit, own, one)
    c, d = jnp.where(first_bit, three, two), jnp.where(first_bit, two, three)
    pieces = [
        jnp.where(second_bit, c, a),
        jnp.where(second_bit, d, b),
        jnp.where(second_bit, a, c),
        jnp.where(second_bit, b, d),
    ]
    return jnp.concatenate(pieces, 0)


def scatter_low(partial):
    low = lax.axis_index("seq") % split
    rows = partial.shape[0] // split

    def block(at):
        return lax.dynamic_slice_in_dim(partial, at * rows, rows, 0)

    arrived = [swap_low(low_bits(block(low ^ k)), k) for k in range(1, split)]
    return sum(a.astype(jnp.float32) for a in [block(low)] + arrived)


def sum_low(partial):
    low_partial = low_bits(partial)
    arrived = [swap_low(low_partial, k) for k in range(1, split)]
    return partial + sum(a.astype(jnp.float32) for a in arrived)


def gather_high(value):
    high_count = lax.axis_size("seq") // split
    if high_count > 4:
        return lax.all_gather(value, "seq", axis_index_groups=high_groups())
    high = lax.axis_index("seq") // split
    turned = [turn_high(value, k) for k in range(1, high_count)]
    line = turned[::-1] + [value] + turned[::-1]
    return lax.dynamic_slice_in_dim(jnp.stack(line), high_count - 1 - high, high_count, 0)


def gather_core(own):
    full = jnp.stack([own, swap_core(own)])
    return full.reshape((-1,) + own.shape[1:])


def after(value, *others):
    return lax.optimization_barrier((value,) + others)[0]


def pad_rows(value, rows):
    return jnp.pad(value, ((0, rows - value.shape[0]), (0, 0)))


def fold_core(partial, rows):
    high_count = lax.axis_size("seq") // split
    blocks = partial.reshape(2, high_count, rows, partial.shape[-1])
    arrived = swap_core(low_bits(blocks[1]))
    return low_bits(blocks[0].astype(jnp.float32) + arrived.astype(jnp.float32))


def fold_high(mine):
    high_count = lax.axis_size("seq") // split
    if high_count > 4:
        return lax.psum_scatter(
            mine.astype(jnp.float32), "seq", scatter_dimension=0, axis_index_groups=high_groups()
        )
    high = lax.axis_index("seq") // split

    def block(at):
        return lax.dynamic_index_in_dim(mine, at % high_count, 0, False)

    arrived = [turn_high(block(high + k), k) for k in range(1, high_count)]
    return sum(a.astype(jnp.float32) for a in [block(high)] + arrived)


def sum_all(partial):
    high_count = lax.axis_size("seq") // split
    total = partial + swap_core(partial)
    step = 1
    while step < high_count * split:
        total = total + swap_low(total, step)
        step *= 2
    return total


def entering_state(grow, state, reverse):
    high_count = lax.axis_size("seq") // split
    packed = jnp.concatenate([grow, state], 0)
    states = grow.shape[0]
    if high_count > 4:
        high = lax.axis_index("seq") // split
        every = lax.all_gather(packed, "seq", axis_index_groups=high_groups())

        def one(turn, total):
            source = high_count - 1 - turn if reverse else turn
            piece = lax.dynamic_index_in_dim(every, source, 0, False)
            return piece[states:] + piece[:states] * total

        ahead = high_count - 1 - high if reverse else high
        return lax.fori_loop(0, ahead, one, jnp.zeros_like(state))
    total = jnp.zeros_like(state)
    near = [from_high(packed, -k if reverse else k) for k in range(1, high_count)]
    for piece in near[::-1]:
        total = piece[states:] + piece[:states] * total
    return total


def shards_general(
    tokens,
    routes,
    lengths,
    grad_out,
    norm_gains,
    router,
    in_weight,
    conv_weight,
    x_weight,
    dt_weight,
    dt_bias,
    a_log,
    skip_gain,
    out_weight,
    expert_in,
    expert_out,
):
    channels, tap_count = conv_weight.shape
    dt_rank = dt_weight.shape[1]
    states = a_log.shape[1]
    expert_count, hidden, model_width = expert_in.shape
    own_rows = tokens.shape[0]
    row_count = own_rows * split
    high_count = lax.axis_size("seq") // split
    low = lax.axis_index("seq") % split
    high = lax.axis_index("seq") // split
    coef_count = dt_rank + 2 * states
    channel_rows = -(-channels // 16) * 16
    width = 2 * high_count * channel_rows
    hidden_rows = expert_count * hidden
    small_width = -(-(coef_count + dt_rank + tap_count + 2 + states) // lanes) * lanes

    small = jnp.concatenate(
        [x_weight, dt_weight, conv_weight, dt_bias[:, None], a_log, skip_gain[:, None]], 1
    )
    small = jnp.pad(small, ((0, 0), (0, small_width - small.shape[1])))
    inputs = tokens.astype(jnp.float32)
    edge = 16
    halo = from_high(tokens[own_rows - edge :], 1).astype(jnp.float32)
    normed_own = low_bits(norm_rows(jnp.concatenate([inputs, halo], 0), norm_gains[0]))
    payload = pad_rows(jnp.concatenate([in_weight[0], small], 1), channel_rows)
    first_full = gather_core(gather_high(payload)).reshape(width, -1)
    normed = gather_low(normed_own).reshape(split, own_rows + edge, model_width)
    normed_edge = normed[split - 1, own_rows:]
    normed = normed[:, :own_rows].reshape(row_count, model_width)
    first_in, small_full = first_full[:, :model_width], first_full[:, model_width:]
    x_full = small_full[:, :coef_count]
    at = coef_count
    dt_full = small_full[:, at : at + dt_rank]
    at = at + dt_rank
    conv_taps = small_full[:, at : at + tap_count].astype(jnp.float32)
    at = at + tap_count
    bias_vals = small_full[:, at].astype(jnp.float32)
    at = at + 1
    decay_rate = -jnp.exp(small_full[:, at : at + states].astype(jnp.float32)).T
    at = at + states
    skip_vals = small_full[:, at].astype(jnp.float32)
    rate = decay_rate * log2e

    early_part = jnp.concatenate(
        [
            pad_rows(in_weight[1], channel_rows),
            pad_rows(out_weight, channel_rows),
            expert_in[0],
        ],
        0,
    )
    early_part = gather_high(after(early_part, first_full))
    routed_part = jnp.concatenate(
        [grad_out, routes[:, None].astype(jnp.float32) * jnp.ones((1, lanes), jnp.float32)], 1
    )
    routed_part = gather_low(after(low_bits(routed_part), normed))
    grad_rows = routed_part[:, :model_width]
    routes_all = routed_part[:, model_width : model_width + 1].astype(jnp.int32)
    late_part = jnp.concatenate(
        [expert_in[1:].reshape(-1, model_width), expert_out.reshape(-1, model_width)], 0
    )

    place = high * row_count + jnp.arange(row_count, dtype=jnp.int32)
    first_len = lengths[0, 0]
    offset = jnp.where(place < first_len, place, place - first_len)
    reset = jnp.where(offset[:, None] == 0, 1e30, 0.0) * jnp.ones((1, lanes), jnp.float32)
    valid_rows = [
        (offset >= tap_count - 1 - k).astype(jnp.float32)[:, None] for k in range(tap_count)
    ]

    all_input = low_bits(matmul_nt(jnp.concatenate([normed_edge, normed], 0), first_in))
    conv_input = all_input[edge:]
    window = all_input[edge - (tap_count - 1) :].astype(jnp.float32)
    conv_sum = sum(
        conv_taps[:, k] * window[k : k + row_count] * valid_rows[k] for k in range(tap_count)
    )
    mixed_in = low_bits(jax.nn.silu(conv_sum))
    mixed_val = mixed_in.astype(jnp.float32)
    coef_pad = jnp.pad(x_full, ((0, 0), (0, lanes - coef_count)))
    coef_rows = sum_low(matmul(mixed_in, coef_pad))
    dt_low = low_bits(coef_rows[:, :dt_rank])
    dt_pre = matmul_nt(dt_low, dt_full) + bias_vals
    step_size = jax.nn.softplus(dt_pre)
    drive = step_size * mixed_val
    first_b, first_c = dt_rank, dt_rank + states
    peers = high_count - 1 if high_count <= 4 else 0
    grow, state, enter = scan_ends(
        step_size, reset, drive, coef_rows, rate, first_b, False, peers
    )
    slice_grow = grow[:, subs - 1]
    if not peers:
        enter = entering_state(slice_grow, state[:, subs - 1], False)
    enter, early_part, late_part = lax.optimization_barrier((enter, early_part, late_part))
    early_full = gather_core(early_part)
    late_part = gather_high(late_part)
    y_scan, start, hist = scan_forward(
        step_size, reset, drive, coef_rows, rate, grow, state, enter, first_b, first_c
    )
    y_scan, early_full = lax.optimization_barrier((y_scan, early_full))
    second_in = early_full[:, :channel_rows].reshape(width, model_width)
    out_full = early_full[:, channel_rows : 2 * channel_rows].reshape(width, model_width)
    z_gate = matmul_nt(normed, second_in)
    y_value = y_scan + skip_vals * mixed_val
    gate_z = jax.nn.silu(z_gate)
    gated = low_bits(y_value * gate_z)
    resid = inputs + scatter_low(matmul(gated, out_full))

    resid, late_part = lax.optimization_barrier((resid, late_part))
    late_full = gather_core(late_part)
    second_own = low_bits(norm_rows(resid, norm_gains[1]))
    second = gather_low(second_own)

    def gate_of(rows, row_routes):
        logits = matmul(rows, router)
        chosen = row_routes == jnp.arange(expert_count, dtype=jnp.int32)[None, :]
        chosen = chosen.astype(jnp.float32)
        probs = jax.nn.softmax(logits, -1)
        return logits, chosen, jnp.sum(probs * chosen, -1, keepdims=True)

    gate_rows = gate_of(second, routes_all)[2]
    routed = low_bits(gate_rows * grad_rows.astype(jnp.float32))
    parts = [(early_full[:, 2 * channel_rows :], 0)]
    parts += [(late_full, e * hidden) for e in range(2 * expert_count - 1)]
    step_rows = hidden
    if hidden % 16:
        step_rows = 2 * high_count * hidden // 4
        parts = [
            (w[:, a : a + hidden].reshape(4, step_rows, model_width), 0) for w, a in parts
        ]
    sums, hidden_grads = run_experts(
        second, routed, routed_part[:, model_width:].astype(jnp.float32), parts, step_rows
    )
    if hidden % 16:
        pieces = hidden_grads.reshape(4, 2 * expert_count, -1, hidden, model_width)
        hidden_grads = pieces.swapaxes(1, 2).reshape(-1, 2 * hidden_rows, model_width)
    hidden_mine = fold_core(hidden_grads, 2 * hidden_rows)
    sums = scatter_low(sums)
    expert_y, d_second = sums[:, :model_width], sums[:, model_width:]
    d_second, hidden_mine = lax.optimization_barrier((d_second, hidden_mine))
    cut = hidden_rows * 2 // 3
    hidden_early = fold_high(hidden_mine[:, :cut])
    hidden_mine = hidden_mine[:, cut:]
    logits, chosen, gate_own = gate_of(second_own, routes[:, None])
    mixed_out = low_bits(resid + gate_own * expert_y)
    d_gate = jnp.sum(expert_y * grad_out, -1, keepdims=True)
    _, soft_pull = jax.vjp(lambda v: jax.nn.softmax(v, -1), logits)
    d_logits = low_bits(soft_pull(chosen * d_gate)[0])
    grad_router = matmul_tn(d_logits, second_own)
    d_second = d_second + matmul_nt(d_logits, router)
    _, norm_pull_two = jax.vjp(norm_rows, resid, norm_gains[1])
    d_resid_norm, d_gain_two = norm_pull_two(d_second)
    d_resid = grad_out + d_resid_norm

    g_branch = gather_low(low_bits(d_resid))
    d_gated = matmul_nt(g_branch, out_full)
    d_y = d_gated * gate_z
    _, silu_pull = jax.vjp(jax.nn.silu, z_gate)
    d_z = silu_pull(d_gated * y_value)[0]
    gate_grads = jnp.concatenate(
        [matmul_tn(low_bits(d_z), normed), matmul_tn(gated, g_branch)], 1
    )
    gate_mine = fold_core(gate_grads, channel_rows)
    back_grow, back_state, back_enter = scan_ends(
        step_size, reset, d_y, coef_rows, rate, first_c, True, peers
    )
    if not peers:
        back_enter = entering_state(slice_grow, back_state[:, 0], True)
    back_enter, hidden_mine = lax.optimization_barrier((back_enter, hidden_mine))
    hidden_late = fold_high(hidden_mine)
    scaled_sum, in_sum, rate_sum, d_in_coef, d_out_coef = scan_backward(
        step_size,
        reset,
        drive,
        d_y,
        coef_rows,
        rate,
        start,
        hist,
        back_grow,
        back_state,
        back_enter,
        first_b,
        first_c,
    )
    d_step = scaled_sum + in_sum * mixed_val
    d_mixed = skip_vals * d_y + in_sum * step_size
    grad_skip = jnp.sum(d_y * mixed_val, 0)
    d_dt = d_step * jax.nn.sigmoid(dt_pre)
    grad_bias = jnp.sum(d_dt, 0)
    g_dt = low_bits(d_dt)
    grad_dt = matmul_tn(g_dt, dt_low)
    part_coef = jnp.concatenate([matmul(g_dt, dt_full), d_in_coef, d_out_coef], 1)
    part_coef = jnp.pad(part_coef, ((0, 0), (0, lanes - coef_count)))
    g_coef = low_bits(sum_low(part_coef)[:, :coef_count])
    grad_x = matmul_tn(mixed_in, g_coef)
    d_mixed = d_mixed + matmul_nt(g_coef, x_full)
    _, conv_pull = jax.vjp(jax.nn.silu, conv_sum)
    d_conv = conv_pull(d_mixed)[0]
    grad_conv = jnp.stack(
        [jnp.sum(d_conv * valid_rows[k] * window[k : k + row_count], 0) for k in range(tap_count)],
        1,
    )
    d_window = sum(
        jnp.pad(conv_taps[:, k] * d_conv * valid_rows[k], ((k, tap_count - 1 - k), (0, 0)))
        for k in range(tap_count)
    )
    from_next = from_high(d_window[: tap_count - 1], -1)
    d_input = d_window[tap_count - 1 :] + jnp.pad(
        from_next, ((row_count - (tap_count - 1), 0), (0, 0))
    )
    g_in = low_bits(d_input)
    g_in, hidden_late, gate_mine = lax.optimization_barrier((g_in, hidden_late, gate_mine))
    hidden_own = jnp.concatenate([hidden_early, hidden_late], 0)
    gate_own_grads = fold_high(gate_mine)
    g_z = low_bits(d_z)
    d_normed = scatter_low(matmul(g_in, first_in) + matmul(g_z, second_in))
    _, norm_pull_one = jax.vjp(norm_rows, inputs, norm_gains[0])
    d_inputs, d_gain_one = norm_pull_one(d_normed)
    grad_tokens = d_resid + d_inputs

    rest = jnp.concatenate(
        [grad_x, grad_dt, grad_conv, grad_bias[:, None], rate_sum.T, grad_skip[:, None]], 1
    )
    rest = jnp.pad(rest, ((0, 0), (0, small_width - rest.shape[1])))
    first_own = fold_high(
        fold_core(jnp.concatenate([matmul_tn(g_in, normed), rest], 1), channel_rows)
    )[:channels]
    rest_own = first_own[:, model_width:]
    gate_own_grads = gate_own_grads[:channels]
    sums = sum_all(jnp.concatenate([jnp.stack([d_gain_one, d_gain_two]), grad_router], 0))
    ends = [0]
    for count in (coef_count, dt_rank, tap_count, 1, states, 1):
        ends.append(ends[-1] + count)
    grad_x, grad_dt, grad_conv, grad_bias, grad_alog, grad_skip = (
        rest_own[:, a:b] for a, b in zip(ends[:-1], ends[1:], strict=True)
    )
    return (
        mixed_out,
        grad_tokens,
        sums[:2],
        sums[2:].T,
        jnp.stack([first_own[:, :model_width], gate_own_grads[:, :model_width]]),
        grad_conv,
        grad_x,
        grad_dt,
        grad_bias[:, 0],
        grad_alog,
        grad_skip[:, 0],
        gate_own_grads[:, model_width:],
        hidden_own[:hidden_rows].reshape(expert_count, hidden, model_width),
        hidden_own[hidden_rows:].reshape(expert_count, hidden, model_width),
    )


def shards_plane(
    tokens,
    routes,
    lengths,
    grad_out,
    norm_gains,
    router,
    in_weight,
    conv_weight,
    x_weight,
    dt_weight,
    dt_bias,
    a_log,
    skip_gain,
    out_weight,
    expert_in,
    expert_out,
):
    channels, tap_count = conv_weight.shape
    dt_rank = dt_weight.shape[1]
    states = a_log.shape[1]
    expert_count, hidden, model_width = expert_in.shape
    own_rows = tokens.shape[0]
    row_count = own_rows * split
    high_count = lax.axis_size("seq") // split
    low = lax.axis_index("seq") % split
    high = lax.axis_index("seq") // split
    coef_count = dt_rank + 2 * states
    channel_rows = -(-channels // 16) * 16
    width = 2 * high_count * channel_rows
    hidden_rows = expert_count * hidden
    small_width = -(-(coef_count + dt_rank + tap_count + 2 + states) // lanes) * lanes

    small = jnp.concatenate(
        [x_weight, dt_weight, conv_weight, dt_bias[:, None], a_log, skip_gain[:, None]], 1
    )
    small = jnp.pad(small, ((0, 0), (0, small_width - small.shape[1])))
    inputs = tokens.astype(jnp.float32)
    def wide(parts, columns):
        part = jnp.concatenate(parts, 1)
        return jnp.pad(part, ((0, 0), (0, columns - part.shape[1])))

    gap = jnp.zeros((channels, 2), jnp.bfloat16)
    a_part = pad_rows(
        jnp.concatenate(
            [
                in_weight[0],
                wide([x_weight], lanes),
                wide([dt_weight], lanes),
                wide([conv_weight, dt_bias[:, None], skip_gain[:, None], gap, a_log], lanes),
            ],
            1,
        ),
        channel_rows,
    )
    b_part = jnp.concatenate(
        [pad_rows(in_weight[1], channel_rows), pad_rows(out_weight, channel_rows)], 0
    )
    c_part = jnp.concatenate(
        [expert_in.reshape(-1, model_width), expert_out.reshape(-1, model_width)], 0
    )
    g_part = low_bits(
        jnp.concatenate(
            [grad_out, routes[:, None].astype(jnp.float32) * jnp.ones((1, lanes), jnp.float32)], 1
        )
    )
    (
        first_full, gate_full, hidden_full, normed, _, routed, input_all, coef, step, z, y, gated, start,
        resid, second, rows,
    ) = run_mixer(
        tokens, norm_gains, lengths, a_part, b_part, c_part, g_part, dt_rank, states, tap_count
    )
    cut = hidden_rows * 2 // 3
    router_lanes = jnp.pad(router, ((0, 0), (0, lanes - expert_count)))
    mixed_out, d_resid, small_sums, dy, gz, later, mine, early, gate_mine = run_turn(
        second, routed, hidden_full, router_lanes, resid, grad_out, norm_gains, lengths, gate_full,
        normed, coef, step, z, y, gated, rows, dt_rank, states, expert_count, cut,
    )
    grad_tokens, sums, late, gate_own, first_own = run_back(
        dy, gz, later, mine, gate_mine, first_full, gate_full, normed, input_all, coef, step, start,
        rows, d_resid, tokens, norm_gains, small_sums, lengths, dt_rank, states, tap_count, cut,
    )
    hidden_own = jnp.concatenate([early, late], 0)
    first_own, gate_first = first_own[:channels], gate_own[:channels]
    misc = first_own[:, model_width + 2 * lanes :]
    return (
        mixed_out,
        grad_tokens,
        sums[:2],
        sums[2 : 2 + expert_count].T,
        jnp.stack([first_own[:, :model_width], gate_first]),
        misc[:, :tap_count],
        first_own[:, model_width : model_width + coef_count],
        first_own[:, model_width + lanes : model_width + lanes + dt_rank],
        misc[:, bias_row],
        misc[:, alog_row : alog_row + states],
        misc[:, skip_row],
        gate_own[channel_rows : channel_rows + channels],
        hidden_own[:hidden_rows].reshape(expert_count, hidden, model_width),
        hidden_own[hidden_rows:].reshape(expert_count, hidden, model_width),
    )


def solution(mesh):
    both = ("grp", "seq")
    in_specs = (
        P(both, None),
        P(both),
        P("grp", None),
        P(both, None),
        P(),
        P(),
        P(None, both, None),
        P(both, None),
        P(both, None),
        P(both, None),
        P(both),
        P(both, None),
        P(both),
        P(both, None),
        P(None, both, None),
        P(None, both, None),
    )
    out_specs = (
        P(both, None),
        P(both, None),
        P(),
        P(),
        P(None, both, None),
        P(both, None),
        P(both, None),
        P(both, None),
        P(both),
        P(both, None),
        P(both),
        P(both, None),
        P(None, both, None),
        P(None, both, None),
    )
    shards = shards_plane if mesh.shape["seq"] == split * split else shards_general
    return jax.shard_map(shards, mesh=mesh, in_specs=in_specs, out_specs=out_specs, check_vma=False)
```

```python
import functools
import math

import jax
import jax.numpy as jnp
from jax import lax
from jax.experimental import pallas as pl
from jax.experimental.pallas import tpu as pltpu
from jax.sharding import PartitionSpec as P

eps_norm = 1e-05
split = 4
lanes = 128
subs = 8
log2e = 1.4426950408889634


def spread(coef_ref, first, spread_ref, steps, states):
    def one(s, _):
        rows = coef_ref[pl.ds(s, subs, stride=steps), :]
        for n in range(states):
            spread_ref[s, n] = jnp.broadcast_to(rows[:, first + n : first + n + 1], (subs, lanes))
        return 0

    lax.fori_loop(0, steps, one, 0, unroll=8)


def chain_rows(grow, state, reverse):
    row = lax.broadcasted_iota(jnp.int32, (subs, lanes), 0)
    shift = 1
    while shift < subs:
        turn = subs - shift if reverse else shift
        has = row < subs - shift if reverse else row >= shift
        near_grow = jnp.where(has, pltpu.roll(grow, turn, 0), 1.0)
        near_state = jnp.where(has, pltpu.roll(state, turn, 0), 0.0)
        state = state + grow * near_state
        grow = grow * near_grow
        shift *= 2
    return grow, state


def ends_kernel(
    first, reverse, states, steps, peers,
    delta_ref, reset_ref, drive_ref, coef_ref, rate_ref,
    grow_ref, state_ref, enter_ref,
    spread_ref, send_ref, arrive_ref, send_sem, arrive_sem,
):
    tile = pl.program_id(0)
    tiles = pl.num_programs(0)
    place = lax.axis_index("seq")
    high, low, core = place // split, place % split, lax.axis_index("grp")

    def other(k):
        return (core, lax.rem(high + (peers + 1 - k if reverse else k), peers + 1) * split + low)

    def copy_to(k, j):
        return pltpu.make_async_remote_copy(
            src_ref=send_ref.at[j],
            dst_ref=arrive_ref.at[k - 1, j],
            send_sem=send_sem.at[k - 1, j],
            recv_sem=arrive_sem.at[k - 1, j],
            device_id=other(k),
            device_id_type=pl.DeviceIdType.MESH,
        )

    @pl.when(tile == 0)
    def _():
        if peers:
            barrier = pltpu.get_barrier_semaphore()
            for k in range(1, peers + 1):
                pl.semaphore_signal(
                    barrier, inc=1, device_id=other(k), device_id_type=pl.DeviceIdType.MESH
                )
        spread(coef_ref, first, spread_ref, steps, states)

    rates = [jnp.broadcast_to(rate_ref[n : n + 1, :], (subs, lanes)) for n in range(states)]

    def one(turn, carry):
        s = steps - 1 - turn if reverse else turn
        total, held = carry
        step = delta_ref[pl.ds(s, subs, stride=steps), :] + reset_ref[pl.ds(s, subs, stride=steps), :]
        drive = drive_ref[pl.ds(s, subs, stride=steps), :]
        after = []
        for n in range(states):
            factor = jnp.exp2(step * rates[n])
            if reverse:
                after.append(factor * (held[n] + spread_ref[s, n] * drive))
            else:
                after.append(factor * held[n] + spread_ref[s, n] * drive)
        return total + step, tuple(after)

    zero = jnp.zeros((subs, lanes), jnp.float32)
    total, held = lax.fori_loop(0, steps, one, (zero, (zero,) * states), unroll=2)
    last = 0 if reverse else subs - 1
    for n in range(states):
        grow, state = chain_rows(jnp.exp2(total * rates[n]), held[n], reverse)
        grow_ref[n] = grow
        state_ref[n] = state
        if peers:
            send_ref[tile, n : n + 1] = grow[last : last + 1]
            send_ref[tile, states + n : states + n + 1] = state[last : last + 1]
    if not peers:
        enter_ref[...] = jnp.zeros_like(enter_ref)
        return

    @pl.when(tile == 0)
    def _():
        pl.semaphore_wait(pltpu.get_barrier_semaphore(), peers)

    for k in range(1, peers + 1):
        copy_to(k, tile).start()

    @pl.when(tile == tiles - 1)
    def _():
        for j in range(enter_ref.shape[1] // lanes):
            total = jnp.zeros((states, lanes), jnp.float32)
            for k in range(peers, 0, -1):
                copy_to(k, j).wait()
                piece = arrive_ref[k - 1, j]
                has = high + k <= peers if reverse else high >= k
                total = jnp.where(has, piece[states:] + piece[:states] * total, 0.0)
            enter_ref[:, j * lanes : (j + 1) * lanes] = total


def scan_ends(delta, reset, drive, coef, rate, first, reverse, peers):
    row_count, width = delta.shape
    states = rate.shape[0]
    steps = row_count // subs
    tiles = width // lanes
    column = pl.BlockSpec((row_count, lanes), lambda j: (0, j))
    whole = pl.BlockSpec((row_count, lanes), lambda j: (0, 0))
    ends = pl.BlockSpec((states, subs, lanes), lambda j: (0, 0, j))
    params = dict(vmem_limit_bytes=48 << 20)
    if peers:
        params.update(collective_id=2 if reverse else 1, has_side_effects=True)
    slots = max(peers, 1)
    return pl.pallas_call(
        functools.partial(ends_kernel, first, reverse, states, steps, peers),
        grid=(tiles,),
        in_specs=[column, whole, column, whole, pl.BlockSpec((states, lanes), lambda j: (0, j))],
        out_specs=[ends, ends, pl.BlockSpec((states, width), lambda j: (0, 0))],
        out_shape=[jax.ShapeDtypeStruct((states, subs, width), jnp.float32)] * 2
        + [jax.ShapeDtypeStruct((states, width), jnp.float32)],
        scratch_shapes=[
            pltpu.VMEM((steps, states, subs, lanes), jnp.float32),
            pltpu.VMEM((tiles, 2 * states, lanes), jnp.float32),
            pltpu.VMEM((slots, tiles, 2 * states, lanes), jnp.float32),
            pltpu.SemaphoreType.DMA((slots, tiles)),
            pltpu.SemaphoreType.DMA((slots, tiles)),
        ],
        compiler_params=pltpu.CompilerParams(**params),
        cost_estimate=pl.CostEstimate(flops=1000, bytes_accessed=1000, transcendentals=0),
    )(delta, reset, drive, coef, rate)


def forward_kernel(first_in, first_out, states, steps, delta_ref, reset_ref, drive_ref, coef_ref, rate_ref, grow_ref, state_ref, enter_ref, y_ref, start_ref, hist_ref, in_ref, out_ref):
    @pl.when(pl.program_id(0) == 0)
    def _():
        spread(coef_ref, first_in, in_ref, steps, states)
        spread(coef_ref, first_out, out_ref, steps, states)

    rates = [jnp.broadcast_to(rate_ref[n : n + 1, :], (subs, lanes)) for n in range(states)]
    row = lax.broadcasted_iota(jnp.int32, (subs, lanes), 0)
    held = []
    for n in range(states):
        near_grow = jnp.where(row >= 1, pltpu.roll(grow_ref[n], 1, 0), 1.0)
        near_state = jnp.where(row >= 1, pltpu.roll(state_ref[n], 1, 0), 0.0)
        start = near_state + near_grow * jnp.broadcast_to(enter_ref[n : n + 1, :], (subs, lanes))
        start_ref[n] = start
        held.append(start)

    def one(s, held):
        step = delta_ref[pl.ds(s, subs, stride=steps), :] + reset_ref[pl.ds(s, subs, stride=steps), :]
        drive = drive_ref[pl.ds(s, subs, stride=steps), :]
        after = []
        y = jnp.zeros((subs, lanes), jnp.float32)
        for n in range(states):
            now = jnp.exp2(step * rates[n]) * held[n] + in_ref[s, n] * drive
            hist_ref[0, s, n] = now
            y = y + out_ref[s, n] * now
            after.append(now)
        y_ref[pl.ds(s, subs, stride=steps), :] = y
        return tuple(after)

    lax.fori_loop(0, steps, one, tuple(held), unroll=2)


def scan_forward(delta, reset, drive, coef, rate, grow, state, enter, first_in, first_out):
    row_count, width = delta.shape
    states = rate.shape[0]
    steps = row_count // subs
    tiles = width // lanes
    column = pl.BlockSpec((row_count, lanes), lambda j: (0, j))
    whole = pl.BlockSpec((row_count, lanes), lambda j: (0, 0))
    ends = pl.BlockSpec((states, subs, lanes), lambda j: (0, 0, j))
    per_state = pl.BlockSpec((states, lanes), lambda j: (0, j))
    return pl.pallas_call(
        functools.partial(forward_kernel, first_in, first_out, states, steps),
        grid=(tiles,),
        in_specs=[column, whole, column, whole, per_state, ends, ends, per_state],
        out_specs=[column, ends, pl.BlockSpec((1, steps, states, subs, lanes), lambda j: (j, 0, 0, 0, 0))],
        out_shape=[
            jax.ShapeDtypeStruct((row_count, width), jnp.float32),
            jax.ShapeDtypeStruct((states, subs, width), jnp.float32),
            jax.ShapeDtypeStruct((tiles, steps, states, subs, lanes), jnp.float32),
        ],
        scratch_shapes=[pltpu.VMEM((steps, states, subs, lanes), jnp.float32)] * 2,
        compiler_params=pltpu.CompilerParams(vmem_limit_bytes=48 << 20),
        cost_estimate=pl.CostEstimate(flops=1000, bytes_accessed=1000, transcendentals=0),
    )(delta, reset, drive, coef, rate, grow, state, enter)


def backward_kernel(first_in, first_out, states, steps, delta_ref, reset_ref, drive_ref, dy_ref, coef_ref, rate_ref, start_ref, hist_ref, grow_ref, state_ref, enter_ref, q_ref, r_ref, rsum_ref, din_ref, dout_ref, in_ref, out_ref, ain_ref, aout_ref):
    tile = pl.program_id(0)

    @pl.when(tile == 0)
    def _():
        spread(coef_ref, first_in, in_ref, steps, states)
        spread(coef_ref, first_out, out_ref, steps, states)
        ain_ref[...] = jnp.zeros_like(ain_ref)
        aout_ref[...] = jnp.zeros_like(aout_ref)

    row = lax.broadcasted_iota(jnp.int32, (subs, lanes), 0)
    rates = [jnp.broadcast_to(rate_ref[n : n + 1, :], (subs, lanes)) for n in range(states)]
    later = []
    for n in range(states):
        near_grow = jnp.where(row < subs - 1, pltpu.roll(grow_ref[n], subs - 1, 0), 1.0)
        near_state = jnp.where(row < subs - 1, pltpu.roll(state_ref[n], subs - 1, 0), 0.0)
        later.append(near_state + near_grow * jnp.broadcast_to(enter_ref[n : n + 1, :], (subs, lanes)))

    def at(s, load_before, carry):
        later, sums = carry
        delta = delta_ref[pl.ds(s, subs, stride=steps), :]
        step = delta + reset_ref[pl.ds(s, subs, stride=steps), :]
        drive = drive_ref[pl.ds(s, subs, stride=steps), :]
        dy = dy_ref[pl.ds(s, subs, stride=steps), :]
        q = jnp.zeros((subs, lanes), jnp.float32)
        r = jnp.zeros((subs, lanes), jnp.float32)
        after, sums_after = [], []
        for n in range(states):
            d_state = out_ref[s, n] * dy + later[n]
            back = jnp.exp2(step * rates[n]) * d_state
            scaled = back * load_before(n)
            sums_after.append(sums[n] + scaled * delta)
            q = q + scaled * rates[n]
            r = r + d_state * in_ref[s, n]
            ain_ref[s, n] += d_state * drive
            aout_ref[s, n] += hist_ref[0, s, n] * dy
            after.append(back)
        q_ref[pl.ds(s, subs, stride=steps), :] = q * (1.0 / log2e)
        r_ref[pl.ds(s, subs, stride=steps), :] = r
        return tuple(after), tuple(sums_after)

    zero = jnp.zeros((subs, lanes), jnp.float32)

    def one(turn, carry):
        s = steps - 1 - turn
        return at(s, lambda n: hist_ref[0, s - 1, n], carry)

    carry = lax.fori_loop(0, steps - 1, one, (tuple(later), (zero,) * states))
    _, sums = at(0, lambda n: start_ref[n], carry)
    for n in range(states):
        rsum_ref[n : n + 1, :] = jnp.sum(sums[n] * rates[n], 0, keepdims=True) * (1.0 / log2e)

    @pl.when(tile == pl.num_programs(0) - 1)
    def _():
        ones = jnp.ones((subs, lanes), jnp.bfloat16)

        def fold(ref, s):
            values = ref[s].reshape(states * subs, lanes)
            high = values.astype(jnp.bfloat16)
            low = (values - high.astype(jnp.float32)).astype(jnp.bfloat16)
            dims = (((1,), (1,)), ((), ()))
            return lax.dot_general(ones, high, dims, preferred_element_type=jnp.float32) + lax.dot_general(ones, low, dims, preferred_element_type=jnp.float32)

        def both(s, _):
            din_ref[pl.ds(s, 1), :] = fold(ain_ref, s)[:1]
            dout_ref[pl.ds(s, 1), :] = fold(aout_ref, s)[:1]
            return 0

        lax.fori_loop(0, steps, both, 0)


def scan_backward(delta, reset, drive, dy, coef, rate, start, hist, grow, state, enter, first_in, first_out):
    row_count, width = delta.shape
    states = rate.shape[0]
    steps = row_count // subs
    tiles = width // lanes
    column = pl.BlockSpec((row_count, lanes), lambda j: (0, j))
    whole = pl.BlockSpec((row_count, lanes), lambda j: (0, 0))
    ends = pl.BlockSpec((states, subs, lanes), lambda j: (0, 0, j))
    per_state = pl.BlockSpec((states, lanes), lambda j: (0, j))
    folded = pl.BlockSpec((steps, states * subs), lambda j: (0, 0))
    q, r, rsum, din, dout = pl.pallas_call(
        functools.partial(backward_kernel, first_in, first_out, states, steps),
        grid=(tiles,),
        in_specs=[column, whole, column, column, whole, per_state, ends, pl.BlockSpec((1, steps, states, subs, lanes), lambda j: (j, 0, 0, 0, 0)), ends, ends, per_state],
        out_specs=[column, column, per_state, folded, folded],
        out_shape=[
            jax.ShapeDtypeStruct((row_count, width), jnp.float32),
            jax.ShapeDtypeStruct((row_count, width), jnp.float32),
            jax.ShapeDtypeStruct((states, width), jnp.float32),
            jax.ShapeDtypeStruct((steps, states * subs), jnp.float32),
            jax.ShapeDtypeStruct((steps, states * subs), jnp.float32),
        ],
        scratch_shapes=[pltpu.VMEM((steps, states, subs, lanes), jnp.float32)] * 4,
        compiler_params=pltpu.CompilerParams(vmem_limit_bytes=56 << 20),
        cost_estimate=pl.CostEstimate(flops=1000, bytes_accessed=1000, transcendentals=0),
    )(delta, reset, drive, dy, coef, rate, start, hist, grow, state, enter)

    def unfold(folded_rows):
        return folded_rows.reshape(steps, states, subs).transpose(2, 0, 1).reshape(row_count, states)

    return q, r, rsum, unfold(din), unfold(dout)


def experts_kernel(
    expert_count, second_ref, routed_ref, route_ref, *refs
):
    weights_in, weights_out = refs[:expert_count], refs[expert_count : 2 * expert_count]
    sums_ref, grads_ref, y_ref, d_ref = refs[2 * expert_count :]
    step = pl.program_id(0)
    blocks, hidden, model_width = weights_in[0].shape
    rows = blocks * hidden

    @pl.when(step == 0)
    def _():
        y_ref[...] = jnp.zeros_like(y_ref)
        d_ref[...] = jnp.zeros_like(d_ref)

    up = jnp.concatenate([w[...].reshape(rows, model_width) for w in weights_in], 0)
    down = jnp.concatenate([w[...].reshape(rows, model_width) for w in weights_out], 0)
    second, routed = second_ref[...], routed_ref[...]
    pre = matmul_nt(second, up)
    column = lax.broadcasted_iota(jnp.int32, (1, expert_count * rows), 1)
    owner = jnp.zeros_like(column)
    for e in range(1, expert_count):
        owner = owner + (column >= e * rows).astype(jnp.int32)
    picked = route_ref[:, :1] == owner.astype(jnp.float32)
    half = 0.5 + 0.5 * lax.erf(pre * (0.5**0.5))
    bell = jnp.exp(-0.5 * pre * pre) * (1.0 / (2.0 * math.pi) ** 0.5)
    act = low_bits(jnp.where(picked, pre * half, 0.0))
    d_pre = low_bits(jnp.where(picked, matmul_nt(routed, down) * (half + pre * bell), 0.0))
    y_ref[...] += matmul(act, down)
    d_ref[...] += matmul(d_pre, up)
    grad_up = low_bits(matmul_tn(d_pre, second))
    grad_down = low_bits(matmul_tn(act, routed))
    for e in range(expert_count):
        for b in range(blocks):
            at = e * rows + b * hidden
            grads_ref[b, e * hidden : (e + 1) * hidden] = grad_up[at : at + hidden]
            to = (expert_count + e) * hidden
            grads_ref[b, to : to + hidden] = grad_down[at : at + hidden]

    @pl.when(step == pl.num_programs(0) - 1)
    def _():
        sums_ref[:, :model_width] = low_bits(y_ref[...])
        sums_ref[:, model_width:] = low_bits(d_ref[...])


def run_experts(second, routed, route_lanes, parts, hidden):
    row_count, model_width = second.shape
    expert_count = len(parts) // 2
    block_count = parts[0][0].shape[0]
    blocks = 2
    fixed = pl.BlockSpec((row_count, model_width), lambda i: (0, 0))

    def spec(first):
        return pl.BlockSpec((blocks, hidden, model_width), lambda i: (i, first // hidden, 0))

    return pl.pallas_call(
        functools.partial(experts_kernel, expert_count),
        grid=(block_count // blocks,),
        in_specs=[fixed, fixed, pl.BlockSpec((row_count, lanes), lambda i: (0, 0))]
        + [spec(first) for _, first in parts],
        out_specs=[
            pl.BlockSpec((row_count, 2 * model_width), lambda i: (0, 0)),
            pl.BlockSpec((blocks, 2 * expert_count * hidden, model_width), lambda i: (i, 0, 0)),
        ],
        out_shape=[
            jax.ShapeDtypeStruct((row_count, 2 * model_width), jnp.bfloat16),
            jax.ShapeDtypeStruct(
                (block_count, 2 * expert_count * hidden, model_width), jnp.bfloat16
            ),
        ],
        scratch_shapes=[pltpu.VMEM((row_count, model_width), jnp.float32)] * 2,
        compiler_params=pltpu.CompilerParams(vmem_limit_bytes=56 << 20),
        cost_estimate=pl.CostEstimate(flops=1000, bytes_accessed=1000, transcendentals=0),
    )(second, routed, route_lanes, *[w for w, _ in parts])


def kernel_place():
    place = lax.axis_index("seq")
    return lax.axis_index("grp"), place // split, place % split


def remote(src, dst, send_sem, arrive_sem, core, high, low):
    return pltpu.make_async_remote_copy(
        src_ref=src,
        dst_ref=dst,
        send_sem=send_sem,
        recv_sem=arrive_sem,
        device_id=(core, high * split + low),
        device_id_type=pl.DeviceIdType.MESH,
    )


def greet_all():
    core, high, low = kernel_place()
    barrier = pltpu.get_barrier_semaphore()
    others = [(core, lax.rem(high + k, split), low) for k in range(1, split)]
    others += [(core, high, lax.rem(low + k, split)) for k in range(1, split)]
    others += [(1 - core, high, low)]
    for c, h, l in others:
        pl.semaphore_signal(
            barrier, inc=1, device_id=(c, h * split + l), device_id_type=pl.DeviceIdType.MESH
        )
    return len(others)


def plane_copies(src_of, dst, sems, slot_by_sender):
    core, high, low = kernel_place()
    copies = []
    for k in range(1, split):
        to = lax.rem(low + k, split)
        slot = low if slot_by_sender else k - 1
        copies.append(
            remote(src_of(to, k), dst.at[slot], sems.at[0, k - 1], sems.at[1, k - 1], core, high, to)
        )
    return copies


def at_ends():
    _, high, _ = kernel_place()
    return (high == 0) | (high == split - 1)


def line_copies(src, dst_of, sems, both=False):
    core, high, low = kernel_place()
    return [
        remote(
            src, dst_of(high), sems.at[0, k - 1], sems.at[1, k - 1], core, lax.rem(high + k, split), low
        )
        for k in ((1, 2, 3) if both else (1, 3))
    ]


def line_relay(dst_of, sems):
    core, high, low = kernel_place()
    block = lax.rem(high * 2, 3) + 3 * (high // 3)
    to = lax.rem(block + 2, split)
    return remote(dst_of(block), dst_of(block), sems.at[0, 1], sems.at[1, 1], core, to, low)


def line_arrived(src, dst_of, sems, k):
    core, high, low = kernel_place()
    at = lax.rem(high + split - k, split)
    remote(src, dst_of(at), sems.at[0, k - 1], sems.at[1, k - 1], core, high, low).wait_recv()


def core_copy(dst_of, sems, k):
    core, high, low = kernel_place()
    at = lax.rem(high + split - k, split)
    return remote(dst_of(at), dst_of(split + at), sems.at[0, k], sems.at[1, k], 1 - core, high, low)


def softplus_of(value):
    return jnp.maximum(value, 0.0) + jnp.log1p(jnp.exp(-jnp.abs(value)))


def sigmoid_of(value):
    return 1.0 / (1.0 + jnp.exp(-value))


def row_loop(count, size, body):
    def one(i, _):
        body(pl.multiple_of(i * size, size))
        return 0

    lax.fori_loop(0, count // size, one, 0)


def scan_one_way(j, first_sub, reverse, states, steps, step_ref, reset_ref, drive_ref, spread_ref, rates):
    def one(turn, carry):
        s = steps - 1 - turn if reverse else turn
        total, held = carry
        step = step_ref[j, pl.ds(s, subs, stride=steps), :] + reset_ref[pl.ds(s, subs, stride=steps), :]
        drive = drive_ref[j, pl.ds(s, subs, stride=steps), :]
        after_step = []
        for n in range(states):
            factor = jnp.exp2(step * rates[n])
            if reverse:
                after_step.append(factor * (held[n] + spread_ref[s, n] * drive))
            else:
                after_step.append(factor * held[n] + spread_ref[s, n] * drive)
        return total + step, tuple(after_step)

    zero = jnp.zeros((subs, lanes), jnp.float32)
    total, held = lax.fori_loop(0, steps, one, (zero, (zero,) * states), unroll=2)
    return [chain_rows(jnp.exp2(total * rates[n]), held[n], reverse) for n in range(states)]


def chain_enter(arrive_ref, j, states, reverse):
    _, high, _ = kernel_place()
    total = jnp.zeros((states, lanes), jnp.float32)
    for k in range(split - 1, 0, -1):
        piece = arrive_ref[k - 1, j]
        has = high + k < split if reverse else high >= k
        total = jnp.where(has, piece[states:] + piece[:states] * total, 0.0)
    return total


def tile_rates(rows_ref, j, states):
    decay = -jnp.exp(rows_ref[j, alog_row : alog_row + states, :])
    return decay


def ends_copies(send_ref, arrive_ref, sems, j, reverse):
    core, high, low = kernel_place()
    copies = []
    for k in range(1, split):
        to = lax.rem(high + split - k, split) if reverse else lax.rem(high + k, split)
        copies.append(
            remote(
                send_ref.at[j],
                arrive_ref.at[k - 1, j],
                sems.at[0, k - 1, j],
                sems.at[1, k - 1, j],
                core,
                to,
                low,
            )
        )
    return copies


alog_row = 8
bias_row = 4
skip_row = 5
early_hidden = 96


def mixer_kernel(
    dt_rank, states, tap_count,
    tokens_ref, gains_ref, lengths_ref, a_ref, b_ref, c_ref, g_ref,
    first_ref, gate_ref, hidden_ref, normed_ref, edge_ref, routed_ref, input_ref, coef_ref,
    step_ref, z_ref, y_ref, gated_ref, start_ref, resid_ref, second_ref, rows_ref,
    in_ref, out_ref, drive_ref, reset_ref, mixed_ref, partial_ref, arrive_ref, coef_send_ref,
    coef_arrive_ref, send_ref, ends_ref, grow_ref, state_ref,
    a_sems, b_sems, c_sems, d_sems, a_core, b_core, c_core, d_core, token_sems, route_sems,
    second_sems, coef_sems, sum_sems, edge_send, edge_arrive, ends_sems, local_sem,
):
    core, high, low = kernel_place()
    own_rows, model_width = tokens_ref.shape
    row_count = own_rows * split
    steps = row_count // subs
    tiles = step_ref.shape[0]
    width = tiles * lanes
    edge = edge_ref.shape[0]
    first_b, first_c = dt_rank, dt_rank + states
    greeted = greet_all()

    def edge_copy(l):
        return remote(
            normed_ref.at[low, pl.ds(own_rows - edge, edge)],
            edge_ref,
            edge_send.at[l],
            edge_arrive,
            core,
            lax.rem(high + 1, split),
            l,
        )

    barrier = pltpu.get_barrier_semaphore()
    for k in range(1, split):
        pl.semaphore_signal(
            barrier,
            inc=1,
            device_id=(core, lax.rem(high + split - 1, split) * split + lax.rem(low + k, split)),
            device_id_type=pl.DeviceIdType.MESH,
        )
    greeted += split - 1
    tokens = tokens_ref[...].astype(jnp.float32)
    normed_ref[low] = low_bits(norm_rows(tokens, gains_ref[0:1, :]))
    local = pltpu.make_async_copy(c_ref, hidden_ref.at[high], local_sem)
    local.start()
    first_ref[high] = a_ref[...]
    gate_ref[high] = b_ref[...]
    routed_ref[low] = g_ref[...]
    pl.semaphore_wait(barrier, greeted)

    @pl.when((low == split - 1) & (high < split - 1))
    def _():
        for l in range(split):
            edge_copy(l).start()

    hidden_count = c_ref.shape[0]
    c_src = c_ref.at[pl.ds(0, early_hidden)]
    d_src = c_ref.at[pl.ds(early_hidden, hidden_count - early_hidden)]

    def a_dst(at):
        return first_ref.at[at]

    def b_dst(at):
        return gate_ref.at[at]

    def c_dst(at):
        return hidden_ref.at[at, pl.ds(0, early_hidden)]

    def d_dst(at):
        return hidden_ref.at[at, pl.ds(early_hidden, hidden_count - early_hidden)]

    token_copies = plane_copies(lambda to, k: normed_ref.at[low], normed_ref, token_sems, True)
    a_copies = line_copies(a_ref, a_dst, a_sems)
    b_copies = line_copies(b_ref, b_dst, b_sems)
    c_copies = line_copies(c_src, c_dst, c_sems)
    d_copies = line_copies(d_src, d_dst, d_sems)
    route_copies = plane_copies(lambda to, k: g_ref, routed_ref, route_sems, True)
    relays = [line_relay(a_dst, a_sems), line_relay(b_dst, b_sems)]
    relays += [line_relay(c_dst, c_sems), line_relay(d_dst, d_sems)]
    for copy in token_copies + a_copies + route_copies:
        copy.start()

    def relay_from_end(i):
        @pl.when(at_ends())
        def _():
            relays[i].start()

    def relay_inside(i):
        @pl.when(jnp.logical_not(at_ends()))
        def _():
            relays[i].start()

    def arrived(src, dst_of, sems, core_sems, ks):
        for k in ks:
            line_arrived(src, dst_of, sems, k)
            copy = core_copy(dst_of, core_sems, k)
            copy.start()
            core_copies.append(copy)

    relay_from_end(0)
    core_copies = [core_copy(a_dst, a_core, 0), core_copy(b_dst, b_core, 0)]
    for copy in core_copies:
        copy.start()

    first_len = lengths_ref[0, 0]

    def offsets(at, rows):
        place = high * row_count + at + lax.broadcasted_iota(jnp.int32, (rows, lanes), 0)
        return jnp.where(place < first_len, place, place - first_len)

    def fill_reset(at):
        reset_ref[pl.ds(at, 64), :] = jnp.where(offsets(at, 64) == 0, 1e30, 0.0)

    row_loop(row_count, 64, fill_reset)

    @pl.when(high == 0)
    def _():
        edge_ref[...] = jnp.zeros_like(edge_ref)

    arrived(a_ref, a_dst, a_sems, a_core, (1, 3))
    relay_inside(0)
    for copy in b_copies:
        copy.start()
    relay_from_end(1)
    for copy in token_copies:
        copy.wait()
    arrived(a_ref, a_dst, a_sems, a_core, (2,))

    @pl.when(high > 0)
    def _():
        edge_copy(0).wait_recv()

    @pl.when((low == split - 1) & (high < split - 1))
    def _():
        for l in range(split):
            edge_copy(l).wait_send()

    for k in range(split):
        core_copy(a_dst, a_core, k).wait_recv()

    weights = first_ref[:, :, :model_width].reshape(width, model_width)
    input_ref[:edge, :] = low_bits(matmul_nt(edge_ref[...], weights)).astype(jnp.float32)
    for l in range(split):
        block = low_bits(matmul_nt(normed_ref[l], weights)).astype(jnp.float32)
        input_ref[edge + l * own_rows : edge + (l + 1) * own_rows, :] = block
    small = first_ref[:, :, model_width + 2 * lanes :].reshape(width, lanes).astype(jnp.float32)
    for j in range(tiles):
        rows_ref[j] = small[j * lanes : (j + 1) * lanes].T

    def convolve(at):
        offset = offsets(at, 32)
        for j in range(tiles):
            span = input_ref[pl.ds(at, 32 + edge), j * lanes : (j + 1) * lanes]
            conv_sum = jnp.zeros((32, lanes), jnp.float32)
            for k in range(tap_count):
                shift = edge - (tap_count - 1) + k
                term = rows_ref[j, k : k + 1, :] * span[shift : shift + 32]
                conv_sum = conv_sum + jnp.where(offset >= tap_count - 1 - k, term, 0.0)
            mixed_ref[pl.ds(at, 32), j * lanes : (j + 1) * lanes] = low_bits(
                conv_sum * sigmoid_of(conv_sum)
            )

    row_loop(row_count, 32, convolve)
    arrived(b_ref, b_dst, b_sems, b_core, (1, 3))
    relay_inside(1)
    local.wait()
    for copy in (core_copy(c_dst, c_core, 0), core_copy(d_dst, d_core, 0)):
        copy.start()
        core_copies.append(copy)
    for copy in c_copies:
        copy.start()
    relay_from_end(2)

    x_full = first_ref[:, :, model_width : model_width + lanes].reshape(width, lanes)
    part = matmul(mixed_ref[...], x_full)
    coef_ref[...] = part
    coef_send_ref[...] = low_bits(part)
    coef_copies = plane_copies(lambda to, k: coef_send_ref, coef_arrive_ref, coef_sems, False)
    for copy in coef_copies:
        copy.start()
    for copy in coef_copies:
        copy.wait()
    total = coef_ref[...]
    for k in range(1, split):
        total = total + coef_arrive_ref[k - 1].astype(jnp.float32)
    coef_ref[...] = total
    dt_full = first_ref[:, :, model_width + lanes : model_width + 2 * lanes].reshape(width, lanes)

    def step_sizes(at):
        pre = matmul_nt(low_bits(coef_ref[pl.ds(at, 128), :]), dt_full)
        for j in range(tiles):
            cols = slice(j * lanes, (j + 1) * lanes)
            step = softplus_of(pre[:, cols] + rows_ref[j, bias_row : bias_row + 1, :])
            step_ref[j, pl.ds(at, 128), :] = step
            drive_ref[j, pl.ds(at, 128), :] = step * mixed_ref[pl.ds(at, 128), cols].astype(
                jnp.float32
            )

    row_loop(row_count, 128, step_sizes)
    spread(coef_ref, first_b, in_ref, steps, states)

    def rates_of(j):
        values = -jnp.exp(rows_ref[j, alog_row : alog_row + states, :]) * log2e
        return [jnp.broadcast_to(values[n : n + 1, :], (subs, lanes)) for n in range(states)]

    def ends_of(j, _):
        found = scan_one_way(
            j, None, False, states, steps, step_ref, reset_ref, drive_ref, in_ref, rates_of(j)
        )
        for n, (grow, state) in enumerate(found):
            grow_ref[j, n] = grow
            state_ref[j, n] = state
            send_ref[j, n : n + 1] = grow[subs - 1 :]
            send_ref[j, states + n : states + n + 1] = state[subs - 1 :]
        for copy in ends_copies(send_ref, ends_ref, ends_sems, j, False):
            copy.start()
        return 0

    lax.fori_loop(0, tiles, ends_of, 0)
    arrived(c_src, c_dst, c_sems, c_core, (1, 3))
    relay_inside(2)
    for copy in d_copies:
        copy.start()
    relay_from_end(3)
    spread(coef_ref, first_c, out_ref, steps, states)
    arrived(b_ref, b_dst, b_sems, b_core, (2,))
    row = lax.broadcasted_iota(jnp.int32, (subs, lanes), 0)

    def forward_of(j, _):
        for copy in ends_copies(send_ref, ends_ref, ends_sems, j, False):
            copy.wait()
        enter = chain_enter(ends_ref, j, states, False)
        rates = rates_of(j)
        held = []
        for n in range(states):
            near_grow = jnp.where(row >= 1, pltpu.roll(grow_ref[j, n], 1, 0), 1.0)
            near_state = jnp.where(row >= 1, pltpu.roll(state_ref[j, n], 1, 0), 0.0)
            start = near_state + near_grow * jnp.broadcast_to(enter[n : n + 1, :], (subs, lanes))
            start_ref[j, n] = start
            held.append(start)

        def one(s, held):
            step = step_ref[j, pl.ds(s, subs, stride=steps), :]
            step = step + reset_ref[pl.ds(s, subs, stride=steps), :]
            drive = drive_ref[j, pl.ds(s, subs, stride=steps), :]
            now_all = []
            y = jnp.zeros((subs, lanes), jnp.float32)
            for n in range(states):
                now = jnp.exp2(step * rates[n]) * held[n] + in_ref[s, n] * drive
                y = y + out_ref[s, n] * now
                now_all.append(now)
            y_ref[j, pl.ds(s, subs, stride=steps), :] = y
            return tuple(now_all)

        lax.fori_loop(0, steps, one, tuple(held), unroll=2)
        return 0

    lax.fori_loop(0, tiles, forward_of, 0)

    for k in range(split):
        core_copy(b_dst, b_core, k).wait_recv()
    channel_rows = width // (2 * split)
    second_in = gate_ref[:, :channel_rows].reshape(width, model_width)
    for l in range(split):
        z_block = matmul_nt(normed_ref[l], second_in)
        rows = slice(l * own_rows, (l + 1) * own_rows)
        for j in range(tiles):
            z_ref[j, rows, :] = z_block[:, j * lanes : (j + 1) * lanes]

    def gate(at):
        for j in range(tiles):
            cols = slice(j * lanes, (j + 1) * lanes)
            mixed = mixed_ref[pl.ds(at, 32), cols].astype(jnp.float32)
            y = y_ref[j, pl.ds(at, 32), :] + rows_ref[j, skip_row : skip_row + 1, :] * mixed
            y_ref[j, pl.ds(at, 32), :] = y
            z = z_ref[j, pl.ds(at, 32), :]
            gated_ref[pl.ds(at, 32), cols] = low_bits(y * z * sigmoid_of(z))

    row_loop(row_count, 32, gate)
    out_full = gate_ref[:, channel_rows:].reshape(width, model_width)

    def out_block(l):
        at = pl.multiple_of(l * own_rows, own_rows)
        return matmul(gated_ref[pl.ds(at, own_rows), :], out_full)

    sum_copies = plane_copies(lambda to, k: partial_ref.at[k - 1], arrive_ref, sum_sems, False)
    for k in range(1, split):
        partial_ref[k - 1] = low_bits(out_block(lax.rem(low + k, split)))
        sum_copies[k - 1].start()
    resid = tokens_ref[...].astype(jnp.float32) + out_block(low)
    arrived(c_src, c_dst, c_sems, c_core, (2,))
    for k in range(1, split):
        sum_copies[k - 1].wait()
        resid = resid + arrive_ref[k - 1].astype(jnp.float32)
    resid_ref[...] = resid
    second_ref[low] = low_bits(norm_rows(resid, gains_ref[1:2, :]))
    second_copies = plane_copies(lambda to, k: second_ref.at[low], second_ref, second_sems, True)
    for copy in second_copies:
        copy.start()
    arrived(d_src, d_dst, d_sems, d_core, (1, 3))
    relay_inside(3)
    arrived(d_src, d_dst, d_sems, d_core, (2,))
    for copy in second_copies + route_copies:
        copy.wait()
    for copy in a_copies + b_copies + c_copies + d_copies + relays + core_copies:
        copy.wait_send()
    for dst_of, sems in ((c_dst, c_core), (d_dst, d_core)):
        for k in range(split):
            core_copy(dst_of, sems, k).wait_recv()


def run_mixer(tokens, gains, lengths, a_part, b_part, c_part, g_part, dt_rank, states, tap_count):
    own_rows, model_width = tokens.shape
    row_count = own_rows * split
    steps = row_count // subs
    blocks = 2 * split
    width = blocks * a_part.shape[0]
    tiles = width // lanes
    vmem = pl.BlockSpec(memory_space=pltpu.VMEM)
    anywhere = pl.BlockSpec(memory_space=pl.ANY)
    f32, bf16 = jnp.float32, jnp.bfloat16
    tiled = (tiles, row_count, lanes)
    outs = [
        ((blocks,) + a_part.shape, bf16),
        ((blocks,) + b_part.shape, bf16),
        ((blocks,) + c_part.shape, bf16),
        ((split, own_rows, model_width), bf16),
        ((16, model_width), bf16),
        ((split,) + g_part.shape, bf16),
        ((row_count + 16, width), f32),
        ((row_count, lanes), f32),
        (tiled, f32),
        (tiled, f32),
        (tiled, f32),
        ((row_count, width), bf16),
        ((tiles, states, subs, lanes), f32),
        ((own_rows, model_width), f32),
        ((split, own_rows, model_width), bf16),
        ((tiles, lanes, lanes), f32),
    ]
    spreads = pltpu.VMEM((steps, states, subs, lanes), f32)
    dma = pltpu.SemaphoreType.DMA
    others = split - 1
    return pl.pallas_call(
        functools.partial(mixer_kernel, dt_rank, states, tap_count),
        in_specs=[vmem, vmem, pl.BlockSpec(memory_space=pltpu.SMEM), vmem, vmem, vmem, vmem],
        out_specs=[anywhere if i == 2 else vmem for i in range(len(outs))],
        out_shape=[jax.ShapeDtypeStruct(shape, kind) for shape, kind in outs],
        scratch_shapes=[
            spreads,
            spreads,
            pltpu.VMEM(tiled, f32),
            pltpu.VMEM((row_count, lanes), f32),
            pltpu.VMEM((row_count, width), bf16),
            pltpu.VMEM((others, own_rows, model_width), bf16),
            pltpu.VMEM((others, own_rows, model_width), bf16),
            pltpu.VMEM((row_count, lanes), bf16),
            pltpu.VMEM((others, row_count, lanes), bf16),
            pltpu.VMEM((tiles, 2 * states, lanes), f32),
            pltpu.VMEM((others, tiles, 2 * states, lanes), f32),
            pltpu.VMEM((tiles, states, subs, lanes), f32),
            pltpu.VMEM((tiles, states, subs, lanes), f32),
        ]
        + [dma((2, others))] * 4
        + [dma((2, split))] * 4
        + [dma((2, others))] * 5
        + [dma((split,)), dma, dma((2, others, tiles)), dma],
        compiler_params=pltpu.CompilerParams(
            collective_id=3, has_side_effects=True, vmem_limit_bytes=60 << 20
        ),
        cost_estimate=pl.CostEstimate(flops=1000, bytes_accessed=1000, transcendentals=0),
    )(tokens, gains, lengths, a_part, b_part, c_part, g_part)


def norm_back(values, gain_row, grads):
    scale = lax.rsqrt(jnp.mean(values * values, -1, keepdims=True) + eps_norm)
    unit = values * scale
    inner = grads * gain_row
    return scale * (inner - unit * jnp.mean(inner * unit, -1, keepdims=True)), grads * unit


def route_probs(rows, router, route_lanes, expert_count):
    logits = matmul(rows, router)
    lane = lax.broadcasted_iota(jnp.int32, logits.shape, 1)
    logits = jnp.where(lane < expert_count, logits, -1e30)
    powers = jnp.exp(logits - jnp.max(logits, -1, keepdims=True))
    probs = powers / jnp.sum(powers, -1, keepdims=True)
    chosen = jnp.where(lane.astype(jnp.float32) == route_lanes, 1.0, 0.0)
    return probs, chosen, jnp.sum(probs * chosen, -1, keepdims=True)


class LineScatter:
    def __init__(self, src_of, arrive_ref, sems):
        core, high, low = kernel_place()
        self.src_of, self.arrive, self.high = src_of, arrive_ref, high
        relay = split

        def send(src, to, slot, index):
            return remote(src, arrive_ref.at[slot], sems.at[0, index], sems.at[1, slot], core, to, low)

        def slot_at(to, sender):
            return lax.rem(to - sender + split, split) - 1

        way = 1 - 2 * (high // (split - 1))
        near, mid, far = high + way, high + 2 * way, high + 3 * way
        self.end_sends = [
            send(src_of(far), near, relay, 0),
            send(src_of(mid), mid, slot_at(mid, high), 1),
            send(src_of(near), near, slot_at(near, high), 2),
        ]
        self.empty_slot = slot_at(high, far)
        self.end_slots = [slot_at(high, near), slot_at(high, mid)]
        beside, other = (split - 1) * (high - 1), split - 1 - high
        self.far_end = split - 1 - beside
        self.inner_sends = [
            send(src_of(other), other, slot_at(other, high), 1),
            send(src_of(beside), beside, slot_at(beside, high), 2),
        ]
        self.relay_send = send(arrive_ref.at[relay], self.far_end, slot_at(self.far_end, high), 0)
        self.inner_slots = [0, 1, 2]
        self.relay = relay
        self.sems = sems

    def landed(self, slot):
        core, high, low = kernel_place()
        remote(
            self.arrive.at[slot], self.arrive.at[slot], self.sems.at[0, 0], self.sems.at[1, slot],
            core, high, low,
        ).wait_recv()

    def start(self):
        @pl.when(at_ends())
        def _():
            for copy in self.end_sends:
                copy.start()
            self.arrive[self.empty_slot] = jnp.zeros(self.arrive.shape[1:], self.arrive.dtype)

        @pl.when(jnp.logical_not(at_ends()))
        def _():
            for copy in self.inner_sends:
                copy.start()

    def pass_on(self):
        @pl.when(jnp.logical_not(at_ends()))
        def _():
            self.landed(self.relay)
            own = self.src_of(self.far_end)
            rows = self.arrive.shape[1]

            def add(at):
                here = pl.ds(at, 16)
                total = self.arrive[self.relay, here].astype(jnp.float32)
                total = total + own[here, :].astype(jnp.float32)
                self.arrive[self.relay, here] = low_bits(total)

            row_loop(rows, 16, add)
            self.relay_send.start()

    def finish(self, out_ref):
        @pl.when(at_ends())
        def _():
            for copy in self.end_sends:
                copy.wait_send()
            for slot in self.end_slots:
                self.landed(slot)

        @pl.when(jnp.logical_not(at_ends()))
        def _():
            for copy in self.inner_sends + [self.relay_send]:
                copy.wait_send()
            for slot in self.inner_slots:
                self.landed(slot)

        own = self.src_of(self.high)

        def one(at):
            rows = pl.ds(at, 16)
            total = own[rows, :].astype(jnp.float32)
            for k in range(split - 1):
                total = total + self.arrive[k, rows].astype(jnp.float32)
            out_ref[rows, :] = total

        row_loop(out_ref.shape[0], 16, one)


def half_copy(src, dst, sems, h):
    core, high, low = kernel_place()
    return remote(src, dst, sems.at[0, h], sems.at[1, h], 1 - core, high, low)


def fill_offsets(reset_ref, lengths_ref, row_count):
    _, high, _ = kernel_place()
    first_len = lengths_ref[0, 0]

    def fill(at):
        place = high * row_count + at + lax.broadcasted_iota(jnp.int32, (64, lanes), 0)
        reset_ref[pl.ds(at, 64), :] = jnp.where((place == 0) | (place == first_len), 1e30, 0.0)

    row_loop(row_count, 64, fill)


def turn_kernel(
    dt_rank, states, expert_count,
    second_ref, routed_ref, hidden_ref, last_ref, router_ref, resid_ref, grad_ref, gains_ref, lengths_ref,
    gate_ref, normed_ref, coef_ref, step_ref, z_ref, y_ref, gated_ref, rows_ref,
    mixed_out_ref, d_resid_ref, small_ref, dy_ref, gz_ref, later_ref, mine_ref, early_ref,
    gate_mine_ref,
    grads_ref, half_ref, y_sum_ref, d_sum_ref, dg_sum_ref, gates_ref, scaled_ref, act_ref, pre_ref,
    part_ref, arrive_ref, y_arrive_ref, branch_ref, out_ref, reset_ref, send_ref,
    ends_ref, early_arrive_ref, gate_half_ref, down_ref, mine_early_ref, growth_ref,
    half_sems, sum_sems, y_sems, branch_sems, early_sems, ends_sems, gate_half_sems, last_sems,
    last_core,
):
    core, high, low = kernel_place()
    _, own_rows, model_width = second_ref.shape
    row_count = own_rows * split
    steps = row_count // subs
    tiles = step_ref.shape[0]
    width = tiles * lanes
    hidden = last_ref.shape[0]
    hidden_rows = 2 * expert_count * hidden
    channel_rows = width // (2 * split)
    greeted = greet_all()
    router = router_ref[...]

    for l in range(split):
        rows = slice(l * own_rows, (l + 1) * own_rows)
        route_lanes = routed_ref[l, :, model_width:].astype(jnp.float32)
        _, _, gate = route_probs(second_ref[l], router, route_lanes, expert_count)
        gates_ref[rows, :] = jnp.broadcast_to(gate, (own_rows, lanes))
        scaled_ref[rows, :] = low_bits(gate * routed_ref[l, :, :model_width].astype(jnp.float32))
    y_sum_ref[...] = jnp.zeros_like(y_sum_ref)
    d_sum_ref[...] = jnp.zeros_like(d_sum_ref)
    dg_sum_ref[...] = jnp.zeros_like(dg_sum_ref)
    span = split * hidden

    pl.semaphore_wait(pltpu.get_barrier_semaphore(), greeted)

    def down_at(at):
        return down_ref.at[at]

    down_ref[high] = last_ref[...]
    last_copies = line_copies(last_ref, down_at, last_sems)
    last_relay = line_relay(down_at, last_sems)
    own_copy = core_copy(down_at, last_core, 0)
    for copy in last_copies + [own_copy]:
        copy.start()
    last_copies.append(own_copy)

    @pl.when(at_ends())
    def _():
        last_relay.start()

    def last_arrived(ks):
        for k in ks:
            line_arrived(last_ref, down_at, last_sems, k)
            copy = core_copy(down_at, last_core, k)
            copy.start()
            last_copies.append(copy)

    def blocks_of(e, first):
        up = hidden_ref[first : first + split, 2 * e * hidden : (2 * e + 1) * hidden]
        up = up.reshape(span, model_width)
        if e < expert_count - 1:
            down = hidden_ref[first : first + split, (2 * e + 1) * hidden : (2 * e + 2) * hidden]
        else:
            down = down_ref[first : first + split]
        down = down.reshape(span, model_width)

        def token_block(l, _):
            at = pl.multiple_of(l * own_rows, own_rows)
            rows = pl.ds(at, own_rows)
            pre = matmul_nt(second_ref[l], up)
            picked = routed_ref[l, :, model_width : model_width + 1].astype(jnp.float32) == e
            half = 0.5 + 0.5 * lax.erf(pre * (0.5**0.5))
            bell = jnp.exp(-0.5 * pre * pre) * (1.0 / (2.0 * math.pi) ** 0.5)
            act = low_bits(jnp.where(picked, pre * half, 0.0))
            d_raw = matmul_nt(routed_ref[l, :, :model_width], down)
            weighted = act.astype(jnp.float32) * d_raw
            dg_sum_ref[rows, :] += sum(weighted[:, c : c + lanes] for c in range(0, span, lanes))
            d_pre = jnp.where(picked, gates_ref[rows, :1] * d_raw * (half + pre * bell), 0.0)
            d_pre = low_bits(d_pre)
            y_sum_ref[rows, :] += matmul(act, down)
            d_sum_ref[rows, :] += matmul(d_pre, up)
            act_ref[rows, :] = act
            pre_ref[rows, :] = d_pre
            return 0

        lax.fori_loop(0, split, token_block, 0)
        second = second_ref[...].reshape(row_count, model_width)
        up_grad = low_bits(matmul_tn(pre_ref[...], second))
        down_grad = low_bits(matmul_tn(act_ref[...], scaled_ref[...]))
        for b in range(split):
            piece = slice(b * hidden, (b + 1) * hidden)
            to = 2 * e * hidden
            grads_ref[first + b, to : to + hidden] = up_grad[piece]
            grads_ref[first + b, to + hidden : to + 2 * hidden] = down_grad[piece]

    def part_of(e):
        return pl.ds(2 * e * hidden, 2 * hidden)

    half_copies = {}

    def send_half(e):
        half_copies[e] = [
            half_copy(
                grads_ref.at[split + h, part_of(e)],
                half_ref.at[h, part_of(e)],
                half_sems.at[e],
                h,
            )
            for h in range(split)
        ]
        for copy in half_copies[e]:
            copy.start()

    def add_half(e):
        for copy in half_copies[e]:
            copy.wait()

        target, base = (mine_early_ref, 0) if e == 0 else (mine_ref, 2 * (e - 1) * hidden)

        def one(i, _):
            h, at = i // (2 * hidden // 32), lax.rem(i, 2 * hidden // 32) * 32
            rows = pl.ds(2 * e * hidden + at, 32)
            target[h, pl.ds(base + at, 32)] = low_bits(
                grads_ref[h, rows].astype(jnp.float32) + half_ref[h, rows].astype(jnp.float32)
            )
            return 0

        lax.fori_loop(0, split * (2 * hidden // 32), one, 0)

    early = LineScatter(lambda to: mine_early_ref.at[to], early_arrive_ref, early_sems)
    for e in range(expert_count):
        blocks_of(e, split)
        send_half(e)
        if e == 0:
            last_arrived((1, 3))

            @pl.when(jnp.logical_not(at_ends()))
            def _():
                last_relay.start()

        blocks_of(e, 0)
        if e == 0:
            last_arrived((2,))
            for k in range(split):
                core_copy(down_at, last_core, k).wait_recv()
            add_half(0)
            early.start()
    for copy in last_copies + [last_relay]:
        copy.wait_send()

    sum_copies = plane_copies(lambda to, k: part_ref.at[k - 1], arrive_ref, sum_sems, False)
    y_copies = plane_copies(
        lambda to, k: part_ref.at[k - 1, :, pl.ds(0, model_width)], y_arrive_ref, y_sems, False
    )
    for k in range(1, split):
        to = pl.ds(pl.multiple_of(lax.rem(low + k, split) * own_rows, own_rows), own_rows)
        part_ref[k - 1, :, :model_width] = low_bits(d_sum_ref[to, :])
        part_ref[k - 1, :, model_width:] = low_bits(dg_sum_ref[to, :])
        sum_copies[k - 1].start()

    early.pass_on()
    for e in range(1, expert_count):
        add_half(e)
    own = pl.ds(pl.multiple_of(low * own_rows, own_rows), own_rows)
    d_second, dg_lanes = d_sum_ref[own, :], dg_sum_ref[own, :]
    for k in range(1, split):
        sum_copies[k - 1].wait()
        d_second = d_second + arrive_ref[k - 1, :, :model_width].astype(jnp.float32)
        dg_lanes = dg_lanes + arrive_ref[k - 1, :, model_width:].astype(jnp.float32)
    d_gate = jnp.sum(dg_lanes, -1, keepdims=True)
    second_own = second_ref[low]
    route_lanes = routed_ref[low, :, model_width:].astype(jnp.float32)
    probs, chosen, gate = route_probs(second_own, router, route_lanes, expert_count)
    d_logits = low_bits(probs * (d_gate * (chosen - gate)))
    d_second = d_second + matmul_nt(d_logits, router)
    d_rows, d_gain = norm_back(resid_ref[...], gains_ref[1:2, :], d_second)
    d_resid = grad_ref[...] + d_rows
    d_resid_ref[...] = d_resid
    branch_ref[low] = low_bits(d_resid)
    branch_copies = plane_copies(lambda to, k: branch_ref.at[low], branch_ref, branch_sems, True)
    for copy in branch_copies:
        copy.start()
    for k in range(1, split):
        to = pl.ds(pl.multiple_of(lax.rem(low + k, split) * own_rows, own_rows), own_rows)
        part_ref[k - 1, :, :model_width] = low_bits(y_sum_ref[to, :])
        y_copies[k - 1].start()
    small_ref[...] = jnp.zeros_like(small_ref)
    small_ref[1:2, :] = jnp.sum(d_gain, 0, keepdims=True)
    small_ref[2 : 2 + expert_count, :] = matmul_tn(d_logits, second_own)[:expert_count]

    fill_offsets(reset_ref, lengths_ref, row_count)
    spread(coef_ref, dt_rank + states, out_ref, steps, states)
    out_full = gate_ref[:, channel_rows:].reshape(width, model_width)
    for copy in branch_copies:
        copy.wait()
    for l in range(split):
        d_gated = matmul_nt(branch_ref[l], out_full)
        rows = slice(l * own_rows, (l + 1) * own_rows)
        for j in range(tiles):
            cols = slice(j * lanes, (j + 1) * lanes)
            z = z_ref[j, rows, :]
            sig = sigmoid_of(z)
            d_tile = d_gated[:, cols]
            dy_ref[j, rows, :] = d_tile * (z * sig)
            d_z = d_tile * y_ref[j, rows, :] * (sig * (1.0 + z * (1.0 - sig)))
            gz_ref[rows, cols] = low_bits(d_z)

    def rates_of(j):
        values = -jnp.exp(rows_ref[j, alog_row : alog_row + states, :]) * log2e
        return [jnp.broadcast_to(values[n : n + 1, :], (subs, lanes)) for n in range(states)]

    def ends_of(j, _):
        found = scan_one_way(
            j, None, True, states, steps, step_ref, reset_ref, dy_ref, out_ref, rates_of(j)
        )
        row = lax.broadcasted_iota(jnp.int32, (subs, lanes), 0)
        for n, (grow, state) in enumerate(found):
            send_ref[j, n : n + 1] = grow[:1]
            send_ref[j, states + n : states + n + 1] = state[:1]
            has = row < subs - 1
            growth_ref[j, n] = jnp.where(has, pltpu.roll(grow, subs - 1, 0), 1.0)
            later_ref[j, n] = jnp.where(has, pltpu.roll(state, subs - 1, 0), 0.0)
        for copy in ends_copies(send_ref, ends_ref, ends_sems, j, True):
            copy.start()
        return 0

    lax.fori_loop(0, tiles, ends_of, 0)

    normed = normed_ref[...].reshape(row_count, model_width)
    branch = branch_ref[...].reshape(row_count, model_width)
    for part, (first_op, second_op) in enumerate(((gz_ref, normed), (gated_ref, branch))):
        half_width = width // 2
        for at in (half_width, 0):
            grad = low_bits(matmul_tn(first_op[:, at : at + half_width], second_op))
            for b in range(split):
                piece = grad[b * channel_rows : (b + 1) * channel_rows]
                to = part * channel_rows
                grads_ref[at // channel_rows + b, to : to + channel_rows] = piece
    gate_rows = 2 * channel_rows
    gate_copies = [
        half_copy(
            grads_ref.at[split + h, pl.ds(0, gate_rows)], gate_half_ref.at[h], gate_half_sems, h
        )
        for h in range(split)
    ]
    for copy in gate_copies:
        copy.start()

    def settle(j, _):
        for copy in ends_copies(send_ref, ends_ref, ends_sems, j, True):
            copy.wait()
        enter = chain_enter(ends_ref, j, states, True)
        for n in range(states):
            entered = jnp.broadcast_to(enter[n : n + 1, :], (subs, lanes))
            later_ref[j, n] += growth_ref[j, n] * entered
        return 0

    lax.fori_loop(0, tiles, settle, 0)
    y = y_sum_ref[own, :]
    for k in range(1, split):
        y_copies[k - 1].wait()
        y = y + y_arrive_ref[k - 1].astype(jnp.float32)
    mixed_out_ref[...] = low_bits(resid_ref[...] + gates_ref[own, :1] * y)
    for h in range(split):
        gate_copies[h].wait()

        def add_gate(at, h=h):
            rows = pl.ds(at, 16)
            total = grads_ref[h, rows].astype(jnp.float32) + gate_half_ref[h, rows].astype(jnp.float32)
            gate_mine_ref[h, rows] = low_bits(total)

        row_loop(gate_rows, 16, add_gate)
    early.finish(early_ref)


def run_turn(
    second, routed, hidden_full, last_part, router_lanes, resid, grad_out, gains, lengths, gate_full, normed,
    coef, step, z, y, gated, rows, dt_rank, states, expert_count,
):
    _, own_rows, model_width = second.shape
    row_count = own_rows * split
    steps = row_count // subs
    tiles = step.shape[0]
    width = tiles * lanes
    hidden = last_part.shape[0]
    hidden_rows = 2 * expert_count * hidden
    cut = 2 * hidden
    gate_rows = gate_full.shape[1]
    others = split - 1
    vmem = pl.BlockSpec(memory_space=pltpu.VMEM)
    f32, bf16 = jnp.float32, jnp.bfloat16
    dma = pltpu.SemaphoreType.DMA
    outs = [
        ((own_rows, model_width), bf16),
        ((own_rows, model_width), f32),
        ((8, model_width), f32),
        ((tiles, row_count, lanes), f32),
        ((row_count, width), bf16),
        ((tiles, states, subs, lanes), f32),
        ((split, hidden_rows - cut, model_width), bf16),
        ((cut, model_width), f32),
        ((split, gate_rows, model_width), bf16),
    ]
    span = split * hidden
    return pl.pallas_call(
        functools.partial(turn_kernel, dt_rank, states, expert_count),
        in_specs=[pl.BlockSpec(memory_space=pltpu.SMEM) if i == 8 else vmem for i in range(17)],
        out_specs=[vmem] * len(outs),
        out_shape=[jax.ShapeDtypeStruct(shape, kind) for shape, kind in outs],
        scratch_shapes=[
            pltpu.VMEM((2 * split, hidden_rows, model_width), bf16),
            pltpu.VMEM((split, hidden_rows, model_width), bf16),
            pltpu.VMEM((row_count, model_width), f32),
            pltpu.VMEM((row_count, model_width), f32),
            pltpu.VMEM((row_count, lanes), f32),
            pltpu.VMEM((row_count, lanes), f32),
            pltpu.VMEM((row_count, model_width), bf16),
            pltpu.VMEM((row_count, span), bf16),
            pltpu.VMEM((row_count, span), bf16),
            pltpu.VMEM((others, own_rows, model_width + lanes), bf16),
            pltpu.VMEM((others, own_rows, model_width + lanes), bf16),
            pltpu.VMEM((others, own_rows, model_width), bf16),
            pltpu.VMEM((split, own_rows, model_width), bf16),
            pltpu.VMEM((steps, states, subs, lanes), f32),
            pltpu.VMEM((row_count, lanes), f32),
            pltpu.VMEM((tiles, 2 * states, lanes), f32),
            pltpu.VMEM((others, tiles, 2 * states, lanes), f32),
            pltpu.VMEM((split + 1, cut, model_width), bf16),
            pltpu.VMEM((split, gate_rows, model_width), bf16),
            pltpu.VMEM((2 * split, hidden, model_width), bf16),
            pltpu.VMEM((split, cut, model_width), bf16),
            pltpu.VMEM((tiles, states, subs, lanes), f32),
            dma((expert_count, 2, split)),
            dma((2, others)),
            dma((2, others)),
            dma((2, others)),
            dma((2, split + 1)),
            dma((2, others, tiles)),
            dma((2, split)),
            dma((2, others)),
            dma((2, split)),
        ],
        compiler_params=pltpu.CompilerParams(
            collective_id=4, has_side_effects=True, vmem_limit_bytes=63 << 20
        ),
        cost_estimate=pl.CostEstimate(flops=1000, bytes_accessed=1000, transcendentals=0),
    )(
        second, routed, hidden_full, last_part, router_lanes, resid, grad_out, gains, lengths, gate_full, normed,
        coef, step, z, y, gated, rows,
    )


def back_kernel(
    dt_rank, states, tap_count,
    dy_ref, gz_ref, later_ref, mine_ref, gate_mine_ref, first_ref, gate_ref, normed_ref, input_ref,
    coef_ref, step_ref, start_ref, rows_ref, d_resid_ref, tokens_ref, gains_ref, small_ref,
    lengths_ref,
    grad_tokens_ref, total_ref, late_ref, gate_own_ref, first_own_ref,
    in_ref, out_ref, hist_ref, acc_in_ref, acc_out_ref, mixed_ref, conv_ref, q_ref, r_ref, reset_ref,
    gdt_ref, gin_ref, halo_ref, part_ref, arrive_ref, fold_ref, coef_send_ref,
    coef_arrive_ref, gcoef_ref, misc_ref, select_ref, payload_ref, half_ref, mine_first_ref,
    late_arrive_ref, gate_arrive_ref, first_arrive_ref, core_slots, plane_slots, line_slots,
    late_sems, gate_sems, first_sems, half_sems, halo_sems, coef_sems, sum_sems, core_sems,
    plane_sems, line_sems,
):
    core, high, low = kernel_place()
    _, own_rows, model_width = normed_ref.shape
    row_count = own_rows * split
    steps = row_count // subs
    tiles = step_ref.shape[0]
    width = tiles * lanes
    channel_rows = width // (2 * split)
    edge = input_ref.shape[0] - row_count
    greeted = greet_all()
    first_len = lengths_ref[0, 0]

    def offsets(at, rows):
        place = high * row_count + at + lax.broadcasted_iota(jnp.int32, (rows, lanes), 0)
        return jnp.where(place < first_len, place, place - first_len)

    fill_offsets(reset_ref, lengths_ref, row_count)
    pl.semaphore_wait(pltpu.get_barrier_semaphore(), greeted)
    late = LineScatter(lambda to: mine_ref.at[to], late_arrive_ref, late_sems)
    gate = LineScatter(lambda to: gate_mine_ref.at[to], gate_arrive_ref, gate_sems)
    late.start()

    def convolve(at):
        offset = offsets(at, 32)
        for j in range(tiles):
            span = input_ref[pl.ds(at, 32 + edge), j * lanes : (j + 1) * lanes]
            conv_sum = jnp.zeros((32, lanes), jnp.float32)
            for k in range(tap_count):
                shift = edge - (tap_count - 1) + k
                term = rows_ref[j, k : k + 1, :] * span[shift : shift + 32]
                conv_sum = conv_sum + jnp.where(offset >= tap_count - 1 - k, term, 0.0)
            conv_ref[j, pl.ds(at, 32), :] = conv_sum
            mixed = low_bits(conv_sum * sigmoid_of(conv_sum)).astype(jnp.float32)
            mixed_ref[j, pl.ds(at, 32), :] = mixed

    row_loop(row_count, 32, convolve)
    spread(coef_ref, dt_rank, in_ref, steps, states)
    spread(coef_ref, dt_rank + states, out_ref, steps, states)
    late.pass_on()
    gate.start()
    acc_in_ref[...] = jnp.zeros_like(acc_in_ref)
    acc_out_ref[...] = jnp.zeros_like(acc_out_ref)
    misc_ref[...] = jnp.zeros_like(misc_ref)

    def back_of(j, _):
        values = -jnp.exp(rows_ref[j, alog_row : alog_row + states, :]) * log2e
        rates = [jnp.broadcast_to(values[n : n + 1, :], (subs, lanes)) for n in range(states)]

        def forward(s, held):
            step = step_ref[j, pl.ds(s, subs, stride=steps), :]
            drive = step * mixed_ref[j, pl.ds(s, subs, stride=steps), :]
            step = step + reset_ref[pl.ds(s, subs, stride=steps), :]
            now_all = []
            for n in range(states):
                now = jnp.exp2(step * rates[n]) * held[n] + in_ref[s, n] * drive
                hist_ref[s + 1, n] = now
                now_all.append(now)
            return tuple(now_all)

        held = []
        for n in range(states):
            hist_ref[0, n] = start_ref[j, n]
            held.append(start_ref[j, n])
        lax.fori_loop(0, steps, forward, tuple(held), unroll=2)

        def backward(turn, carry):
            s = steps - 1 - turn
            later, sums = carry
            delta = step_ref[j, pl.ds(s, subs, stride=steps), :]
            drive = delta * mixed_ref[j, pl.ds(s, subs, stride=steps), :]
            step = delta + reset_ref[pl.ds(s, subs, stride=steps), :]
            dy = dy_ref[j, pl.ds(s, subs, stride=steps), :]
            rows = pl.ds(pl.multiple_of(s * subs, subs), subs)
            q = jnp.zeros((subs, lanes), jnp.float32)
            r = jnp.zeros((subs, lanes), jnp.float32)
            later_next, sums_next = [], []
            for n in range(states):
                cols = slice(n * lanes, (n + 1) * lanes)
                d_state = out_ref[s, n] * dy + later[n]
                back = jnp.exp2(step * rates[n]) * d_state
                scaled = back * hist_ref[s, n]
                sums_next.append(sums[n] + scaled * delta)
                q = q + scaled * rates[n]
                r = r + d_state * in_ref[s, n]
                acc_in_ref[rows, cols] += d_state * drive
                acc_out_ref[rows, cols] += hist_ref[s + 1, n] * dy
                later_next.append(back)
            q_ref[j, pl.ds(s, subs, stride=steps), :] = q * (1.0 / log2e)
            r_ref[j, pl.ds(s, subs, stride=steps), :] = r
            return tuple(later_next), tuple(sums_next)

        zero = jnp.zeros((subs, lanes), jnp.float32)
        later = tuple(later_ref[j, n] for n in range(states))
        _, sums = lax.fori_loop(0, steps, backward, (later, (zero,) * states))
        for n in range(states):
            total = jnp.sum(sums[n] * rates[n], 0, keepdims=True) * (1.0 / log2e)
            misc_ref[j, alog_row + n : alog_row + n + 1, :] = total
        return 0

    lax.fori_loop(0, tiles, back_of, 0)

    source = lax.broadcasted_iota(jnp.int32, select_ref.shape, 0) // lanes
    target = lax.broadcasted_iota(jnp.int32, select_ref.shape, 1)

    def fold(acc_ref, first, fresh):
        select_ref[...] = jnp.where(target == first + source, 1.0, 0.0).astype(jnp.bfloat16)

        def one(at):
            values = acc_ref[pl.ds(at, 128), :]
            coarse = low_bits(values)
            fine = low_bits(values - coarse.astype(jnp.float32))
            found = matmul(coarse, select_ref[...]) + matmul(fine, select_ref[...])
            for i in range(128 // subs):
                rows = pl.ds(at // subs + i, subs, stride=steps)
                piece = found[i * subs : (i + 1) * subs]
                fold_ref[rows, :] = piece if fresh else fold_ref[rows, :] + piece

        row_loop(row_count, 128, one)

    fold(acc_in_ref, dt_rank, True)
    fold(acc_out_ref, dt_rank + states, False)
    dt_full = first_ref[:, :, model_width + lanes : model_width + 2 * lanes].reshape(width, lanes)

    def step_grads(at):
        rows = pl.ds(at, 128)
        pre = matmul_nt(low_bits(coef_ref[rows, :]), dt_full)
        for j in range(tiles):
            cols = slice(j * lanes, (j + 1) * lanes)
            mixed = mixed_ref[j, rows, :]
            d_step = q_ref[j, rows, :] + r_ref[j, rows, :] * mixed
            d_dt = d_step * sigmoid_of(pre[:, cols] + rows_ref[j, bias_row : bias_row + 1, :])
            gdt_ref[rows, cols] = low_bits(d_dt)
            misc_ref[j, bias_row : bias_row + 1, :] += jnp.sum(d_dt, 0, keepdims=True)
            misc_ref[j, skip_row : skip_row + 1, :] += jnp.sum(
                dy_ref[j, rows, :] * mixed, 0, keepdims=True
            )
        part = fold_ref[rows, :] + matmul(gdt_ref[rows, :], dt_full)
        fold_ref[rows, :] = part
        coef_send_ref[rows, :] = low_bits(part)

    row_loop(row_count, 128, step_grads)
    gate.pass_on()
    coef_copies = plane_copies(lambda to, k: coef_send_ref, coef_arrive_ref, coef_sems, False)
    for copy in coef_copies:
        copy.start()
    low_coef = low_bits(coef_ref[...])
    for j in range(tiles):
        rows = slice(j * lanes, (j + 1) * lanes)
        payload_ref[rows, model_width + lanes : model_width + 2 * lanes] = low_bits(
            matmul_tn(gdt_ref[:, rows], low_coef)
        )
    for copy in coef_copies:
        copy.wait()
    total = fold_ref[...]
    for k in range(1, split):
        total = total + coef_arrive_ref[k - 1].astype(jnp.float32)
    gcoef_ref[...] = low_bits(total)
    x_full = first_ref[:, :, model_width : model_width + lanes].reshape(width, lanes)

    def conv_grads(at):
        rows = pl.ds(at, 128)
        from_coef = matmul_nt(gcoef_ref[rows, :], x_full)
        for j in range(tiles):
            cols = slice(j * lanes, (j + 1) * lanes)
            d_mixed = rows_ref[j, skip_row : skip_row + 1, :] * dy_ref[j, rows, :]
            d_mixed = d_mixed + r_ref[j, rows, :] * step_ref[j, rows, :] + from_coef[:, cols]
            conv = conv_ref[j, rows, :]
            sig = sigmoid_of(conv)
            q_ref[j, rows, :] = d_mixed * (sig * (1.0 + conv * (1.0 - sig)))

    row_loop(row_count, 128, conv_grads)

    def halo_copy():
        return remote(
            q_ref.at[:, pl.ds(0, subs)], halo_ref, halo_sems.at[0], halo_sems.at[1],
            core, lax.rem(high + split - 1, split), low,
        )

    @pl.when(high > 0)
    def _():
        halo_copy().start()

    def tap_grads(at):
        offset = offsets(at, 32)
        for j in range(tiles):
            cols = slice(j * lanes, (j + 1) * lanes)
            span = input_ref[pl.ds(at, 32 + edge), cols]
            d_conv = q_ref[j, pl.ds(at, 32), :]
            for k in range(tap_count):
                shift = edge - (tap_count - 1) + k
                term = jnp.where(offset >= tap_count - 1 - k, d_conv * span[shift : shift + 32], 0.0)
                misc_ref[j, k : k + 1, :] += jnp.sum(term, 0, keepdims=True)

    row_loop(row_count, 32, tap_grads)

    @pl.when(high < split - 1)
    def _():
        halo_copy().wait_recv()
        q_ref[:, row_count:, :] = halo_ref[...]

    @pl.when(high == split - 1)
    def _():
        q_ref[:, row_count:, :] = jnp.zeros_like(halo_ref)

    def input_grads(at):
        masks = [offsets(at + m, 32) >= m for m in range(tap_count)]
        for j in range(tiles):
            cols = slice(j * lanes, (j + 1) * lanes)
            span = q_ref[j, pl.ds(at, 32 + subs), :]
            d_input = jnp.zeros((32, lanes), jnp.float32)
            for m in range(tap_count):
                k = tap_count - 1 - m
                term = rows_ref[j, k : k + 1, :] * span[m : m + 32]
                d_input = d_input + jnp.where(masks[m], term, 0.0)
            gin_ref[pl.ds(at, 32), cols] = low_bits(d_input)

    row_loop(row_count, 32, input_grads)

    first_in = first_ref[:, :, :model_width].reshape(width, model_width)
    second_in = gate_ref[:, :channel_rows].reshape(width, model_width)

    def normed_block(l):
        rows = pl.ds(pl.multiple_of(l * own_rows, own_rows), own_rows)
        return matmul(gin_ref[rows, :], first_in) + matmul(gz_ref[rows, :], second_in)

    normed = normed_ref[...].reshape(row_count, model_width)
    for j in range(tiles):
        rows = slice(j * lanes, (j + 1) * lanes)
        payload_ref[rows, model_width : model_width + lanes] = low_bits(
            matmul_tn(low_bits(mixed_ref[j]), gcoef_ref[...])
        )
        payload_ref[rows, model_width + 2 * lanes :] = low_bits(misc_ref[j].T)
    half_width = width // 2
    half = remote(
        payload_ref.at[pl.ds(half_width, half_width)], half_ref, half_sems.at[0], half_sems.at[1],
        1 - core, high, low,
    )

    def first_half(at):
        payload_ref[at : at + half_width, :model_width] = low_bits(
            matmul_tn(gin_ref[:, at : at + half_width], normed)
        )

    first_half(half_width)
    half.start()
    sum_copies = plane_copies(lambda to, k: part_ref.at[k - 1], arrive_ref, sum_sems, False)
    for k in range(1, split):
        part_ref[k - 1] = low_bits(normed_block(lax.rem(low + k, split)))
        sum_copies[k - 1].start()
    first_half(0)
    half.wait()

    def add_half(at):
        rows = pl.ds(at, 64)
        both = payload_ref[rows, :].astype(jnp.float32) + half_ref[rows, :].astype(jnp.float32)
        mine_first_ref[rows, :] = low_bits(both)

    row_loop(half_width, 64, add_half)
    first = LineScatter(
        lambda to: mine_first_ref.at[pl.ds(pl.multiple_of(to * channel_rows, 16), channel_rows)],
        first_arrive_ref,
        first_sems,
    )
    first.start()
    grad_tokens_ref[...] = normed_block(low)
    late.finish(late_ref)
    first.pass_on()
    gate.finish(gate_own_ref)
    d_normed = grad_tokens_ref[...]
    for k in range(1, split):
        sum_copies[k - 1].wait()
        d_normed = d_normed + arrive_ref[k - 1].astype(jnp.float32)
    tokens = tokens_ref[...].astype(jnp.float32)
    d_rows, d_gain = norm_back(tokens, gains_ref[0:1, :], d_normed)
    grad_tokens_ref[...] = d_resid_ref[...] + d_rows

    core_slots[core] = small_ref[...]
    core_slots[core, 0:1, :] = jnp.sum(d_gain, 0, keepdims=True)
    hop = remote(
        core_slots.at[core], core_slots.at[core], core_sems.at[0], core_sems.at[1], 1 - core, high, low
    )
    hop.start()
    hop.wait()
    plane_slots[low] = core_slots[0] + core_slots[1]
    plane = plane_copies(lambda to, k: plane_slots.at[low], plane_slots, plane_sems, True)
    for copy in plane:
        copy.start()
    for copy in plane:
        copy.wait()
    line_slots[high] = (plane_slots[0] + plane_slots[1]) + (plane_slots[2] + plane_slots[3])
    line = line_copies(line_slots.at[high], lambda at: line_slots.at[at], line_sems, True)
    for copy in line:
        copy.start()

    for k in range(1, split):
        line_arrived(line_slots.at[high], lambda at: line_slots.at[at], line_sems, k)
    for copy in line:
        copy.wait_send()
    total_ref[...] = (line_slots[0] + line_slots[1]) + (line_slots[2] + line_slots[3])
    first.finish(first_own_ref)

    @pl.when(high > 0)
    def _():
        halo_copy().wait_send()


def run_back(
    dy, gz, later, mine, gate_mine, first_full, gate_full, normed, input_all, coef, step, start, rows,
    d_resid, tokens, gains, small, lengths, dt_rank, states, tap_count,
):
    _, own_rows, model_width = normed.shape
    row_count = own_rows * split
    steps = row_count // subs
    tiles = step.shape[0]
    width = tiles * lanes
    channel_rows = width // (2 * split)
    others = split - 1
    late_rows = mine.shape[1]
    gate_rows = gate_mine.shape[1]
    first_columns = first_full.shape[2]
    vmem = pl.BlockSpec(memory_space=pltpu.VMEM)
    specs = [vmem] * 17
    specs.append(pl.BlockSpec(memory_space=pltpu.SMEM))
    f32, bf16 = jnp.float32, jnp.bfloat16
    dma = pltpu.SemaphoreType.DMA
    outs = [
        (own_rows, model_width),
        (8, model_width),
        (late_rows, model_width),
        (gate_rows, model_width),
        (channel_rows, first_columns),
    ]
    tiled = pltpu.VMEM((tiles, row_count, lanes), f32)
    spreads = pltpu.VMEM((steps, states, subs, lanes), f32)
    summed = pltpu.VMEM((row_count, states * lanes), f32)
    return pl.pallas_call(
        functools.partial(back_kernel, dt_rank, states, tap_count),
        in_specs=specs,
        out_specs=[vmem] * len(outs),
        out_shape=[jax.ShapeDtypeStruct(shape, f32) for shape in outs],
        scratch_shapes=[
            spreads,
            spreads,
            pltpu.VMEM((steps + 1, states, subs, lanes), f32),
            summed,
            summed,
            tiled,
            tiled,
            pltpu.VMEM((tiles, row_count + subs, lanes), f32),
            tiled,
            pltpu.VMEM((row_count, lanes), f32),
            pltpu.VMEM((row_count, width), bf16),
            pltpu.VMEM((row_count, width), bf16),
            pltpu.VMEM((tiles, subs, lanes), f32),
            pltpu.VMEM((others, own_rows, model_width), bf16),
            pltpu.VMEM((others, own_rows, model_width), bf16),
            pltpu.VMEM((row_count, lanes), f32),
            pltpu.VMEM((row_count, lanes), bf16),
            pltpu.VMEM((others, row_count, lanes), bf16),
            pltpu.VMEM((row_count, lanes), bf16),
            pltpu.VMEM((tiles, lanes, lanes), f32),
            pltpu.VMEM((states * lanes, lanes), bf16),
            pltpu.VMEM((width, first_columns), bf16),
            pltpu.VMEM((width // 2, first_columns), bf16),
            pltpu.VMEM((width // 2, first_columns), bf16),
            pltpu.VMEM((split + 1, late_rows, model_width), bf16),
            pltpu.VMEM((split + 1, gate_rows, model_width), bf16),
            pltpu.VMEM((split + 1, channel_rows, first_columns), bf16),
            pltpu.VMEM((2, 8, model_width), f32),
            pltpu.VMEM((split, 8, model_width), f32),
            pltpu.VMEM((split, 8, model_width), f32),
        ]
        + [dma((2, split + 1))] * 3
        + [dma((2,)), dma((2,)), dma((2, others)), dma((2, others)), dma((2,))]
        + [dma((2, others)), dma((2, others))],
        compiler_params=pltpu.CompilerParams(
            collective_id=5, has_side_effects=True, vmem_limit_bytes=63 << 20
        ),
        cost_estimate=pl.CostEstimate(flops=1000, bytes_accessed=1000, transcendentals=0),
    )(
        dy, gz, later, mine, gate_mine, first_full, gate_full, normed, input_all, coef, step, start,
        rows, d_resid, tokens, gains, small, lengths,
    )


def norm_rows(values, gain_row):
    return values * lax.rsqrt(jnp.mean(values * values, -1, keepdims=True) + eps_norm) * gain_row


def matmul(first_op, second_op):
    return jnp.dot(first_op, second_op, preferred_element_type=jnp.float32)


def matmul_nt(first_op, second_op):
    return lax.dot_general(
        first_op, second_op, (((1,), (1,)), ((), ())), preferred_element_type=jnp.float32
    )


def matmul_tn(first_op, second_op):
    return lax.dot_general(
        first_op, second_op, (((0,), (0,)), ((), ())), preferred_element_type=jnp.float32
    )


def low_bits(value):
    return value.astype(jnp.bfloat16)


def swap_low(value, k):
    count = lax.axis_size("seq")
    return lax.ppermute(value, "seq", [(s, s ^ k) for s in range(count)])


def turn_high(value, k):
    count = lax.axis_size("seq")
    return lax.ppermute(value, "seq", [(s, (s + split * k) % count) for s in range(count)])


def from_high(value, k):
    count = lax.axis_size("seq")
    pairs = [(s, s + split * k) for s in range(count) if 0 <= s + split * k < count]
    return lax.ppermute(value, "seq", pairs)


def swap_core(value):
    return lax.ppermute(value, "grp", [(0, 1), (1, 0)])


def high_groups():
    count = lax.axis_size("seq")
    return [[h * split + l for h in range(count // split)] for l in range(split)]


def gather_low(value):
    low = lax.axis_index("seq") % split
    first_bit, second_bit = low % 2 == 1, low // 2 == 1
    own, one, two, three = [value] + [swap_low(value, k) for k in range(1, split)]
    a, b = jnp.where(first_bit, one, own), jnp.where(first_bit, own, one)
    c, d = jnp.where(first_bit, three, two), jnp.where(first_bit, two, three)
    pieces = [
        jnp.where(second_bit, c, a),
        jnp.where(second_bit, d, b),
        jnp.where(second_bit, a, c),
        jnp.where(second_bit, b, d),
    ]
    return jnp.concatenate(pieces, 0)


def scatter_low(partial):
    low = lax.axis_index("seq") % split
    rows = partial.shape[0] // split

    def block(at):
        return lax.dynamic_slice_in_dim(partial, at * rows, rows, 0)

    arrived = [swap_low(low_bits(block(low ^ k)), k) for k in range(1, split)]
    return sum(a.astype(jnp.float32) for a in [block(low)] + arrived)


def sum_low(partial):
    low_partial = low_bits(partial)
    arrived = [swap_low(low_partial, k) for k in range(1, split)]
    return partial + sum(a.astype(jnp.float32) for a in arrived)


def gather_high(value):
    high_count = lax.axis_size("seq") // split
    if high_count > 4:
        return lax.all_gather(value, "seq", axis_index_groups=high_groups())
    high = lax.axis_index("seq") // split
    turned = [turn_high(value, k) for k in range(1, high_count)]
    line = turned[::-1] + [value] + turned[::-1]
    return lax.dynamic_slice_in_dim(jnp.stack(line), high_count - 1 - high, high_count, 0)


def gather_core(own):
    full = jnp.stack([own, swap_core(own)])
    return full.reshape((-1,) + own.shape[1:])


def after(value, *others):
    return lax.optimization_barrier((value,) + others)[0]


def pad_rows(value, rows):
    return jnp.pad(value, ((0, rows - value.shape[0]), (0, 0)))


def fold_core(partial, rows):
    high_count = lax.axis_size("seq") // split
    blocks = partial.reshape(2, high_count, rows, partial.shape[-1])
    arrived = swap_core(low_bits(blocks[1]))
    return low_bits(blocks[0].astype(jnp.float32) + arrived.astype(jnp.float32))


def fold_high(mine):
    high_count = lax.axis_size("seq") // split
    if high_count > 4:
        return lax.psum_scatter(
            mine.astype(jnp.float32), "seq", scatter_dimension=0, axis_index_groups=high_groups()
        )
    high = lax.axis_index("seq") // split

    def block(at):
        return lax.dynamic_index_in_dim(mine, at % high_count, 0, False)

    arrived = [turn_high(block(high + k), k) for k in range(1, high_count)]
    return sum(a.astype(jnp.float32) for a in [block(high)] + arrived)


def sum_all(partial):
    high_count = lax.axis_size("seq") // split
    total = partial + swap_core(partial)
    step = 1
    while step < high_count * split:
        total = total + swap_low(total, step)
        step *= 2
    return total


def entering_state(grow, state, reverse):
    high_count = lax.axis_size("seq") // split
    packed = jnp.concatenate([grow, state], 0)
    states = grow.shape[0]
    if high_count > 4:
        high = lax.axis_index("seq") // split
        every = lax.all_gather(packed, "seq", axis_index_groups=high_groups())

        def one(turn, total):
            source = high_count - 1 - turn if reverse else turn
            piece = lax.dynamic_index_in_dim(every, source, 0, False)
            return piece[states:] + piece[:states] * total

        ahead = high_count - 1 - high if reverse else high
        return lax.fori_loop(0, ahead, one, jnp.zeros_like(state))
    total = jnp.zeros_like(state)
    near = [from_high(packed, -k if reverse else k) for k in range(1, high_count)]
    for piece in near[::-1]:
        total = piece[states:] + piece[:states] * total
    return total


def shards_general(
    tokens,
    routes,
    lengths,
    grad_out,
    norm_gains,
    router,
    in_weight,
    conv_weight,
    x_weight,
    dt_weight,
    dt_bias,
    a_log,
    skip_gain,
    out_weight,
    expert_in,
    expert_out,
):
    channels, tap_count = conv_weight.shape
    dt_rank = dt_weight.shape[1]
    states = a_log.shape[1]
    expert_count, hidden, model_width = expert_in.shape
    own_rows = tokens.shape[0]
    row_count = own_rows * split
    high_count = lax.axis_size("seq") // split
    low = lax.axis_index("seq") % split
    high = lax.axis_index("seq") // split
    coef_count = dt_rank + 2 * states
    channel_rows = -(-channels // 16) * 16
    width = 2 * high_count * channel_rows
    hidden_rows = expert_count * hidden
    small_width = -(-(coef_count + dt_rank + tap_count + 2 + states) // lanes) * lanes

    small = jnp.concatenate(
        [x_weight, dt_weight, conv_weight, dt_bias[:, None], a_log, skip_gain[:, None]], 1
    )
    small = jnp.pad(small, ((0, 0), (0, small_width - small.shape[1])))
    inputs = tokens.astype(jnp.float32)
    edge = 16
    halo = from_high(tokens[own_rows - edge :], 1).astype(jnp.float32)
    normed_own = low_bits(norm_rows(jnp.concatenate([inputs, halo], 0), norm_gains[0]))
    payload = pad_rows(jnp.concatenate([in_weight[0], small], 1), channel_rows)
    first_full = gather_core(gather_high(payload)).reshape(width, -1)
    normed = gather_low(normed_own).reshape(split, own_rows + edge, model_width)
    normed_edge = normed[split - 1, own_rows:]
    normed = normed[:, :own_rows].reshape(row_count, model_width)
    first_in, small_full = first_full[:, :model_width], first_full[:, model_width:]
    x_full = small_full[:, :coef_count]
    at = coef_count
    dt_full = small_full[:, at : at + dt_rank]
    at = at + dt_rank
    conv_taps = small_full[:, at : at + tap_count].astype(jnp.float32)
    at = at + tap_count
    bias_vals = small_full[:, at].astype(jnp.float32)
    at = at + 1
    decay_rate = -jnp.exp(small_full[:, at : at + states].astype(jnp.float32)).T
    at = at + states
    skip_vals = small_full[:, at].astype(jnp.float32)
    rate = decay_rate * log2e

    early_part = jnp.concatenate(
        [
            pad_rows(in_weight[1], channel_rows),
            pad_rows(out_weight, channel_rows),
            expert_in[0],
        ],
        0,
    )
    early_part = gather_high(after(early_part, first_full))
    routed_part = jnp.concatenate(
        [grad_out, routes[:, None].astype(jnp.float32) * jnp.ones((1, lanes), jnp.float32)], 1
    )
    routed_part = gather_low(after(low_bits(routed_part), normed))
    grad_rows = routed_part[:, :model_width]
    routes_all = routed_part[:, model_width : model_width + 1].astype(jnp.int32)
    late_part = jnp.concatenate(
        [expert_in[1:].reshape(-1, model_width), expert_out.reshape(-1, model_width)], 0
    )

    place = high * row_count + jnp.arange(row_count, dtype=jnp.int32)
    first_len = lengths[0, 0]
    offset = jnp.where(place < first_len, place, place - first_len)
    reset = jnp.where(offset[:, None] == 0, 1e30, 0.0) * jnp.ones((1, lanes), jnp.float32)
    valid_rows = [
        (offset >= tap_count - 1 - k).astype(jnp.float32)[:, None] for k in range(tap_count)
    ]

    all_input = low_bits(matmul_nt(jnp.concatenate([normed_edge, normed], 0), first_in))
    conv_input = all_input[edge:]
    window = all_input[edge - (tap_count - 1) :].astype(jnp.float32)
    conv_sum = sum(
        conv_taps[:, k] * window[k : k + row_count] * valid_rows[k] for k in range(tap_count)
    )
    mixed_in = low_bits(jax.nn.silu(conv_sum))
    mixed_val = mixed_in.astype(jnp.float32)
    coef_pad = jnp.pad(x_full, ((0, 0), (0, lanes - coef_count)))
    coef_rows = sum_low(matmul(mixed_in, coef_pad))
    dt_low = low_bits(coef_rows[:, :dt_rank])
    dt_pre = matmul_nt(dt_low, dt_full) + bias_vals
    step_size = jax.nn.softplus(dt_pre)
    drive = step_size * mixed_val
    first_b, first_c = dt_rank, dt_rank + states
    peers = high_count - 1 if high_count <= 4 else 0
    grow, state, enter = scan_ends(
        step_size, reset, drive, coef_rows, rate, first_b, False, peers
    )
    slice_grow = grow[:, subs - 1]
    if not peers:
        enter = entering_state(slice_grow, state[:, subs - 1], False)
    enter, early_part, late_part = lax.optimization_barrier((enter, early_part, late_part))
    early_full = gather_core(early_part)
    late_part = gather_high(late_part)
    y_scan, start, hist = scan_forward(
        step_size, reset, drive, coef_rows, rate, grow, state, enter, first_b, first_c
    )
    y_scan, early_full = lax.optimization_barrier((y_scan, early_full))
    second_in = early_full[:, :channel_rows].reshape(width, model_width)
    out_full = early_full[:, channel_rows : 2 * channel_rows].reshape(width, model_width)
    z_gate = matmul_nt(normed, second_in)
    y_value = y_scan + skip_vals * mixed_val
    gate_z = jax.nn.silu(z_gate)
    gated = low_bits(y_value * gate_z)
    resid = inputs + scatter_low(matmul(gated, out_full))

    resid, late_part = lax.optimization_barrier((resid, late_part))
    late_full = gather_core(late_part)
    second_own = low_bits(norm_rows(resid, norm_gains[1]))
    second = gather_low(second_own)

    def gate_of(rows, row_routes):
        logits = matmul(rows, router)
        chosen = row_routes == jnp.arange(expert_count, dtype=jnp.int32)[None, :]
        chosen = chosen.astype(jnp.float32)
        probs = jax.nn.softmax(logits, -1)
        return logits, chosen, jnp.sum(probs * chosen, -1, keepdims=True)

    gate_rows = gate_of(second, routes_all)[2]
    routed = low_bits(gate_rows * grad_rows.astype(jnp.float32))
    parts = [(early_full[:, 2 * channel_rows :], 0)]
    parts += [(late_full, e * hidden) for e in range(2 * expert_count - 1)]
    step_rows = hidden
    if hidden % 16:
        step_rows = 2 * high_count * hidden // 4
        parts = [
            (w[:, a : a + hidden].reshape(4, step_rows, model_width), 0) for w, a in parts
        ]
    sums, hidden_grads = run_experts(
        second, routed, routed_part[:, model_width:].astype(jnp.float32), parts, step_rows
    )
    if hidden % 16:
        pieces = hidden_grads.reshape(4, 2 * expert_count, -1, hidden, model_width)
        hidden_grads = pieces.swapaxes(1, 2).reshape(-1, 2 * hidden_rows, model_width)
    hidden_mine = fold_core(hidden_grads, 2 * hidden_rows)
    sums = scatter_low(sums)
    expert_y, d_second = sums[:, :model_width], sums[:, model_width:]
    d_second, hidden_mine = lax.optimization_barrier((d_second, hidden_mine))
    cut = hidden_rows * 2 // 3
    hidden_early = fold_high(hidden_mine[:, :cut])
    hidden_mine = hidden_mine[:, cut:]
    logits, chosen, gate_own = gate_of(second_own, routes[:, None])
    mixed_out = low_bits(resid + gate_own * expert_y)
    d_gate = jnp.sum(expert_y * grad_out, -1, keepdims=True)
    _, soft_pull = jax.vjp(lambda v: jax.nn.softmax(v, -1), logits)
    d_logits = low_bits(soft_pull(chosen * d_gate)[0])
    grad_router = matmul_tn(d_logits, second_own)
    d_second = d_second + matmul_nt(d_logits, router)
    _, norm_pull_two = jax.vjp(norm_rows, resid, norm_gains[1])
    d_resid_norm, d_gain_two = norm_pull_two(d_second)
    d_resid = grad_out + d_resid_norm

    g_branch = gather_low(low_bits(d_resid))
    d_gated = matmul_nt(g_branch, out_full)
    d_y = d_gated * gate_z
    _, silu_pull = jax.vjp(jax.nn.silu, z_gate)
    d_z = silu_pull(d_gated * y_value)[0]
    gate_grads = jnp.concatenate(
        [matmul_tn(low_bits(d_z), normed), matmul_tn(gated, g_branch)], 1
    )
    gate_mine = fold_core(gate_grads, channel_rows)
    back_grow, back_state, back_enter = scan_ends(
        step_size, reset, d_y, coef_rows, rate, first_c, True, peers
    )
    if not peers:
        back_enter = entering_state(slice_grow, back_state[:, 0], True)
    back_enter, hidden_mine = lax.optimization_barrier((back_enter, hidden_mine))
    hidden_late = fold_high(hidden_mine)
    scaled_sum, in_sum, rate_sum, d_in_coef, d_out_coef = scan_backward(
        step_size,
        reset,
        drive,
        d_y,
        coef_rows,
        rate,
        start,
        hist,
        back_grow,
        back_state,
        back_enter,
        first_b,
        first_c,
    )
    d_step = scaled_sum + in_sum * mixed_val
    d_mixed = skip_vals * d_y + in_sum * step_size
    grad_skip = jnp.sum(d_y * mixed_val, 0)
    d_dt = d_step * jax.nn.sigmoid(dt_pre)
    grad_bias = jnp.sum(d_dt, 0)
    g_dt = low_bits(d_dt)
    grad_dt = matmul_tn(g_dt, dt_low)
    part_coef = jnp.concatenate([matmul(g_dt, dt_full), d_in_coef, d_out_coef], 1)
    part_coef = jnp.pad(part_coef, ((0, 0), (0, lanes - coef_count)))
    g_coef = low_bits(sum_low(part_coef)[:, :coef_count])
    grad_x = matmul_tn(mixed_in, g_coef)
    d_mixed = d_mixed + matmul_nt(g_coef, x_full)
    _, conv_pull = jax.vjp(jax.nn.silu, conv_sum)
    d_conv = conv_pull(d_mixed)[0]
    grad_conv = jnp.stack(
        [jnp.sum(d_conv * valid_rows[k] * window[k : k + row_count], 0) for k in range(tap_count)],
        1,
    )
    d_window = sum(
        jnp.pad(conv_taps[:, k] * d_conv * valid_rows[k], ((k, tap_count - 1 - k), (0, 0)))
        for k in range(tap_count)
    )
    from_next = from_high(d_window[: tap_count - 1], -1)
    d_input = d_window[tap_count - 1 :] + jnp.pad(
        from_next, ((row_count - (tap_count - 1), 0), (0, 0))
    )
    g_in = low_bits(d_input)
    g_in, hidden_late, gate_mine = lax.optimization_barrier((g_in, hidden_late, gate_mine))
    hidden_own = jnp.concatenate([hidden_early, hidden_late], 0)
    gate_own_grads = fold_high(gate_mine)
    g_z = low_bits(d_z)
    d_normed = scatter_low(matmul(g_in, first_in) + matmul(g_z, second_in))
    _, norm_pull_one = jax.vjp(norm_rows, inputs, norm_gains[0])
    d_inputs, d_gain_one = norm_pull_one(d_normed)
    grad_tokens = d_resid + d_inputs

    rest = jnp.concatenate(
        [grad_x, grad_dt, grad_conv, grad_bias[:, None], rate_sum.T, grad_skip[:, None]], 1
    )
    rest = jnp.pad(rest, ((0, 0), (0, small_width - rest.shape[1])))
    first_own = fold_high(
        fold_core(jnp.concatenate([matmul_tn(g_in, normed), rest], 1), channel_rows)
    )[:channels]
    rest_own = first_own[:, model_width:]
    gate_own_grads = gate_own_grads[:channels]
    sums = sum_all(jnp.concatenate([jnp.stack([d_gain_one, d_gain_two]), grad_router], 0))
    ends = [0]
    for count in (coef_count, dt_rank, tap_count, 1, states, 1):
        ends.append(ends[-1] + count)
    grad_x, grad_dt, grad_conv, grad_bias, grad_alog, grad_skip = (
        rest_own[:, a:b] for a, b in zip(ends[:-1], ends[1:], strict=True)
    )
    return (
        mixed_out,
        grad_tokens,
        sums[:2],
        sums[2:].T,
        jnp.stack([first_own[:, :model_width], gate_own_grads[:, :model_width]]),
        grad_conv,
        grad_x,
        grad_dt,
        grad_bias[:, 0],
        grad_alog,
        grad_skip[:, 0],
        gate_own_grads[:, model_width:],
        hidden_own[:hidden_rows].reshape(expert_count, hidden, model_width),
        hidden_own[hidden_rows:].reshape(expert_count, hidden, model_width),
    )


def shards_plane(
    tokens,
    routes,
    lengths,
    grad_out,
    norm_gains,
    router,
    in_weight,
    conv_weight,
    x_weight,
    dt_weight,
    dt_bias,
    a_log,
    skip_gain,
    out_weight,
    expert_in,
    expert_out,
):
    channels, tap_count = conv_weight.shape
    dt_rank = dt_weight.shape[1]
    states = a_log.shape[1]
    expert_count, hidden, model_width = expert_in.shape
    own_rows = tokens.shape[0]
    row_count = own_rows * split
    high_count = lax.axis_size("seq") // split
    low = lax.axis_index("seq") % split
    high = lax.axis_index("seq") // split
    coef_count = dt_rank + 2 * states
    channel_rows = -(-channels // 16) * 16
    width = 2 * high_count * channel_rows
    hidden_rows = expert_count * hidden
    small_width = -(-(coef_count + dt_rank + tap_count + 2 + states) // lanes) * lanes

    small = jnp.concatenate(
        [x_weight, dt_weight, conv_weight, dt_bias[:, None], a_log, skip_gain[:, None]], 1
    )
    small = jnp.pad(small, ((0, 0), (0, small_width - small.shape[1])))
    inputs = tokens.astype(jnp.float32)
    def wide(parts, columns):
        part = jnp.concatenate(parts, 1)
        return jnp.pad(part, ((0, 0), (0, columns - part.shape[1])))

    gap = jnp.zeros((channels, 2), jnp.bfloat16)
    a_part = pad_rows(
        jnp.concatenate(
            [
                in_weight[0],
                wide([x_weight], lanes),
                wide([dt_weight], lanes),
                wide([conv_weight, dt_bias[:, None], skip_gain[:, None], gap, a_log], lanes),
            ],
            1,
        ),
        channel_rows,
    )
    b_part = jnp.concatenate(
        [pad_rows(in_weight[1], channel_rows), pad_rows(out_weight, channel_rows)], 0
    )
    c_parts = []
    for e in range(expert_count):
        c_parts += [expert_in[e], expert_out[e]]
    c_part, last_part = jnp.concatenate(c_parts[:-1], 0), c_parts[-1]
    g_part = low_bits(
        jnp.concatenate(
            [grad_out, routes[:, None].astype(jnp.float32) * jnp.ones((1, lanes), jnp.float32)], 1
        )
    )
    (
        first_full, gate_full, hidden_full, normed, _, routed, input_all, coef, step, z, y, gated, start,
        resid, second, rows,
    ) = run_mixer(
        tokens, norm_gains, lengths, a_part, b_part, c_part, g_part, dt_rank, states, tap_count
    )
    router_lanes = jnp.pad(router, ((0, 0), (0, lanes - expert_count)))
    mixed_out, d_resid, small_sums, dy, gz, later, mine, early, gate_mine = run_turn(
        second, routed, hidden_full, last_part, router_lanes, resid, grad_out, norm_gains, lengths, gate_full,
        normed, coef, step, z, y, gated, rows, dt_rank, states, expert_count,
    )
    grad_tokens, sums, late, gate_own, first_own = run_back(
        dy, gz, later, mine, gate_mine, first_full, gate_full, normed, input_all, coef, step, start,
        rows, d_resid, tokens, norm_gains, small_sums, lengths, dt_rank, states, tap_count,
    )
    hidden_own = jnp.concatenate([early, late], 0).reshape(expert_count, 2, hidden, model_width)
    first_own, gate_first = first_own[:channels], gate_own[:channels]
    misc = first_own[:, model_width + 2 * lanes :]
    return (
        mixed_out,
        grad_tokens,
        sums[:2],
        sums[2 : 2 + expert_count].T,
        jnp.stack([first_own[:, :model_width], gate_first]),
        misc[:, :tap_count],
        first_own[:, model_width : model_width + coef_count],
        first_own[:, model_width + lanes : model_width + lanes + dt_rank],
        misc[:, bias_row],
        misc[:, alog_row : alog_row + states],
        misc[:, skip_row],
        gate_own[channel_rows : channel_rows + channels],
        hidden_own[:, 0],
        hidden_own[:, 1],
    )


def solution(mesh):
    both = ("grp", "seq")
    in_specs = (
        P(both, None),
        P(both),
        P("grp", None),
        P(both, None),
        P(),
        P(),
        P(None, both, None),
        P(both, None),
        P(both, None),
        P(both, None),
        P(both),
        P(both, None),
        P(both),
        P(both, None),
        P(None, both, None),
        P(None, both, None),
    )
    out_specs = (
        P(both, None),
        P(both, None),
        P(),
        P(),
        P(None, both, None),
        P(both, None),
        P(both, None),
        P(both, None),
        P(both),
        P(both, None),
        P(both),
        P(both, None),
        P(None, both, None),
        P(None, both, None),
    )
    shards = shards_plane if mesh.shape["seq"] == split * split else shards_general
    return jax.shard_map(shards, mesh=mesh, in_specs=in_specs, out_specs=out_specs, check_vma=False)
```

```python
import functools
import math

import jax
import jax.numpy as jnp
from jax import lax
from jax.experimental import pallas as pl
from jax.experimental.pallas import tpu as pltpu
from jax.sharding import PartitionSpec as P

eps_norm = 1e-05
split = 4
lanes = 128
subs = 8
log2e = 1.4426950408889634


def spread(coef_ref, first, spread_ref, steps, states):
    def one(s, _):
        rows = coef_ref[pl.ds(s, subs, stride=steps), :]
        for n in range(states):
            spread_ref[s, n] = jnp.broadcast_to(rows[:, first + n : first + n + 1], (subs, lanes))
        return 0

    lax.fori_loop(0, steps, one, 0, unroll=8)


def chain_rows(grow, state, reverse):
    row = lax.broadcasted_iota(jnp.int32, (subs, lanes), 0)
    shift = 1
    while shift < subs:
        turn = subs - shift if reverse else shift
        has = row < subs - shift if reverse else row >= shift
        near_grow = jnp.where(has, pltpu.roll(grow, turn, 0), 1.0)
        near_state = jnp.where(has, pltpu.roll(state, turn, 0), 0.0)
        state = state + grow * near_state
        grow = grow * near_grow
        shift *= 2
    return grow, state


def ends_kernel(
    first, reverse, states, steps, peers,
    delta_ref, reset_ref, drive_ref, coef_ref, rate_ref,
    grow_ref, state_ref, enter_ref,
    spread_ref, send_ref, arrive_ref, send_sem, arrive_sem,
):
    tile = pl.program_id(0)
    tiles = pl.num_programs(0)
    place = lax.axis_index("seq")
    high, low, core = place // split, place % split, lax.axis_index("grp")

    def other(k):
        return (core, lax.rem(high + (peers + 1 - k if reverse else k), peers + 1) * split + low)

    def copy_to(k, j):
        return pltpu.make_async_remote_copy(
            src_ref=send_ref.at[j],
            dst_ref=arrive_ref.at[k - 1, j],
            send_sem=send_sem.at[k - 1, j],
            recv_sem=arrive_sem.at[k - 1, j],
            device_id=other(k),
            device_id_type=pl.DeviceIdType.MESH,
        )

    @pl.when(tile == 0)
    def _():
        if peers:
            barrier = pltpu.get_barrier_semaphore()
            for k in range(1, peers + 1):
                pl.semaphore_signal(
                    barrier, inc=1, device_id=other(k), device_id_type=pl.DeviceIdType.MESH
                )
        spread(coef_ref, first, spread_ref, steps, states)

    rates = [jnp.broadcast_to(rate_ref[n : n + 1, :], (subs, lanes)) for n in range(states)]

    def one(turn, carry):
        s = steps - 1 - turn if reverse else turn
        total, held = carry
        step = delta_ref[pl.ds(s, subs, stride=steps), :] + reset_ref[pl.ds(s, subs, stride=steps), :]
        drive = drive_ref[pl.ds(s, subs, stride=steps), :]
        after = []
        for n in range(states):
            factor = jnp.exp2(step * rates[n])
            if reverse:
                after.append(factor * (held[n] + spread_ref[s, n] * drive))
            else:
                after.append(factor * held[n] + spread_ref[s, n] * drive)
        return total + step, tuple(after)

    zero = jnp.zeros((subs, lanes), jnp.float32)
    total, held = lax.fori_loop(0, steps, one, (zero, (zero,) * states), unroll=2)
    last = 0 if reverse else subs - 1
    for n in range(states):
        grow, state = chain_rows(jnp.exp2(total * rates[n]), held[n], reverse)
        grow_ref[n] = grow
        state_ref[n] = state
        if peers:
            send_ref[tile, n : n + 1] = grow[last : last + 1]
            send_ref[tile, states + n : states + n + 1] = state[last : last + 1]
    if not peers:
        enter_ref[...] = jnp.zeros_like(enter_ref)
        return

    @pl.when(tile == 0)
    def _():
        pl.semaphore_wait(pltpu.get_barrier_semaphore(), peers)

    for k in range(1, peers + 1):
        copy_to(k, tile).start()

    @pl.when(tile == tiles - 1)
    def _():
        for j in range(enter_ref.shape[1] // lanes):
            total = jnp.zeros((states, lanes), jnp.float32)
            for k in range(peers, 0, -1):
                copy_to(k, j).wait()
                piece = arrive_ref[k - 1, j]
                has = high + k <= peers if reverse else high >= k
                total = jnp.where(has, piece[states:] + piece[:states] * total, 0.0)
            enter_ref[:, j * lanes : (j + 1) * lanes] = total


def scan_ends(delta, reset, drive, coef, rate, first, reverse, peers):
    row_count, width = delta.shape
    states = rate.shape[0]
    steps = row_count // subs
    tiles = width // lanes
    column = pl.BlockSpec((row_count, lanes), lambda j: (0, j))
    whole = pl.BlockSpec((row_count, lanes), lambda j: (0, 0))
    ends = pl.BlockSpec((states, subs, lanes), lambda j: (0, 0, j))
    params = dict(vmem_limit_bytes=48 << 20)
    if peers:
        params.update(collective_id=2 if reverse else 1, has_side_effects=True)
    slots = max(peers, 1)
    return pl.pallas_call(
        functools.partial(ends_kernel, first, reverse, states, steps, peers),
        grid=(tiles,),
        in_specs=[column, whole, column, whole, pl.BlockSpec((states, lanes), lambda j: (0, j))],
        out_specs=[ends, ends, pl.BlockSpec((states, width), lambda j: (0, 0))],
        out_shape=[jax.ShapeDtypeStruct((states, subs, width), jnp.float32)] * 2
        + [jax.ShapeDtypeStruct((states, width), jnp.float32)],
        scratch_shapes=[
            pltpu.VMEM((steps, states, subs, lanes), jnp.float32),
            pltpu.VMEM((tiles, 2 * states, lanes), jnp.float32),
            pltpu.VMEM((slots, tiles, 2 * states, lanes), jnp.float32),
            pltpu.SemaphoreType.DMA((slots, tiles)),
            pltpu.SemaphoreType.DMA((slots, tiles)),
        ],
        compiler_params=pltpu.CompilerParams(**params),
        cost_estimate=pl.CostEstimate(flops=1000, bytes_accessed=1000, transcendentals=0),
    )(delta, reset, drive, coef, rate)


def forward_kernel(first_in, first_out, states, steps, delta_ref, reset_ref, drive_ref, coef_ref, rate_ref, grow_ref, state_ref, enter_ref, y_ref, start_ref, hist_ref, in_ref, out_ref):
    @pl.when(pl.program_id(0) == 0)
    def _():
        spread(coef_ref, first_in, in_ref, steps, states)
        spread(coef_ref, first_out, out_ref, steps, states)

    rates = [jnp.broadcast_to(rate_ref[n : n + 1, :], (subs, lanes)) for n in range(states)]
    row = lax.broadcasted_iota(jnp.int32, (subs, lanes), 0)
    held = []
    for n in range(states):
        near_grow = jnp.where(row >= 1, pltpu.roll(grow_ref[n], 1, 0), 1.0)
        near_state = jnp.where(row >= 1, pltpu.roll(state_ref[n], 1, 0), 0.0)
        start = near_state + near_grow * jnp.broadcast_to(enter_ref[n : n + 1, :], (subs, lanes))
        start_ref[n] = start
        held.append(start)

    def one(s, held):
        step = delta_ref[pl.ds(s, subs, stride=steps), :] + reset_ref[pl.ds(s, subs, stride=steps), :]
        drive = drive_ref[pl.ds(s, subs, stride=steps), :]
        after = []
        y = jnp.zeros((subs, lanes), jnp.float32)
        for n in range(states):
            now = jnp.exp2(step * rates[n]) * held[n] + in_ref[s, n] * drive
            hist_ref[0, s, n] = now
            y = y + out_ref[s, n] * now
            after.append(now)
        y_ref[pl.ds(s, subs, stride=steps), :] = y
        return tuple(after)

    lax.fori_loop(0, steps, one, tuple(held), unroll=2)


def scan_forward(delta, reset, drive, coef, rate, grow, state, enter, first_in, first_out):
    row_count, width = delta.shape
    states = rate.shape[0]
    steps = row_count // subs
    tiles = width // lanes
    column = pl.BlockSpec((row_count, lanes), lambda j: (0, j))
    whole = pl.BlockSpec((row_count, lanes), lambda j: (0, 0))
    ends = pl.BlockSpec((states, subs, lanes), lambda j: (0, 0, j))
    per_state = pl.BlockSpec((states, lanes), lambda j: (0, j))
    return pl.pallas_call(
        functools.partial(forward_kernel, first_in, first_out, states, steps),
        grid=(tiles,),
        in_specs=[column, whole, column, whole, per_state, ends, ends, per_state],
        out_specs=[column, ends, pl.BlockSpec((1, steps, states, subs, lanes), lambda j: (j, 0, 0, 0, 0))],
        out_shape=[
            jax.ShapeDtypeStruct((row_count, width), jnp.float32),
            jax.ShapeDtypeStruct((states, subs, width), jnp.float32),
            jax.ShapeDtypeStruct((tiles, steps, states, subs, lanes), jnp.float32),
        ],
        scratch_shapes=[pltpu.VMEM((steps, states, subs, lanes), jnp.float32)] * 2,
        compiler_params=pltpu.CompilerParams(vmem_limit_bytes=48 << 20),
        cost_estimate=pl.CostEstimate(flops=1000, bytes_accessed=1000, transcendentals=0),
    )(delta, reset, drive, coef, rate, grow, state, enter)


def backward_kernel(first_in, first_out, states, steps, delta_ref, reset_ref, drive_ref, dy_ref, coef_ref, rate_ref, start_ref, hist_ref, grow_ref, state_ref, enter_ref, q_ref, r_ref, rsum_ref, din_ref, dout_ref, in_ref, out_ref, ain_ref, aout_ref):
    tile = pl.program_id(0)

    @pl.when(tile == 0)
    def _():
        spread(coef_ref, first_in, in_ref, steps, states)
        spread(coef_ref, first_out, out_ref, steps, states)
        ain_ref[...] = jnp.zeros_like(ain_ref)
        aout_ref[...] = jnp.zeros_like(aout_ref)

    row = lax.broadcasted_iota(jnp.int32, (subs, lanes), 0)
    rates = [jnp.broadcast_to(rate_ref[n : n + 1, :], (subs, lanes)) for n in range(states)]
    later = []
    for n in range(states):
        near_grow = jnp.where(row < subs - 1, pltpu.roll(grow_ref[n], subs - 1, 0), 1.0)
        near_state = jnp.where(row < subs - 1, pltpu.roll(state_ref[n], subs - 1, 0), 0.0)
        later.append(near_state + near_grow * jnp.broadcast_to(enter_ref[n : n + 1, :], (subs, lanes)))

    def at(s, load_before, carry):
        later, sums = carry
        delta = delta_ref[pl.ds(s, subs, stride=steps), :]
        step = delta + reset_ref[pl.ds(s, subs, stride=steps), :]
        drive = drive_ref[pl.ds(s, subs, stride=steps), :]
        dy = dy_ref[pl.ds(s, subs, stride=steps), :]
        q = jnp.zeros((subs, lanes), jnp.float32)
        r = jnp.zeros((subs, lanes), jnp.float32)
        after, sums_after = [], []
        for n in range(states):
            d_state = out_ref[s, n] * dy + later[n]
            back = jnp.exp2(step * rates[n]) * d_state
            scaled = back * load_before(n)
            sums_after.append(sums[n] + scaled * delta)
            q = q + scaled * rates[n]
            r = r + d_state * in_ref[s, n]
            ain_ref[s, n] += d_state * drive
            aout_ref[s, n] += hist_ref[0, s, n] * dy
            after.append(back)
        q_ref[pl.ds(s, subs, stride=steps), :] = q * (1.0 / log2e)
        r_ref[pl.ds(s, subs, stride=steps), :] = r
        return tuple(after), tuple(sums_after)

    zero = jnp.zeros((subs, lanes), jnp.float32)

    def one(turn, carry):
        s = steps - 1 - turn
        return at(s, lambda n: hist_ref[0, s - 1, n], carry)

    carry = lax.fori_loop(0, steps - 1, one, (tuple(later), (zero,) * states))
    _, sums = at(0, lambda n: start_ref[n], carry)
    for n in range(states):
        rsum_ref[n : n + 1, :] = jnp.sum(sums[n] * rates[n], 0, keepdims=True) * (1.0 / log2e)

    @pl.when(tile == pl.num_programs(0) - 1)
    def _():
        ones = jnp.ones((subs, lanes), jnp.bfloat16)

        def fold(ref, s):
            values = ref[s].reshape(states * subs, lanes)
            high = values.astype(jnp.bfloat16)
            low = (values - high.astype(jnp.float32)).astype(jnp.bfloat16)
            dims = (((1,), (1,)), ((), ()))
            return lax.dot_general(ones, high, dims, preferred_element_type=jnp.float32) + lax.dot_general(ones, low, dims, preferred_element_type=jnp.float32)

        def both(s, _):
            din_ref[pl.ds(s, 1), :] = fold(ain_ref, s)[:1]
            dout_ref[pl.ds(s, 1), :] = fold(aout_ref, s)[:1]
            return 0

        lax.fori_loop(0, steps, both, 0)


def scan_backward(delta, reset, drive, dy, coef, rate, start, hist, grow, state, enter, first_in, first_out):
    row_count, width = delta.shape
    states = rate.shape[0]
    steps = row_count // subs
    tiles = width // lanes
    column = pl.BlockSpec((row_count, lanes), lambda j: (0, j))
    whole = pl.BlockSpec((row_count, lanes), lambda j: (0, 0))
    ends = pl.BlockSpec((states, subs, lanes), lambda j: (0, 0, j))
    per_state = pl.BlockSpec((states, lanes), lambda j: (0, j))
    folded = pl.BlockSpec((steps, states * subs), lambda j: (0, 0))
    q, r, rsum, din, dout = pl.pallas_call(
        functools.partial(backward_kernel, first_in, first_out, states, steps),
        grid=(tiles,),
        in_specs=[column, whole, column, column, whole, per_state, ends, pl.BlockSpec((1, steps, states, subs, lanes), lambda j: (j, 0, 0, 0, 0)), ends, ends, per_state],
        out_specs=[column, column, per_state, folded, folded],
        out_shape=[
            jax.ShapeDtypeStruct((row_count, width), jnp.float32),
            jax.ShapeDtypeStruct((row_count, width), jnp.float32),
            jax.ShapeDtypeStruct((states, width), jnp.float32),
            jax.ShapeDtypeStruct((steps, states * subs), jnp.float32),
            jax.ShapeDtypeStruct((steps, states * subs), jnp.float32),
        ],
        scratch_shapes=[pltpu.VMEM((steps, states, subs, lanes), jnp.float32)] * 4,
        compiler_params=pltpu.CompilerParams(vmem_limit_bytes=56 << 20),
        cost_estimate=pl.CostEstimate(flops=1000, bytes_accessed=1000, transcendentals=0),
    )(delta, reset, drive, dy, coef, rate, start, hist, grow, state, enter)

    def unfold(folded_rows):
        return folded_rows.reshape(steps, states, subs).transpose(2, 0, 1).reshape(row_count, states)

    return q, r, rsum, unfold(din), unfold(dout)


def experts_kernel(
    expert_count, second_ref, routed_ref, route_ref, *refs
):
    weights_in, weights_out = refs[:expert_count], refs[expert_count : 2 * expert_count]
    sums_ref, grads_ref, y_ref, d_ref = refs[2 * expert_count :]
    step = pl.program_id(0)
    blocks, hidden, model_width = weights_in[0].shape
    rows = blocks * hidden

    @pl.when(step == 0)
    def _():
        y_ref[...] = jnp.zeros_like(y_ref)
        d_ref[...] = jnp.zeros_like(d_ref)

    up = jnp.concatenate([w[...].reshape(rows, model_width) for w in weights_in], 0)
    down = jnp.concatenate([w[...].reshape(rows, model_width) for w in weights_out], 0)
    second, routed = second_ref[...], routed_ref[...]
    pre = matmul_nt(second, up)
    column = lax.broadcasted_iota(jnp.int32, (1, expert_count * rows), 1)
    owner = jnp.zeros_like(column)
    for e in range(1, expert_count):
        owner = owner + (column >= e * rows).astype(jnp.int32)
    picked = route_ref[:, :1] == owner.astype(jnp.float32)
    half = 0.5 + 0.5 * lax.erf(pre * (0.5**0.5))
    bell = jnp.exp(-0.5 * pre * pre) * (1.0 / (2.0 * math.pi) ** 0.5)
    act = low_bits(jnp.where(picked, pre * half, 0.0))
    d_pre = low_bits(jnp.where(picked, matmul_nt(routed, down) * (half + pre * bell), 0.0))
    y_ref[...] += matmul(act, down)
    d_ref[...] += matmul(d_pre, up)
    grad_up = low_bits(matmul_tn(d_pre, second))
    grad_down = low_bits(matmul_tn(act, routed))
    for e in range(expert_count):
        for b in range(blocks):
            at = e * rows + b * hidden
            grads_ref[b, e * hidden : (e + 1) * hidden] = grad_up[at : at + hidden]
            to = (expert_count + e) * hidden
            grads_ref[b, to : to + hidden] = grad_down[at : at + hidden]

    @pl.when(step == pl.num_programs(0) - 1)
    def _():
        sums_ref[:, :model_width] = low_bits(y_ref[...])
        sums_ref[:, model_width:] = low_bits(d_ref[...])


def run_experts(second, routed, route_lanes, parts, hidden):
    row_count, model_width = second.shape
    expert_count = len(parts) // 2
    block_count = parts[0][0].shape[0]
    blocks = 2
    fixed = pl.BlockSpec((row_count, model_width), lambda i: (0, 0))

    def spec(first):
        return pl.BlockSpec((blocks, hidden, model_width), lambda i: (i, first // hidden, 0))

    return pl.pallas_call(
        functools.partial(experts_kernel, expert_count),
        grid=(block_count // blocks,),
        in_specs=[fixed, fixed, pl.BlockSpec((row_count, lanes), lambda i: (0, 0))]
        + [spec(first) for _, first in parts],
        out_specs=[
            pl.BlockSpec((row_count, 2 * model_width), lambda i: (0, 0)),
            pl.BlockSpec((blocks, 2 * expert_count * hidden, model_width), lambda i: (i, 0, 0)),
        ],
        out_shape=[
            jax.ShapeDtypeStruct((row_count, 2 * model_width), jnp.bfloat16),
            jax.ShapeDtypeStruct(
                (block_count, 2 * expert_count * hidden, model_width), jnp.bfloat16
            ),
        ],
        scratch_shapes=[pltpu.VMEM((row_count, model_width), jnp.float32)] * 2,
        compiler_params=pltpu.CompilerParams(vmem_limit_bytes=56 << 20),
        cost_estimate=pl.CostEstimate(flops=1000, bytes_accessed=1000, transcendentals=0),
    )(second, routed, route_lanes, *[w for w, _ in parts])


def kernel_place():
    place = lax.axis_index("seq")
    return lax.axis_index("grp"), place // split, place % split


def remote(src, dst, send_sem, arrive_sem, core, high, low):
    return pltpu.make_async_remote_copy(
        src_ref=src,
        dst_ref=dst,
        send_sem=send_sem,
        recv_sem=arrive_sem,
        device_id=(core, high * split + low),
        device_id_type=pl.DeviceIdType.MESH,
    )


def greet_all():
    core, high, low = kernel_place()
    barrier = pltpu.get_barrier_semaphore()
    others = [(core, lax.rem(high + k, split), low) for k in range(1, split)]
    others += [(core, high, lax.rem(low + k, split)) for k in range(1, split)]
    others += [(1 - core, high, low)]
    for c, h, l in others:
        pl.semaphore_signal(
            barrier, inc=1, device_id=(c, h * split + l), device_id_type=pl.DeviceIdType.MESH
        )
    return len(others)


def plane_copies(src_of, dst, sems, slot_by_sender):
    core, high, low = kernel_place()
    copies = []
    for k in range(1, split):
        to = lax.rem(low + k, split)
        slot = low if slot_by_sender else k - 1
        copies.append(
            remote(src_of(to, k), dst.at[slot], sems.at[0, k - 1], sems.at[1, k - 1], core, high, to)
        )
    return copies


def at_ends():
    _, high, _ = kernel_place()
    return (high == 0) | (high == split - 1)


def line_copies(src, dst_of, sems, both=False):
    core, high, low = kernel_place()
    return [
        remote(
            src, dst_of(high), sems.at[0, k - 1], sems.at[1, k - 1], core, lax.rem(high + k, split), low
        )
        for k in ((1, 2, 3) if both else (1, 3))
    ]


def line_relay(dst_of, sems):
    core, high, low = kernel_place()
    block = lax.rem(high * 2, 3) + 3 * (high // 3)
    to = lax.rem(block + 2, split)
    return remote(dst_of(block), dst_of(block), sems.at[0, 1], sems.at[1, 1], core, to, low)


def line_arrived(src, dst_of, sems, k):
    core, high, low = kernel_place()
    at = lax.rem(high + split - k, split)
    remote(src, dst_of(at), sems.at[0, k - 1], sems.at[1, k - 1], core, high, low).wait_recv()


def core_copy(dst_of, sems, k):
    core, high, low = kernel_place()
    at = lax.rem(high + split - k, split)
    return remote(dst_of(at), dst_of(split + at), sems.at[0, k], sems.at[1, k], 1 - core, high, low)


def softplus_of(value):
    return jnp.maximum(value, 0.0) + jnp.log1p(jnp.exp(-jnp.abs(value)))


def sigmoid_of(value):
    return 1.0 / (1.0 + jnp.exp(-value))


def row_loop(count, size, body):
    def one(i, _):
        body(pl.multiple_of(i * size, size))
        return 0

    lax.fori_loop(0, count // size, one, 0)


def scan_one_way(j, first_sub, reverse, states, steps, step_ref, reset_ref, drive_ref, spread_ref, rates):
    def one(turn, carry):
        s = steps - 1 - turn if reverse else turn
        total, held = carry
        step = step_ref[j, pl.ds(s, subs, stride=steps), :] + reset_ref[pl.ds(s, subs, stride=steps), :]
        drive = drive_ref[j, pl.ds(s, subs, stride=steps), :]
        after_step = []
        for n in range(states):
            factor = jnp.exp2(step * rates[n])
            if reverse:
                after_step.append(factor * (held[n] + spread_ref[s, n] * drive))
            else:
                after_step.append(factor * held[n] + spread_ref[s, n] * drive)
        return total + step, tuple(after_step)

    zero = jnp.zeros((subs, lanes), jnp.float32)
    total, held = lax.fori_loop(0, steps, one, (zero, (zero,) * states), unroll=2)
    return [chain_rows(jnp.exp2(total * rates[n]), held[n], reverse) for n in range(states)]


def chain_enter(arrive_ref, j, states, reverse):
    _, high, _ = kernel_place()
    total = jnp.zeros((states, lanes), jnp.float32)
    for k in range(split - 1, 0, -1):
        piece = arrive_ref[k - 1, j]
        has = high + k < split if reverse else high >= k
        total = jnp.where(has, piece[states:] + piece[:states] * total, 0.0)
    return total


def tile_rates(rows_ref, j, states):
    decay = -jnp.exp(rows_ref[j, alog_row : alog_row + states, :])
    return decay


def ends_copies(send_ref, arrive_ref, sems, j, reverse):
    core, high, low = kernel_place()
    copies = []
    for k in range(1, split):
        to = lax.rem(high + split - k, split) if reverse else lax.rem(high + k, split)
        copies.append(
            remote(
                send_ref.at[j],
                arrive_ref.at[k - 1, j],
                sems.at[0, k - 1, j],
                sems.at[1, k - 1, j],
                core,
                to,
                low,
            )
        )
    return copies


alog_row = 8
bias_row = 4
skip_row = 5
early_hidden = 96


def mixer_kernel(
    dt_rank, states, tap_count,
    tokens_ref, gains_ref, lengths_ref, in_weight_ref, conv_weight_ref, x_weight_ref, dt_weight_ref,
    dt_bias_ref, a_log_ref, skip_ref, out_weight_ref, expert_in_ref, expert_out_ref, grad_ref,
    routes_ref,
    first_out, gate_out, hidden_ref, normed_out, routed_out, input_out, coef_out, step_out, z_out,
    y_out, gated_out, start_out, resid_ref, second_out, rows_out, in_out, out_out,
    first_ref, gate_ref, normed_ref, edge_ref, routed_ref, input_ref, coef_ref, step_ref, z_ref,
    y_ref, gated_ref, start_ref, second_ref, rows_ref, c_ref, out_sems,
    in_ref, out_ref, drive_ref, reset_ref, mixed_ref, partial_ref, arrive_ref, coef_send_ref,
    coef_arrive_ref, send_ref, ends_ref, grow_ref, state_ref,
    a_sems, b_sems, c_sems, d_sems, a_core, b_core, c_core, d_core, token_sems, route_sems,
    second_sems, coef_sems, sum_sems, edge_send, edge_arrive, ends_sems, local_sem,
):
    core, high, low = kernel_place()
    own_rows, model_width = tokens_ref.shape
    row_count = own_rows * split
    steps = row_count // subs
    tiles = step_ref.shape[0]
    width = tiles * lanes
    edge = edge_ref.shape[0]
    first_b, first_c = dt_rank, dt_rank + states
    channels = in_weight_ref.shape[1]
    channel_rows = width // (2 * split)
    greeted = greet_all()
    stores = []

    def store(ref, out):
        copy = pltpu.make_async_copy(ref, out, out_sems.at[len(stores)])
        copy.start()
        stores.append(copy)

    def edge_copy(l):
        return remote(
            normed_ref.at[low, pl.ds(own_rows - edge, edge)],
            edge_ref,
            edge_send.at[l],
            edge_arrive,
            core,
            lax.rem(high + 1, split),
            l,
        )

    barrier = pltpu.get_barrier_semaphore()
    for k in range(1, split):
        pl.semaphore_signal(
            barrier,
            inc=1,
            device_id=(core, lax.rem(high + split - 1, split) * split + lax.rem(low + k, split)),
            device_id_type=pl.DeviceIdType.MESH,
        )
    greeted += split - 1
    tokens = tokens_ref[...].astype(jnp.float32)
    normed_ref[low] = low_bits(norm_rows(tokens, gains_ref[0:1, :]))
    gap = channel_rows - channels

    def filled(value):
        value = value.astype(jnp.float32)
        if gap:
            value = jnp.concatenate([value, jnp.zeros((gap, value.shape[1]), jnp.float32)], 0)
        return low_bits(value)

    def widened(value, first):
        at = lax.broadcasted_iota(jnp.int32, (value.shape[1], lanes), 0) + first
        to = lax.broadcasted_iota(jnp.int32, (value.shape[1], lanes), 1)
        return matmul(value, jnp.where(at == to, 1.0, 0.0).astype(jnp.bfloat16))

    first_ref[high, :, :model_width] = filled(in_weight_ref[0])
    first_ref[high, :, model_width : model_width + lanes] = filled(widened(x_weight_ref[...], 0))
    first_ref[high, :, model_width + lanes : model_width + 2 * lanes] = filled(
        widened(dt_weight_ref[...], 0)
    )
    rows_ref[0] = jnp.zeros((lanes, lanes), jnp.float32)
    for row, ref in (
        (0, conv_weight_ref), (bias_row, dt_bias_ref), (skip_row, skip_ref), (alog_row, a_log_ref)
    ):
        rows_ref[0, row : row + ref.shape[0], :channels] = ref[...].astype(jnp.float32)
    first_ref[high, :, model_width + 2 * lanes :] = filled(rows_ref[0].T[:channels])
    pl.semaphore_wait(barrier, greeted)

    @pl.when((low == split - 1) & (high < split - 1))
    def _():
        for l in range(split):
            edge_copy(l).start()

    hidden_count = c_ref.shape[0]
    c_src = c_ref.at[pl.ds(0, early_hidden)]
    d_src = c_ref.at[pl.ds(early_hidden, hidden_count - early_hidden)]
    a_ref, b_ref, g_ref = first_ref.at[high], gate_ref.at[high], routed_ref.at[low]

    def a_dst(at):
        return first_ref.at[at]

    def b_dst(at):
        return gate_ref.at[at]

    def c_dst(at):
        return hidden_ref.at[at, pl.ds(0, early_hidden)]

    def d_dst(at):
        return hidden_ref.at[at, pl.ds(early_hidden, hidden_count - early_hidden)]

    token_copies = plane_copies(lambda to, k: normed_ref.at[low], normed_ref, token_sems, True)
    a_copies = line_copies(a_ref, a_dst, a_sems)
    b_copies = line_copies(b_ref, b_dst, b_sems)
    c_copies = line_copies(c_src, c_dst, c_sems)
    d_copies = line_copies(d_src, d_dst, d_sems)
    route_copies = plane_copies(lambda to, k: g_ref, routed_ref, route_sems, True)
    relays = [line_relay(a_dst, a_sems), line_relay(b_dst, b_sems)]
    relays += [line_relay(c_dst, c_sems), line_relay(d_dst, d_sems)]
    for copy in token_copies + a_copies:
        copy.start()

    def relay_from_end(i):
        @pl.when(at_ends())
        def _():
            relays[i].start()

    def relay_inside(i):
        @pl.when(jnp.logical_not(at_ends()))
        def _():
            relays[i].start()

    def arrived(src, dst_of, sems, core_sems, ks):
        for k in ks:
            line_arrived(src, dst_of, sems, k)
            copy = core_copy(dst_of, core_sems, k)
            copy.start()
            core_copies.append(copy)

    relay_from_end(0)
    core_copies = [core_copy(a_dst, a_core, 0)]
    core_copies[0].start()
    routed_ref[low, :, :model_width] = low_bits(grad_ref[...])
    routes = jnp.broadcast_to(routes_ref[...].astype(jnp.float32), (own_rows, own_rows)).T
    routed_ref[low, :, model_width:] = low_bits(routes)
    gate_ref[high, :channel_rows] = filled(in_weight_ref[1])
    gate_ref[high, channel_rows:] = filled(out_weight_ref[...])
    hidden = expert_in_ref.shape[1]
    for part in range(hidden_count // hidden):
        source = expert_out_ref if part % 2 else expert_in_ref
        c_ref[part * hidden : (part + 1) * hidden] = source[part // 2]
    local = pltpu.make_async_copy(c_ref, hidden_ref.at[high], local_sem)
    local.start()
    core_copies.append(core_copy(b_dst, b_core, 0))
    for copy in core_copies[1:] + route_copies:
        copy.start()

    first_len = lengths_ref[0, 0]

    def offsets(at, rows):
        place = high * row_count + at + lax.broadcasted_iota(jnp.int32, (rows, lanes), 0)
        return jnp.where(place < first_len, place, place - first_len)

    def fill_reset(at):
        reset_ref[pl.ds(at, 64), :] = jnp.where(offsets(at, 64) == 0, 1e30, 0.0)

    row_loop(row_count, 64, fill_reset)

    @pl.when(high == 0)
    def _():
        edge_ref[...] = jnp.zeros_like(edge_ref)

    arrived(a_ref, a_dst, a_sems, a_core, (1, 3))
    relay_inside(0)
    for copy in b_copies:
        copy.start()
    relay_from_end(1)
    for copy in token_copies:
        copy.wait()
    arrived(a_ref, a_dst, a_sems, a_core, (2,))

    @pl.when(high > 0)
    def _():
        edge_copy(0).wait_recv()

    @pl.when((low == split - 1) & (high < split - 1))
    def _():
        for l in range(split):
            edge_copy(l).wait_send()

    for k in range(split):
        core_copy(a_dst, a_core, k).wait_recv()

    weights = first_ref[:, :, :model_width].reshape(width, model_width)
    input_ref[:edge, :] = low_bits(matmul_nt(edge_ref[...], weights)).astype(jnp.float32)
    for l in range(split):
        block = low_bits(matmul_nt(normed_ref[l], weights)).astype(jnp.float32)
        input_ref[edge + l * own_rows : edge + (l + 1) * own_rows, :] = block
    store(first_ref, first_out)
    store(normed_ref, normed_out)
    store(input_ref, input_out)
    small = first_ref[:, :, model_width + 2 * lanes :].reshape(width, lanes).astype(jnp.float32)
    for j in range(tiles):
        rows_ref[j] = small[j * lanes : (j + 1) * lanes].T

    store(rows_ref, rows_out)

    def convolve(at):
        offset = offsets(at, 32)
        for j in range(tiles):
            span = input_ref[pl.ds(at, 32 + edge), j * lanes : (j + 1) * lanes]
            conv_sum = jnp.zeros((32, lanes), jnp.float32)
            for k in range(tap_count):
                shift = edge - (tap_count - 1) + k
                term = rows_ref[j, k : k + 1, :] * span[shift : shift + 32]
                conv_sum = conv_sum + jnp.where(offset >= tap_count - 1 - k, term, 0.0)
            mixed_ref[pl.ds(at, 32), j * lanes : (j + 1) * lanes] = low_bits(
                conv_sum * sigmoid_of(conv_sum)
            )

    row_loop(row_count, 32, convolve)
    arrived(b_ref, b_dst, b_sems, b_core, (1, 3))
    relay_inside(1)
    local.wait()
    for copy in (core_copy(c_dst, c_core, 0), core_copy(d_dst, d_core, 0)):
        copy.start()
        core_copies.append(copy)
    for copy in c_copies:
        copy.start()
    relay_from_end(2)

    x_full = first_ref[:, :, model_width : model_width + lanes].reshape(width, lanes)
    part = matmul(mixed_ref[...], x_full)
    coef_ref[...] = part
    coef_send_ref[...] = low_bits(part)
    coef_copies = plane_copies(lambda to, k: coef_send_ref, coef_arrive_ref, coef_sems, False)
    for copy in coef_copies:
        copy.start()
    for copy in coef_copies:
        copy.wait()
    total = coef_ref[...]
    for k in range(1, split):
        total = total + coef_arrive_ref[k - 1].astype(jnp.float32)
    coef_ref[...] = total
    dt_full = first_ref[:, :, model_width + lanes : model_width + 2 * lanes].reshape(width, lanes)

    def step_sizes(at):
        pre = matmul_nt(low_bits(coef_ref[pl.ds(at, 128), :]), dt_full)
        for j in range(tiles):
            cols = slice(j * lanes, (j + 1) * lanes)
            step = softplus_of(pre[:, cols] + rows_ref[j, bias_row : bias_row + 1, :])
            step_ref[j, pl.ds(at, 128), :] = step
            drive_ref[j, pl.ds(at, 128), :] = step * mixed_ref[pl.ds(at, 128), cols].astype(
                jnp.float32
            )

    row_loop(row_count, 128, step_sizes)
    store(coef_ref, coef_out)
    store(step_ref, step_out)
    spread(coef_ref, first_b, in_ref, steps, states)
    store(in_ref, in_out)

    def rates_of(j):
        values = -jnp.exp(rows_ref[j, alog_row : alog_row + states, :]) * log2e
        return [jnp.broadcast_to(values[n : n + 1, :], (subs, lanes)) for n in range(states)]

    def ends_of(j, _):
        found = scan_one_way(
            j, None, False, states, steps, step_ref, reset_ref, drive_ref, in_ref, rates_of(j)
        )
        for n, (grow, state) in enumerate(found):
            grow_ref[j, n] = grow
            state_ref[j, n] = state
            send_ref[j, n : n + 1] = grow[subs - 1 :]
            send_ref[j, states + n : states + n + 1] = state[subs - 1 :]
        for copy in ends_copies(send_ref, ends_ref, ends_sems, j, False):
            copy.start()
        return 0

    lax.fori_loop(0, tiles, ends_of, 0)
    arrived(c_src, c_dst, c_sems, c_core, (1, 3))
    relay_inside(2)
    for copy in d_copies:
        copy.start()
    relay_from_end(3)
    spread(coef_ref, first_c, out_ref, steps, states)
    store(out_ref, out_out)
    arrived(b_ref, b_dst, b_sems, b_core, (2,))
    row = lax.broadcasted_iota(jnp.int32, (subs, lanes), 0)

    def forward_of(j, _):
        for copy in ends_copies(send_ref, ends_ref, ends_sems, j, False):
            copy.wait()
        enter = chain_enter(ends_ref, j, states, False)
        rates = rates_of(j)
        held = []
        for n in range(states):
            near_grow = jnp.where(row >= 1, pltpu.roll(grow_ref[j, n], 1, 0), 1.0)
            near_state = jnp.where(row >= 1, pltpu.roll(state_ref[j, n], 1, 0), 0.0)
            start = near_state + near_grow * jnp.broadcast_to(enter[n : n + 1, :], (subs, lanes))
            start_ref[j, n] = start
            held.append(start)

        def one(s, held):
            step = step_ref[j, pl.ds(s, subs, stride=steps), :]
            step = step + reset_ref[pl.ds(s, subs, stride=steps), :]
            drive = drive_ref[j, pl.ds(s, subs, stride=steps), :]
            now_all = []
            y = jnp.zeros((subs, lanes), jnp.float32)
            for n in range(states):
                now = jnp.exp2(step * rates[n]) * held[n] + in_ref[s, n] * drive
                y = y + out_ref[s, n] * now
                now_all.append(now)
            y_ref[j, pl.ds(s, subs, stride=steps), :] = y
            return tuple(now_all)

        lax.fori_loop(0, steps, one, tuple(held), unroll=2)
        return 0

    lax.fori_loop(0, tiles, forward_of, 0)

    for k in range(split):
        core_copy(b_dst, b_core, k).wait_recv()
    store(gate_ref, gate_out)
    store(start_ref, start_out)
    second_in = gate_ref[:, :channel_rows].reshape(width, model_width)
    for l in range(split):
        z_block = matmul_nt(normed_ref[l], second_in)
        rows = slice(l * own_rows, (l + 1) * own_rows)
        for j in range(tiles):
            z_ref[j, rows, :] = z_block[:, j * lanes : (j + 1) * lanes]

    def gate(at):
        for j in range(tiles):
            cols = slice(j * lanes, (j + 1) * lanes)
            mixed = mixed_ref[pl.ds(at, 32), cols].astype(jnp.float32)
            y = y_ref[j, pl.ds(at, 32), :] + rows_ref[j, skip_row : skip_row + 1, :] * mixed
            y_ref[j, pl.ds(at, 32), :] = y
            z = z_ref[j, pl.ds(at, 32), :]
            gated_ref[pl.ds(at, 32), cols] = low_bits(y * z * sigmoid_of(z))

    row_loop(row_count, 32, gate)
    store(z_ref, z_out)
    store(y_ref, y_out)
    store(gated_ref, gated_out)
    out_full = gate_ref[:, channel_rows:].reshape(width, model_width)

    def out_block(l):
        at = pl.multiple_of(l * own_rows, own_rows)
        return matmul(gated_ref[pl.ds(at, own_rows), :], out_full)

    sum_copies = plane_copies(lambda to, k: partial_ref.at[k - 1], arrive_ref, sum_sems, False)
    for k in range(1, split):
        partial_ref[k - 1] = low_bits(out_block(lax.rem(low + k, split)))
        sum_copies[k - 1].start()
    resid = tokens_ref[...].astype(jnp.float32) + out_block(low)
    arrived(c_src, c_dst, c_sems, c_core, (2,))
    for k in range(1, split):
        sum_copies[k - 1].wait()
        resid = resid + arrive_ref[k - 1].astype(jnp.float32)
    resid_ref[...] = resid
    second_ref[low] = low_bits(norm_rows(resid, gains_ref[1:2, :]))
    second_copies = plane_copies(lambda to, k: second_ref.at[low], second_ref, second_sems, True)
    for copy in second_copies:
        copy.start()
    arrived(d_src, d_dst, d_sems, d_core, (1, 3))
    relay_inside(3)
    arrived(d_src, d_dst, d_sems, d_core, (2,))
    for copy in second_copies + route_copies:
        copy.wait()
    store(second_ref, second_out)
    store(routed_ref, routed_out)
    for copy in a_copies + b_copies + c_copies + d_copies + relays + core_copies:
        copy.wait_send()
    for dst_of, sems in ((c_dst, c_core), (d_dst, d_core)):
        for k in range(split):
            core_copy(dst_of, sems, k).wait_recv()
    for copy in stores:
        copy.wait()


def run_mixer(
    tokens, gains, lengths, in_weight, conv_weight, x_weight, dt_weight, dt_bias, a_log, skip_gain,
    out_weight, expert_in, expert_out, grad_out, routes,
):
    own_rows, model_width = tokens.shape
    tap_count, channels = conv_weight.shape
    dt_rank, states = dt_weight.shape[1], a_log.shape[0]
    expert_count, hidden, _ = expert_in.shape
    row_count = own_rows * split
    steps = row_count // subs
    blocks = 2 * split
    channel_rows = -(-channels // 16) * 16
    width = blocks * channel_rows
    tiles = width // lanes
    vmem = pl.BlockSpec(memory_space=pltpu.VMEM)
    anywhere = pl.BlockSpec(memory_space=pl.ANY)
    f32, bf16 = jnp.float32, jnp.bfloat16
    tiled = (tiles, row_count, lanes)
    hidden_part = ((2 * expert_count - 1) * hidden, model_width)
    first = ((blocks, channel_rows, model_width + 3 * lanes), bf16)
    gate = ((blocks, 2 * channel_rows, model_width), bf16)
    normed = ((split, own_rows, model_width), bf16)
    edge = ((16, model_width), bf16)
    routed = ((split, own_rows, model_width + lanes), bf16)
    inputs = ((row_count + 16, width), f32)
    coef = ((row_count, lanes), f32)
    gated = ((row_count, width), bf16)
    start = ((tiles, states, subs, lanes), f32)
    resid = ((own_rows, model_width), f32)
    rows = ((tiles, lanes, lanes), f32)
    kept = [first, gate, normed, edge, routed, inputs, coef, (tiled, f32), (tiled, f32)]
    kept += [(tiled, f32), gated, start, normed, rows, (hidden_part, bf16)]
    outs = [first, gate, ((blocks,) + hidden_part, bf16), normed, routed, inputs, coef]
    spread_out = ((steps, states, subs, lanes), f32)
    outs += [(tiled, f32)] * 3 + [gated, start, resid, normed, rows, spread_out, spread_out]
    spreads = pltpu.VMEM((steps, states, subs, lanes), f32)
    dma = pltpu.SemaphoreType.DMA
    others = split - 1
    return pl.pallas_call(
        functools.partial(mixer_kernel, dt_rank, states, tap_count),
        in_specs=[pl.BlockSpec(memory_space=pltpu.SMEM) if i == 2 else vmem for i in range(15)],
        out_specs=[vmem if i == 12 else anywhere for i in range(len(outs))],
        out_shape=[jax.ShapeDtypeStruct(shape, kind) for shape, kind in outs],
        scratch_shapes=[pltpu.VMEM(shape, kind) for shape, kind in kept]
        + [dma((len(outs),))]
        + [
            spreads,
            spreads,
            pltpu.VMEM(tiled, f32),
            pltpu.VMEM((row_count, lanes), f32),
            pltpu.VMEM((row_count, width), bf16),
            pltpu.VMEM((others, own_rows, model_width), bf16),
            pltpu.VMEM((others, own_rows, model_width), bf16),
            pltpu.VMEM((row_count, lanes), bf16),
            pltpu.VMEM((others, row_count, lanes), bf16),
            pltpu.VMEM((tiles, 2 * states, lanes), f32),
            pltpu.VMEM((others, tiles, 2 * states, lanes), f32),
            pltpu.VMEM((tiles, states, subs, lanes), f32),
            pltpu.VMEM((tiles, states, subs, lanes), f32),
        ]
        + [dma((2, others))] * 4
        + [dma((2, split))] * 4
        + [dma((2, others))] * 5
        + [dma((split,)), dma, dma((2, others, tiles)), dma],
        compiler_params=pltpu.CompilerParams(
            collective_id=3, has_side_effects=True, vmem_limit_bytes=60 << 20
        ),
        cost_estimate=pl.CostEstimate(flops=1000, bytes_accessed=1000, transcendentals=0),
    )(
        tokens, gains, lengths, in_weight, conv_weight, x_weight, dt_weight, dt_bias, a_log, skip_gain,
        out_weight, expert_in, expert_out, grad_out, routes,
    )


def norm_back(values, gain_row, grads):
    scale = lax.rsqrt(jnp.mean(values * values, -1, keepdims=True) + eps_norm)
    unit = values * scale
    inner = grads * gain_row
    return scale * (inner - unit * jnp.mean(inner * unit, -1, keepdims=True)), grads * unit


def route_probs(rows, router, route_lanes, expert_count):
    logits = matmul_nt(rows, router)
    lane = lax.broadcasted_iota(jnp.int32, logits.shape, 1)
    logits = jnp.where(lane < expert_count, logits, -1e30)
    powers = jnp.exp(logits - jnp.max(logits, -1, keepdims=True))
    probs = powers / jnp.sum(powers, -1, keepdims=True)
    chosen = jnp.where(lane.astype(jnp.float32) == route_lanes, 1.0, 0.0)
    return probs, chosen, jnp.sum(probs * chosen, -1, keepdims=True)


class LineScatter:
    def __init__(self, src_of, arrive_ref, sems):
        core, high, low = kernel_place()
        self.src_of, self.arrive, self.high = src_of, arrive_ref, high
        relay = split

        def send(src, to, slot, index):
            return remote(src, arrive_ref.at[slot], sems.at[0, index], sems.at[1, slot], core, to, low)

        def slot_at(to, sender):
            return lax.rem(to - sender + split, split) - 1

        way = 1 - 2 * (high // (split - 1))
        near, mid, far = high + way, high + 2 * way, high + 3 * way
        self.end_sends = [
            send(src_of(far), near, relay, 0),
            send(src_of(mid), mid, slot_at(mid, high), 1),
            send(src_of(near), near, slot_at(near, high), 2),
        ]
        self.empty_slot = slot_at(high, far)
        self.end_slots = [slot_at(high, near), slot_at(high, mid)]
        beside, other = (split - 1) * (high - 1), split - 1 - high
        self.far_end = split - 1 - beside
        self.inner_sends = [
            send(src_of(other), other, slot_at(other, high), 1),
            send(src_of(beside), beside, slot_at(beside, high), 2),
        ]
        self.relay_send = send(arrive_ref.at[relay], self.far_end, slot_at(self.far_end, high), 0)
        self.inner_slots = [0, 1, 2]
        self.relay = relay
        self.sems = sems

    def landed(self, slot):
        core, high, low = kernel_place()
        remote(
            self.arrive.at[slot], self.arrive.at[slot], self.sems.at[0, 0], self.sems.at[1, slot],
            core, high, low,
        ).wait_recv()

    def start(self):
        @pl.when(at_ends())
        def _():
            for copy in self.end_sends:
                copy.start()
            self.arrive[self.empty_slot] = jnp.zeros(self.arrive.shape[1:], self.arrive.dtype)

        @pl.when(jnp.logical_not(at_ends()))
        def _():
            for copy in self.inner_sends:
                copy.start()

    def pass_on(self):
        @pl.when(jnp.logical_not(at_ends()))
        def _():
            self.landed(self.relay)
            own = self.src_of(self.far_end)
            rows = self.arrive.shape[1]

            def add(at):
                here = pl.ds(at, 16)
                total = self.arrive[self.relay, here].astype(jnp.float32)
                total = total + own[here, :].astype(jnp.float32)
                self.arrive[self.relay, here] = low_bits(total)

            row_loop(rows, 16, add)
            self.relay_send.start()

    def finish(self, out_ref):
        @pl.when(at_ends())
        def _():
            for copy in self.end_sends:
                copy.wait_send()
            for slot in self.end_slots:
                self.landed(slot)

        @pl.when(jnp.logical_not(at_ends()))
        def _():
            for copy in self.inner_sends + [self.relay_send]:
                copy.wait_send()
            for slot in self.inner_slots:
                self.landed(slot)

        own = self.src_of(self.high)

        def one(at):
            rows = pl.ds(at, 16)
            total = own[rows, :].astype(jnp.float32)
            for k in range(split - 1):
                total = total + self.arrive[k, rows].astype(jnp.float32)
            out_ref[rows, :] = total

        row_loop(out_ref.shape[0], 16, one)


def half_copy(src, dst, sems, h):
    core, high, low = kernel_place()
    return remote(src, dst, sems.at[0, h], sems.at[1, h], 1 - core, high, low)


def fill_offsets(reset_ref, lengths_ref, row_count):
    _, high, _ = kernel_place()
    first_len = lengths_ref[0, 0]

    def fill(at):
        place = high * row_count + at + lax.broadcasted_iota(jnp.int32, (64, lanes), 0)
        reset_ref[pl.ds(at, 64), :] = jnp.where((place == 0) | (place == first_len), 1e30, 0.0)

    row_loop(row_count, 64, fill)


def turn_kernel(
    states, expert_count,
    second_ref, routed_ref, hidden_hbm, weights_ref, router_ref, resid_ref, grad_ref, gains_ref,
    lengths_ref,
    gate_hbm, normed_hbm, out_hbm, step_hbm, z_hbm, y_hbm, gated_hbm, rows_hbm,
    mixed_out_ref, d_resid_ref, small_ref, dy_out, gz_out, later_ref, mine_out, early_ref,
    gate_mine_ref,
    hidden_ref, gate_ref, normed_ref, out_ref, step_ref, z_ref, y_ref, gated_ref, rows_ref, dy_ref,
    gz_ref, mine_ref, load_sems, store_sems,
    grads_ref, half_ref, y_sum_ref, d_sum_ref, dg_sum_ref, gates_ref, scaled_ref, act_ref, pre_ref,
    part_ref, arrive_ref, y_arrive_ref, branch_ref, reset_ref, send_ref,
    ends_ref, early_arrive_ref, gate_half_ref, down_ref, mine_early_ref, growth_ref,
    half_sems, sum_sems, y_sems, branch_sems, early_sems, ends_sems, gate_half_sems, last_sems,
    last_core,
):
    core, high, low = kernel_place()
    _, own_rows, model_width = second_ref.shape
    row_count = own_rows * split
    steps = row_count // subs
    tiles = step_ref.shape[0]
    width = tiles * lanes
    loads = [
        pltpu.make_async_copy(source, target, load_sems.at[i])
        for i, (source, target) in enumerate(
            (
                (hidden_hbm, hidden_ref),
                (gate_hbm, gate_ref),
                (z_hbm, z_ref),
                (y_hbm, y_ref),
                (step_hbm, step_ref),
                (rows_hbm, rows_ref),
                (out_hbm, out_ref),
                (normed_hbm, normed_ref),
                (gated_hbm, gated_ref),
            )
        )
    ]
    for copy in loads:
        copy.start()
    stores = [
        pltpu.make_async_copy(source, target, store_sems.at[i])
        for i, (source, target) in enumerate(((dy_ref, dy_out), (gz_ref, gz_out), (mine_ref, mine_out)))
    ]
    hidden = weights_ref.shape[1]
    last_ref = weights_ref.at[expert_count - 1]
    hidden_rows = 2 * expert_count * hidden
    channel_rows = width // (2 * split)
    greeted = greet_all()
    at = lax.broadcasted_iota(jnp.int32, (lanes, expert_count), 0)
    to = lax.broadcasted_iota(jnp.int32, (lanes, expert_count), 1)
    router = low_bits(
        matmul(jnp.where(at == to, 1.0, 0.0).astype(jnp.bfloat16), router_ref[...])
    )

    for l in range(split):
        rows = slice(l * own_rows, (l + 1) * own_rows)
        route_lanes = routed_ref[l, :, model_width:].astype(jnp.float32)
        _, _, gate = route_probs(second_ref[l], router, route_lanes, expert_count)
        gates_ref[rows, :] = jnp.broadcast_to(gate, (own_rows, lanes))
        scaled_ref[rows, :] = low_bits(gate * routed_ref[l, :, :model_width].astype(jnp.float32))
    y_sum_ref[...] = jnp.zeros_like(y_sum_ref)
    d_sum_ref[...] = jnp.zeros_like(d_sum_ref)
    dg_sum_ref[...] = jnp.zeros_like(dg_sum_ref)
    span = split * hidden

    pl.semaphore_wait(pltpu.get_barrier_semaphore(), greeted)

    loads[0].wait()

    def down_at(at):
        return down_ref.at[at]

    down_ref[high] = last_ref[...]
    last_copies = line_copies(last_ref, down_at, last_sems)
    last_relay = line_relay(down_at, last_sems)
    own_copy = core_copy(down_at, last_core, 0)
    for copy in last_copies + [own_copy]:
        copy.start()
    last_copies.append(own_copy)

    @pl.when(at_ends())
    def _():
        last_relay.start()

    def last_arrived(ks):
        for k in ks:
            line_arrived(last_ref, down_at, last_sems, k)
            copy = core_copy(down_at, last_core, k)
            copy.start()
            last_copies.append(copy)

    def halves_of(e, first):
        up = hidden_ref[first : first + split, 2 * e * hidden : (2 * e + 1) * hidden]
        up = up.reshape(span, model_width)
        if e < expert_count - 1:
            down = hidden_ref[first : first + split, (2 * e + 1) * hidden : (2 * e + 2) * hidden]
        else:
            down = down_ref[first : first + split]
        return up, down.reshape(span, model_width)

    def token_block(e, first, l):
        up, down = halves_of(e, first)
        cols = slice(0, span) if first else slice(span, 2 * span)
        rows = pl.ds(pl.multiple_of(l * own_rows, own_rows), own_rows)
        pre = matmul_nt(second_ref[l], up)
        picked = routed_ref[l, :, model_width : model_width + 1].astype(jnp.float32) == e
        half = 0.5 + 0.5 * lax.erf(pre * (0.5**0.5))
        bell = jnp.exp(-0.5 * pre * pre) * (1.0 / (2.0 * math.pi) ** 0.5)
        act = low_bits(jnp.where(picked, pre * half, 0.0))
        d_raw = matmul_nt(routed_ref[l, :, :model_width], down)
        weighted = act.astype(jnp.float32) * d_raw
        dg_sum_ref[rows, :] += sum(weighted[:, c : c + lanes] for c in range(0, span, lanes))
        d_pre = jnp.where(picked, gates_ref[rows, :1] * d_raw * (half + pre * bell), 0.0)
        d_pre = low_bits(d_pre)
        y_sum_ref[rows, :] += matmul(act, down)
        d_sum_ref[rows, :] += matmul(d_pre, up)
        act_ref[rows, cols] = act
        pre_ref[rows, cols] = d_pre

    def weight_grads(e, first):
        cols = slice(0, span) if first else slice(span, 2 * span)
        second = second_ref[...].reshape(row_count, model_width)
        up_grad = low_bits(matmul_tn(pre_ref[:, cols], second))
        down_grad = low_bits(matmul_tn(act_ref[:, cols], scaled_ref[...]))
        for b in range(split):
            piece = slice(b * hidden, (b + 1) * hidden)
            to = 2 * e * hidden
            grads_ref[first + b, to : to + hidden] = up_grad[piece]
            grads_ref[first + b, to + hidden : to + 2 * hidden] = down_grad[piece]

    def part_of(e):
        return pl.ds(2 * e * hidden, 2 * hidden)

    half_copies = {}

    def send_half(e):
        half_copies[e] = [
            half_copy(
                grads_ref.at[split + h, part_of(e)],
                half_ref.at[h, part_of(e)],
                half_sems.at[e],
                h,
            )
            for h in range(split)
        ]
        for copy in half_copies[e]:
            copy.start()

    def add_half(e):
        for copy in half_copies[e]:
            copy.wait()

        target, base = (mine_early_ref, 0) if e == 0 else (mine_ref, 2 * (e - 1) * hidden)

        def one(i, _):
            h, at = i // (2 * hidden // 32), lax.rem(i, 2 * hidden // 32) * 32
            rows = pl.ds(2 * e * hidden + at, 32)
            target[h, pl.ds(base + at, 32)] = low_bits(
                grads_ref[h, rows].astype(jnp.float32) + half_ref[h, rows].astype(jnp.float32)
            )
            return 0

        lax.fori_loop(0, split * (2 * hidden // 32), one, 0)

    early = LineScatter(lambda to: mine_early_ref.at[to], early_arrive_ref, early_sems)
    final = expert_count - 1
    for e in range(final):
        for first in (split, 0):
            lax.fori_loop(0, split, lambda l, _: (token_block(e, first, l), 0)[1], 0)
            weight_grads(e, first)
            if first:
                send_half(e)
                if e == 0:
                    last_arrived((1, 3))

                    @pl.when(jnp.logical_not(at_ends()))
                    def _():
                        last_relay.start()

    last_arrived((2,))
    for k in range(split):
        core_copy(down_at, last_core, k).wait_recv()

    def sum_copy(index):
        to = lax.rem(low + 1 + index, split)
        return remote(
            part_ref.at[index], arrive_ref.at[index], sum_sems.at[0, index], sum_sems.at[1, index],
            core, high, to,
        )

    def last_block(index, _):
        l = lax.rem(low + 1 + index, split)
        token_block(final, split, l)
        token_block(final, 0, l)

        @pl.when(index < split - 1)
        def _():
            rows = pl.ds(pl.multiple_of(l * own_rows, own_rows), own_rows)
            part_ref[index, :, :model_width] = low_bits(d_sum_ref[rows, :])
            part_ref[index, :, model_width:] = low_bits(dg_sum_ref[rows, :])
            sum_copy(index).start()

        return 0

    lax.fori_loop(0, split, last_block, 0)
    weight_grads(final, split)
    send_half(final)
    for e in range(final):
        add_half(e)
    early.start()
    weight_grads(final, 0)
    for copy in last_copies + [last_relay]:
        copy.wait_send()

    y_copies = plane_copies(
        lambda to, k: part_ref.at[k - 1, :, pl.ds(0, model_width)], y_arrive_ref, y_sems, False
    )
    own = pl.ds(pl.multiple_of(low * own_rows, own_rows), own_rows)
    d_second, dg_lanes = d_sum_ref[own, :], dg_sum_ref[own, :]
    for k in range(1, split):
        sum_copy(k - 1).wait()
        d_second = d_second + arrive_ref[k - 1, :, :model_width].astype(jnp.float32)
        dg_lanes = dg_lanes + arrive_ref[k - 1, :, model_width:].astype(jnp.float32)
    d_gate = jnp.sum(dg_lanes, -1, keepdims=True)
    second_own = second_ref[low]
    route_lanes = routed_ref[low, :, model_width:].astype(jnp.float32)
    probs, chosen, gate = route_probs(second_own, router, route_lanes, expert_count)
    d_logits = low_bits(probs * (d_gate * (chosen - gate)))
    d_second = d_second + matmul(d_logits, router)
    d_rows, d_gain = norm_back(resid_ref[...], gains_ref[1:2, :], d_second)
    d_resid = grad_ref[...] + d_rows
    d_resid_ref[...] = d_resid
    branch_ref[low] = low_bits(d_resid)
    branch_copies = plane_copies(lambda to, k: branch_ref.at[low], branch_ref, branch_sems, True)
    for copy in branch_copies:
        copy.start()
    for k in range(1, split):
        to = pl.ds(pl.multiple_of(lax.rem(low + k, split) * own_rows, own_rows), own_rows)
        part_ref[k - 1, :, :model_width] = low_bits(y_sum_ref[to, :])
        y_copies[k - 1].start()
    small_ref[...] = jnp.zeros_like(small_ref)
    small_ref[1:2, :] = jnp.sum(d_gain, 0, keepdims=True)
    small_ref[2 : 2 + expert_count, :] = matmul_tn(d_logits, second_own)[:expert_count]

    early.pass_on()
    add_half(final)
    stores[2].start()
    for copy in loads[1:]:
        copy.wait()
    fill_offsets(reset_ref, lengths_ref, row_count)
    out_full = gate_ref[:, channel_rows:].reshape(width, model_width)
    for copy in branch_copies:
        copy.wait()
    for l in range(split):
        d_gated = matmul_nt(branch_ref[l], out_full)
        rows = slice(l * own_rows, (l + 1) * own_rows)
        for j in range(tiles):
            cols = slice(j * lanes, (j + 1) * lanes)
            z = z_ref[j, rows, :]
            sig = sigmoid_of(z)
            d_tile = d_gated[:, cols]
            dy_ref[j, rows, :] = d_tile * (z * sig)
            d_z = d_tile * y_ref[j, rows, :] * (sig * (1.0 + z * (1.0 - sig)))
            gz_ref[rows, cols] = low_bits(d_z)

    def rates_of(j):
        values = -jnp.exp(rows_ref[j, alog_row : alog_row + states, :]) * log2e
        return [jnp.broadcast_to(values[n : n + 1, :], (subs, lanes)) for n in range(states)]

    def ends_of(j, _):
        found = scan_one_way(
            j, None, True, states, steps, step_ref, reset_ref, dy_ref, out_ref, rates_of(j)
        )
        row = lax.broadcasted_iota(jnp.int32, (subs, lanes), 0)
        for n, (grow, state) in enumerate(found):
            send_ref[j, n : n + 1] = grow[:1]
            send_ref[j, states + n : states + n + 1] = state[:1]
            has = row < subs - 1
            growth_ref[j, n] = jnp.where(has, pltpu.roll(grow, subs - 1, 0), 1.0)
            later_ref[j, n] = jnp.where(has, pltpu.roll(state, subs - 1, 0), 0.0)
        for copy in ends_copies(send_ref, ends_ref, ends_sems, j, True):
            copy.start()
        return 0

    stores[0].start()
    stores[1].start()
    lax.fori_loop(0, tiles, ends_of, 0)

    normed = normed_ref[...].reshape(row_count, model_width)
    branch = branch_ref[...].reshape(row_count, model_width)
    for part, (first_op, second_op) in enumerate(((gz_ref, normed), (gated_ref, branch))):
        half_width = width // 2
        for at in (half_width, 0):
            grad = low_bits(matmul_tn(first_op[:, at : at + half_width], second_op))
            for b in range(split):
                piece = grad[b * channel_rows : (b + 1) * channel_rows]
                to = part * channel_rows
                grads_ref[at // channel_rows + b, to : to + channel_rows] = piece
    gate_rows = 2 * channel_rows
    gate_copies = [
        half_copy(
            grads_ref.at[split + h, pl.ds(0, gate_rows)], gate_half_ref.at[h], gate_half_sems, h
        )
        for h in range(split)
    ]
    for copy in gate_copies:
        copy.start()

    def settle(j, _):
        for copy in ends_copies(send_ref, ends_ref, ends_sems, j, True):
            copy.wait()
        enter = chain_enter(ends_ref, j, states, True)
        for n in range(states):
            entered = jnp.broadcast_to(enter[n : n + 1, :], (subs, lanes))
            later_ref[j, n] += growth_ref[j, n] * entered
        return 0

    lax.fori_loop(0, tiles, settle, 0)
    y = y_sum_ref[own, :]
    for k in range(1, split):
        y_copies[k - 1].wait()
        y = y + y_arrive_ref[k - 1].astype(jnp.float32)
    mixed_out_ref[...] = low_bits(resid_ref[...] + gates_ref[own, :1] * y)
    for h in range(split):
        gate_copies[h].wait()

        def add_gate(at, h=h):
            rows = pl.ds(at, 16)
            total = grads_ref[h, rows].astype(jnp.float32) + gate_half_ref[h, rows].astype(jnp.float32)
            gate_mine_ref[h, rows] = low_bits(total)

        row_loop(gate_rows, 16, add_gate)
    early.finish(early_ref)
    for copy in stores:
        copy.wait()


def run_turn(
    second, routed, hidden_full, last_part, router_lanes, resid, grad_out, gains, lengths, gate_full, normed,
    spread_out, step, z, y, gated, rows, states, expert_count,
):
    _, own_rows, model_width = second.shape
    row_count = own_rows * split
    steps = row_count // subs
    tiles = step.shape[0]
    width = tiles * lanes
    hidden = last_part.shape[1]
    hidden_rows = 2 * expert_count * hidden
    cut = 2 * hidden
    gate_rows = gate_full.shape[1]
    others = split - 1
    vmem = pl.BlockSpec(memory_space=pltpu.VMEM)
    f32, bf16 = jnp.float32, jnp.bfloat16
    dma = pltpu.SemaphoreType.DMA
    outs = [
        ((own_rows, model_width), bf16),
        ((own_rows, model_width), f32),
        ((8, model_width), f32),
        ((tiles, row_count, lanes), f32),
        ((row_count, width), bf16),
        ((tiles, states, subs, lanes), f32),
        ((split, hidden_rows - cut, model_width), bf16),
        ((cut, model_width), f32),
        ((split, gate_rows, model_width), bf16),
    ]
    span = split * hidden
    anywhere = pl.BlockSpec(memory_space=pl.ANY)
    specs = [anywhere if i == 2 or i > 8 else vmem for i in range(17)]
    specs[8] = pl.BlockSpec(memory_space=pltpu.SMEM)
    loaded = [hidden_full, gate_full, normed, spread_out, step, z, y, gated, rows]
    return pl.pallas_call(
        functools.partial(turn_kernel, states, expert_count),
        in_specs=specs,
        out_specs=[anywhere if i in (3, 4, 6) else vmem for i in range(len(outs))],
        out_shape=[jax.ShapeDtypeStruct(shape, kind) for shape, kind in outs],
        scratch_shapes=[pltpu.VMEM(value.shape, value.dtype) for value in loaded]
        + [pltpu.VMEM(*outs[i]) for i in (3, 4, 6)]
        + [dma((len(loaded),)), dma((3,))]
        + [
            pltpu.VMEM((2 * split, hidden_rows, model_width), bf16),
            pltpu.VMEM((split, hidden_rows, model_width), bf16),
            pltpu.VMEM((row_count, model_width), f32),
            pltpu.VMEM((row_count, model_width), f32),
            pltpu.VMEM((row_count, lanes), f32),
            pltpu.VMEM((row_count, lanes), f32),
            pltpu.VMEM((row_count, model_width), bf16),
            pltpu.VMEM((row_count, 2 * span), bf16),
            pltpu.VMEM((row_count, 2 * span), bf16),
            pltpu.VMEM((others, own_rows, model_width + lanes), bf16),
            pltpu.VMEM((others, own_rows, model_width + lanes), bf16),
            pltpu.VMEM((others, own_rows, model_width), bf16),
            pltpu.VMEM((split, own_rows, model_width), bf16),
            pltpu.VMEM((row_count, lanes), f32),
            pltpu.VMEM((tiles, 2 * states, lanes), f32),
            pltpu.VMEM((others, tiles, 2 * states, lanes), f32),
            pltpu.VMEM((split + 1, cut, model_width), bf16),
            pltpu.VMEM((split, gate_rows, model_width), bf16),
            pltpu.VMEM((2 * split, hidden, model_width), bf16),
            pltpu.VMEM((split, cut, model_width), bf16),
            pltpu.VMEM((tiles, states, subs, lanes), f32),
            dma((expert_count, 2, split)),
            dma((2, others)),
            dma((2, others)),
            dma((2, others)),
            dma((2, split + 1)),
            dma((2, others, tiles)),
            dma((2, split)),
            dma((2, others)),
            dma((2, split)),
        ],
        compiler_params=pltpu.CompilerParams(
            collective_id=4, has_side_effects=True, vmem_limit_bytes=63 << 20
        ),
        cost_estimate=pl.CostEstimate(flops=1000, bytes_accessed=1000, transcendentals=0),
    )(
        second, routed, hidden_full, last_part, router_lanes, resid, grad_out, gains, lengths, gate_full, normed,
        spread_out, step, z, y, gated, rows,
    )


def back_kernel(
    dt_rank, states, tap_count,
    dy_hbm, gz_hbm, later_hbm, mine_ref, gate_mine_hbm, first_hbm, gate_hbm, normed_hbm, input_ref,
    coef_ref, step_hbm, start_hbm, rows_ref, d_resid_ref, tokens_ref, gains_ref, small_ref,
    lengths_ref, in_hbm, out_hbm,
    grad_tokens_ref, total_ref, late_ref, gate_own_ref, first_own_ref,
    dy_ref, gz_ref, later_ref, gate_mine_ref, first_ref, gate_ref, normed_ref, step_ref, start_ref,
    in_ref, out_ref, load_sems,
    hist_ref, acc_in_ref, acc_out_ref, mixed_ref, conv_ref, q_ref, r_ref, reset_ref,
    gdt_ref, gin_ref, halo_ref, part_ref, arrive_ref, fold_ref, coef_send_ref,
    coef_arrive_ref, gcoef_ref, misc_ref, select_ref, payload_ref, half_ref, mine_first_ref,
    late_arrive_ref, gate_arrive_ref, first_arrive_ref, core_slots, plane_slots, line_slots,
    late_sems, gate_sems, first_sems, half_sems, halo_sems, coef_sems, sum_sems, core_sems,
    plane_sems, line_sems,
):
    core, high, low = kernel_place()
    _, own_rows, model_width = normed_ref.shape
    row_count = own_rows * split
    steps = row_count // subs
    tiles = step_ref.shape[0]
    loads = [
        pltpu.make_async_copy(source, target, load_sems.at[i])
        for i, (source, target) in enumerate(
            (
                (step_hbm, step_ref),
                (start_hbm, start_ref),
                (gate_mine_hbm, gate_mine_ref),
                (in_hbm, in_ref),
                (dy_hbm, dy_ref),
                (later_hbm, later_ref),
                (out_hbm, out_ref),
                (first_hbm, first_ref),
                (gate_hbm, gate_ref),
                (gz_hbm, gz_ref),
                (normed_hbm, normed_ref),
            )
        )
    ]
    for copy in loads:
        copy.start()
    width = tiles * lanes
    channel_rows = width // (2 * split)
    edge = input_ref.shape[0] - row_count
    greeted = greet_all()
    first_len = lengths_ref[0, 0]

    def offsets(at, rows):
        place = high * row_count + at + lax.broadcasted_iota(jnp.int32, (rows, lanes), 0)
        return jnp.where(place < first_len, place, place - first_len)

    fill_offsets(reset_ref, lengths_ref, row_count)
    pl.semaphore_wait(pltpu.get_barrier_semaphore(), greeted)
    late = LineScatter(lambda to: mine_ref.at[to], late_arrive_ref, late_sems)
    gate = LineScatter(lambda to: gate_mine_ref.at[to], gate_arrive_ref, gate_sems)
    late.start()

    def convolve(at):
        offset = offsets(at, 32)
        for j in range(tiles):
            span = input_ref[pl.ds(at, 32 + edge), j * lanes : (j + 1) * lanes]
            conv_sum = jnp.zeros((32, lanes), jnp.float32)
            for k in range(tap_count):
                shift = edge - (tap_count - 1) + k
                term = rows_ref[j, k : k + 1, :] * span[shift : shift + 32]
                conv_sum = conv_sum + jnp.where(offset >= tap_count - 1 - k, term, 0.0)
            conv_ref[j, pl.ds(at, 32), :] = conv_sum
            mixed = low_bits(conv_sum * sigmoid_of(conv_sum)).astype(jnp.float32)
            mixed_ref[j, pl.ds(at, 32), :] = mixed

    row_loop(row_count, 32, convolve)
    late.pass_on()
    for copy in loads[:7]:
        copy.wait()
    gate.start()
    acc_in_ref[...] = jnp.zeros_like(acc_in_ref)
    acc_out_ref[...] = jnp.zeros_like(acc_out_ref)
    misc_ref[...] = jnp.zeros_like(misc_ref)

    def back_of(j, _):
        values = -jnp.exp(rows_ref[j, alog_row : alog_row + states, :]) * log2e
        rates = [jnp.broadcast_to(values[n : n + 1, :], (subs, lanes)) for n in range(states)]

        def forward(s, held):
            step = step_ref[j, pl.ds(s, subs, stride=steps), :]
            drive = step * mixed_ref[j, pl.ds(s, subs, stride=steps), :]
            step = step + reset_ref[pl.ds(s, subs, stride=steps), :]
            now_all = []
            for n in range(states):
                now = jnp.exp2(step * rates[n]) * held[n] + in_ref[s, n] * drive
                hist_ref[s + 1, n] = now
                now_all.append(now)
            return tuple(now_all)

        held = []
        for n in range(states):
            hist_ref[0, n] = start_ref[j, n]
            held.append(start_ref[j, n])
        lax.fori_loop(0, steps, forward, tuple(held), unroll=2)

        def backward(turn, carry):
            s = steps - 1 - turn
            later, sums = carry
            delta = step_ref[j, pl.ds(s, subs, stride=steps), :]
            drive = delta * mixed_ref[j, pl.ds(s, subs, stride=steps), :]
            step = delta + reset_ref[pl.ds(s, subs, stride=steps), :]
            dy = dy_ref[j, pl.ds(s, subs, stride=steps), :]
            rows = pl.ds(pl.multiple_of(s * subs, subs), subs)
            q = jnp.zeros((subs, lanes), jnp.float32)
            r = jnp.zeros((subs, lanes), jnp.float32)
            later_next, sums_next = [], []
            for n in range(states):
                cols = slice(n * lanes, (n + 1) * lanes)
                d_state = out_ref[s, n] * dy + later[n]
                back = jnp.exp2(step * rates[n]) * d_state
                scaled = back * hist_ref[s, n]
                sums_next.append(sums[n] + scaled * delta)
                q = q + scaled * rates[n]
                r = r + d_state * in_ref[s, n]
                acc_in_ref[rows, cols] += d_state * drive
                acc_out_ref[rows, cols] += hist_ref[s + 1, n] * dy
                later_next.append(back)
            q_ref[j, pl.ds(s, subs, stride=steps), :] = q * (1.0 / log2e)
            r_ref[j, pl.ds(s, subs, stride=steps), :] = r
            return tuple(later_next), tuple(sums_next)

        zero = jnp.zeros((subs, lanes), jnp.float32)
        later = tuple(later_ref[j, n] for n in range(states))
        _, sums = lax.fori_loop(0, steps, backward, (later, (zero,) * states))
        for n in range(states):
            total = jnp.sum(sums[n] * rates[n], 0, keepdims=True) * (1.0 / log2e)
            misc_ref[j, alog_row + n : alog_row + n + 1, :] = total
        return 0

    lax.fori_loop(0, tiles, back_of, 0)

    for copy in loads[7:]:
        copy.wait()

    source = lax.broadcasted_iota(jnp.int32, select_ref.shape, 0) // lanes
    target = lax.broadcasted_iota(jnp.int32, select_ref.shape, 1)

    def fold(acc_ref, first, fresh):
        select_ref[...] = jnp.where(target == first + source, 1.0, 0.0).astype(jnp.bfloat16)

        def one(at):
            values = acc_ref[pl.ds(at, 128), :]
            coarse = low_bits(values)
            fine = low_bits(values - coarse.astype(jnp.float32))
            found = matmul(coarse, select_ref[...]) + matmul(fine, select_ref[...])
            for i in range(128 // subs):
                rows = pl.ds(at // subs + i, subs, stride=steps)
                piece = found[i * subs : (i + 1) * subs]
                fold_ref[rows, :] = piece if fresh else fold_ref[rows, :] + piece

        row_loop(row_count, 128, one)

    fold(acc_in_ref, dt_rank, True)
    fold(acc_out_ref, dt_rank + states, False)
    dt_full = first_ref[:, :, model_width + lanes : model_width + 2 * lanes].reshape(width, lanes)

    def step_grads(at):
        rows = pl.ds(at, 128)
        pre = matmul_nt(low_bits(coef_ref[rows, :]), dt_full)
        for j in range(tiles):
            cols = slice(j * lanes, (j + 1) * lanes)
            mixed = mixed_ref[j, rows, :]
            d_step = q_ref[j, rows, :] + r_ref[j, rows, :] * mixed
            d_dt = d_step * sigmoid_of(pre[:, cols] + rows_ref[j, bias_row : bias_row + 1, :])
            gdt_ref[rows, cols] = low_bits(d_dt)
            misc_ref[j, bias_row : bias_row + 1, :] += jnp.sum(d_dt, 0, keepdims=True)
            misc_ref[j, skip_row : skip_row + 1, :] += jnp.sum(
                dy_ref[j, rows, :] * mixed, 0, keepdims=True
            )
        part = fold_ref[rows, :] + matmul(gdt_ref[rows, :], dt_full)
        fold_ref[rows, :] = part
        coef_send_ref[rows, :] = low_bits(part)

    row_loop(row_count, 128, step_grads)
    gate.pass_on()
    coef_copies = plane_copies(lambda to, k: coef_send_ref, coef_arrive_ref, coef_sems, False)
    for copy in coef_copies:
        copy.start()
    low_coef = low_bits(coef_ref[...])
    for j in range(tiles):
        rows = slice(j * lanes, (j + 1) * lanes)
        payload_ref[rows, model_width + lanes : model_width + 2 * lanes] = low_bits(
            matmul_tn(gdt_ref[:, rows], low_coef)
        )
    for copy in coef_copies:
        copy.wait()
    total = fold_ref[...]
    for k in range(1, split):
        total = total + coef_arrive_ref[k - 1].astype(jnp.float32)
    gcoef_ref[...] = low_bits(total)
    x_full = first_ref[:, :, model_width : model_width + lanes].reshape(width, lanes)

    def conv_grads(at):
        rows = pl.ds(at, 128)
        from_coef = matmul_nt(gcoef_ref[rows, :], x_full)
        for j in range(tiles):
            cols = slice(j * lanes, (j + 1) * lanes)
            d_mixed = rows_ref[j, skip_row : skip_row + 1, :] * dy_ref[j, rows, :]
            d_mixed = d_mixed + r_ref[j, rows, :] * step_ref[j, rows, :] + from_coef[:, cols]
            conv = conv_ref[j, rows, :]
            sig = sigmoid_of(conv)
            q_ref[j, rows, :] = d_mixed * (sig * (1.0 + conv * (1.0 - sig)))

    row_loop(row_count, 128, conv_grads)

    def halo_copy():
        return remote(
            q_ref.at[:, pl.ds(0, subs)], halo_ref, halo_sems.at[0], halo_sems.at[1],
            core, lax.rem(high + split - 1, split), low,
        )

    @pl.when(high > 0)
    def _():
        halo_copy().start()

    def tap_grads(at):
        offset = offsets(at, 32)
        for j in range(tiles):
            cols = slice(j * lanes, (j + 1) * lanes)
            span = input_ref[pl.ds(at, 32 + edge), cols]
            d_conv = q_ref[j, pl.ds(at, 32), :]
            for k in range(tap_count):
                shift = edge - (tap_count - 1) + k
                term = jnp.where(offset >= tap_count - 1 - k, d_conv * span[shift : shift + 32], 0.0)
                misc_ref[j, k : k + 1, :] += jnp.sum(term, 0, keepdims=True)

    row_loop(row_count, 32, tap_grads)

    @pl.when(high < split - 1)
    def _():
        halo_copy().wait_recv()
        q_ref[:, row_count:, :] = halo_ref[...]

    @pl.when(high == split - 1)
    def _():
        q_ref[:, row_count:, :] = jnp.zeros_like(halo_ref)

    def input_grads(at):
        masks = [offsets(at + m, 32) >= m for m in range(tap_count)]
        for j in range(tiles):
            cols = slice(j * lanes, (j + 1) * lanes)
            span = q_ref[j, pl.ds(at, 32 + subs), :]
            d_input = jnp.zeros((32, lanes), jnp.float32)
            for m in range(tap_count):
                k = tap_count - 1 - m
                term = rows_ref[j, k : k + 1, :] * span[m : m + 32]
                d_input = d_input + jnp.where(masks[m], term, 0.0)
            gin_ref[pl.ds(at, 32), cols] = low_bits(d_input)

    row_loop(row_count, 32, input_grads)

    first_in = first_ref[:, :, :model_width].reshape(width, model_width)
    second_in = gate_ref[:, :channel_rows].reshape(width, model_width)

    def normed_block(l):
        rows = pl.ds(pl.multiple_of(l * own_rows, own_rows), own_rows)
        return matmul(gin_ref[rows, :], first_in) + matmul(gz_ref[rows, :], second_in)

    normed = normed_ref[...].reshape(row_count, model_width)
    for j in range(tiles):
        rows = slice(j * lanes, (j + 1) * lanes)
        payload_ref[rows, model_width : model_width + lanes] = low_bits(
            matmul_tn(low_bits(mixed_ref[j]), gcoef_ref[...])
        )
        payload_ref[rows, model_width + 2 * lanes :] = low_bits(misc_ref[j].T)
    half_width = width // 2
    half = remote(
        payload_ref.at[pl.ds(half_width, half_width)], half_ref, half_sems.at[0], half_sems.at[1],
        1 - core, high, low,
    )

    def first_half(at):
        payload_ref[at : at + half_width, :model_width] = low_bits(
            matmul_tn(gin_ref[:, at : at + half_width], normed)
        )

    first_half(half_width)
    half.start()
    sum_copies = plane_copies(lambda to, k: part_ref.at[k - 1], arrive_ref, sum_sems, False)
    gain = jnp.zeros((1, model_width), jnp.float32)
    for k in range(1, split + 1):
        l = lax.rem(low + k, split)
        block = normed_block(l)
        gain = gain + jnp.sum(block * normed_ref[l].astype(jnp.float32), 0, keepdims=True)
        if k < split:
            part_ref[k - 1] = low_bits(block)
            sum_copies[k - 1].start()
        else:
            grad_tokens_ref[...] = block

    line_slots[high] = small_ref[...]
    line_slots[high, 0:1, :] = gain / gains_ref[0:1, :]
    line = line_copies(line_slots.at[high], lambda at: line_slots.at[at], line_sems, True)
    for copy in line:
        copy.start()
    first_half(0)
    half.wait()

    def add_half(at):
        rows = pl.ds(at, 64)
        both = payload_ref[rows, :].astype(jnp.float32) + half_ref[rows, :].astype(jnp.float32)
        mine_first_ref[rows, :] = low_bits(both)

    row_loop(half_width, 64, add_half)
    first = LineScatter(
        lambda to: mine_first_ref.at[pl.ds(pl.multiple_of(to * channel_rows, 16), channel_rows)],
        first_arrive_ref,
        first_sems,
    )
    first.start()
    for k in range(1, split):
        line_arrived(line_slots.at[high], lambda at: line_slots.at[at], line_sems, k)
    core_slots[core] = (line_slots[0] + line_slots[1]) + (line_slots[2] + line_slots[3])
    hop = remote(
        core_slots.at[core], core_slots.at[core], core_sems.at[0], core_sems.at[1], 1 - core, high, low
    )
    hop.start()
    late.finish(late_ref)
    hop.wait()
    plane_slots[low] = core_slots[0] + core_slots[1]
    plane = plane_copies(lambda to, k: plane_slots.at[low], plane_slots, plane_sems, True)
    for copy in plane:
        copy.start()
    first.pass_on()
    gate.finish(gate_own_ref)
    d_normed = grad_tokens_ref[...]
    for k in range(1, split):
        sum_copies[k - 1].wait()
        d_normed = d_normed + arrive_ref[k - 1].astype(jnp.float32)
    tokens = tokens_ref[...].astype(jnp.float32)
    d_rows, _ = norm_back(tokens, gains_ref[0:1, :], d_normed)
    grad_tokens_ref[...] = d_resid_ref[...] + d_rows
    for copy in plane:
        copy.wait()
    for copy in line:
        copy.wait_send()
    total_ref[...] = (plane_slots[0] + plane_slots[1]) + (plane_slots[2] + plane_slots[3])
    first.finish(first_own_ref)

    @pl.when(high > 0)
    def _():
        halo_copy().wait_send()


def run_back(
    dy, gz, later, mine, gate_mine, first_full, gate_full, normed, input_all, coef, step, start, rows,
    d_resid, tokens, gains, small, lengths, spread_in, spread_out, dt_rank, states, tap_count,
):
    _, own_rows, model_width = normed.shape
    row_count = own_rows * split
    steps = row_count // subs
    tiles = step.shape[0]
    width = tiles * lanes
    channel_rows = width // (2 * split)
    others = split - 1
    late_rows = mine.shape[1]
    gate_rows = gate_mine.shape[1]
    first_columns = first_full.shape[2]
    vmem = pl.BlockSpec(memory_space=pltpu.VMEM)
    specs = [pl.BlockSpec(memory_space=pl.ANY) if i in (0, 1, 2, 4, 5, 6, 7, 10, 11) else vmem for i in range(17)]
    loaded = [dy, gz, later, gate_mine, first_full, gate_full, normed, step, start]
    loaded += [spread_in, spread_out]
    specs.append(pl.BlockSpec(memory_space=pltpu.SMEM))
    specs += [pl.BlockSpec(memory_space=pl.ANY)] * 2
    f32, bf16 = jnp.float32, jnp.bfloat16
    dma = pltpu.SemaphoreType.DMA
    outs = [
        (own_rows, model_width),
        (8, model_width),
        (late_rows, model_width),
        (gate_rows, model_width),
        (channel_rows, first_columns),
    ]
    tiled = pltpu.VMEM((tiles, row_count, lanes), f32)
    summed = pltpu.VMEM((row_count, states * lanes), f32)
    return pl.pallas_call(
        functools.partial(back_kernel, dt_rank, states, tap_count),
        in_specs=specs,
        out_specs=[vmem] * len(outs),
        out_shape=[jax.ShapeDtypeStruct(shape, f32) for shape in outs],
        scratch_shapes=[pltpu.VMEM(value.shape, value.dtype) for value in loaded]
        + [dma((len(loaded),))]
        + [
            pltpu.VMEM((steps + 1, states, subs, lanes), f32),
            summed,
            summed,
            tiled,
            tiled,
            pltpu.VMEM((tiles, row_count + subs, lanes), f32),
            tiled,
            pltpu.VMEM((row_count, lanes), f32),
            pltpu.VMEM((row_count, width), bf16),
            pltpu.VMEM((row_count, width), bf16),
            pltpu.VMEM((tiles, subs, lanes), f32),
            pltpu.VMEM((others, own_rows, model_width), bf16),
            pltpu.VMEM((others, own_rows, model_width), bf16),
            pltpu.VMEM((row_count, lanes), f32),
            pltpu.VMEM((row_count, lanes), bf16),
            pltpu.VMEM((others, row_count, lanes), bf16),
            pltpu.VMEM((row_count, lanes), bf16),
            pltpu.VMEM((tiles, lanes, lanes), f32),
            pltpu.VMEM((states * lanes, lanes), bf16),
            pltpu.VMEM((width, first_columns), bf16),
            pltpu.VMEM((width // 2, first_columns), bf16),
            pltpu.VMEM((width // 2, first_columns), bf16),
            pltpu.VMEM((split + 1, late_rows, model_width), bf16),
            pltpu.VMEM((split + 1, gate_rows, model_width), bf16),
            pltpu.VMEM((split + 1, channel_rows, first_columns), bf16),
            pltpu.VMEM((2, 8, model_width), f32),
            pltpu.VMEM((split, 8, model_width), f32),
            pltpu.VMEM((split, 8, model_width), f32),
        ]
        + [dma((2, split + 1))] * 3
        + [dma((2,)), dma((2,)), dma((2, others)), dma((2, others)), dma((2,))]
        + [dma((2, others)), dma((2, others))],
        compiler_params=pltpu.CompilerParams(
            collective_id=5, has_side_effects=True, vmem_limit_bytes=63 << 20
        ),
        cost_estimate=pl.CostEstimate(flops=1000, bytes_accessed=1000, transcendentals=0),
    )(
        dy, gz, later, mine, gate_mine, first_full, gate_full, normed, input_all, coef, step, start,
        rows, d_resid, tokens, gains, small, lengths, spread_in, spread_out,
    )


def results_kernel(
    tap_count, states, coef_count, dt_rank, expert_count,
    mixed_ref, tokens_ref, total_ref, early_ref, late_ref, gate_ref, first_ref,
    mixed_out, tokens_out, gains_out, router_out, in_out, conv_out, x_out, dt_out, bias_out, alog_out,
    skip_out, out_out, up_out, down_out,
):
    channels, model_width = out_out.shape
    hidden = up_out.shape[1]
    channel_rows = first_ref.shape[0]
    mixed_out[...] = mixed_ref[...]
    tokens_out[...] = tokens_ref[...]
    gains_out[...] = total_ref[:2]
    router_out[...] = total_ref[2 : 2 + expert_count]
    in_out[0] = first_ref[:channels, :model_width]
    in_out[1] = gate_ref[:channels]
    out_out[...] = gate_ref[channel_rows : channel_rows + channels]
    at = model_width
    x_out[...] = first_ref[:channels, at : at + lanes][:, :coef_count]
    dt_out[...] = first_ref[:channels, at + lanes : at + 2 * lanes][:, :dt_rank]
    misc = first_ref[:, at + 2 * lanes :]
    rows = misc.T
    conv_out[...] = rows[:tap_count, :channels]
    alog_out[...] = rows[alog_row : alog_row + states, :channels]
    bias_out[...] = rows[bias_row : bias_row + 1, :channels]
    skip_out[...] = rows[skip_row : skip_row + 1, :channels]
    for e in range(expert_count):
        source, first = (early_ref, 0) if e == 0 else (late_ref, 2 * (e - 1) * hidden)
        up_out[e] = source[first : first + hidden]
        down_out[e] = source[first + hidden : first + 2 * hidden]


def run_results(parts, channels, tap_count, states, coef_count, dt_rank, expert_count, hidden):
    own_rows, model_width = parts[0].shape
    f32 = jnp.float32
    shapes = [
        (own_rows, model_width),
        (2, model_width),
        (expert_count, model_width),
        (2, channels, model_width),
        (tap_count, channels),
        (channels, coef_count),
        (channels, dt_rank),
        (1, channels),
        (states, channels),
        (1, channels),
        (channels, model_width),
        (expert_count, hidden, model_width),
        (expert_count, hidden, model_width),
    ]
    vmem = pl.BlockSpec(memory_space=pltpu.VMEM)
    return pl.pallas_call(
        functools.partial(results_kernel, tap_count, states, coef_count, dt_rank, expert_count),
        in_specs=[vmem] * len(parts),
        out_specs=[vmem] * (len(shapes) + 1),
        out_shape=[jax.ShapeDtypeStruct((own_rows, model_width), jnp.bfloat16)]
        + [jax.ShapeDtypeStruct(shape, f32) for shape in shapes],
        compiler_params=pltpu.CompilerParams(vmem_limit_bytes=62 << 20),
        cost_estimate=pl.CostEstimate(flops=1000, bytes_accessed=1000, transcendentals=0),
    )(*parts)


def norm_rows(values, gain_row):
    return values * lax.rsqrt(jnp.mean(values * values, -1, keepdims=True) + eps_norm) * gain_row


def matmul(first_op, second_op):
    return jnp.dot(first_op, second_op, preferred_element_type=jnp.float32)


def matmul_nt(first_op, second_op):
    return lax.dot_general(
        first_op, second_op, (((1,), (1,)), ((), ())), preferred_element_type=jnp.float32
    )


def matmul_tn(first_op, second_op):
    return lax.dot_general(
        first_op, second_op, (((0,), (0,)), ((), ())), preferred_element_type=jnp.float32
    )


def low_bits(value):
    return value.astype(jnp.bfloat16)


def swap_low(value, k):
    count = lax.axis_size("seq")
    return lax.ppermute(value, "seq", [(s, s ^ k) for s in range(count)])


def turn_high(value, k):
    count = lax.axis_size("seq")
    return lax.ppermute(value, "seq", [(s, (s + split * k) % count) for s in range(count)])


def from_high(value, k):
    count = lax.axis_size("seq")
    pairs = [(s, s + split * k) for s in range(count) if 0 <= s + split * k < count]
    return lax.ppermute(value, "seq", pairs)


def swap_core(value):
    return lax.ppermute(value, "grp", [(0, 1), (1, 0)])


def high_groups():
    count = lax.axis_size("seq")
    return [[h * split + l for h in range(count // split)] for l in range(split)]


def gather_low(value):
    low = lax.axis_index("seq") % split
    first_bit, second_bit = low % 2 == 1, low // 2 == 1
    own, one, two, three = [value] + [swap_low(value, k) for k in range(1, split)]
    a, b = jnp.where(first_bit, one, own), jnp.where(first_bit, own, one)
    c, d = jnp.where(first_bit, three, two), jnp.where(first_bit, two, three)
    pieces = [
        jnp.where(second_bit, c, a),
        jnp.where(second_bit, d, b),
        jnp.where(second_bit, a, c),
        jnp.where(second_bit, b, d),
    ]
    return jnp.concatenate(pieces, 0)


def scatter_low(partial):
    low = lax.axis_index("seq") % split
    rows = partial.shape[0] // split

    def block(at):
        return lax.dynamic_slice_in_dim(partial, at * rows, rows, 0)

    arrived = [swap_low(low_bits(block(low ^ k)), k) for k in range(1, split)]
    return sum(a.astype(jnp.float32) for a in [block(low)] + arrived)


def sum_low(partial):
    low_partial = low_bits(partial)
    arrived = [swap_low(low_partial, k) for k in range(1, split)]
    return partial + sum(a.astype(jnp.float32) for a in arrived)


def gather_high(value):
    high_count = lax.axis_size("seq") // split
    if high_count > 4:
        return lax.all_gather(value, "seq", axis_index_groups=high_groups())
    high = lax.axis_index("seq") // split
    turned = [turn_high(value, k) for k in range(1, high_count)]
    line = turned[::-1] + [value] + turned[::-1]
    return lax.dynamic_slice_in_dim(jnp.stack(line), high_count - 1 - high, high_count, 0)


def gather_core(own):
    full = jnp.stack([own, swap_core(own)])
    return full.reshape((-1,) + own.shape[1:])


def after(value, *others):
    return lax.optimization_barrier((value,) + others)[0]


def pad_rows(value, rows):
    return jnp.pad(value, ((0, rows - value.shape[0]), (0, 0)))


def fold_core(partial, rows):
    high_count = lax.axis_size("seq") // split
    blocks = partial.reshape(2, high_count, rows, partial.shape[-1])
    arrived = swap_core(low_bits(blocks[1]))
    return low_bits(blocks[0].astype(jnp.float32) + arrived.astype(jnp.float32))


def fold_high(mine):
    high_count = lax.axis_size("seq") // split
    if high_count > 4:
        return lax.psum_scatter(
            mine.astype(jnp.float32), "seq", scatter_dimension=0, axis_index_groups=high_groups()
        )
    high = lax.axis_index("seq") // split

    def block(at):
        return lax.dynamic_index_in_dim(mine, at % high_count, 0, False)

    arrived = [turn_high(block(high + k), k) for k in range(1, high_count)]
    return sum(a.astype(jnp.float32) for a in [block(high)] + arrived)


def sum_all(partial):
    high_count = lax.axis_size("seq") // split
    total = partial + swap_core(partial)
    step = 1
    while step < high_count * split:
        total = total + swap_low(total, step)
        step *= 2
    return total


def entering_state(grow, state, reverse):
    high_count = lax.axis_size("seq") // split
    packed = jnp.concatenate([grow, state], 0)
    states = grow.shape[0]
    if high_count > 4:
        high = lax.axis_index("seq") // split
        every = lax.all_gather(packed, "seq", axis_index_groups=high_groups())

        def one(turn, total):
            source = high_count - 1 - turn if reverse else turn
            piece = lax.dynamic_index_in_dim(every, source, 0, False)
            return piece[states:] + piece[:states] * total

        ahead = high_count - 1 - high if reverse else high
        return lax.fori_loop(0, ahead, one, jnp.zeros_like(state))
    total = jnp.zeros_like(state)
    near = [from_high(packed, -k if reverse else k) for k in range(1, high_count)]
    for piece in near[::-1]:
        total = piece[states:] + piece[:states] * total
    return total


def shards_general(
    tokens,
    routes,
    lengths,
    grad_out,
    norm_gains,
    router,
    in_weight,
    conv_weight,
    x_weight,
    dt_weight,
    dt_bias,
    a_log,
    skip_gain,
    out_weight,
    expert_in,
    expert_out,
):
    channels, tap_count = conv_weight.shape
    dt_rank = dt_weight.shape[1]
    states = a_log.shape[1]
    expert_count, hidden, model_width = expert_in.shape
    own_rows = tokens.shape[0]
    row_count = own_rows * split
    high_count = lax.axis_size("seq") // split
    low = lax.axis_index("seq") % split
    high = lax.axis_index("seq") // split
    coef_count = dt_rank + 2 * states
    channel_rows = -(-channels // 16) * 16
    width = 2 * high_count * channel_rows
    hidden_rows = expert_count * hidden
    small_width = -(-(coef_count + dt_rank + tap_count + 2 + states) // lanes) * lanes

    small = jnp.concatenate(
        [x_weight, dt_weight, conv_weight, dt_bias[:, None], a_log, skip_gain[:, None]], 1
    )
    small = jnp.pad(small, ((0, 0), (0, small_width - small.shape[1])))
    inputs = tokens.astype(jnp.float32)
    edge = 16
    halo = from_high(tokens[own_rows - edge :], 1).astype(jnp.float32)
    normed_own = low_bits(norm_rows(jnp.concatenate([inputs, halo], 0), norm_gains[0]))
    payload = pad_rows(jnp.concatenate([in_weight[0], small], 1), channel_rows)
    first_full = gather_core(gather_high(payload)).reshape(width, -1)
    normed = gather_low(normed_own).reshape(split, own_rows + edge, model_width)
    normed_edge = normed[split - 1, own_rows:]
    normed = normed[:, :own_rows].reshape(row_count, model_width)
    first_in, small_full = first_full[:, :model_width], first_full[:, model_width:]
    x_full = small_full[:, :coef_count]
    at = coef_count
    dt_full = small_full[:, at : at + dt_rank]
    at = at + dt_rank
    conv_taps = small_full[:, at : at + tap_count].astype(jnp.float32)
    at = at + tap_count
    bias_vals = small_full[:, at].astype(jnp.float32)
    at = at + 1
    decay_rate = -jnp.exp(small_full[:, at : at + states].astype(jnp.float32)).T
    at = at + states
    skip_vals = small_full[:, at].astype(jnp.float32)
    rate = decay_rate * log2e

    early_part = jnp.concatenate(
        [
            pad_rows(in_weight[1], channel_rows),
            pad_rows(out_weight, channel_rows),
            expert_in[0],
        ],
        0,
    )
    early_part = gather_high(after(early_part, first_full))
    routed_part = jnp.concatenate(
        [grad_out, routes[:, None].astype(jnp.float32) * jnp.ones((1, lanes), jnp.float32)], 1
    )
    routed_part = gather_low(after(low_bits(routed_part), normed))
    grad_rows = routed_part[:, :model_width]
    routes_all = routed_part[:, model_width : model_width + 1].astype(jnp.int32)
    late_part = jnp.concatenate(
        [expert_in[1:].reshape(-1, model_width), expert_out.reshape(-1, model_width)], 0
    )

    place = high * row_count + jnp.arange(row_count, dtype=jnp.int32)
    first_len = lengths[0, 0]
    offset = jnp.where(place < first_len, place, place - first_len)
    reset = jnp.where(offset[:, None] == 0, 1e30, 0.0) * jnp.ones((1, lanes), jnp.float32)
    valid_rows = [
        (offset >= tap_count - 1 - k).astype(jnp.float32)[:, None] for k in range(tap_count)
    ]

    all_input = low_bits(matmul_nt(jnp.concatenate([normed_edge, normed], 0), first_in))
    conv_input = all_input[edge:]
    window = all_input[edge - (tap_count - 1) :].astype(jnp.float32)
    conv_sum = sum(
        conv_taps[:, k] * window[k : k + row_count] * valid_rows[k] for k in range(tap_count)
    )
    mixed_in = low_bits(jax.nn.silu(conv_sum))
    mixed_val = mixed_in.astype(jnp.float32)
    coef_pad = jnp.pad(x_full, ((0, 0), (0, lanes - coef_count)))
    coef_rows = sum_low(matmul(mixed_in, coef_pad))
    dt_low = low_bits(coef_rows[:, :dt_rank])
    dt_pre = matmul_nt(dt_low, dt_full) + bias_vals
    step_size = jax.nn.softplus(dt_pre)
    drive = step_size * mixed_val
    first_b, first_c = dt_rank, dt_rank + states
    peers = high_count - 1 if high_count <= 4 else 0
    grow, state, enter = scan_ends(
        step_size, reset, drive, coef_rows, rate, first_b, False, peers
    )
    slice_grow = grow[:, subs - 1]
    if not peers:
        enter = entering_state(slice_grow, state[:, subs - 1], False)
    enter, early_part, late_part = lax.optimization_barrier((enter, early_part, late_part))
    early_full = gather_core(early_part)
    late_part = gather_high(late_part)
    y_scan, start, hist = scan_forward(
        step_size, reset, drive, coef_rows, rate, grow, state, enter, first_b, first_c
    )
    y_scan, early_full = lax.optimization_barrier((y_scan, early_full))
    second_in = early_full[:, :channel_rows].reshape(width, model_width)
    out_full = early_full[:, channel_rows : 2 * channel_rows].reshape(width, model_width)
    z_gate = matmul_nt(normed, second_in)
    y_value = y_scan + skip_vals * mixed_val
    gate_z = jax.nn.silu(z_gate)
    gated = low_bits(y_value * gate_z)
    resid = inputs + scatter_low(matmul(gated, out_full))

    resid, late_part = lax.optimization_barrier((resid, late_part))
    late_full = gather_core(late_part)
    second_own = low_bits(norm_rows(resid, norm_gains[1]))
    second = gather_low(second_own)

    def gate_of(rows, row_routes):
        logits = matmul(rows, router)
        chosen = row_routes == jnp.arange(expert_count, dtype=jnp.int32)[None, :]
        chosen = chosen.astype(jnp.float32)
        probs = jax.nn.softmax(logits, -1)
        return logits, chosen, jnp.sum(probs * chosen, -1, keepdims=True)

    gate_rows = gate_of(second, routes_all)[2]
    routed = low_bits(gate_rows * grad_rows.astype(jnp.float32))
    parts = [(early_full[:, 2 * channel_rows :], 0)]
    parts += [(late_full, e * hidden) for e in range(2 * expert_count - 1)]
    step_rows = hidden
    if hidden % 16:
        step_rows = 2 * high_count * hidden // 4
        parts = [
            (w[:, a : a + hidden].reshape(4, step_rows, model_width), 0) for w, a in parts
        ]
    sums, hidden_grads = run_experts(
        second, routed, routed_part[:, model_width:].astype(jnp.float32), parts, step_rows
    )
    if hidden % 16:
        pieces = hidden_grads.reshape(4, 2 * expert_count, -1, hidden, model_width)
        hidden_grads = pieces.swapaxes(1, 2).reshape(-1, 2 * hidden_rows, model_width)
    hidden_mine = fold_core(hidden_grads, 2 * hidden_rows)
    sums = scatter_low(sums)
    expert_y, d_second = sums[:, :model_width], sums[:, model_width:]
    d_second, hidden_mine = lax.optimization_barrier((d_second, hidden_mine))
    cut = hidden_rows * 2 // 3
    hidden_early = fold_high(hidden_mine[:, :cut])
    hidden_mine = hidden_mine[:, cut:]
    logits, chosen, gate_own = gate_of(second_own, routes[:, None])
    mixed_out = low_bits(resid + gate_own * expert_y)
    d_gate = jnp.sum(expert_y * grad_out, -1, keepdims=True)
    _, soft_pull = jax.vjp(lambda v: jax.nn.softmax(v, -1), logits)
    d_logits = low_bits(soft_pull(chosen * d_gate)[0])
    grad_router = matmul_tn(d_logits, second_own)
    d_second = d_second + matmul_nt(d_logits, router)
    _, norm_pull_two = jax.vjp(norm_rows, resid, norm_gains[1])
    d_resid_norm, d_gain_two = norm_pull_two(d_second)
    d_resid = grad_out + d_resid_norm

    g_branch = gather_low(low_bits(d_resid))
    d_gated = matmul_nt(g_branch, out_full)
    d_y = d_gated * gate_z
    _, silu_pull = jax.vjp(jax.nn.silu, z_gate)
    d_z = silu_pull(d_gated * y_value)[0]
    gate_grads = jnp.concatenate(
        [matmul_tn(low_bits(d_z), normed), matmul_tn(gated, g_branch)], 1
    )
    gate_mine = fold_core(gate_grads, channel_rows)
    back_grow, back_state, back_enter = scan_ends(
        step_size, reset, d_y, coef_rows, rate, first_c, True, peers
    )
    if not peers:
        back_enter = entering_state(slice_grow, back_state[:, 0], True)
    back_enter, hidden_mine = lax.optimization_barrier((back_enter, hidden_mine))
    hidden_late = fold_high(hidden_mine)
    scaled_sum, in_sum, rate_sum, d_in_coef, d_out_coef = scan_backward(
        step_size,
        reset,
        drive,
        d_y,
        coef_rows,
        rate,
        start,
        hist,
        back_grow,
        back_state,
        back_enter,
        first_b,
        first_c,
    )
    d_step = scaled_sum + in_sum * mixed_val
    d_mixed = skip_vals * d_y + in_sum * step_size
    grad_skip = jnp.sum(d_y * mixed_val, 0)
    d_dt = d_step * jax.nn.sigmoid(dt_pre)
    grad_bias = jnp.sum(d_dt, 0)
    g_dt = low_bits(d_dt)
    grad_dt = matmul_tn(g_dt, dt_low)
    part_coef = jnp.concatenate([matmul(g_dt, dt_full), d_in_coef, d_out_coef], 1)
    part_coef = jnp.pad(part_coef, ((0, 0), (0, lanes - coef_count)))
    g_coef = low_bits(sum_low(part_coef)[:, :coef_count])
    grad_x = matmul_tn(mixed_in, g_coef)
    d_mixed = d_mixed + matmul_nt(g_coef, x_full)
    _, conv_pull = jax.vjp(jax.nn.silu, conv_sum)
    d_conv = conv_pull(d_mixed)[0]
    grad_conv = jnp.stack(
        [jnp.sum(d_conv * valid_rows[k] * window[k : k + row_count], 0) for k in range(tap_count)],
        1,
    )
    d_window = sum(
        jnp.pad(conv_taps[:, k] * d_conv * valid_rows[k], ((k, tap_count - 1 - k), (0, 0)))
        for k in range(tap_count)
    )
    from_next = from_high(d_window[: tap_count - 1], -1)
    d_input = d_window[tap_count - 1 :] + jnp.pad(
        from_next, ((row_count - (tap_count - 1), 0), (0, 0))
    )
    g_in = low_bits(d_input)
    g_in, hidden_late, gate_mine = lax.optimization_barrier((g_in, hidden_late, gate_mine))
    hidden_own = jnp.concatenate([hidden_early, hidden_late], 0)
    gate_own_grads = fold_high(gate_mine)
    g_z = low_bits(d_z)
    d_normed = scatter_low(matmul(g_in, first_in) + matmul(g_z, second_in))
    _, norm_pull_one = jax.vjp(norm_rows, inputs, norm_gains[0])
    d_inputs, d_gain_one = norm_pull_one(d_normed)
    grad_tokens = d_resid + d_inputs

    rest = jnp.concatenate(
        [grad_x, grad_dt, grad_conv, grad_bias[:, None], rate_sum.T, grad_skip[:, None]], 1
    )
    rest = jnp.pad(rest, ((0, 0), (0, small_width - rest.shape[1])))
    first_own = fold_high(
        fold_core(jnp.concatenate([matmul_tn(g_in, normed), rest], 1), channel_rows)
    )[:channels]
    rest_own = first_own[:, model_width:]
    gate_own_grads = gate_own_grads[:channels]
    sums = sum_all(jnp.concatenate([jnp.stack([d_gain_one, d_gain_two]), grad_router], 0))
    ends = [0]
    for count in (coef_count, dt_rank, tap_count, 1, states, 1):
        ends.append(ends[-1] + count)
    grad_x, grad_dt, grad_conv, grad_bias, grad_alog, grad_skip = (
        rest_own[:, a:b] for a, b in zip(ends[:-1], ends[1:], strict=True)
    )
    return (
        mixed_out,
        grad_tokens,
        sums[:2],
        sums[2:].T,
        jnp.stack([first_own[:, :model_width], gate_own_grads[:, :model_width]]),
        grad_conv,
        grad_x,
        grad_dt,
        grad_bias[:, 0],
        grad_alog,
        grad_skip[:, 0],
        gate_own_grads[:, model_width:],
        hidden_own[:hidden_rows].reshape(expert_count, hidden, model_width),
        hidden_own[hidden_rows:].reshape(expert_count, hidden, model_width),
    )


def shards_plane(
    tokens,
    routes,
    lengths,
    grad_out,
    norm_gains,
    router,
    in_weight,
    conv_weight,
    x_weight,
    dt_weight,
    dt_bias,
    a_log,
    skip_gain,
    out_weight,
    expert_in,
    expert_out,
):
    channels, tap_count = conv_weight.shape
    dt_rank, states = dt_weight.shape[1], a_log.shape[1]
    expert_count, hidden, _ = expert_in.shape
    coef_count = dt_rank + 2 * states
    (
        first_full, gate_full, hidden_full, normed, routed, input_all, coef, step, z, y, gated, start,
        resid, second, rows, spread_in, spread_out,
    ) = run_mixer(
        tokens, norm_gains, lengths, in_weight, conv_weight.T, x_weight, dt_weight, dt_bias[None], a_log.T,
        skip_gain[None], out_weight, expert_in, expert_out, grad_out, routes[None],
    )
    mixed_out, d_resid, small_sums, dy, gz, later, mine, early, gate_mine = run_turn(
        second, routed, hidden_full, expert_out, router.T, resid, grad_out, norm_gains, lengths,
        gate_full, normed, spread_out, step, z, y, gated, rows, states, expert_count,
    )
    grad_tokens, sums, late, gate_own, first_own = run_back(
        dy, gz, later, mine, gate_mine, first_full, gate_full, normed, input_all, coef, step, start,
        rows, d_resid, tokens, norm_gains, small_sums, lengths, spread_in, spread_out, dt_rank, states,
        tap_count,
    )
    (
        mixed_out, grad_tokens, grad_gains, grad_router, grad_in, grad_conv, grad_x, grad_dt, grad_bias,
        grad_alog, grad_skip, grad_out_w, grad_up, grad_down,
    ) = run_results(
        (mixed_out, grad_tokens, sums, early, late, gate_own, first_own),
        channels, tap_count, states, coef_count, dt_rank, expert_count, hidden,
    )
    return (
        mixed_out,
        grad_tokens,
        grad_gains,
        grad_router.T,
        grad_in,
        grad_conv.T,
        grad_x,
        grad_dt,
        grad_bias[0],
        grad_alog.T,
        grad_skip[0],
        grad_out_w,
        grad_up,
        grad_down,
    )


def solution(mesh):
    both = ("grp", "seq")
    in_specs = (
        P(both, None),
        P(both),
        P("grp", None),
        P(both, None),
        P(),
        P(),
        P(None, both, None),
        P(both, None),
        P(both, None),
        P(both, None),
        P(both),
        P(both, None),
        P(both),
        P(both, None),
        P(None, both, None),
        P(None, both, None),
    )
    out_specs = (
        P(both, None),
        P(both, None),
        P(),
        P(),
        P(None, both, None),
        P(both, None),
        P(both, None),
        P(both, None),
        P(both),
        P(both, None),
        P(both),
        P(both, None),
        P(None, both, None),
        P(None, both, None),
    )
    shards = shards_plane if mesh.shape["seq"] == split * split else shards_general
    return jax.shard_map(shards, mesh=mesh, in_specs=in_specs, out_specs=out_specs, check_vma=False)
```

```python
import functools
import math

import jax
import jax.numpy as jnp
from jax import lax
from jax.experimental import pallas as pl
from jax.experimental.pallas import tpu as pltpu
from jax.sharding import PartitionSpec as P

eps_norm = 1e-05
split = 4
lanes = 128
subs = 8
log2e = 1.4426950408889634


def spread(coef_ref, first, spread_ref, steps, states):
    def one(s, _):
        rows = coef_ref[pl.ds(s, subs, stride=steps), :]
        for n in range(states):
            spread_ref[s, n] = jnp.broadcast_to(rows[:, first + n : first + n + 1], (subs, lanes))
        return 0

    lax.fori_loop(0, steps, one, 0, unroll=8)


def chain_rows(grow, state, reverse):
    row = lax.broadcasted_iota(jnp.int32, (subs, lanes), 0)
    shift = 1
    while shift < subs:
        turn = subs - shift if reverse else shift
        has = row < subs - shift if reverse else row >= shift
        near_grow = jnp.where(has, pltpu.roll(grow, turn, 0), 1.0)
        near_state = jnp.where(has, pltpu.roll(state, turn, 0), 0.0)
        state = state + grow * near_state
        grow = grow * near_grow
        shift *= 2
    return grow, state


def ends_kernel(
    first, reverse, states, steps, peers,
    delta_ref, reset_ref, drive_ref, coef_ref, rate_ref,
    grow_ref, state_ref, enter_ref,
    spread_ref, send_ref, arrive_ref, send_sem, arrive_sem,
):
    tile = pl.program_id(0)
    tiles = pl.num_programs(0)
    place = lax.axis_index("seq")
    high, low, core = place // split, place % split, lax.axis_index("grp")

    def other(k):
        return (core, lax.rem(high + (peers + 1 - k if reverse else k), peers + 1) * split + low)

    def copy_to(k, j):
        return pltpu.make_async_remote_copy(
            src_ref=send_ref.at[j],
            dst_ref=arrive_ref.at[k - 1, j],
            send_sem=send_sem.at[k - 1, j],
            recv_sem=arrive_sem.at[k - 1, j],
            device_id=other(k),
            device_id_type=pl.DeviceIdType.MESH,
        )

    @pl.when(tile == 0)
    def _():
        if peers:
            barrier = pltpu.get_barrier_semaphore()
            for k in range(1, peers + 1):
                pl.semaphore_signal(
                    barrier, inc=1, device_id=other(k), device_id_type=pl.DeviceIdType.MESH
                )
        spread(coef_ref, first, spread_ref, steps, states)

    rates = [jnp.broadcast_to(rate_ref[n : n + 1, :], (subs, lanes)) for n in range(states)]

    def one(turn, carry):
        s = steps - 1 - turn if reverse else turn
        total, held = carry
        step = delta_ref[pl.ds(s, subs, stride=steps), :] + reset_ref[pl.ds(s, subs, stride=steps), :]
        drive = drive_ref[pl.ds(s, subs, stride=steps), :]
        after = []
        for n in range(states):
            factor = jnp.exp2(step * rates[n])
            if reverse:
                after.append(factor * (held[n] + spread_ref[s, n] * drive))
            else:
                after.append(factor * held[n] + spread_ref[s, n] * drive)
        return total + step, tuple(after)

    zero = jnp.zeros((subs, lanes), jnp.float32)
    total, held = lax.fori_loop(0, steps, one, (zero, (zero,) * states), unroll=2)
    last = 0 if reverse else subs - 1
    for n in range(states):
        grow, state = chain_rows(jnp.exp2(total * rates[n]), held[n], reverse)
        grow_ref[n] = grow
        state_ref[n] = state
        if peers:
            send_ref[tile, n : n + 1] = grow[last : last + 1]
            send_ref[tile, states + n : states + n + 1] = state[last : last + 1]
    if not peers:
        enter_ref[...] = jnp.zeros_like(enter_ref)
        return

    @pl.when(tile == 0)
    def _():
        pl.semaphore_wait(pltpu.get_barrier_semaphore(), peers)

    for k in range(1, peers + 1):
        copy_to(k, tile).start()

    @pl.when(tile == tiles - 1)
    def _():
        for j in range(enter_ref.shape[1] // lanes):
            total = jnp.zeros((states, lanes), jnp.float32)
            for k in range(peers, 0, -1):
                copy_to(k, j).wait()
                piece = arrive_ref[k - 1, j]
                has = high + k <= peers if reverse else high >= k
                total = jnp.where(has, piece[states:] + piece[:states] * total, 0.0)
            enter_ref[:, j * lanes : (j + 1) * lanes] = total


def scan_ends(delta, reset, drive, coef, rate, first, reverse, peers):
    row_count, width = delta.shape
    states = rate.shape[0]
    steps = row_count // subs
    tiles = width // lanes
    column = pl.BlockSpec((row_count, lanes), lambda j: (0, j))
    whole = pl.BlockSpec((row_count, lanes), lambda j: (0, 0))
    ends = pl.BlockSpec((states, subs, lanes), lambda j: (0, 0, j))
    params = dict(vmem_limit_bytes=48 << 20)
    if peers:
        params.update(collective_id=2 if reverse else 1, has_side_effects=True)
    slots = max(peers, 1)
    return pl.pallas_call(
        functools.partial(ends_kernel, first, reverse, states, steps, peers),
        grid=(tiles,),
        in_specs=[column, whole, column, whole, pl.BlockSpec((states, lanes), lambda j: (0, j))],
        out_specs=[ends, ends, pl.BlockSpec((states, width), lambda j: (0, 0))],
        out_shape=[jax.ShapeDtypeStruct((states, subs, width), jnp.float32)] * 2
        + [jax.ShapeDtypeStruct((states, width), jnp.float32)],
        scratch_shapes=[
            pltpu.VMEM((steps, states, subs, lanes), jnp.float32),
            pltpu.VMEM((tiles, 2 * states, lanes), jnp.float32),
            pltpu.VMEM((slots, tiles, 2 * states, lanes), jnp.float32),
            pltpu.SemaphoreType.DMA((slots, tiles)),
            pltpu.SemaphoreType.DMA((slots, tiles)),
        ],
        compiler_params=pltpu.CompilerParams(**params),
        cost_estimate=pl.CostEstimate(flops=1000, bytes_accessed=1000, transcendentals=0),
    )(delta, reset, drive, coef, rate)


def forward_kernel(first_in, first_out, states, steps, delta_ref, reset_ref, drive_ref, coef_ref, rate_ref, grow_ref, state_ref, enter_ref, y_ref, start_ref, hist_ref, in_ref, out_ref):
    @pl.when(pl.program_id(0) == 0)
    def _():
        spread(coef_ref, first_in, in_ref, steps, states)
        spread(coef_ref, first_out, out_ref, steps, states)

    rates = [jnp.broadcast_to(rate_ref[n : n + 1, :], (subs, lanes)) for n in range(states)]
    row = lax.broadcasted_iota(jnp.int32, (subs, lanes), 0)
    held = []
    for n in range(states):
        near_grow = jnp.where(row >= 1, pltpu.roll(grow_ref[n], 1, 0), 1.0)
        near_state = jnp.where(row >= 1, pltpu.roll(state_ref[n], 1, 0), 0.0)
        start = near_state + near_grow * jnp.broadcast_to(enter_ref[n : n + 1, :], (subs, lanes))
        start_ref[n] = start
        held.append(start)

    def one(s, held):
        step = delta_ref[pl.ds(s, subs, stride=steps), :] + reset_ref[pl.ds(s, subs, stride=steps), :]
        drive = drive_ref[pl.ds(s, subs, stride=steps), :]
        after = []
        y = jnp.zeros((subs, lanes), jnp.float32)
        for n in range(states):
            now = jnp.exp2(step * rates[n]) * held[n] + in_ref[s, n] * drive
            hist_ref[0, s, n] = now
            y = y + out_ref[s, n] * now
            after.append(now)
        y_ref[pl.ds(s, subs, stride=steps), :] = y
        return tuple(after)

    lax.fori_loop(0, steps, one, tuple(held), unroll=2)


def scan_forward(delta, reset, drive, coef, rate, grow, state, enter, first_in, first_out):
    row_count, width = delta.shape
    states = rate.shape[0]
    steps = row_count // subs
    tiles = width // lanes
    column = pl.BlockSpec((row_count, lanes), lambda j: (0, j))
    whole = pl.BlockSpec((row_count, lanes), lambda j: (0, 0))
    ends = pl.BlockSpec((states, subs, lanes), lambda j: (0, 0, j))
    per_state = pl.BlockSpec((states, lanes), lambda j: (0, j))
    return pl.pallas_call(
        functools.partial(forward_kernel, first_in, first_out, states, steps),
        grid=(tiles,),
        in_specs=[column, whole, column, whole, per_state, ends, ends, per_state],
        out_specs=[column, ends, pl.BlockSpec((1, steps, states, subs, lanes), lambda j: (j, 0, 0, 0, 0))],
        out_shape=[
            jax.ShapeDtypeStruct((row_count, width), jnp.float32),
            jax.ShapeDtypeStruct((states, subs, width), jnp.float32),
            jax.ShapeDtypeStruct((tiles, steps, states, subs, lanes), jnp.float32),
        ],
        scratch_shapes=[pltpu.VMEM((steps, states, subs, lanes), jnp.float32)] * 2,
        compiler_params=pltpu.CompilerParams(vmem_limit_bytes=48 << 20),
        cost_estimate=pl.CostEstimate(flops=1000, bytes_accessed=1000, transcendentals=0),
    )(delta, reset, drive, coef, rate, grow, state, enter)


def backward_kernel(first_in, first_out, states, steps, delta_ref, reset_ref, drive_ref, dy_ref, coef_ref, rate_ref, start_ref, hist_ref, grow_ref, state_ref, enter_ref, q_ref, r_ref, rsum_ref, din_ref, dout_ref, in_ref, out_ref, ain_ref, aout_ref):
    tile = pl.program_id(0)

    @pl.when(tile == 0)
    def _():
        spread(coef_ref, first_in, in_ref, steps, states)
        spread(coef_ref, first_out, out_ref, steps, states)
        ain_ref[...] = jnp.zeros_like(ain_ref)
        aout_ref[...] = jnp.zeros_like(aout_ref)

    row = lax.broadcasted_iota(jnp.int32, (subs, lanes), 0)
    rates = [jnp.broadcast_to(rate_ref[n : n + 1, :], (subs, lanes)) for n in range(states)]
    later = []
    for n in range(states):
        near_grow = jnp.where(row < subs - 1, pltpu.roll(grow_ref[n], subs - 1, 0), 1.0)
        near_state = jnp.where(row < subs - 1, pltpu.roll(state_ref[n], subs - 1, 0), 0.0)
        later.append(near_state + near_grow * jnp.broadcast_to(enter_ref[n : n + 1, :], (subs, lanes)))

    def at(s, load_before, carry):
        later, sums = carry
        delta = delta_ref[pl.ds(s, subs, stride=steps), :]
        step = delta + reset_ref[pl.ds(s, subs, stride=steps), :]
        drive = drive_ref[pl.ds(s, subs, stride=steps), :]
        dy = dy_ref[pl.ds(s, subs, stride=steps), :]
        q = jnp.zeros((subs, lanes), jnp.float32)
        r = jnp.zeros((subs, lanes), jnp.float32)
        after, sums_after = [], []
        for n in range(states):
            d_state = out_ref[s, n] * dy + later[n]
            back = jnp.exp2(step * rates[n]) * d_state
            scaled = back * load_before(n)
            sums_after.append(sums[n] + scaled * delta)
            q = q + scaled * rates[n]
            r = r + d_state * in_ref[s, n]
            ain_ref[s, n] += d_state * drive
            aout_ref[s, n] += hist_ref[0, s, n] * dy
            after.append(back)
        q_ref[pl.ds(s, subs, stride=steps), :] = q * (1.0 / log2e)
        r_ref[pl.ds(s, subs, stride=steps), :] = r
        return tuple(after), tuple(sums_after)

    zero = jnp.zeros((subs, lanes), jnp.float32)

    def one(turn, carry):
        s = steps - 1 - turn
        return at(s, lambda n: hist_ref[0, s - 1, n], carry)

    carry = lax.fori_loop(0, steps - 1, one, (tuple(later), (zero,) * states))
    _, sums = at(0, lambda n: start_ref[n], carry)
    for n in range(states):
        rsum_ref[n : n + 1, :] = jnp.sum(sums[n] * rates[n], 0, keepdims=True) * (1.0 / log2e)

    @pl.when(tile == pl.num_programs(0) - 1)
    def _():
        ones = jnp.ones((subs, lanes), jnp.bfloat16)

        def fold(ref, s):
            values = ref[s].reshape(states * subs, lanes)
            high = values.astype(jnp.bfloat16)
            low = (values - high.astype(jnp.float32)).astype(jnp.bfloat16)
            dims = (((1,), (1,)), ((), ()))
            return lax.dot_general(ones, high, dims, preferred_element_type=jnp.float32) + lax.dot_general(ones, low, dims, preferred_element_type=jnp.float32)

        def both(s, _):
            din_ref[pl.ds(s, 1), :] = fold(ain_ref, s)[:1]
            dout_ref[pl.ds(s, 1), :] = fold(aout_ref, s)[:1]
            return 0

        lax.fori_loop(0, steps, both, 0)


def scan_backward(delta, reset, drive, dy, coef, rate, start, hist, grow, state, enter, first_in, first_out):
    row_count, width = delta.shape
    states = rate.shape[0]
    steps = row_count // subs
    tiles = width // lanes
    column = pl.BlockSpec((row_count, lanes), lambda j: (0, j))
    whole = pl.BlockSpec((row_count, lanes), lambda j: (0, 0))
    ends = pl.BlockSpec((states, subs, lanes), lambda j: (0, 0, j))
    per_state = pl.BlockSpec((states, lanes), lambda j: (0, j))
    folded = pl.BlockSpec((steps, states * subs), lambda j: (0, 0))
    q, r, rsum, din, dout = pl.pallas_call(
        functools.partial(backward_kernel, first_in, first_out, states, steps),
        grid=(tiles,),
        in_specs=[column, whole, column, column, whole, per_state, ends, pl.BlockSpec((1, steps, states, subs, lanes), lambda j: (j, 0, 0, 0, 0)), ends, ends, per_state],
        out_specs=[column, column, per_state, folded, folded],
        out_shape=[
            jax.ShapeDtypeStruct((row_count, width), jnp.float32),
            jax.ShapeDtypeStruct((row_count, width), jnp.float32),
            jax.ShapeDtypeStruct((states, width), jnp.float32),
            jax.ShapeDtypeStruct((steps, states * subs), jnp.float32),
            jax.ShapeDtypeStruct((steps, states * subs), jnp.float32),
        ],
        scratch_shapes=[pltpu.VMEM((steps, states, subs, lanes), jnp.float32)] * 4,
        compiler_params=pltpu.CompilerParams(vmem_limit_bytes=56 << 20),
        cost_estimate=pl.CostEstimate(flops=1000, bytes_accessed=1000, transcendentals=0),
    )(delta, reset, drive, dy, coef, rate, start, hist, grow, state, enter)

    def unfold(folded_rows):
        return folded_rows.reshape(steps, states, subs).transpose(2, 0, 1).reshape(row_count, states)

    return q, r, rsum, unfold(din), unfold(dout)


def experts_kernel(
    expert_count, second_ref, routed_ref, route_ref, *refs
):
    weights_in, weights_out = refs[:expert_count], refs[expert_count : 2 * expert_count]
    sums_ref, grads_ref, y_ref, d_ref = refs[2 * expert_count :]
    step = pl.program_id(0)
    blocks, hidden, model_width = weights_in[0].shape
    rows = blocks * hidden

    @pl.when(step == 0)
    def _():
        y_ref[...] = jnp.zeros_like(y_ref)
        d_ref[...] = jnp.zeros_like(d_ref)

    up = jnp.concatenate([w[...].reshape(rows, model_width) for w in weights_in], 0)
    down = jnp.concatenate([w[...].reshape(rows, model_width) for w in weights_out], 0)
    second, routed = second_ref[...], routed_ref[...]
    pre = matmul_nt(second, up)
    column = lax.broadcasted_iota(jnp.int32, (1, expert_count * rows), 1)
    owner = jnp.zeros_like(column)
    for e in range(1, expert_count):
        owner = owner + (column >= e * rows).astype(jnp.int32)
    picked = route_ref[:, :1] == owner.astype(jnp.float32)
    half = 0.5 + 0.5 * lax.erf(pre * (0.5**0.5))
    bell = jnp.exp(-0.5 * pre * pre) * (1.0 / (2.0 * math.pi) ** 0.5)
    act = low_bits(jnp.where(picked, pre * half, 0.0))
    d_pre = low_bits(jnp.where(picked, matmul_nt(routed, down) * (half + pre * bell), 0.0))
    y_ref[...] += matmul(act, down)
    d_ref[...] += matmul(d_pre, up)
    grad_up = low_bits(matmul_tn(d_pre, second))
    grad_down = low_bits(matmul_tn(act, routed))
    for e in range(expert_count):
        for b in range(blocks):
            at = e * rows + b * hidden
            grads_ref[b, e * hidden : (e + 1) * hidden] = grad_up[at : at + hidden]
            to = (expert_count + e) * hidden
            grads_ref[b, to : to + hidden] = grad_down[at : at + hidden]

    @pl.when(step == pl.num_programs(0) - 1)
    def _():
        sums_ref[:, :model_width] = low_bits(y_ref[...])
        sums_ref[:, model_width:] = low_bits(d_ref[...])


def run_experts(second, routed, route_lanes, parts, hidden):
    row_count, model_width = second.shape
    expert_count = len(parts) // 2
    block_count = parts[0][0].shape[0]
    blocks = 2
    fixed = pl.BlockSpec((row_count, model_width), lambda i: (0, 0))

    def spec(first):
        return pl.BlockSpec((blocks, hidden, model_width), lambda i: (i, first // hidden, 0))

    return pl.pallas_call(
        functools.partial(experts_kernel, expert_count),
        grid=(block_count // blocks,),
        in_specs=[fixed, fixed, pl.BlockSpec((row_count, lanes), lambda i: (0, 0))]
        + [spec(first) for _, first in parts],
        out_specs=[
            pl.BlockSpec((row_count, 2 * model_width), lambda i: (0, 0)),
            pl.BlockSpec((blocks, 2 * expert_count * hidden, model_width), lambda i: (i, 0, 0)),
        ],
        out_shape=[
            jax.ShapeDtypeStruct((row_count, 2 * model_width), jnp.bfloat16),
            jax.ShapeDtypeStruct(
                (block_count, 2 * expert_count * hidden, model_width), jnp.bfloat16
            ),
        ],
        scratch_shapes=[pltpu.VMEM((row_count, model_width), jnp.float32)] * 2,
        compiler_params=pltpu.CompilerParams(vmem_limit_bytes=56 << 20),
        cost_estimate=pl.CostEstimate(flops=1000, bytes_accessed=1000, transcendentals=0),
    )(second, routed, route_lanes, *[w for w, _ in parts])


def kernel_place():
    place = lax.axis_index("seq")
    return lax.axis_index("grp"), place // split, place % split


def remote(src, dst, send_sem, arrive_sem, core, high, low):
    return pltpu.make_async_remote_copy(
        src_ref=src,
        dst_ref=dst,
        send_sem=send_sem,
        recv_sem=arrive_sem,
        device_id=(core, high * split + low),
        device_id_type=pl.DeviceIdType.MESH,
    )


def greet_all():
    core, high, low = kernel_place()
    barrier = pltpu.get_barrier_semaphore()
    others = [(core, lax.rem(high + k, split), low) for k in range(1, split)]
    others += [(core, high, lax.rem(low + k, split)) for k in range(1, split)]
    others += [(1 - core, high, low)]
    for c, h, l in others:
        pl.semaphore_signal(
            barrier, inc=1, device_id=(c, h * split + l), device_id_type=pl.DeviceIdType.MESH
        )
    return len(others)


def plane_copies(src_of, dst, sems, slot_by_sender):
    core, high, low = kernel_place()
    copies = []
    for k in range(1, split):
        to = lax.rem(low + k, split)
        slot = low if slot_by_sender else k - 1
        copies.append(
            remote(src_of(to, k), dst.at[slot], sems.at[0, k - 1], sems.at[1, k - 1], core, high, to)
        )
    return copies


def at_ends():
    _, high, _ = kernel_place()
    return (high == 0) | (high == split - 1)


def line_copies(src, dst_of, sems, both=False):
    core, high, low = kernel_place()
    return [
        remote(
            src, dst_of(high), sems.at[0, k - 1], sems.at[1, k - 1], core, lax.rem(high + k, split), low
        )
        for k in ((1, 2, 3) if both else (1, 3))
    ]


def line_relay(dst_of, sems):
    core, high, low = kernel_place()
    block = lax.rem(high * 2, 3) + 3 * (high // 3)
    to = lax.rem(block + 2, split)
    return remote(dst_of(block), dst_of(block), sems.at[0, 1], sems.at[1, 1], core, to, low)


def line_arrived(src, dst_of, sems, k):
    core, high, low = kernel_place()
    at = lax.rem(high + split - k, split)
    remote(src, dst_of(at), sems.at[0, k - 1], sems.at[1, k - 1], core, high, low).wait_recv()


def core_copy(dst_of, sems, k):
    core, high, low = kernel_place()
    at = lax.rem(high + split - k, split)
    return remote(dst_of(at), dst_of(split + at), sems.at[0, k], sems.at[1, k], 1 - core, high, low)


def softplus_of(value):
    return jnp.maximum(value, 0.0) + jnp.log1p(jnp.exp(-jnp.abs(value)))


def sigmoid_of(value):
    return 1.0 / (1.0 + jnp.exp(-value))


def row_loop(count, size, body):
    def one(i, _):
        body(pl.multiple_of(i * size, size))
        return 0

    lax.fori_loop(0, count // size, one, 0)


def step_rows(s):
    return pl.ds(pl.multiple_of(s * subs, subs), subs)


def scan_one_way(j, reverse, states, steps, step_ref, drive_of, spread_ref, rates):
    def one(turn, carry):
        s = steps - 1 - turn if reverse else turn
        total, held = carry
        step = step_ref[j, step_rows(s), :]
        drive = drive_of(s)
        after_step = []
        for n in range(states):
            factor = jnp.exp2(step * rates[n])
            if reverse:
                after_step.append(factor * (held[n] + spread_ref[s, n] * drive))
            else:
                after_step.append(factor * held[n] + spread_ref[s, n] * drive)
        return total + step, tuple(after_step)

    zero = jnp.zeros((subs, lanes), jnp.float32)
    total, held = lax.fori_loop(0, steps, one, (zero, (zero,) * states), unroll=2)
    return [chain_rows(jnp.exp2(total * rates[n]), held[n], reverse) for n in range(states)]


def chain_enter(arrive_ref, j, states, reverse):
    _, high, _ = kernel_place()
    total = jnp.zeros((states, lanes), jnp.float32)
    for k in range(split - 1, 0, -1):
        piece = arrive_ref[k - 1, j]
        has = high + k < split if reverse else high >= k
        total = jnp.where(has, piece[states:] + piece[:states] * total, 0.0)
    return total


def tile_rates(rows_ref, j, states):
    decay = -jnp.exp(rows_ref[j, alog_row : alog_row + states, :])
    return decay


def ends_copies(send_ref, arrive_ref, sems, j, reverse):
    core, high, low = kernel_place()
    copies = []
    for k in range(1, split):
        to = lax.rem(high + split - k, split) if reverse else lax.rem(high + k, split)
        copies.append(
            remote(
                send_ref.at[j],
                arrive_ref.at[k - 1, j],
                sems.at[0, k - 1, j],
                sems.at[1, k - 1, j],
                core,
                to,
                low,
            )
        )
    return copies


alog_row = 8
bias_row = 4
skip_row = 5
early_hidden = 64


def mixer_kernel(
    dt_rank, states, tap_count,
    tokens_ref, gains_ref, lengths_ref, in_weight_ref, conv_weight_ref, x_weight_ref, dt_weight_ref,
    dt_bias_ref, a_log_ref, skip_ref, out_weight_ref, expert_in_ref, expert_out_ref, grad_ref,
    routes_ref,
    first_out, gate_out, hidden_ref, normed_out, routed_out, input_out, coef_out, step_out, z_out,
    y_out, gated_out, start_out, resid_ref, second_out, rows_out, in_out, out_out, drive_out,
    first_ref, gate_ref, normed_ref, edge_ref, routed_ref, input_ref, coef_ref, step_ref, z_ref,
    y_ref, gated_ref, start_ref, second_ref, rows_ref, c_ref, out_sems,
    in_ref, out_ref, drive_ref, mixed_ref, partial_ref, arrive_ref, coef_send_ref,
    coef_arrive_ref, send_ref, ends_ref, grow_ref, state_ref,
    a_sems, b_sems, c_sems, d_sems, a_core, b_core, c_core, d_core, token_sems, route_sems,
    second_sems, coef_sems, sum_sems, edge_send, edge_arrive, ends_sems, local_sem,
):
    core, high, low = kernel_place()
    own_rows, model_width = tokens_ref.shape
    row_count = own_rows * split
    steps = row_count // subs
    tiles = step_ref.shape[0]
    width = tiles * lanes
    edge = edge_ref.shape[0]
    first_b, first_c = dt_rank, dt_rank + states
    channels = in_weight_ref.shape[1]
    channel_rows = width // (2 * split)
    greeted = greet_all()
    stores = []

    def store(ref, out):
        copy = pltpu.make_async_copy(ref, out, out_sems.at[len(stores)])
        copy.start()
        stores.append(copy)

    def edge_copy(l):
        return remote(
            normed_ref.at[low, pl.ds(own_rows - edge, edge)],
            edge_ref,
            edge_send.at[l],
            edge_arrive,
            core,
            lax.rem(high + 1, split),
            l,
        )

    barrier = pltpu.get_barrier_semaphore()
    for k in range(1, split):
        pl.semaphore_signal(
            barrier,
            inc=1,
            device_id=(core, lax.rem(high + split - 1, split) * split + lax.rem(low + k, split)),
            device_id_type=pl.DeviceIdType.MESH,
        )
    greeted += split - 1
    tokens = tokens_ref[...].astype(jnp.float32)
    normed_ref[low] = low_bits(norm_rows(tokens, gains_ref[0:1, :]))
    gap = channel_rows - channels

    def filled(value):
        value = value.astype(jnp.float32)
        if gap:
            value = jnp.concatenate([value, jnp.zeros((gap, value.shape[1]), jnp.float32)], 0)
        return low_bits(value)

    def widened(value, first):
        at = lax.broadcasted_iota(jnp.int32, (value.shape[1], lanes), 0) + first
        to = lax.broadcasted_iota(jnp.int32, (value.shape[1], lanes), 1)
        return matmul(value, jnp.where(at == to, 1.0, 0.0).astype(jnp.bfloat16))

    first_ref[high, :, :model_width] = filled(in_weight_ref[0])
    first_ref[high, :, model_width : model_width + lanes] = filled(widened(x_weight_ref[...], 0))
    first_ref[high, :, model_width + lanes : model_width + 2 * lanes] = filled(
        widened(dt_weight_ref[...], 0)
    )
    rows_ref[0] = jnp.zeros((lanes, lanes), jnp.float32)
    for row, ref in (
        (0, conv_weight_ref), (bias_row, dt_bias_ref), (skip_row, skip_ref), (alog_row, a_log_ref)
    ):
        rows_ref[0, row : row + ref.shape[0], :channels] = ref[...].astype(jnp.float32)
    first_ref[high, :, model_width + 2 * lanes :] = filled(rows_ref[0].T[:channels])
    pl.semaphore_wait(barrier, greeted)

    @pl.when((low == split - 1) & (high < split - 1))
    def _():
        for l in range(split):
            edge_copy(l).start()

    hidden_count = c_ref.shape[0]
    c_src = c_ref.at[pl.ds(0, early_hidden)]
    d_src = c_ref.at[pl.ds(early_hidden, hidden_count - early_hidden)]
    a_ref, b_ref, g_ref = first_ref.at[high], gate_ref.at[high], routed_ref.at[low]

    def a_dst(at):
        return first_ref.at[at]

    def b_dst(at):
        return gate_ref.at[at]

    def c_dst(at):
        return hidden_ref.at[at, pl.ds(0, early_hidden)]

    def d_dst(at):
        return hidden_ref.at[at, pl.ds(early_hidden, hidden_count - early_hidden)]

    token_copies = plane_copies(lambda to, k: normed_ref.at[low], normed_ref, token_sems, True)
    a_copies = line_copies(a_ref, a_dst, a_sems)
    b_copies = line_copies(b_ref, b_dst, b_sems)
    c_copies = line_copies(c_src, c_dst, c_sems)
    d_copies = line_copies(d_src, d_dst, d_sems)
    route_copies = plane_copies(lambda to, k: g_ref, routed_ref, route_sems, True)
    relays = [line_relay(a_dst, a_sems), line_relay(b_dst, b_sems)]
    relays += [line_relay(c_dst, c_sems), line_relay(d_dst, d_sems)]
    for copy in token_copies + a_copies:
        copy.start()

    def relay_from_end(i):
        @pl.when(at_ends())
        def _():
            relays[i].start()

    def relay_inside(i):
        @pl.when(jnp.logical_not(at_ends()))
        def _():
            relays[i].start()

    def arrived(src, dst_of, sems, core_sems, ks):
        for k in ks:
            line_arrived(src, dst_of, sems, k)
            copy = core_copy(dst_of, core_sems, k)
            copy.start()
            core_copies.append(copy)

    relay_from_end(0)
    core_copies = [core_copy(a_dst, a_core, 0)]
    core_copies[0].start()
    routed_ref[low, :, :model_width] = low_bits(grad_ref[...])
    routes = jnp.broadcast_to(routes_ref[...].astype(jnp.float32), (own_rows, own_rows)).T
    routed_ref[low, :, model_width:] = low_bits(routes)
    gate_ref[high, :channel_rows] = filled(in_weight_ref[1])
    gate_ref[high, channel_rows:] = filled(out_weight_ref[...])
    hidden = expert_in_ref.shape[1]
    for part in range(hidden_count // hidden):
        source = expert_out_ref if part % 2 else expert_in_ref
        c_ref[part * hidden : (part + 1) * hidden] = source[part // 2]
    local = pltpu.make_async_copy(c_ref, hidden_ref.at[high], local_sem)
    local.start()
    core_copies.append(core_copy(b_dst, b_core, 0))
    for copy in core_copies[1:] + route_copies:
        copy.start()

    first_len = lengths_ref[0, 0]

    def offsets(at, rows):
        place = high * row_count + at + lax.broadcasted_iota(jnp.int32, (rows, lanes), 0)
        return jnp.where(place < first_len, place, place - first_len)

    @pl.when(high == 0)
    def _():
        edge_ref[...] = jnp.zeros_like(edge_ref)

    arrived(a_ref, a_dst, a_sems, a_core, (1, 3))
    relay_inside(0)
    for copy in b_copies + c_copies:
        copy.start()
    local.wait()
    relay_from_end(1)
    relay_from_end(2)
    for copy in (core_copy(c_dst, c_core, 0), core_copy(d_dst, d_core, 0)):
        copy.start()
        core_copies.append(copy)
    for copy in token_copies:
        copy.wait()
    arrived(a_ref, a_dst, a_sems, a_core, (2,))

    @pl.when(high > 0)
    def _():
        edge_copy(0).wait_recv()

    @pl.when((low == split - 1) & (high < split - 1))
    def _():
        for l in range(split):
            edge_copy(l).wait_send()

    for k in range(split):
        core_copy(a_dst, a_core, k).wait_recv()

    weights = first_ref[:, :, :model_width].reshape(width, model_width)
    input_ref[:edge, :] = low_bits(matmul_nt(edge_ref[...], weights)).astype(jnp.float32)
    for l in range(split):
        block = low_bits(matmul_nt(normed_ref[l], weights)).astype(jnp.float32)
        input_ref[edge + l * own_rows : edge + (l + 1) * own_rows, :] = block
    store(first_ref, first_out)
    store(normed_ref, normed_out)
    store(input_ref, input_out)
    small = first_ref[:, :, model_width + 2 * lanes :].reshape(width, lanes).astype(jnp.float32)
    for j in range(tiles):
        rows_ref[j] = small[j * lanes : (j + 1) * lanes].T

    store(rows_ref, rows_out)

    def convolve(at):
        offset = offsets(at, 32)
        for j in range(tiles):
            span = input_ref[pl.ds(at, 32 + edge), j * lanes : (j + 1) * lanes]
            conv_sum = jnp.zeros((32, lanes), jnp.float32)
            for k in range(tap_count):
                shift = edge - (tap_count - 1) + k
                term = rows_ref[j, k : k + 1, :] * span[shift : shift + 32]
                conv_sum = conv_sum + jnp.where(offset >= tap_count - 1 - k, term, 0.0)
            mixed_ref[pl.ds(at, 32), j * lanes : (j + 1) * lanes] = low_bits(
                conv_sum * sigmoid_of(conv_sum)
            )

    row_loop(row_count, 32, convolve)

    x_full = first_ref[:, :, model_width : model_width + lanes].reshape(width, lanes)
    part = matmul(mixed_ref[...], x_full)
    coef_ref[...] = part
    coef_send_ref[...] = low_bits(part)
    coef_copies = plane_copies(lambda to, k: coef_send_ref, coef_arrive_ref, coef_sems, False)
    for copy in coef_copies:
        copy.start()
    for copy in coef_copies:
        copy.wait()
    arrived(b_ref, b_dst, b_sems, b_core, (1, 3))
    relay_inside(1)
    total = coef_ref[...]
    for k in range(1, split):
        total = total + coef_arrive_ref[k - 1].astype(jnp.float32)
    coef_ref[...] = total
    dt_full = first_ref[:, :, model_width + lanes : model_width + 2 * lanes].reshape(width, lanes)

    def step_sizes(chunk):
        at = pl.multiple_of(chunk * steps, steps)
        pre = matmul_nt(low_bits(coef_ref[pl.ds(at, steps), :]), dt_full)
        reset = jnp.where(offsets(at, steps) == 0, 1e30, 0.0)
        rows = pl.ds(chunk, steps, stride=subs)
        for j in range(tiles):
            cols = slice(j * lanes, (j + 1) * lanes)
            step = softplus_of(pre[:, cols] + rows_ref[j, bias_row : bias_row + 1, :])
            step_ref[j, rows, :] = step + reset
            drive_ref[j, rows, :] = step * mixed_ref[pl.ds(at, steps), cols].astype(jnp.float32)

    lax.fori_loop(0, subs, lambda chunk, _: (step_sizes(chunk), 0)[1], 0)
    store(drive_ref, drive_out)
    store(coef_ref, coef_out)
    store(step_ref, step_out)
    spread(coef_ref, first_b, in_ref, steps, states)
    store(in_ref, in_out)

    def rates_of(j):
        values = -jnp.exp(rows_ref[j, alog_row : alog_row + states, :]) * log2e
        return [jnp.broadcast_to(values[n : n + 1, :], (subs, lanes)) for n in range(states)]

    def ends_of(j, _):
        found = scan_one_way(
            j,
            False,
            states,
            steps,
            step_ref,
            lambda s: drive_ref[j, step_rows(s), :],
            in_ref,
            rates_of(j),
        )
        for n, (grow, state) in enumerate(found):
            grow_ref[j, n] = grow
            state_ref[j, n] = state
            send_ref[j, n : n + 1] = grow[subs - 1 :]
            send_ref[j, states + n : states + n + 1] = state[subs - 1 :]
        for copy in ends_copies(send_ref, ends_ref, ends_sems, j, False):
            copy.start()
        return 0

    lax.fori_loop(0, tiles, ends_of, 0)
    arrived(c_src, c_dst, c_sems, c_core, (1, 3))
    relay_inside(2)
    for copy in d_copies:
        copy.start()
    relay_from_end(3)
    spread(coef_ref, first_c, out_ref, steps, states)
    store(out_ref, out_out)
    arrived(b_ref, b_dst, b_sems, b_core, (2,))
    row = lax.broadcasted_iota(jnp.int32, (subs, lanes), 0)

    def forward_of(j, _):
        for copy in ends_copies(send_ref, ends_ref, ends_sems, j, False):
            copy.wait()
        enter = chain_enter(ends_ref, j, states, False)
        rates = rates_of(j)
        held = []
        for n in range(states):
            near_grow = jnp.where(row >= 1, pltpu.roll(grow_ref[j, n], 1, 0), 1.0)
            near_state = jnp.where(row >= 1, pltpu.roll(state_ref[j, n], 1, 0), 0.0)
            start = near_state + near_grow * jnp.broadcast_to(enter[n : n + 1, :], (subs, lanes))
            start_ref[j, n] = start
            held.append(start)

        def one(s, held):
            step = step_ref[j, step_rows(s), :]
            drive = drive_ref[j, step_rows(s), :]
            now_all = []
            y = jnp.zeros((subs, lanes), jnp.float32)
            for n in range(states):
                now = jnp.exp2(step * rates[n]) * held[n] + in_ref[s, n] * drive
                y = y + out_ref[s, n] * now
                now_all.append(now)
            y_ref[j, pl.ds(s, subs, stride=steps), :] = y
            return tuple(now_all)

        lax.fori_loop(0, steps, one, tuple(held), unroll=2)
        return 0

    lax.fori_loop(0, tiles, forward_of, 0)

    for k in range(split):
        core_copy(b_dst, b_core, k).wait_recv()
    store(gate_ref, gate_out)
    store(start_ref, start_out)
    second_in = gate_ref[:, :channel_rows].reshape(width, model_width)
    for l in range(split):
        z_block = matmul_nt(normed_ref[l], second_in)
        rows = slice(l * own_rows, (l + 1) * own_rows)
        for j in range(tiles):
            z_ref[j, rows, :] = z_block[:, j * lanes : (j + 1) * lanes]

    def gate(at):
        for j in range(tiles):
            cols = slice(j * lanes, (j + 1) * lanes)
            mixed = mixed_ref[pl.ds(at, 32), cols].astype(jnp.float32)
            y = y_ref[j, pl.ds(at, 32), :] + rows_ref[j, skip_row : skip_row + 1, :] * mixed
            y_ref[j, pl.ds(at, 32), :] = y
            z = z_ref[j, pl.ds(at, 32), :]
            gated_ref[pl.ds(at, 32), cols] = low_bits(y * z * sigmoid_of(z))

    row_loop(row_count, 32, gate)
    store(z_ref, z_out)
    store(y_ref, y_out)
    store(gated_ref, gated_out)
    out_full = gate_ref[:, channel_rows:].reshape(width, model_width)

    def out_block(l):
        at = pl.multiple_of(l * own_rows, own_rows)
        return matmul(gated_ref[pl.ds(at, own_rows), :], out_full)

    sum_copies = plane_copies(lambda to, k: partial_ref.at[k - 1], arrive_ref, sum_sems, False)
    for k in range(1, split):
        partial_ref[k - 1] = low_bits(out_block(lax.rem(low + k, split)))
        sum_copies[k - 1].start()
    resid = tokens_ref[...].astype(jnp.float32) + out_block(low)
    arrived(c_src, c_dst, c_sems, c_core, (2,))
    for copy in route_copies:
        copy.wait()
    store(routed_ref, routed_out)
    for k in range(1, split):
        sum_copies[k - 1].wait()
        resid = resid + arrive_ref[k - 1].astype(jnp.float32)
    resid_ref[...] = resid
    second_ref[low] = low_bits(norm_rows(resid, gains_ref[1:2, :]))
    second_copies = plane_copies(lambda to, k: second_ref.at[low], second_ref, second_sems, True)
    for copy in second_copies:
        copy.start()
    arrived(d_src, d_dst, d_sems, d_core, (1, 3))
    relay_inside(3)
    arrived(d_src, d_dst, d_sems, d_core, (2,))
    for copy in second_copies:
        copy.wait()
    store(second_ref, second_out)
    for copy in a_copies + b_copies + c_copies + d_copies + relays + core_copies:
        copy.wait_send()
    for dst_of, sems in ((c_dst, c_core), (d_dst, d_core)):
        for k in range(split):
            core_copy(dst_of, sems, k).wait_recv()
    for copy in stores:
        copy.wait()


def run_mixer(
    tokens, gains, lengths, in_weight, conv_weight, x_weight, dt_weight, dt_bias, a_log, skip_gain,
    out_weight, expert_in, expert_out, grad_out, routes,
):
    own_rows, model_width = tokens.shape
    tap_count, channels = conv_weight.shape
    dt_rank, states = dt_weight.shape[1], a_log.shape[0]
    expert_count, hidden, _ = expert_in.shape
    row_count = own_rows * split
    steps = row_count // subs
    blocks = 2 * split
    channel_rows = -(-channels // 16) * 16
    width = blocks * channel_rows
    tiles = width // lanes
    vmem = pl.BlockSpec(memory_space=pltpu.VMEM)
    anywhere = pl.BlockSpec(memory_space=pl.ANY)
    f32, bf16 = jnp.float32, jnp.bfloat16
    tiled = (tiles, row_count, lanes)
    hidden_part = ((2 * expert_count - 1) * hidden, model_width)
    first = ((blocks, channel_rows, model_width + 3 * lanes), bf16)
    gate = ((blocks, 2 * channel_rows, model_width), bf16)
    normed = ((split, own_rows, model_width), bf16)
    edge = ((16, model_width), bf16)
    routed = ((split, own_rows, model_width + lanes), bf16)
    inputs = ((row_count + 16, width), f32)
    coef = ((row_count, lanes), f32)
    gated = ((row_count, width), bf16)
    start = ((tiles, states, subs, lanes), f32)
    resid = ((own_rows, model_width), f32)
    rows = ((tiles, lanes, lanes), f32)
    kept = [first, gate, normed, edge, routed, inputs, coef, (tiled, f32), (tiled, f32)]
    kept += [(tiled, f32), gated, start, normed, rows, (hidden_part, bf16)]
    outs = [first, gate, ((blocks,) + hidden_part, bf16), normed, routed, inputs, coef]
    spread_out = ((steps, states, subs, lanes), f32)
    outs += [(tiled, f32)] * 3 + [gated, start, resid, normed, rows, spread_out, spread_out, (tiled, f32)]
    spreads = pltpu.VMEM((steps, states, subs, lanes), f32)
    dma = pltpu.SemaphoreType.DMA
    others = split - 1
    return pl.pallas_call(
        functools.partial(mixer_kernel, dt_rank, states, tap_count),
        in_specs=[pl.BlockSpec(memory_space=pltpu.SMEM) if i == 2 else vmem for i in range(15)],
        out_specs=[vmem if i == 12 else anywhere for i in range(len(outs))],
        out_shape=[jax.ShapeDtypeStruct(shape, kind) for shape, kind in outs],
        scratch_shapes=[pltpu.VMEM(shape, kind) for shape, kind in kept]
        + [dma((len(outs),))]
        + [
            spreads,
            spreads,
            pltpu.VMEM(tiled, f32),
            pltpu.VMEM((row_count, width), bf16),
            pltpu.VMEM((others, own_rows, model_width), bf16),
            pltpu.VMEM((others, own_rows, model_width), bf16),
            pltpu.VMEM((row_count, lanes), bf16),
            pltpu.VMEM((others, row_count, lanes), bf16),
            pltpu.VMEM((tiles, 2 * states, lanes), f32),
            pltpu.VMEM((others, tiles, 2 * states, lanes), f32),
            pltpu.VMEM((tiles, states, subs, lanes), f32),
            pltpu.VMEM((tiles, states, subs, lanes), f32),
        ]
        + [dma((2, others))] * 4
        + [dma((2, split))] * 4
        + [dma((2, others))] * 5
        + [dma((split,)), dma, dma((2, others, tiles)), dma],
        compiler_params=pltpu.CompilerParams(
            collective_id=3, has_side_effects=True, vmem_limit_bytes=60 << 20
        ),
        cost_estimate=pl.CostEstimate(flops=1000, bytes_accessed=1000, transcendentals=0),
    )(
        tokens, gains, lengths, in_weight, conv_weight, x_weight, dt_weight, dt_bias, a_log, skip_gain,
        out_weight, expert_in, expert_out, grad_out, routes,
    )


def norm_back(values, gain_row, grads):
    scale = lax.rsqrt(jnp.mean(values * values, -1, keepdims=True) + eps_norm)
    unit = values * scale
    inner = grads * gain_row
    return scale * (inner - unit * jnp.mean(inner * unit, -1, keepdims=True)), grads * unit


def route_probs(rows, router, route_lanes, expert_count):
    logits = matmul_nt(rows, router)
    lane = lax.broadcasted_iota(jnp.int32, logits.shape, 1)
    logits = jnp.where(lane < expert_count, logits, -1e30)
    powers = jnp.exp(logits - jnp.max(logits, -1, keepdims=True))
    probs = powers / jnp.sum(powers, -1, keepdims=True)
    chosen = jnp.where(lane.astype(jnp.float32) == route_lanes, 1.0, 0.0)
    return probs, chosen, jnp.sum(probs * chosen, -1, keepdims=True)


class LineScatter:
    def __init__(self, src_of, arrive_ref, sems):
        core, high, low = kernel_place()
        self.src_of, self.arrive, self.high = src_of, arrive_ref, high
        relay = split

        def send(src, to, slot, index):
            return remote(src, arrive_ref.at[slot], sems.at[0, index], sems.at[1, slot], core, to, low)

        def slot_at(to, sender):
            return lax.rem(to - sender + split, split) - 1

        way = 1 - 2 * (high // (split - 1))
        near, mid, far = high + way, high + 2 * way, high + 3 * way
        self.end_sends = [
            send(src_of(far), near, relay, 0),
            send(src_of(mid), mid, slot_at(mid, high), 1),
            send(src_of(near), near, slot_at(near, high), 2),
        ]
        self.empty_slot = slot_at(high, far)
        self.end_slots = [slot_at(high, near), slot_at(high, mid)]
        beside, other = (split - 1) * (high - 1), split - 1 - high
        self.far_end = split - 1 - beside
        self.inner_sends = [
            send(src_of(other), other, slot_at(other, high), 1),
            send(src_of(beside), beside, slot_at(beside, high), 2),
        ]
        self.relay_send = send(arrive_ref.at[relay], self.far_end, slot_at(self.far_end, high), 0)
        self.inner_slots = [0, 1, 2]
        self.relay = relay
        self.sems = sems

    def landed(self, slot):
        core, high, low = kernel_place()
        remote(
            self.arrive.at[slot], self.arrive.at[slot], self.sems.at[0, 0], self.sems.at[1, slot],
            core, high, low,
        ).wait_recv()

    def start(self):
        @pl.when(at_ends())
        def _():
            for copy in self.end_sends:
                copy.start()
            self.arrive[self.empty_slot] = jnp.zeros(self.arrive.shape[1:], self.arrive.dtype)

        @pl.when(jnp.logical_not(at_ends()))
        def _():
            for copy in self.inner_sends:
                copy.start()

    def pass_on(self):
        @pl.when(jnp.logical_not(at_ends()))
        def _():
            self.landed(self.relay)
            own = self.src_of(self.far_end)
            rows = self.arrive.shape[1]

            def add(at):
                here = pl.ds(at, 16)
                total = self.arrive[self.relay, here].astype(jnp.float32)
                total = total + own[here, :].astype(jnp.float32)
                self.arrive[self.relay, here] = low_bits(total)

            row_loop(rows, 16, add)
            self.relay_send.start()

    def finish(self, out_ref):
        @pl.when(at_ends())
        def _():
            for copy in self.end_sends:
                copy.wait_send()
            for slot in self.end_slots:
                self.landed(slot)

        @pl.when(jnp.logical_not(at_ends()))
        def _():
            for copy in self.inner_sends + [self.relay_send]:
                copy.wait_send()
            for slot in self.inner_slots:
                self.landed(slot)

        own = self.src_of(self.high)

        def one(at):
            rows = pl.ds(at, 16)
            total = own[rows, :].astype(jnp.float32)
            for k in range(split - 1):
                total = total + self.arrive[k, rows].astype(jnp.float32)
            out_ref[rows, :] = total

        row_loop(out_ref.shape[0], 16, one)


def half_copy(src, dst, sems, h):
    core, high, low = kernel_place()
    return remote(src, dst, sems.at[0, h], sems.at[1, h], 1 - core, high, low)


def turn_kernel(
    states, expert_count,
    second_ref, routed_ref, hidden_hbm, weights_ref, router_ref, resid_ref, grad_ref, gains_ref,
    gate_hbm, normed_hbm, out_hbm, step_hbm, z_hbm, y_hbm, gated_hbm, rows_hbm,
    mixed_out_ref, d_resid_ref, small_ref, dy_out, gz_out, later_ref, mine_out, early_ref,
    gate_mine_ref, mid_ref,
    hidden_ref, gate_ref, normed_ref, out_ref, step_ref, z_ref, y_ref, gated_ref, rows_ref, dy_ref,
    gz_ref, load_sems, store_sems,
    grads_ref, half_ref, y_sum_ref, d_sum_ref, dg_sum_ref, gates_ref, scaled_ref, act_ref, pre_ref,
    part_ref, arrive_ref, y_arrive_ref, branch_ref, send_ref,
    ends_ref, early_arrive_ref, gate_half_ref, down_ref, growth_ref,
    mid_arrive_ref,
    half_sems, sum_sems, y_sems, branch_sems, early_sems, ends_sems, gate_half_sems, last_sems,
    last_core, mid_sems,
):
    core, high, low = kernel_place()
    _, own_rows, model_width = second_ref.shape
    row_count = own_rows * split
    steps = row_count // subs
    tiles = step_ref.shape[0]
    width = tiles * lanes
    loads = [
        pltpu.make_async_copy(source, target, load_sems.at[i])
        for i, (source, target) in enumerate(
            (
                (hidden_hbm, hidden_ref),
                (gate_hbm, gate_ref),
                (z_hbm, z_ref),
                (y_hbm, y_ref),
                (step_hbm, step_ref),
                (rows_hbm, rows_ref),
                (out_hbm, out_ref),
                (normed_hbm, normed_ref),
                (gated_hbm, gated_ref),
            )
        )
    ]
    for copy in loads:
        copy.start()
    hidden = weights_ref.shape[1]
    stores = [
        pltpu.make_async_copy(source, target, store_sems.at[i])
        for i, (source, target) in enumerate(
            (
                (dy_ref, dy_out),
                (gz_ref, gz_out),
                (half_ref.at[:, pl.ds(3 * hidden, hidden)], mine_out),
            )
        )
    ]
    last_ref = weights_ref.at[expert_count - 1]
    hidden_rows = 2 * expert_count * hidden
    channel_rows = width // (2 * split)
    greeted = greet_all()
    at = lax.broadcasted_iota(jnp.int32, (lanes, expert_count), 0)
    to = lax.broadcasted_iota(jnp.int32, (lanes, expert_count), 1)
    router = low_bits(
        matmul(jnp.where(at == to, 1.0, 0.0).astype(jnp.bfloat16), router_ref[...])
    )

    for l in range(split):
        rows = slice(l * own_rows, (l + 1) * own_rows)
        route_lanes = routed_ref[l, :, model_width:].astype(jnp.float32)
        _, _, gate = route_probs(second_ref[l], router, route_lanes, expert_count)
        gates_ref[rows, :] = jnp.broadcast_to(gate, (own_rows, lanes))
        scaled_ref[rows, :] = low_bits(gate * routed_ref[l, :, :model_width].astype(jnp.float32))
    y_sum_ref[...] = jnp.zeros_like(y_sum_ref)
    d_sum_ref[...] = jnp.zeros_like(d_sum_ref)
    dg_sum_ref[...] = jnp.zeros_like(dg_sum_ref)
    span = split * hidden

    pl.semaphore_wait(pltpu.get_barrier_semaphore(), greeted)

    loads[0].wait()

    def down_at(at):
        return down_ref.at[at]

    down_ref[high] = last_ref[...]
    last_copies = line_copies(last_ref, down_at, last_sems)
    last_relay = line_relay(down_at, last_sems)
    own_copy = core_copy(down_at, last_core, 0)
    for copy in last_copies + [own_copy]:
        copy.start()
    last_copies.append(own_copy)

    @pl.when(at_ends())
    def _():
        last_relay.start()

    def last_arrived(ks):
        for k in ks:
            line_arrived(last_ref, down_at, last_sems, k)
            copy = core_copy(down_at, last_core, k)
            copy.start()
            last_copies.append(copy)

    def halves_of(e, first):
        up = hidden_ref[first : first + split, 2 * e * hidden : (2 * e + 1) * hidden]
        up = up.reshape(span, model_width)
        if e < expert_count - 1:
            down = hidden_ref[first : first + split, (2 * e + 1) * hidden : (2 * e + 2) * hidden]
        else:
            down = down_ref[first : first + split]
        return up, down.reshape(span, model_width)

    def token_block(e, first, l):
        up, down = halves_of(e, first)
        cols = slice(0, span) if first else slice(span, 2 * span)
        rows = pl.ds(pl.multiple_of(l * own_rows, own_rows), own_rows)
        pre = matmul_nt(second_ref[l], up)
        picked = routed_ref[l, :, model_width : model_width + 1].astype(jnp.float32) == e
        half = 0.5 + 0.5 * lax.erf(pre * (0.5**0.5))
        bell = jnp.exp(-0.5 * pre * pre) * (1.0 / (2.0 * math.pi) ** 0.5)
        act = low_bits(jnp.where(picked, pre * half, 0.0))
        d_raw = matmul_nt(routed_ref[l, :, :model_width], down)
        weighted = act.astype(jnp.float32) * d_raw
        dg_sum_ref[rows, :] += sum(weighted[:, c : c + lanes] for c in range(0, span, lanes))
        d_pre = jnp.where(picked, gates_ref[rows, :1] * d_raw * (half + pre * bell), 0.0)
        d_pre = low_bits(d_pre)
        y_sum_ref[rows, :] += matmul(act, down)
        d_sum_ref[rows, :] += matmul(d_pre, up)
        act_ref[rows, cols] = act
        pre_ref[rows, cols] = d_pre

    def weight_grads(e, first):
        cols = slice(0, span) if first else slice(span, 2 * span)
        second = second_ref[...].reshape(row_count, model_width)
        up_grad = low_bits(matmul_tn(pre_ref[:, cols], second))
        down_grad = low_bits(matmul_tn(act_ref[:, cols], scaled_ref[...]))
        for b in range(split):
            piece = slice(b * hidden, (b + 1) * hidden)
            to = 2 * e * hidden
            grads_ref[first + b, to : to + hidden] = up_grad[piece]
            grads_ref[first + b, to + hidden : to + 2 * hidden] = down_grad[piece]

    def part_of(e):
        return pl.ds(2 * e * hidden, 2 * hidden)

    half_copies = {}

    def send_half(e):
        half_copies[e] = [
            half_copy(
                grads_ref.at[split + h, part_of(e)],
                half_ref.at[h, part_of(e)],
                half_sems.at[e],
                h,
            )
            for h in range(split)
        ]
        for copy in half_copies[e]:
            copy.start()

    def add_half(e):
        for copy in half_copies[e]:
            copy.wait()

        def one(i, _):
            h, at = i // (2 * hidden // 32), lax.rem(i, 2 * hidden // 32) * 32
            rows = pl.ds(2 * e * hidden + at, 32)
            half_ref[h, rows] = low_bits(
                grads_ref[h, rows].astype(jnp.float32) + half_ref[h, rows].astype(jnp.float32)
            )
            return 0

        lax.fori_loop(0, split * (2 * hidden // 32), one, 0)

    mid = LineScatter(
        lambda to: half_ref.at[to, pl.ds(2 * hidden, hidden)], mid_arrive_ref, mid_sems
    )
    early = LineScatter(lambda to: half_ref.at[to, part_of(0)], early_arrive_ref, early_sems)
    final = expert_count - 1
    for e in range(final):
        for first in (split, 0):
            lax.fori_loop(0, split, lambda l, _: (token_block(e, first, l), 0)[1], 0)
            weight_grads(e, first)
            if first:
                send_half(e)
                if e == 0:
                    last_arrived((1, 3))

                    @pl.when(jnp.logical_not(at_ends()))
                    def _():
                        last_relay.start()

    last_arrived((2,))
    for e in range(final):
        add_half(e)
    early.start()
    for k in range(split):
        core_copy(down_at, last_core, k).wait_recv()

    def sum_copy(index):
        to = lax.rem(low + 1 + index, split)
        return remote(
            part_ref.at[index], arrive_ref.at[index], sum_sems.at[0, index], sum_sems.at[1, index],
            core, high, to,
        )

    def last_block(index, _):
        l = lax.rem(low + 1 + index, split)
        token_block(final, split, l)
        token_block(final, 0, l)

        @pl.when(index < split - 1)
        def _():
            rows = pl.ds(pl.multiple_of(l * own_rows, own_rows), own_rows)
            part_ref[index, :, :model_width] = low_bits(d_sum_ref[rows, :])
            part_ref[index, :, model_width:] = low_bits(dg_sum_ref[rows, :])
            sum_copy(index).start()

        return 0

    lax.fori_loop(0, split, last_block, 0)
    weight_grads(final, split)
    send_half(final)
    weight_grads(final, 0)
    early.pass_on()
    for copy in last_copies + [last_relay]:
        copy.wait_send()

    y_copies = plane_copies(
        lambda to, k: part_ref.at[k - 1, :, pl.ds(0, model_width)], y_arrive_ref, y_sems, False
    )
    own = pl.ds(pl.multiple_of(low * own_rows, own_rows), own_rows)
    d_second, dg_lanes = d_sum_ref[own, :], dg_sum_ref[own, :]
    for k in range(1, split):
        sum_copy(k - 1).wait()
        d_second = d_second + arrive_ref[k - 1, :, :model_width].astype(jnp.float32)
        dg_lanes = dg_lanes + arrive_ref[k - 1, :, model_width:].astype(jnp.float32)
    d_gate = jnp.sum(dg_lanes, -1, keepdims=True)
    second_own = second_ref[low]
    route_lanes = routed_ref[low, :, model_width:].astype(jnp.float32)
    probs, chosen, gate = route_probs(second_own, router, route_lanes, expert_count)
    d_logits = low_bits(probs * (d_gate * (chosen - gate)))
    d_second = d_second + matmul(d_logits, router)
    d_rows, d_gain = norm_back(resid_ref[...], gains_ref[1:2, :], d_second)
    d_resid = grad_ref[...] + d_rows
    d_resid_ref[...] = d_resid
    branch_ref[low] = low_bits(d_resid)
    branch_copies = plane_copies(lambda to, k: branch_ref.at[low], branch_ref, branch_sems, True)
    for copy in branch_copies:
        copy.start()
    for k in range(1, split):
        to = pl.ds(pl.multiple_of(lax.rem(low + k, split) * own_rows, own_rows), own_rows)
        part_ref[k - 1, :, :model_width] = low_bits(y_sum_ref[to, :])
        y_copies[k - 1].start()
    small_ref[...] = jnp.zeros_like(small_ref)
    small_ref[1:2, :] = jnp.sum(d_gain, 0, keepdims=True)
    small_ref[2 : 2 + expert_count, :] = matmul_tn(d_logits, second_own)[:expert_count]

    add_half(final)
    mid.start()
    stores[2].start()
    for copy in loads[1:]:
        copy.wait()
    out_full = gate_ref[:, channel_rows:].reshape(width, model_width)
    for copy in branch_copies:
        copy.wait()
    for l in range(split):
        d_gated = matmul_nt(branch_ref[l], out_full)
        rows = slice(l * own_rows, (l + 1) * own_rows)
        for j in range(tiles):
            cols = slice(j * lanes, (j + 1) * lanes)
            z = z_ref[j, rows, :]
            sig = sigmoid_of(z)
            d_tile = d_gated[:, cols]
            dy_ref[j, rows, :] = d_tile * (z * sig)
            d_z = d_tile * y_ref[j, rows, :] * (sig * (1.0 + z * (1.0 - sig)))
            gz_ref[rows, cols] = low_bits(d_z)

    def rates_of(j):
        values = -jnp.exp(rows_ref[j, alog_row : alog_row + states, :]) * log2e
        return [jnp.broadcast_to(values[n : n + 1, :], (subs, lanes)) for n in range(states)]

    def ends_of(j, _):
        found = scan_one_way(
            j,
            True,
            states,
            steps,
            step_ref,
            lambda s: dy_ref[j, pl.ds(s, subs, stride=steps), :],
            out_ref,
            rates_of(j),
        )
        row = lax.broadcasted_iota(jnp.int32, (subs, lanes), 0)
        for n, (grow, state) in enumerate(found):
            send_ref[j, n : n + 1] = grow[:1]
            send_ref[j, states + n : states + n + 1] = state[:1]
            has = row < subs - 1
            growth_ref[j, n] = jnp.where(has, pltpu.roll(grow, subs - 1, 0), 1.0)
            later_ref[j, n] = jnp.where(has, pltpu.roll(state, subs - 1, 0), 0.0)
        for copy in ends_copies(send_ref, ends_ref, ends_sems, j, True):
            copy.start()
        return 0

    stores[0].start()
    stores[1].start()
    mid.pass_on()
    lax.fori_loop(0, tiles, ends_of, 0)

    normed = normed_ref[...].reshape(row_count, model_width)
    branch = branch_ref[...].reshape(row_count, model_width)
    for part, (first_op, second_op) in enumerate(((gz_ref, normed), (gated_ref, branch))):
        half_width = width // 2
        for at in (half_width, 0):
            grad = low_bits(matmul_tn(first_op[:, at : at + half_width], second_op))
            for b in range(split):
                piece = grad[b * channel_rows : (b + 1) * channel_rows]
                to = part * channel_rows
                grads_ref[at // channel_rows + b, to : to + channel_rows] = piece
    gate_rows = 2 * channel_rows
    gate_copies = [
        half_copy(
            grads_ref.at[split + h, pl.ds(0, gate_rows)], gate_half_ref.at[h], gate_half_sems, h
        )
        for h in range(split)
    ]
    for copy in gate_copies:
        copy.start()

    def settle(j, _):
        for copy in ends_copies(send_ref, ends_ref, ends_sems, j, True):
            copy.wait()
        enter = chain_enter(ends_ref, j, states, True)
        for n in range(states):
            entered = jnp.broadcast_to(enter[n : n + 1, :], (subs, lanes))
            later_ref[j, n] += growth_ref[j, n] * entered
        return 0

    lax.fori_loop(0, tiles, settle, 0)
    y = y_sum_ref[own, :]
    for k in range(1, split):
        y_copies[k - 1].wait()
        y = y + y_arrive_ref[k - 1].astype(jnp.float32)
    mixed_out_ref[...] = low_bits(resid_ref[...] + gates_ref[own, :1] * y)
    for h in range(split):
        gate_copies[h].wait()

        def add_gate(at, h=h):
            rows = pl.ds(at, 16)
            total = grads_ref[h, rows].astype(jnp.float32) + gate_half_ref[h, rows].astype(jnp.float32)
            gate_mine_ref[h, rows] = low_bits(total)

        row_loop(gate_rows, 16, add_gate)
    early.finish(early_ref)
    mid.finish(mid_ref)
    for copy in stores:
        copy.wait()


def run_turn(
    second, routed, hidden_full, last_part, router_lanes, resid, grad_out, gains, gate_full, normed,
    spread_out, step, z, y, gated, rows, states, expert_count,
):
    _, own_rows, model_width = second.shape
    row_count = own_rows * split
    steps = row_count // subs
    tiles = step.shape[0]
    width = tiles * lanes
    hidden = last_part.shape[1]
    hidden_rows = 2 * expert_count * hidden
    cut = 2 * hidden
    gate_rows = gate_full.shape[1]
    others = split - 1
    vmem = pl.BlockSpec(memory_space=pltpu.VMEM)
    f32, bf16 = jnp.float32, jnp.bfloat16
    dma = pltpu.SemaphoreType.DMA
    outs = [
        ((own_rows, model_width), bf16),
        ((own_rows, model_width), f32),
        ((8, model_width), f32),
        ((tiles, row_count, lanes), f32),
        ((row_count, width), bf16),
        ((tiles, states, subs, lanes), f32),
        ((split, hidden, model_width), bf16),
        ((cut, model_width), f32),
        ((split, gate_rows, model_width), bf16),
        ((hidden, model_width), f32),
    ]
    span = split * hidden
    anywhere = pl.BlockSpec(memory_space=pl.ANY)
    specs = [anywhere if i == 2 or i > 7 else vmem for i in range(16)]
    loaded = [hidden_full, gate_full, normed, spread_out, step, z, y, gated, rows]
    return pl.pallas_call(
        functools.partial(turn_kernel, states, expert_count),
        in_specs=specs,
        out_specs=[anywhere if i in (3, 4, 6) else vmem for i in range(len(outs))],
        out_shape=[jax.ShapeDtypeStruct(shape, kind) for shape, kind in outs],
        scratch_shapes=[pltpu.VMEM(value.shape, value.dtype) for value in loaded]
        + [pltpu.VMEM(*outs[i]) for i in (3, 4)]
        + [dma((len(loaded),)), dma((3,))]
        + [
            pltpu.VMEM((2 * split, hidden_rows, model_width), bf16),
            pltpu.VMEM((split, hidden_rows, model_width), bf16),
            pltpu.VMEM((row_count, model_width), f32),
            pltpu.VMEM((row_count, model_width), f32),
            pltpu.VMEM((row_count, lanes), f32),
            pltpu.VMEM((row_count, lanes), f32),
            pltpu.VMEM((row_count, model_width), bf16),
            pltpu.VMEM((row_count, 2 * span), bf16),
            pltpu.VMEM((row_count, 2 * span), bf16),
            pltpu.VMEM((others, own_rows, model_width + lanes), bf16),
            pltpu.VMEM((others, own_rows, model_width + lanes), bf16),
            pltpu.VMEM((others, own_rows, model_width), bf16),
            pltpu.VMEM((split, own_rows, model_width), bf16),
            pltpu.VMEM((tiles, 2 * states, lanes), f32),
            pltpu.VMEM((others, tiles, 2 * states, lanes), f32),
            pltpu.VMEM((split + 1, cut, model_width), bf16),
            pltpu.VMEM((split, gate_rows, model_width), bf16),
            pltpu.VMEM((2 * split, hidden, model_width), bf16),
            pltpu.VMEM((tiles, states, subs, lanes), f32),
            pltpu.VMEM((split + 1, hidden, model_width), bf16),
            dma((expert_count, 2, split)),
            dma((2, others)),
            dma((2, others)),
            dma((2, others)),
            dma((2, split + 1)),
            dma((2, others, tiles)),
            dma((2, split)),
            dma((2, others)),
            dma((2, split)),
            dma((2, split + 1)),
        ],
        compiler_params=pltpu.CompilerParams(
            collective_id=4, has_side_effects=True, vmem_limit_bytes=63 << 20
        ),
        cost_estimate=pl.CostEstimate(flops=1000, bytes_accessed=1000, transcendentals=0),
    )(
        second, routed, hidden_full, last_part, router_lanes, resid, grad_out, gains, gate_full, normed,
        spread_out, step, z, y, gated, rows,
    )


def back_kernel(
    dt_rank, states, tap_count,
    dy_hbm, gz_hbm, later_hbm, mine_ref, gate_mine_hbm, first_hbm, gate_hbm, normed_hbm, input_ref,
    coef_ref, step_hbm, start_hbm, rows_ref, d_resid_ref, tokens_ref, gains_ref, small_ref,
    lengths_ref, in_hbm, out_hbm, drive_hbm,
    grad_tokens_ref, total_ref, late_ref, second_own_ref, out_own_ref, first_own_ref,
    dy_ref, gz_ref, later_ref, gate_mine_ref, first_ref, gate_ref, normed_ref, step_ref, start_ref,
    in_ref, out_ref, drive_ref, load_sems,
    hist_ref, acc_in_ref, acc_out_ref, conv_ref, q_ref, r_ref,
    gdt_ref, gin_ref, halo_ref, part_ref, arrive_ref, fold_ref, coef_send_ref,
    coef_arrive_ref, gcoef_ref, misc_ref, select_ref, payload_ref, half_ref, mine_first_ref,
    late_arrive_ref, second_arrive_ref, out_arrive_ref, first_arrive_ref, core_slots, plane_slots, line_slots,
    late_sems, second_sems, out_sems, first_sems, half_sems, halo_sems, coef_sems, sum_sems, core_sems,
    plane_sems, line_sems,
):
    core, high, low = kernel_place()
    _, own_rows, model_width = normed_ref.shape
    row_count = own_rows * split
    steps = row_count // subs
    tiles = step_ref.shape[0]
    loads = [
        pltpu.make_async_copy(source, target, load_sems.at[i])
        for i, (source, target) in enumerate(
            (
                (step_hbm, step_ref),
                (start_hbm, start_ref),
                (gate_mine_hbm, gate_mine_ref),
                (in_hbm, in_ref),
                (drive_hbm, drive_ref),
                (dy_hbm, dy_ref),
                (later_hbm, later_ref),
                (out_hbm, out_ref),
                (first_hbm, first_ref),
                (gate_hbm, gate_ref),
                (gz_hbm, gz_ref),
                (normed_hbm, normed_ref),
            )
        )
    ]
    for copy in loads:
        copy.start()
    width = tiles * lanes
    channel_rows = width // (2 * split)
    edge = input_ref.shape[0] - row_count
    greeted = greet_all()
    first_len = lengths_ref[0, 0]

    def offsets(at, rows):
        place = high * row_count + at + lax.broadcasted_iota(jnp.int32, (rows, lanes), 0)
        return jnp.where(place < first_len, place, place - first_len)

    late = LineScatter(lambda to: mine_ref.at[to], late_arrive_ref, late_sems)
    gate_parts = [
        LineScatter(
            lambda to: gate_mine_ref.at[to, pl.ds(0, channel_rows)], second_arrive_ref, second_sems
        ),
        LineScatter(
            lambda to: gate_mine_ref.at[to, pl.ds(channel_rows, channel_rows)], out_arrive_ref, out_sems
        ),
    ]
    def convolve(at):
        offset = offsets(at, 32)
        for j in range(tiles):
            span = input_ref[pl.ds(at, 32 + edge), j * lanes : (j + 1) * lanes]
            conv_sum = jnp.zeros((32, lanes), jnp.float32)
            for k in range(tap_count):
                shift = edge - (tap_count - 1) + k
                term = rows_ref[j, k : k + 1, :] * span[shift : shift + 32]
                conv_sum = conv_sum + jnp.where(offset >= tap_count - 1 - k, term, 0.0)
            conv_ref[j, pl.ds(at, 32), :] = conv_sum

    row_loop(row_count, 32, convolve)
    pl.semaphore_wait(pltpu.get_barrier_semaphore(), greeted)
    late.start()
    for copy in loads[:8]:
        copy.wait()
    acc_in_ref[...] = jnp.zeros_like(acc_in_ref)
    acc_out_ref[...] = jnp.zeros_like(acc_out_ref)
    misc_ref[...] = jnp.zeros_like(misc_ref)

    def back_of(j, _):
        @pl.when(j == 2)
        def _():
            late.pass_on()
            for part in gate_parts:
                part.start()

        values = -jnp.exp(rows_ref[j, alog_row : alog_row + states, :]) * log2e
        rates = [jnp.broadcast_to(values[n : n + 1, :], (subs, lanes)) for n in range(states)]

        def forward(s, held):
            step = step_ref[j, step_rows(s), :]
            drive = drive_ref[j, step_rows(s), :]
            now_all = []
            for n in range(states):
                now = jnp.exp2(step * rates[n]) * held[n] + in_ref[s, n] * drive
                hist_ref[s + 1, n] = now
                now_all.append(now)
            return tuple(now_all)

        held = []
        for n in range(states):
            hist_ref[0, n] = start_ref[j, n]
            held.append(start_ref[j, n])
        lax.fori_loop(0, steps, forward, tuple(held), unroll=2)

        def backward(turn, carry):
            s = steps - 1 - turn
            later, sums = carry
            step = step_ref[j, step_rows(s), :]
            drive = drive_ref[j, step_rows(s), :]
            dy = dy_ref[j, pl.ds(s, subs, stride=steps), :]
            rows = step_rows(s)
            q = jnp.zeros((subs, lanes), jnp.float32)
            r = jnp.zeros((subs, lanes), jnp.float32)
            later_next, sums_next = [], []
            for n in range(states):
                cols = slice(n * lanes, (n + 1) * lanes)
                d_state = out_ref[s, n] * dy + later[n]
                back = jnp.exp2(step * rates[n]) * d_state
                scaled = back * hist_ref[s, n]
                sums_next.append(sums[n] + scaled * step)
                q = q + scaled * rates[n]
                r = r + d_state * in_ref[s, n]
                acc_in_ref[rows, cols] += d_state * drive
                acc_out_ref[rows, cols] += hist_ref[s + 1, n] * dy
                later_next.append(back)
            q_ref[j, pl.ds(s, subs, stride=steps), :] = q * (1.0 / log2e)
            r_ref[j, pl.ds(s, subs, stride=steps), :] = r
            return tuple(later_next), tuple(sums_next)

        zero = jnp.zeros((subs, lanes), jnp.float32)
        later = tuple(later_ref[j, n] for n in range(states))
        _, sums = lax.fori_loop(0, steps, backward, (later, (zero,) * states))
        for n in range(states):
            total = jnp.sum(sums[n] * rates[n], 0, keepdims=True) * (1.0 / log2e)
            misc_ref[j, alog_row + n : alog_row + n + 1, :] = total
        return 0

    lax.fori_loop(0, tiles, back_of, 0)

    for copy in loads[8:]:
        copy.wait()

    source = lax.broadcasted_iota(jnp.int32, select_ref.shape, 0) // lanes
    target = lax.broadcasted_iota(jnp.int32, select_ref.shape, 1)

    def fold(acc_ref, first, fresh):
        select_ref[...] = jnp.where(target == first + source, 1.0, 0.0).astype(jnp.bfloat16)

        def one(at):
            values = acc_ref[pl.ds(at, 128), :]
            coarse = low_bits(values)
            fine = low_bits(values - coarse.astype(jnp.float32))
            found = matmul(coarse, select_ref[...]) + matmul(fine, select_ref[...])
            for i in range(128 // subs):
                rows = pl.ds(at // subs + i, subs, stride=steps)
                piece = found[i * subs : (i + 1) * subs]
                fold_ref[rows, :] = piece if fresh else fold_ref[rows, :] + piece

        row_loop(row_count, 128, one)

    fold(acc_in_ref, dt_rank, True)
    fold(acc_out_ref, dt_rank + states, False)
    dt_full = first_ref[:, :, model_width + lanes : model_width + 2 * lanes].reshape(width, lanes)

    def mixed_of(j, rows):
        conv = conv_ref[j, rows, :]
        return low_bits(conv * sigmoid_of(conv)).astype(jnp.float32)

    def step_grads(at):
        rows = pl.ds(at, 128)
        pre = matmul_nt(low_bits(coef_ref[rows, :]), dt_full)
        for j in range(tiles):
            cols = slice(j * lanes, (j + 1) * lanes)
            mixed = mixed_of(j, rows)
            in_sum = r_ref[j, rows, :]
            d_step = q_ref[j, rows, :] + in_sum * mixed
            biased = pre[:, cols] + rows_ref[j, bias_row : bias_row + 1, :]
            r_ref[j, rows, :] = in_sum * softplus_of(biased)
            d_dt = d_step * sigmoid_of(biased)
            gdt_ref[rows, cols] = low_bits(d_dt)
            misc_ref[j, bias_row : bias_row + 1, :] += jnp.sum(d_dt, 0, keepdims=True)
            misc_ref[j, skip_row : skip_row + 1, :] += jnp.sum(
                dy_ref[j, rows, :] * mixed, 0, keepdims=True
            )
        part = fold_ref[rows, :] + matmul(gdt_ref[rows, :], dt_full)
        fold_ref[rows, :] = part
        coef_send_ref[rows, :] = low_bits(part)

    row_loop(row_count, 128, step_grads)
    coef_copies = plane_copies(lambda to, k: coef_send_ref, coef_arrive_ref, coef_sems, False)
    for copy in coef_copies:
        copy.start()
    low_coef = low_bits(coef_ref[...])
    for j in range(tiles):
        rows = slice(j * lanes, (j + 1) * lanes)
        payload_ref[rows, model_width + lanes : model_width + 2 * lanes] = low_bits(
            matmul_tn(gdt_ref[:, rows], low_coef)
        )
    for copy in coef_copies:
        copy.wait()
    total = fold_ref[...]
    for k in range(1, split):
        total = total + coef_arrive_ref[k - 1].astype(jnp.float32)
    gcoef_ref[...] = low_bits(total)
    x_full = first_ref[:, :, model_width : model_width + lanes].reshape(width, lanes)

    def conv_grads(at):
        rows = pl.ds(at, 128)
        from_coef = matmul_nt(gcoef_ref[rows, :], x_full)
        for j in range(tiles):
            cols = slice(j * lanes, (j + 1) * lanes)
            d_mixed = rows_ref[j, skip_row : skip_row + 1, :] * dy_ref[j, rows, :]
            d_mixed = d_mixed + r_ref[j, rows, :] + from_coef[:, cols]
            conv = conv_ref[j, rows, :]
            sig = sigmoid_of(conv)
            q_ref[j, rows, :] = d_mixed * (sig * (1.0 + conv * (1.0 - sig)))

    row_loop(row_count, 128, conv_grads)

    def halo_copy():
        return remote(
            q_ref.at[:, pl.ds(0, subs)], halo_ref, halo_sems.at[0], halo_sems.at[1],
            core, lax.rem(high + split - 1, split), low,
        )

    for part in gate_parts:
        part.pass_on()

    @pl.when(high > 0)
    def _():
        halo_copy().start()

    def tap_grads(at):
        offset = offsets(at, 32)
        for j in range(tiles):
            cols = slice(j * lanes, (j + 1) * lanes)
            span = input_ref[pl.ds(at, 32 + edge), cols]
            d_conv = q_ref[j, pl.ds(at, 32), :]
            for k in range(tap_count):
                shift = edge - (tap_count - 1) + k
                term = jnp.where(offset >= tap_count - 1 - k, d_conv * span[shift : shift + 32], 0.0)
                misc_ref[j, k : k + 1, :] += jnp.sum(term, 0, keepdims=True)

    row_loop(row_count, 32, tap_grads)

    @pl.when(high < split - 1)
    def _():
        halo_copy().wait_recv()
        q_ref[:, row_count:, :] = halo_ref[...]

    @pl.when(high == split - 1)
    def _():
        q_ref[:, row_count:, :] = jnp.zeros_like(halo_ref)

    def input_grads(at):
        masks = [offsets(at + m, 32) >= m for m in range(tap_count)]
        for j in range(tiles):
            cols = slice(j * lanes, (j + 1) * lanes)
            span = q_ref[j, pl.ds(at, 32 + subs), :]
            d_input = jnp.zeros((32, lanes), jnp.float32)
            for m in range(tap_count):
                k = tap_count - 1 - m
                term = rows_ref[j, k : k + 1, :] * span[m : m + 32]
                d_input = d_input + jnp.where(masks[m], term, 0.0)
            gin_ref[pl.ds(at, 32), cols] = low_bits(d_input)

    row_loop(row_count, 32, input_grads)

    first_in = first_ref[:, :, :model_width].reshape(width, model_width)
    second_in = gate_ref[:, :channel_rows].reshape(width, model_width)

    def normed_block(l):
        rows = pl.ds(pl.multiple_of(l * own_rows, own_rows), own_rows)
        return matmul(gin_ref[rows, :], first_in) + matmul(gz_ref[rows, :], second_in)

    normed = normed_ref[...].reshape(row_count, model_width)
    for j in range(tiles):
        rows = slice(j * lanes, (j + 1) * lanes)
        payload_ref[rows, model_width : model_width + lanes] = low_bits(
            matmul_tn(low_bits(mixed_of(j, slice(0, row_count))), gcoef_ref[...])
        )
        payload_ref[rows, model_width + 2 * lanes :] = low_bits(misc_ref[j].T)
    half_width = width // 2
    half = remote(
        payload_ref.at[pl.ds(half_width, half_width)], half_ref, half_sems.at[0], half_sems.at[1],
        1 - core, high, low,
    )

    def first_half(at):
        payload_ref[at : at + half_width, :model_width] = low_bits(
            matmul_tn(gin_ref[:, at : at + half_width], normed)
        )

    first_half(half_width)
    half.start()
    sum_copies = plane_copies(lambda to, k: part_ref.at[k - 1], arrive_ref, sum_sems, False)
    gain = jnp.zeros((1, model_width), jnp.float32)
    for k in range(1, split + 1):
        l = lax.rem(low + k, split)
        block = normed_block(l)
        gain = gain + jnp.sum(block * normed_ref[l].astype(jnp.float32), 0, keepdims=True)
        if k < split:
            part_ref[k - 1] = low_bits(block)
            sum_copies[k - 1].start()
        else:
            grad_tokens_ref[...] = block

    line_slots[high] = small_ref[...]
    line_slots[high, 0:1, :] = gain / gains_ref[0:1, :]
    line = line_copies(line_slots.at[high], lambda at: line_slots.at[at], line_sems, True)
    for copy in line:
        copy.start()
    first_half(0)
    half.wait()

    def add_half(at):
        rows = pl.ds(at, 64)
        both = payload_ref[rows, :].astype(jnp.float32) + half_ref[rows, :].astype(jnp.float32)
        mine_first_ref[rows, :] = low_bits(both)

    row_loop(half_width, 64, add_half)
    first = LineScatter(
        lambda to: mine_first_ref.at[pl.ds(pl.multiple_of(to * channel_rows, 16), channel_rows)],
        first_arrive_ref,
        first_sems,
    )
    first.start()
    for k in range(1, split):
        line_arrived(line_slots.at[high], lambda at: line_slots.at[at], line_sems, k)
    core_slots[core] = (line_slots[0] + line_slots[1]) + (line_slots[2] + line_slots[3])
    hop = remote(
        core_slots.at[core], core_slots.at[core], core_sems.at[0], core_sems.at[1], 1 - core, high, low
    )
    hop.start()
    late.finish(late_ref)
    hop.wait()
    plane_slots[low] = core_slots[0] + core_slots[1]
    plane = plane_copies(lambda to, k: plane_slots.at[low], plane_slots, plane_sems, True)
    for copy in plane:
        copy.start()
    first.pass_on()
    gate_parts[0].finish(second_own_ref)
    gate_parts[1].finish(out_own_ref)
    d_normed = grad_tokens_ref[...]
    for k in range(1, split):
        sum_copies[k - 1].wait()
        d_normed = d_normed + arrive_ref[k - 1].astype(jnp.float32)
    tokens = tokens_ref[...].astype(jnp.float32)
    d_rows, _ = norm_back(tokens, gains_ref[0:1, :], d_normed)
    grad_tokens_ref[...] = d_resid_ref[...] + d_rows
    for copy in plane:
        copy.wait()
    for copy in line:
        copy.wait_send()
    total_ref[...] = (plane_slots[0] + plane_slots[1]) + (plane_slots[2] + plane_slots[3])
    first.finish(first_own_ref)

    @pl.when(high > 0)
    def _():
        halo_copy().wait_send()


def run_back(
    dy, gz, later, mine, gate_mine, first_full, gate_full, normed, input_all, coef, step, start, rows,
    d_resid, tokens, gains, small, lengths, spread_in, spread_out, drive, dt_rank, states,
    tap_count,
):
    _, own_rows, model_width = normed.shape
    row_count = own_rows * split
    steps = row_count // subs
    tiles = step.shape[0]
    width = tiles * lanes
    channel_rows = width // (2 * split)
    others = split - 1
    late_rows = mine.shape[1]
    first_columns = first_full.shape[2]
    vmem = pl.BlockSpec(memory_space=pltpu.VMEM)
    specs = [pl.BlockSpec(memory_space=pl.ANY) if i in (0, 1, 2, 4, 5, 6, 7, 10, 11) else vmem for i in range(17)]
    loaded = [dy, gz, later, gate_mine, first_full, gate_full, normed, step, start]
    loaded += [spread_in, spread_out, drive]
    specs.append(pl.BlockSpec(memory_space=pltpu.SMEM))
    specs += [pl.BlockSpec(memory_space=pl.ANY)] * 3
    f32, bf16 = jnp.float32, jnp.bfloat16
    dma = pltpu.SemaphoreType.DMA
    outs = [
        (own_rows, model_width),
        (8, model_width),
        (late_rows, model_width),
        (channel_rows, model_width),
        (channel_rows, model_width),
        (channel_rows, first_columns),
    ]
    tiled = pltpu.VMEM((tiles, row_count, lanes), f32)
    summed = pltpu.VMEM((row_count, states * lanes), f32)
    return pl.pallas_call(
        functools.partial(back_kernel, dt_rank, states, tap_count),
        in_specs=specs,
        out_specs=[vmem] * len(outs),
        out_shape=[jax.ShapeDtypeStruct(shape, f32) for shape in outs],
        scratch_shapes=[pltpu.VMEM(value.shape, value.dtype) for value in loaded]
        + [dma((len(loaded),))]
        + [
            pltpu.VMEM((steps + 1, states, subs, lanes), f32),
            summed,
            summed,
            tiled,
            pltpu.VMEM((tiles, row_count + subs, lanes), f32),
            tiled,
            pltpu.VMEM((row_count, width), bf16),
            pltpu.VMEM((row_count, width), bf16),
            pltpu.VMEM((tiles, subs, lanes), f32),
            pltpu.VMEM((others, own_rows, model_width), bf16),
            pltpu.VMEM((others, own_rows, model_width), bf16),
            pltpu.VMEM((row_count, lanes), f32),
            pltpu.VMEM((row_count, lanes), bf16),
            pltpu.VMEM((others, row_count, lanes), bf16),
            pltpu.VMEM((row_count, lanes), bf16),
            pltpu.VMEM((tiles, lanes, lanes), f32),
            pltpu.VMEM((states * lanes, lanes), bf16),
            pltpu.VMEM((width, first_columns), bf16),
            pltpu.VMEM((width // 2, first_columns), bf16),
            pltpu.VMEM((width // 2, first_columns), bf16),
            pltpu.VMEM((split + 1, late_rows, model_width), bf16),
            pltpu.VMEM((split + 1, channel_rows, model_width), bf16),
            pltpu.VMEM((split + 1, channel_rows, model_width), bf16),
            pltpu.VMEM((split + 1, channel_rows, first_columns), bf16),
            pltpu.VMEM((2, 8, model_width), f32),
            pltpu.VMEM((split, 8, model_width), f32),
            pltpu.VMEM((split, 8, model_width), f32),
        ]
        + [dma((2, split + 1))] * 4
        + [dma((2,)), dma((2,)), dma((2, others)), dma((2, others)), dma((2,))]
        + [dma((2, others)), dma((2, others))],
        compiler_params=pltpu.CompilerParams(
            collective_id=5, has_side_effects=True, vmem_limit_bytes=63 << 20
        ),
        cost_estimate=pl.CostEstimate(flops=1000, bytes_accessed=1000, transcendentals=0),
    )(
        dy, gz, later, mine, gate_mine, first_full, gate_full, normed, input_all, coef, step, start,
        rows, d_resid, tokens, gains, small, lengths, spread_in, spread_out, drive,
    )


def results_kernel(
    tap_count, states, coef_count, dt_rank, expert_count,
    mixed_ref, tokens_ref, total_ref, early_ref, mid_ref, late_ref, second_ref, out_ref, first_ref,
    mixed_out, tokens_out, gains_out, router_out, in_out, conv_out, x_out, dt_out, bias_out, alog_out,
    skip_out, out_out, up_out, down_out,
):
    channels, model_width = out_out.shape
    hidden = up_out.shape[1]
    mixed_out[...] = mixed_ref[...]
    tokens_out[...] = tokens_ref[...]
    gains_out[...] = total_ref[:2]
    router_out[...] = total_ref[2 : 2 + expert_count]
    in_out[0] = first_ref[:channels, :model_width]
    in_out[1] = second_ref[:channels]
    out_out[...] = out_ref[:channels]
    at = model_width
    x_out[...] = first_ref[:channels, at : at + lanes][:, :coef_count]
    dt_out[...] = first_ref[:channels, at + lanes : at + 2 * lanes][:, :dt_rank]
    misc = first_ref[:, at + 2 * lanes :]
    rows = misc.T
    conv_out[...] = rows[:tap_count, :channels]
    alog_out[...] = rows[alog_row : alog_row + states, :channels]
    bias_out[...] = rows[bias_row : bias_row + 1, :channels]
    skip_out[...] = rows[skip_row : skip_row + 1, :channels]
    up_out[0], down_out[0] = early_ref[:hidden], early_ref[hidden:]
    up_out[1], down_out[1] = mid_ref[...], late_ref[...]


def run_results(parts, channels, tap_count, states, coef_count, dt_rank, expert_count, hidden):
    own_rows, model_width = parts[0].shape
    f32 = jnp.float32
    shapes = [
        (own_rows, model_width),
        (2, model_width),
        (expert_count, model_width),
        (2, channels, model_width),
        (tap_count, channels),
        (channels, coef_count),
        (channels, dt_rank),
        (1, channels),
        (states, channels),
        (1, channels),
        (channels, model_width),
        (expert_count, hidden, model_width),
        (expert_count, hidden, model_width),
    ]
    vmem = pl.BlockSpec(memory_space=pltpu.VMEM)
    return pl.pallas_call(
        functools.partial(results_kernel, tap_count, states, coef_count, dt_rank, expert_count),
        in_specs=[vmem] * len(parts),
        out_specs=[vmem] * (len(shapes) + 1),
        out_shape=[jax.ShapeDtypeStruct((own_rows, model_width), jnp.bfloat16)]
        + [jax.ShapeDtypeStruct(shape, f32) for shape in shapes],
        compiler_params=pltpu.CompilerParams(vmem_limit_bytes=62 << 20),
        cost_estimate=pl.CostEstimate(flops=1000, bytes_accessed=1000, transcendentals=0),
    )(*parts)


def norm_rows(values, gain_row):
    return values * lax.rsqrt(jnp.mean(values * values, -1, keepdims=True) + eps_norm) * gain_row


def matmul(first_op, second_op):
    return jnp.dot(first_op, second_op, preferred_element_type=jnp.float32)


def matmul_nt(first_op, second_op):
    return lax.dot_general(
        first_op, second_op, (((1,), (1,)), ((), ())), preferred_element_type=jnp.float32
    )


def matmul_tn(first_op, second_op):
    return lax.dot_general(
        first_op, second_op, (((0,), (0,)), ((), ())), preferred_element_type=jnp.float32
    )


def low_bits(value):
    return value.astype(jnp.bfloat16)


def swap_low(value, k):
    count = lax.axis_size("seq")
    return lax.ppermute(value, "seq", [(s, s ^ k) for s in range(count)])


def turn_high(value, k):
    count = lax.axis_size("seq")
    return lax.ppermute(value, "seq", [(s, (s + split * k) % count) for s in range(count)])


def from_high(value, k):
    count = lax.axis_size("seq")
    pairs = [(s, s + split * k) for s in range(count) if 0 <= s + split * k < count]
    return lax.ppermute(value, "seq", pairs)


def swap_core(value):
    return lax.ppermute(value, "grp", [(0, 1), (1, 0)])


def high_groups():
    count = lax.axis_size("seq")
    return [[h * split + l for h in range(count // split)] for l in range(split)]


def gather_low(value):
    low = lax.axis_index("seq") % split
    first_bit, second_bit = low % 2 == 1, low // 2 == 1
    own, one, two, three = [value] + [swap_low(value, k) for k in range(1, split)]
    a, b = jnp.where(first_bit, one, own), jnp.where(first_bit, own, one)
    c, d = jnp.where(first_bit, three, two), jnp.where(first_bit, two, three)
    pieces = [
        jnp.where(second_bit, c, a),
        jnp.where(second_bit, d, b),
        jnp.where(second_bit, a, c),
        jnp.where(second_bit, b, d),
    ]
    return jnp.concatenate(pieces, 0)


def scatter_low(partial):
    low = lax.axis_index("seq") % split
    rows = partial.shape[0] // split

    def block(at):
        return lax.dynamic_slice_in_dim(partial, at * rows, rows, 0)

    arrived = [swap_low(low_bits(block(low ^ k)), k) for k in range(1, split)]
    return sum(a.astype(jnp.float32) for a in [block(low)] + arrived)


def sum_low(partial):
    low_partial = low_bits(partial)
    arrived = [swap_low(low_partial, k) for k in range(1, split)]
    return partial + sum(a.astype(jnp.float32) for a in arrived)


def gather_high(value):
    high_count = lax.axis_size("seq") // split
    if high_count > 4:
        return lax.all_gather(value, "seq", axis_index_groups=high_groups())
    high = lax.axis_index("seq") // split
    turned = [turn_high(value, k) for k in range(1, high_count)]
    line = turned[::-1] + [value] + turned[::-1]
    return lax.dynamic_slice_in_dim(jnp.stack(line), high_count - 1 - high, high_count, 0)


def gather_core(own):
    full = jnp.stack([own, swap_core(own)])
    return full.reshape((-1,) + own.shape[1:])


def after(value, *others):
    return lax.optimization_barrier((value,) + others)[0]


def pad_rows(value, rows):
    return jnp.pad(value, ((0, rows - value.shape[0]), (0, 0)))


def fold_core(partial, rows):
    high_count = lax.axis_size("seq") // split
    blocks = partial.reshape(2, high_count, rows, partial.shape[-1])
    arrived = swap_core(low_bits(blocks[1]))
    return low_bits(blocks[0].astype(jnp.float32) + arrived.astype(jnp.float32))


def fold_high(mine):
    high_count = lax.axis_size("seq") // split
    if high_count > 4:
        return lax.psum_scatter(
            mine.astype(jnp.float32), "seq", scatter_dimension=0, axis_index_groups=high_groups()
        )
    high = lax.axis_index("seq") // split

    def block(at):
        return lax.dynamic_index_in_dim(mine, at % high_count, 0, False)

    arrived = [turn_high(block(high + k), k) for k in range(1, high_count)]
    return sum(a.astype(jnp.float32) for a in [block(high)] + arrived)


def sum_all(partial):
    high_count = lax.axis_size("seq") // split
    total = partial + swap_core(partial)
    step = 1
    while step < high_count * split:
        total = total + swap_low(total, step)
        step *= 2
    return total


def entering_state(grow, state, reverse):
    high_count = lax.axis_size("seq") // split
    packed = jnp.concatenate([grow, state], 0)
    states = grow.shape[0]
    if high_count > 4:
        high = lax.axis_index("seq") // split
        every = lax.all_gather(packed, "seq", axis_index_groups=high_groups())

        def one(turn, total):
            source = high_count - 1 - turn if reverse else turn
            piece = lax.dynamic_index_in_dim(every, source, 0, False)
            return piece[states:] + piece[:states] * total

        ahead = high_count - 1 - high if reverse else high
        return lax.fori_loop(0, ahead, one, jnp.zeros_like(state))
    total = jnp.zeros_like(state)
    near = [from_high(packed, -k if reverse else k) for k in range(1, high_count)]
    for piece in near[::-1]:
        total = piece[states:] + piece[:states] * total
    return total


def shards_general(
    tokens,
    routes,
    lengths,
    grad_out,
    norm_gains,
    router,
    in_weight,
    conv_weight,
    x_weight,
    dt_weight,
    dt_bias,
    a_log,
    skip_gain,
    out_weight,
    expert_in,
    expert_out,
):
    channels, tap_count = conv_weight.shape
    dt_rank = dt_weight.shape[1]
    states = a_log.shape[1]
    expert_count, hidden, model_width = expert_in.shape
    own_rows = tokens.shape[0]
    row_count = own_rows * split
    high_count = lax.axis_size("seq") // split
    low = lax.axis_index("seq") % split
    high = lax.axis_index("seq") // split
    coef_count = dt_rank + 2 * states
    channel_rows = -(-channels // 16) * 16
    width = 2 * high_count * channel_rows
    hidden_rows = expert_count * hidden
    small_width = -(-(coef_count + dt_rank + tap_count + 2 + states) // lanes) * lanes

    small = jnp.concatenate(
        [x_weight, dt_weight, conv_weight, dt_bias[:, None], a_log, skip_gain[:, None]], 1
    )
    small = jnp.pad(small, ((0, 0), (0, small_width - small.shape[1])))
    inputs = tokens.astype(jnp.float32)
    edge = 16
    halo = from_high(tokens[own_rows - edge :], 1).astype(jnp.float32)
    normed_own = low_bits(norm_rows(jnp.concatenate([inputs, halo], 0), norm_gains[0]))
    payload = pad_rows(jnp.concatenate([in_weight[0], small], 1), channel_rows)
    first_full = gather_core(gather_high(payload)).reshape(width, -1)
    normed = gather_low(normed_own).reshape(split, own_rows + edge, model_width)
    normed_edge = normed[split - 1, own_rows:]
    normed = normed[:, :own_rows].reshape(row_count, model_width)
    first_in, small_full = first_full[:, :model_width], first_full[:, model_width:]
    x_full = small_full[:, :coef_count]
    at = coef_count
    dt_full = small_full[:, at : at + dt_rank]
    at = at + dt_rank
    conv_taps = small_full[:, at : at + tap_count].astype(jnp.float32)
    at = at + tap_count
    bias_vals = small_full[:, at].astype(jnp.float32)
    at = at + 1
    decay_rate = -jnp.exp(small_full[:, at : at + states].astype(jnp.float32)).T
    at = at + states
    skip_vals = small_full[:, at].astype(jnp.float32)
    rate = decay_rate * log2e

    early_part = jnp.concatenate(
        [
            pad_rows(in_weight[1], channel_rows),
            pad_rows(out_weight, channel_rows),
            expert_in[0],
        ],
        0,
    )
    early_part = gather_high(after(early_part, first_full))
    routed_part = jnp.concatenate(
        [grad_out, routes[:, None].astype(jnp.float32) * jnp.ones((1, lanes), jnp.float32)], 1
    )
    routed_part = gather_low(after(low_bits(routed_part), normed))
    grad_rows = routed_part[:, :model_width]
    routes_all = routed_part[:, model_width : model_width + 1].astype(jnp.int32)
    late_part = jnp.concatenate(
        [expert_in[1:].reshape(-1, model_width), expert_out.reshape(-1, model_width)], 0
    )

    place = high * row_count + jnp.arange(row_count, dtype=jnp.int32)
    first_len = lengths[0, 0]
    offset = jnp.where(place < first_len, place, place - first_len)
    reset = jnp.where(offset[:, None] == 0, 1e30, 0.0) * jnp.ones((1, lanes), jnp.float32)
    valid_rows = [
        (offset >= tap_count - 1 - k).astype(jnp.float32)[:, None] for k in range(tap_count)
    ]

    all_input = low_bits(matmul_nt(jnp.concatenate([normed_edge, normed], 0), first_in))
    conv_input = all_input[edge:]
    window = all_input[edge - (tap_count - 1) :].astype(jnp.float32)
    conv_sum = sum(
        conv_taps[:, k] * window[k : k + row_count] * valid_rows[k] for k in range(tap_count)
    )
    mixed_in = low_bits(jax.nn.silu(conv_sum))
    mixed_val = mixed_in.astype(jnp.float32)
    coef_pad = jnp.pad(x_full, ((0, 0), (0, lanes - coef_count)))
    coef_rows = sum_low(matmul(mixed_in, coef_pad))
    dt_low = low_bits(coef_rows[:, :dt_rank])
    dt_pre = matmul_nt(dt_low, dt_full) + bias_vals
    step_size = jax.nn.softplus(dt_pre)
    drive = step_size * mixed_val
    first_b, first_c = dt_rank, dt_rank + states
    peers = high_count - 1 if high_count <= 4 else 0
    grow, state, enter = scan_ends(
        step_size, reset, drive, coef_rows, rate, first_b, False, peers
    )
    slice_grow = grow[:, subs - 1]
    if not peers:
        enter = entering_state(slice_grow, state[:, subs - 1], False)
    enter, early_part, late_part = lax.optimization_barrier((enter, early_part, late_part))
    early_full = gather_core(early_part)
    late_part = gather_high(late_part)
    y_scan, start, hist = scan_forward(
        step_size, reset, drive, coef_rows, rate, grow, state, enter, first_b, first_c
    )
    y_scan, early_full = lax.optimization_barrier((y_scan, early_full))
    second_in = early_full[:, :channel_rows].reshape(width, model_width)
    out_full = early_full[:, channel_rows : 2 * channel_rows].reshape(width, model_width)
    z_gate = matmul_nt(normed, second_in)
    y_value = y_scan + skip_vals * mixed_val
    gate_z = jax.nn.silu(z_gate)
    gated = low_bits(y_value * gate_z)
    resid = inputs + scatter_low(matmul(gated, out_full))

    resid, late_part = lax.optimization_barrier((resid, late_part))
    late_full = gather_core(late_part)
    second_own = low_bits(norm_rows(resid, norm_gains[1]))
    second = gather_low(second_own)

    def gate_of(rows, row_routes):
        logits = matmul(rows, router)
        chosen = row_routes == jnp.arange(expert_count, dtype=jnp.int32)[None, :]
        chosen = chosen.astype(jnp.float32)
        probs = jax.nn.softmax(logits, -1)
        return logits, chosen, jnp.sum(probs * chosen, -1, keepdims=True)

    gate_rows = gate_of(second, routes_all)[2]
    routed = low_bits(gate_rows * grad_rows.astype(jnp.float32))
    parts = [(early_full[:, 2 * channel_rows :], 0)]
    parts += [(late_full, e * hidden) for e in range(2 * expert_count - 1)]
    step_rows = hidden
    if hidden % 16:
        step_rows = 2 * high_count * hidden // 4
        parts = [
            (w[:, a : a + hidden].reshape(4, step_rows, model_width), 0) for w, a in parts
        ]
    sums, hidden_grads = run_experts(
        second, routed, routed_part[:, model_width:].astype(jnp.float32), parts, step_rows
    )
    if hidden % 16:
        pieces = hidden_grads.reshape(4, 2 * expert_count, -1, hidden, model_width)
        hidden_grads = pieces.swapaxes(1, 2).reshape(-1, 2 * hidden_rows, model_width)
    hidden_mine = fold_core(hidden_grads, 2 * hidden_rows)
    sums = scatter_low(sums)
    expert_y, d_second = sums[:, :model_width], sums[:, model_width:]
    d_second, hidden_mine = lax.optimization_barrier((d_second, hidden_mine))
    cut = hidden_rows * 2 // 3
    hidden_early = fold_high(hidden_mine[:, :cut])
    hidden_mine = hidden_mine[:, cut:]
    logits, chosen, gate_own = gate_of(second_own, routes[:, None])
    mixed_out = low_bits(resid + gate_own * expert_y)
    d_gate = jnp.sum(expert_y * grad_out, -1, keepdims=True)
    _, soft_pull = jax.vjp(lambda v: jax.nn.softmax(v, -1), logits)
    d_logits = low_bits(soft_pull(chosen * d_gate)[0])
    grad_router = matmul_tn(d_logits, second_own)
    d_second = d_second + matmul_nt(d_logits, router)
    _, norm_pull_two = jax.vjp(norm_rows, resid, norm_gains[1])
    d_resid_norm, d_gain_two = norm_pull_two(d_second)
    d_resid = grad_out + d_resid_norm

    g_branch = gather_low(low_bits(d_resid))
    d_gated = matmul_nt(g_branch, out_full)
    d_y = d_gated * gate_z
    _, silu_pull = jax.vjp(jax.nn.silu, z_gate)
    d_z = silu_pull(d_gated * y_value)[0]
    gate_grads = jnp.concatenate(
        [matmul_tn(low_bits(d_z), normed), matmul_tn(gated, g_branch)], 1
    )
    gate_mine = fold_core(gate_grads, channel_rows)
    back_grow, back_state, back_enter = scan_ends(
        step_size, reset, d_y, coef_rows, rate, first_c, True, peers
    )
    if not peers:
        back_enter = entering_state(slice_grow, back_state[:, 0], True)
    back_enter, hidden_mine = lax.optimization_barrier((back_enter, hidden_mine))
    hidden_late = fold_high(hidden_mine)
    scaled_sum, in_sum, rate_sum, d_in_coef, d_out_coef = scan_backward(
        step_size,
        reset,
        drive,
        d_y,
        coef_rows,
        rate,
        start,
        hist,
        back_grow,
        back_state,
        back_enter,
        first_b,
        first_c,
    )
    d_step = scaled_sum + in_sum * mixed_val
    d_mixed = skip_vals * d_y + in_sum * step_size
    grad_skip = jnp.sum(d_y * mixed_val, 0)
    d_dt = d_step * jax.nn.sigmoid(dt_pre)
    grad_bias = jnp.sum(d_dt, 0)
    g_dt = low_bits(d_dt)
    grad_dt = matmul_tn(g_dt, dt_low)
    part_coef = jnp.concatenate([matmul(g_dt, dt_full), d_in_coef, d_out_coef], 1)
    part_coef = jnp.pad(part_coef, ((0, 0), (0, lanes - coef_count)))
    g_coef = low_bits(sum_low(part_coef)[:, :coef_count])
    grad_x = matmul_tn(mixed_in, g_coef)
    d_mixed = d_mixed + matmul_nt(g_coef, x_full)
    _, conv_pull = jax.vjp(jax.nn.silu, conv_sum)
    d_conv = conv_pull(d_mixed)[0]
    grad_conv = jnp.stack(
        [jnp.sum(d_conv * valid_rows[k] * window[k : k + row_count], 0) for k in range(tap_count)],
        1,
    )
    d_window = sum(
        jnp.pad(conv_taps[:, k] * d_conv * valid_rows[k], ((k, tap_count - 1 - k), (0, 0)))
        for k in range(tap_count)
    )
    from_next = from_high(d_window[: tap_count - 1], -1)
    d_input = d_window[tap_count - 1 :] + jnp.pad(
        from_next, ((row_count - (tap_count - 1), 0), (0, 0))
    )
    g_in = low_bits(d_input)
    g_in, hidden_late, gate_mine = lax.optimization_barrier((g_in, hidden_late, gate_mine))
    hidden_own = jnp.concatenate([hidden_early, hidden_late], 0)
    gate_own_grads = fold_high(gate_mine)
    g_z = low_bits(d_z)
    d_normed = scatter_low(matmul(g_in, first_in) + matmul(g_z, second_in))
    _, norm_pull_one = jax.vjp(norm_rows, inputs, norm_gains[0])
    d_inputs, d_gain_one = norm_pull_one(d_normed)
    grad_tokens = d_resid + d_inputs

    rest = jnp.concatenate(
        [grad_x, grad_dt, grad_conv, grad_bias[:, None], rate_sum.T, grad_skip[:, None]], 1
    )
    rest = jnp.pad(rest, ((0, 0), (0, small_width - rest.shape[1])))
    first_own = fold_high(
        fold_core(jnp.concatenate([matmul_tn(g_in, normed), rest], 1), channel_rows)
    )[:channels]
    rest_own = first_own[:, model_width:]
    gate_own_grads = gate_own_grads[:channels]
    sums = sum_all(jnp.concatenate([jnp.stack([d_gain_one, d_gain_two]), grad_router], 0))
    ends = [0]
    for count in (coef_count, dt_rank, tap_count, 1, states, 1):
        ends.append(ends[-1] + count)
    grad_x, grad_dt, grad_conv, grad_bias, grad_alog, grad_skip = (
        rest_own[:, a:b] for a, b in zip(ends[:-1], ends[1:], strict=True)
    )
    return (
        mixed_out,
        grad_tokens,
        sums[:2],
        sums[2:].T,
        jnp.stack([first_own[:, :model_width], gate_own_grads[:, :model_width]]),
        grad_conv,
        grad_x,
        grad_dt,
        grad_bias[:, 0],
        grad_alog,
        grad_skip[:, 0],
        gate_own_grads[:, model_width:],
        hidden_own[:hidden_rows].reshape(expert_count, hidden, model_width),
        hidden_own[hidden_rows:].reshape(expert_count, hidden, model_width),
    )


def shards_plane(
    tokens,
    routes,
    lengths,
    grad_out,
    norm_gains,
    router,
    in_weight,
    conv_weight,
    x_weight,
    dt_weight,
    dt_bias,
    a_log,
    skip_gain,
    out_weight,
    expert_in,
    expert_out,
):
    channels, tap_count = conv_weight.shape
    dt_rank, states = dt_weight.shape[1], a_log.shape[1]
    expert_count, hidden, _ = expert_in.shape
    coef_count = dt_rank + 2 * states
    (
        first_full, gate_full, hidden_full, normed, routed, input_all, coef, step, z, y, gated, start,
        resid, second, rows, spread_in, spread_out, drive,
    ) = run_mixer(
        tokens, norm_gains, lengths, in_weight, conv_weight.T, x_weight, dt_weight, dt_bias[None], a_log.T,
        skip_gain[None], out_weight, expert_in, expert_out, grad_out, routes[None],
    )
    mixed_out, d_resid, small_sums, dy, gz, later, mine, early, gate_mine, mid = run_turn(
        second, routed, hidden_full, expert_out, router.T, resid, grad_out, norm_gains,
        gate_full, normed, spread_out, step, z, y, gated, rows, states, expert_count,
    )
    grad_tokens, sums, late, second_own, out_own, first_own = run_back(
        dy, gz, later, mine, gate_mine, first_full, gate_full, normed, input_all, coef, step, start,
        rows, d_resid, tokens, norm_gains, small_sums, lengths, spread_in, spread_out, drive, dt_rank,
        states, tap_count,
    )
    (
        mixed_out, grad_tokens, grad_gains, grad_router, grad_in, grad_conv, grad_x, grad_dt, grad_bias,
        grad_alog, grad_skip, grad_out_w, grad_up, grad_down,
    ) = run_results(
        (mixed_out, grad_tokens, sums, early, mid, late, second_own, out_own, first_own),
        channels, tap_count, states, coef_count, dt_rank, expert_count, hidden,
    )
    return (
        mixed_out,
        grad_tokens,
        grad_gains,
        grad_router.T,
        grad_in,
        grad_conv.T,
        grad_x,
        grad_dt,
        grad_bias[0],
        grad_alog.T,
        grad_skip[0],
        grad_out_w,
        grad_up,
        grad_down,
    )


def solution(mesh):
    both = ("grp", "seq")
    in_specs = (
        P(both, None),
        P(both),
        P("grp", None),
        P(both, None),
        P(),
        P(),
        P(None, both, None),
        P(both, None),
        P(both, None),
        P(both, None),
        P(both),
        P(both, None),
        P(both),
        P(both, None),
        P(None, both, None),
        P(None, both, None),
    )
    out_specs = (
        P(both, None),
        P(both, None),
        P(),
        P(),
        P(None, both, None),
        P(both, None),
        P(both, None),
        P(both, None),
        P(both),
        P(both, None),
        P(both),
        P(both, None),
        P(None, both, None),
        P(None, both, None),
    )
    shards = shards_plane if mesh.shape["seq"] == split * split else shards_general
    return jax.shard_map(shards, mesh=mesh, in_specs=in_specs, out_specs=out_specs, check_vma=False)
```

```python
import functools
import math

import jax
import jax.numpy as jnp
from jax import lax
from jax.experimental import pallas as pl
from jax.experimental.pallas import tpu as pltpu
from jax.sharding import PartitionSpec as P

eps_norm = 1e-05
split = 4
lanes = 128
subs = 8
log2e = 1.4426950408889634


def spread(coef_ref, first, spread_ref, steps, states):
    def one(s, _):
        rows = coef_ref[pl.ds(s, subs, stride=steps), :]
        for n in range(states):
            spread_ref[s, n] = jnp.broadcast_to(rows[:, first + n : first + n + 1], (subs, lanes))
        return 0

    lax.fori_loop(0, steps, one, 0, unroll=8)


def chain_rows(grow, state, reverse):
    row = lax.broadcasted_iota(jnp.int32, (subs, lanes), 0)
    shift = 1
    while shift < subs:
        turn = subs - shift if reverse else shift
        has = row < subs - shift if reverse else row >= shift
        near_grow = jnp.where(has, pltpu.roll(grow, turn, 0), 1.0)
        near_state = jnp.where(has, pltpu.roll(state, turn, 0), 0.0)
        state = state + grow * near_state
        grow = grow * near_grow
        shift *= 2
    return grow, state


def ends_kernel(
    first, reverse, states, steps, peers,
    delta_ref, reset_ref, drive_ref, coef_ref, rate_ref,
    grow_ref, state_ref, enter_ref,
    spread_ref, send_ref, arrive_ref, send_sem, arrive_sem,
):
    tile = pl.program_id(0)
    tiles = pl.num_programs(0)
    place = lax.axis_index("seq")
    high, low, core = place // split, place % split, lax.axis_index("grp")

    def other(k):
        return (core, lax.rem(high + (peers + 1 - k if reverse else k), peers + 1) * split + low)

    def copy_to(k, j):
        return pltpu.make_async_remote_copy(
            src_ref=send_ref.at[j],
            dst_ref=arrive_ref.at[k - 1, j],
            send_sem=send_sem.at[k - 1, j],
            recv_sem=arrive_sem.at[k - 1, j],
            device_id=other(k),
            device_id_type=pl.DeviceIdType.MESH,
        )

    @pl.when(tile == 0)
    def _():
        if peers:
            barrier = pltpu.get_barrier_semaphore()
            for k in range(1, peers + 1):
                pl.semaphore_signal(
                    barrier, inc=1, device_id=other(k), device_id_type=pl.DeviceIdType.MESH
                )
        spread(coef_ref, first, spread_ref, steps, states)

    rates = [jnp.broadcast_to(rate_ref[n : n + 1, :], (subs, lanes)) for n in range(states)]

    def one(turn, carry):
        s = steps - 1 - turn if reverse else turn
        total, held = carry
        step = delta_ref[pl.ds(s, subs, stride=steps), :] + reset_ref[pl.ds(s, subs, stride=steps), :]
        drive = drive_ref[pl.ds(s, subs, stride=steps), :]
        after = []
        for n in range(states):
            factor = jnp.exp2(step * rates[n])
            if reverse:
                after.append(factor * (held[n] + spread_ref[s, n] * drive))
            else:
                after.append(factor * held[n] + spread_ref[s, n] * drive)
        return total + step, tuple(after)

    zero = jnp.zeros((subs, lanes), jnp.float32)
    total, held = lax.fori_loop(0, steps, one, (zero, (zero,) * states), unroll=2)
    last = 0 if reverse else subs - 1
    for n in range(states):
        grow, state = chain_rows(jnp.exp2(total * rates[n]), held[n], reverse)
        grow_ref[n] = grow
        state_ref[n] = state
        if peers:
            send_ref[tile, n : n + 1] = grow[last : last + 1]
            send_ref[tile, states + n : states + n + 1] = state[last : last + 1]
    if not peers:
        enter_ref[...] = jnp.zeros_like(enter_ref)
        return

    @pl.when(tile == 0)
    def _():
        pl.semaphore_wait(pltpu.get_barrier_semaphore(), peers)

    for k in range(1, peers + 1):
        copy_to(k, tile).start()

    @pl.when(tile == tiles - 1)
    def _():
        for j in range(enter_ref.shape[1] // lanes):
            total = jnp.zeros((states, lanes), jnp.float32)
            for k in range(peers, 0, -1):
                copy_to(k, j).wait()
                piece = arrive_ref[k - 1, j]
                has = high + k <= peers if reverse else high >= k
                total = jnp.where(has, piece[states:] + piece[:states] * total, 0.0)
            enter_ref[:, j * lanes : (j + 1) * lanes] = total


def scan_ends(delta, reset, drive, coef, rate, first, reverse, peers):
    row_count, width = delta.shape
    states = rate.shape[0]
    steps = row_count // subs
    tiles = width // lanes
    column = pl.BlockSpec((row_count, lanes), lambda j: (0, j))
    whole = pl.BlockSpec((row_count, lanes), lambda j: (0, 0))
    ends = pl.BlockSpec((states, subs, lanes), lambda j: (0, 0, j))
    params = dict(vmem_limit_bytes=48 << 20)
    if peers:
        params.update(collective_id=2 if reverse else 1, has_side_effects=True)
    slots = max(peers, 1)
    return pl.pallas_call(
        functools.partial(ends_kernel, first, reverse, states, steps, peers),
        grid=(tiles,),
        in_specs=[column, whole, column, whole, pl.BlockSpec((states, lanes), lambda j: (0, j))],
        out_specs=[ends, ends, pl.BlockSpec((states, width), lambda j: (0, 0))],
        out_shape=[jax.ShapeDtypeStruct((states, subs, width), jnp.float32)] * 2
        + [jax.ShapeDtypeStruct((states, width), jnp.float32)],
        scratch_shapes=[
            pltpu.VMEM((steps, states, subs, lanes), jnp.float32),
            pltpu.VMEM((tiles, 2 * states, lanes), jnp.float32),
            pltpu.VMEM((slots, tiles, 2 * states, lanes), jnp.float32),
            pltpu.SemaphoreType.DMA((slots, tiles)),
            pltpu.SemaphoreType.DMA((slots, tiles)),
        ],
        compiler_params=pltpu.CompilerParams(**params),
        cost_estimate=pl.CostEstimate(flops=1000, bytes_accessed=1000, transcendentals=0),
    )(delta, reset, drive, coef, rate)


def forward_kernel(first_in, first_out, states, steps, delta_ref, reset_ref, drive_ref, coef_ref, rate_ref, grow_ref, state_ref, enter_ref, y_ref, start_ref, hist_ref, in_ref, out_ref):
    @pl.when(pl.program_id(0) == 0)
    def _():
        spread(coef_ref, first_in, in_ref, steps, states)
        spread(coef_ref, first_out, out_ref, steps, states)

    rates = [jnp.broadcast_to(rate_ref[n : n + 1, :], (subs, lanes)) for n in range(states)]
    row = lax.broadcasted_iota(jnp.int32, (subs, lanes), 0)
    held = []
    for n in range(states):
        near_grow = jnp.where(row >= 1, pltpu.roll(grow_ref[n], 1, 0), 1.0)
        near_state = jnp.where(row >= 1, pltpu.roll(state_ref[n], 1, 0), 0.0)
        start = near_state + near_grow * jnp.broadcast_to(enter_ref[n : n + 1, :], (subs, lanes))
        start_ref[n] = start
        held.append(start)

    def one(s, held):
        step = delta_ref[pl.ds(s, subs, stride=steps), :] + reset_ref[pl.ds(s, subs, stride=steps), :]
        drive = drive_ref[pl.ds(s, subs, stride=steps), :]
        after = []
        y = jnp.zeros((subs, lanes), jnp.float32)
        for n in range(states):
            now = jnp.exp2(step * rates[n]) * held[n] + in_ref[s, n] * drive
            hist_ref[0, s, n] = now
            y = y + out_ref[s, n] * now
            after.append(now)
        y_ref[pl.ds(s, subs, stride=steps), :] = y
        return tuple(after)

    lax.fori_loop(0, steps, one, tuple(held), unroll=2)


def scan_forward(delta, reset, drive, coef, rate, grow, state, enter, first_in, first_out):
    row_count, width = delta.shape
    states = rate.shape[0]
    steps = row_count // subs
    tiles = width // lanes
    column = pl.BlockSpec((row_count, lanes), lambda j: (0, j))
    whole = pl.BlockSpec((row_count, lanes), lambda j: (0, 0))
    ends = pl.BlockSpec((states, subs, lanes), lambda j: (0, 0, j))
    per_state = pl.BlockSpec((states, lanes), lambda j: (0, j))
    return pl.pallas_call(
        functools.partial(forward_kernel, first_in, first_out, states, steps),
        grid=(tiles,),
        in_specs=[column, whole, column, whole, per_state, ends, ends, per_state],
        out_specs=[column, ends, pl.BlockSpec((1, steps, states, subs, lanes), lambda j: (j, 0, 0, 0, 0))],
        out_shape=[
            jax.ShapeDtypeStruct((row_count, width), jnp.float32),
            jax.ShapeDtypeStruct((states, subs, width), jnp.float32),
            jax.ShapeDtypeStruct((tiles, steps, states, subs, lanes), jnp.float32),
        ],
        scratch_shapes=[pltpu.VMEM((steps, states, subs, lanes), jnp.float32)] * 2,
        compiler_params=pltpu.CompilerParams(vmem_limit_bytes=48 << 20),
        cost_estimate=pl.CostEstimate(flops=1000, bytes_accessed=1000, transcendentals=0),
    )(delta, reset, drive, coef, rate, grow, state, enter)


def backward_kernel(first_in, first_out, states, steps, delta_ref, reset_ref, drive_ref, dy_ref, coef_ref, rate_ref, start_ref, hist_ref, grow_ref, state_ref, enter_ref, q_ref, r_ref, rsum_ref, din_ref, dout_ref, in_ref, out_ref, ain_ref, aout_ref):
    tile = pl.program_id(0)

    @pl.when(tile == 0)
    def _():
        spread(coef_ref, first_in, in_ref, steps, states)
        spread(coef_ref, first_out, out_ref, steps, states)
        ain_ref[...] = jnp.zeros_like(ain_ref)
        aout_ref[...] = jnp.zeros_like(aout_ref)

    row = lax.broadcasted_iota(jnp.int32, (subs, lanes), 0)
    rates = [jnp.broadcast_to(rate_ref[n : n + 1, :], (subs, lanes)) for n in range(states)]
    later = []
    for n in range(states):
        near_grow = jnp.where(row < subs - 1, pltpu.roll(grow_ref[n], subs - 1, 0), 1.0)
        near_state = jnp.where(row < subs - 1, pltpu.roll(state_ref[n], subs - 1, 0), 0.0)
        later.append(near_state + near_grow * jnp.broadcast_to(enter_ref[n : n + 1, :], (subs, lanes)))

    def at(s, load_before, carry):
        later, sums = carry
        delta = delta_ref[pl.ds(s, subs, stride=steps), :]
        step = delta + reset_ref[pl.ds(s, subs, stride=steps), :]
        drive = drive_ref[pl.ds(s, subs, stride=steps), :]
        dy = dy_ref[pl.ds(s, subs, stride=steps), :]
        q = jnp.zeros((subs, lanes), jnp.float32)
        r = jnp.zeros((subs, lanes), jnp.float32)
        after, sums_after = [], []
        for n in range(states):
            d_state = out_ref[s, n] * dy + later[n]
            back = jnp.exp2(step * rates[n]) * d_state
            scaled = back * load_before(n)
            sums_after.append(sums[n] + scaled * delta)
            q = q + scaled * rates[n]
            r = r + d_state * in_ref[s, n]
            ain_ref[s, n] += d_state * drive
            aout_ref[s, n] += hist_ref[0, s, n] * dy
            after.append(back)
        q_ref[pl.ds(s, subs, stride=steps), :] = q * (1.0 / log2e)
        r_ref[pl.ds(s, subs, stride=steps), :] = r
        return tuple(after), tuple(sums_after)

    zero = jnp.zeros((subs, lanes), jnp.float32)

    def one(turn, carry):
        s = steps - 1 - turn
        return at(s, lambda n: hist_ref[0, s - 1, n], carry)

    carry = lax.fori_loop(0, steps - 1, one, (tuple(later), (zero,) * states))
    _, sums = at(0, lambda n: start_ref[n], carry)
    for n in range(states):
        rsum_ref[n : n + 1, :] = jnp.sum(sums[n] * rates[n], 0, keepdims=True) * (1.0 / log2e)

    @pl.when(tile == pl.num_programs(0) - 1)
    def _():
        ones = jnp.ones((subs, lanes), jnp.bfloat16)

        def fold(ref, s):
            values = ref[s].reshape(states * subs, lanes)
            high = values.astype(jnp.bfloat16)
            low = (values - high.astype(jnp.float32)).astype(jnp.bfloat16)
            dims = (((1,), (1,)), ((), ()))
            return lax.dot_general(ones, high, dims, preferred_element_type=jnp.float32) + lax.dot_general(ones, low, dims, preferred_element_type=jnp.float32)

        def both(s, _):
            din_ref[pl.ds(s, 1), :] = fold(ain_ref, s)[:1]
            dout_ref[pl.ds(s, 1), :] = fold(aout_ref, s)[:1]
            return 0

        lax.fori_loop(0, steps, both, 0)


def scan_backward(delta, reset, drive, dy, coef, rate, start, hist, grow, state, enter, first_in, first_out):
    row_count, width = delta.shape
    states = rate.shape[0]
    steps = row_count // subs
    tiles = width // lanes
    column = pl.BlockSpec((row_count, lanes), lambda j: (0, j))
    whole = pl.BlockSpec((row_count, lanes), lambda j: (0, 0))
    ends = pl.BlockSpec((states, subs, lanes), lambda j: (0, 0, j))
    per_state = pl.BlockSpec((states, lanes), lambda j: (0, j))
    folded = pl.BlockSpec((steps, states * subs), lambda j: (0, 0))
    q, r, rsum, din, dout = pl.pallas_call(
        functools.partial(backward_kernel, first_in, first_out, states, steps),
        grid=(tiles,),
        in_specs=[column, whole, column, column, whole, per_state, ends, pl.BlockSpec((1, steps, states, subs, lanes), lambda j: (j, 0, 0, 0, 0)), ends, ends, per_state],
        out_specs=[column, column, per_state, folded, folded],
        out_shape=[
            jax.ShapeDtypeStruct((row_count, width), jnp.float32),
            jax.ShapeDtypeStruct((row_count, width), jnp.float32),
            jax.ShapeDtypeStruct((states, width), jnp.float32),
            jax.ShapeDtypeStruct((steps, states * subs), jnp.float32),
            jax.ShapeDtypeStruct((steps, states * subs), jnp.float32),
        ],
        scratch_shapes=[pltpu.VMEM((steps, states, subs, lanes), jnp.float32)] * 4,
        compiler_params=pltpu.CompilerParams(vmem_limit_bytes=56 << 20),
        cost_estimate=pl.CostEstimate(flops=1000, bytes_accessed=1000, transcendentals=0),
    )(delta, reset, drive, dy, coef, rate, start, hist, grow, state, enter)

    def unfold(folded_rows):
        return folded_rows.reshape(steps, states, subs).transpose(2, 0, 1).reshape(row_count, states)

    return q, r, rsum, unfold(din), unfold(dout)


def experts_kernel(
    expert_count, second_ref, routed_ref, route_ref, *refs
):
    weights_in, weights_out = refs[:expert_count], refs[expert_count : 2 * expert_count]
    sums_ref, grads_ref, y_ref, d_ref = refs[2 * expert_count :]
    step = pl.program_id(0)
    blocks, hidden, model_width = weights_in[0].shape
    rows = blocks * hidden

    @pl.when(step == 0)
    def _():
        y_ref[...] = jnp.zeros_like(y_ref)
        d_ref[...] = jnp.zeros_like(d_ref)

    up = jnp.concatenate([w[...].reshape(rows, model_width) for w in weights_in], 0)
    down = jnp.concatenate([w[...].reshape(rows, model_width) for w in weights_out], 0)
    second, routed = second_ref[...], routed_ref[...]
    pre = matmul_nt(second, up)
    column = lax.broadcasted_iota(jnp.int32, (1, expert_count * rows), 1)
    owner = jnp.zeros_like(column)
    for e in range(1, expert_count):
        owner = owner + (column >= e * rows).astype(jnp.int32)
    picked = route_ref[:, :1] == owner.astype(jnp.float32)
    half = 0.5 + 0.5 * lax.erf(pre * (0.5**0.5))
    bell = jnp.exp(-0.5 * pre * pre) * (1.0 / (2.0 * math.pi) ** 0.5)
    act = low_bits(jnp.where(picked, pre * half, 0.0))
    d_pre = low_bits(jnp.where(picked, matmul_nt(routed, down) * (half + pre * bell), 0.0))
    y_ref[...] += matmul(act, down)
    d_ref[...] += matmul(d_pre, up)
    grad_up = low_bits(matmul_tn(d_pre, second))
    grad_down = low_bits(matmul_tn(act, routed))
    for e in range(expert_count):
        for b in range(blocks):
            at = e * rows + b * hidden
            grads_ref[b, e * hidden : (e + 1) * hidden] = grad_up[at : at + hidden]
            to = (expert_count + e) * hidden
            grads_ref[b, to : to + hidden] = grad_down[at : at + hidden]

    @pl.when(step == pl.num_programs(0) - 1)
    def _():
        sums_ref[:, :model_width] = low_bits(y_ref[...])
        sums_ref[:, model_width:] = low_bits(d_ref[...])


def run_experts(second, routed, route_lanes, parts, hidden):
    row_count, model_width = second.shape
    expert_count = len(parts) // 2
    block_count = parts[0][0].shape[0]
    blocks = 2
    fixed = pl.BlockSpec((row_count, model_width), lambda i: (0, 0))

    def spec(first):
        return pl.BlockSpec((blocks, hidden, model_width), lambda i: (i, first // hidden, 0))

    return pl.pallas_call(
        functools.partial(experts_kernel, expert_count),
        grid=(block_count // blocks,),
        in_specs=[fixed, fixed, pl.BlockSpec((row_count, lanes), lambda i: (0, 0))]
        + [spec(first) for _, first in parts],
        out_specs=[
            pl.BlockSpec((row_count, 2 * model_width), lambda i: (0, 0)),
            pl.BlockSpec((blocks, 2 * expert_count * hidden, model_width), lambda i: (i, 0, 0)),
        ],
        out_shape=[
            jax.ShapeDtypeStruct((row_count, 2 * model_width), jnp.bfloat16),
            jax.ShapeDtypeStruct(
                (block_count, 2 * expert_count * hidden, model_width), jnp.bfloat16
            ),
        ],
        scratch_shapes=[pltpu.VMEM((row_count, model_width), jnp.float32)] * 2,
        compiler_params=pltpu.CompilerParams(vmem_limit_bytes=56 << 20),
        cost_estimate=pl.CostEstimate(flops=1000, bytes_accessed=1000, transcendentals=0),
    )(second, routed, route_lanes, *[w for w, _ in parts])


def kernel_place():
    place = lax.axis_index("seq")
    return lax.axis_index("grp"), place // split, place % split


def remote(src, dst, send_sem, arrive_sem, core, high, low):
    return pltpu.make_async_remote_copy(
        src_ref=src,
        dst_ref=dst,
        send_sem=send_sem,
        recv_sem=arrive_sem,
        device_id=(core, high * split + low),
        device_id_type=pl.DeviceIdType.MESH,
    )


def greet_all():
    core, high, low = kernel_place()
    barrier = pltpu.get_barrier_semaphore()
    others = [(core, lax.rem(high + k, split), low) for k in range(1, split)]
    others += [(core, high, lax.rem(low + k, split)) for k in range(1, split)]
    others += [(1 - core, high, low)]
    for c, h, l in others:
        pl.semaphore_signal(
            barrier, inc=1, device_id=(c, h * split + l), device_id_type=pl.DeviceIdType.MESH
        )
    return len(others)


def plane_copies(src_of, dst, sems, slot_by_sender):
    core, high, low = kernel_place()
    copies = []
    for k in range(1, split):
        to = lax.rem(low + k, split)
        slot = low if slot_by_sender else k - 1
        copies.append(
            remote(src_of(to, k), dst.at[slot], sems.at[0, k - 1], sems.at[1, k - 1], core, high, to)
        )
    return copies


def at_ends():
    _, high, _ = kernel_place()
    return (high == 0) | (high == split - 1)


def line_copies(src, dst_of, sems, both=False):
    core, high, low = kernel_place()
    return [
        remote(
            src, dst_of(high), sems.at[0, k - 1], sems.at[1, k - 1], core, lax.rem(high + k, split), low
        )
        for k in ((1, 2, 3) if both else (1, 3))
    ]


def line_relay(dst_of, sems):
    core, high, low = kernel_place()
    block = lax.rem(high * 2, 3) + 3 * (high // 3)
    to = lax.rem(block + 2, split)
    return remote(dst_of(block), dst_of(block), sems.at[0, 1], sems.at[1, 1], core, to, low)


def line_arrived(src, dst_of, sems, k):
    core, high, low = kernel_place()
    at = lax.rem(high + split - k, split)
    remote(src, dst_of(at), sems.at[0, k - 1], sems.at[1, k - 1], core, high, low).wait_recv()


def core_copy(dst_of, sems, k):
    core, high, low = kernel_place()
    at = lax.rem(high + split - k, split)
    return remote(dst_of(at), dst_of(split + at), sems.at[0, k], sems.at[1, k], 1 - core, high, low)


def softplus_of(value):
    return jnp.maximum(value, 0.0) + jnp.log1p(jnp.exp(-jnp.abs(value)))


def sigmoid_of(value):
    return 1.0 / (1.0 + jnp.exp(-value))


def row_loop(count, size, body):
    def one(i, _):
        body(pl.multiple_of(i * size, size))
        return 0

    lax.fori_loop(0, count // size, one, 0)


def step_rows(s):
    return pl.ds(pl.multiple_of(s * subs, subs), subs)


def scan_one_way(j, reverse, states, steps, step_ref, drive_of, spread_ref, rates):
    def one(turn, carry):
        s = steps - 1 - turn if reverse else turn
        total, held = carry
        step = step_ref[j, step_rows(s), :]
        drive = drive_of(s)
        after_step = []
        for n in range(states):
            factor = jnp.exp2(step * rates[n])
            if reverse:
                after_step.append(factor * (held[n] + spread_ref[s, n] * drive))
            else:
                after_step.append(factor * held[n] + spread_ref[s, n] * drive)
        return total + step, tuple(after_step)

    zero = jnp.zeros((subs, lanes), jnp.float32)
    total, held = lax.fori_loop(0, steps, one, (zero, (zero,) * states), unroll=2)
    return [chain_rows(jnp.exp2(total * rates[n]), held[n], reverse) for n in range(states)]


def chain_enter(arrive_ref, j, states, reverse):
    _, high, _ = kernel_place()
    total = jnp.zeros((states, lanes), jnp.float32)
    for k in range(split - 1, 0, -1):
        piece = arrive_ref[k - 1, j]
        has = high + k < split if reverse else high >= k
        total = jnp.where(has, piece[states:] + piece[:states] * total, 0.0)
    return total


def tile_rates(rows_ref, j, states):
    decay = -jnp.exp(rows_ref[j, alog_row : alog_row + states, :])
    return decay


def ends_copies(send_ref, arrive_ref, sems, j, reverse):
    core, high, low = kernel_place()
    copies = []
    for k in range(1, split):
        to = lax.rem(high + split - k, split) if reverse else lax.rem(high + k, split)
        copies.append(
            remote(
                send_ref.at[j],
                arrive_ref.at[k - 1, j],
                sems.at[0, k - 1, j],
                sems.at[1, k - 1, j],
                core,
                to,
                low,
            )
        )
    return copies


tap_row = lanes - 24
bias_row = lanes - 20
skip_row = lanes - 19
alog_row = lanes - 16
early_hidden = 64


def mixer_kernel(
    dt_rank, states, tap_count,
    tokens_ref, gains_ref, lengths_ref, in_weight_ref, conv_weight_ref, x_weight_ref, dt_weight_ref,
    dt_bias_ref, a_log_ref, skip_ref, out_weight_ref, expert_in_ref, expert_out_ref, grad_ref,
    routes_ref,
    first_out, gate_out, hidden_ref, normed_out, routed_out, input_out, coef_out, step_out, z_out,
    y_out, gated_out, start_out, resid_ref, second_out, rows_out, in_out, out_out, drive_out,
    first_ref, gate_ref, normed_ref, edge_ref, routed_ref, input_ref, coef_ref, step_ref, z_ref,
    y_ref, gated_ref, start_ref, second_ref, rows_ref, c_ref, out_sems,
    in_ref, out_ref, drive_ref, mixed_ref, partial_ref, arrive_ref, coef_send_ref,
    coef_arrive_ref, send_ref, ends_ref, grow_ref, state_ref,
    a_sems, b_sems, c_sems, d_sems, a_core, b_core, c_core, d_core, token_sems, route_sems,
    second_sems, coef_sems, sum_sems, edge_send, edge_arrive, ends_sems, local_sem,
):
    core, high, low = kernel_place()
    own_rows, model_width = tokens_ref.shape
    row_count = own_rows * split
    steps = row_count // subs
    tiles = step_ref.shape[0]
    width = tiles * lanes
    edge = edge_ref.shape[0]
    first_b, first_c = dt_rank, dt_rank + states
    channels = in_weight_ref.shape[1]
    channel_rows = width // (2 * split)
    greeted = greet_all()
    stores = []

    def store(ref, out):
        copy = pltpu.make_async_copy(ref, out, out_sems.at[len(stores)])
        copy.start()
        stores.append(copy)

    def edge_copy(l):
        return remote(
            normed_ref.at[low, pl.ds(own_rows - edge, edge)],
            edge_ref,
            edge_send.at[l],
            edge_arrive,
            core,
            lax.rem(high + 1, split),
            l,
        )

    barrier = pltpu.get_barrier_semaphore()
    for k in range(1, split):
        pl.semaphore_signal(
            barrier,
            inc=1,
            device_id=(core, lax.rem(high + split - 1, split) * split + lax.rem(low + k, split)),
            device_id_type=pl.DeviceIdType.MESH,
        )
    greeted += split - 1
    tokens = tokens_ref[...].astype(jnp.float32)
    normed_ref[low] = low_bits(norm_rows(tokens, gains_ref[0:1, :]))
    gap = channel_rows - channels

    def filled(value):
        value = value.astype(jnp.float32)
        if gap:
            value = jnp.concatenate([value, jnp.zeros((gap, value.shape[1]), jnp.float32)], 0)
        return low_bits(value)

    def widened(value, first):
        at = lax.broadcasted_iota(jnp.int32, (value.shape[1], lanes), 0) + first
        to = lax.broadcasted_iota(jnp.int32, (value.shape[1], lanes), 1)
        return matmul(value, jnp.where(at == to, 1.0, 0.0).astype(jnp.bfloat16))

    first_ref[high, :, :model_width] = filled(in_weight_ref[0])
    first_ref[high, :, model_width + lanes :] = filled(widened(dt_weight_ref[...], 0))
    rows_ref[0] = jnp.zeros((lanes, lanes), jnp.float32)
    for row, ref in (
        (tap_row, conv_weight_ref), (bias_row, dt_bias_ref), (skip_row, skip_ref), (alog_row, a_log_ref)
    ):
        rows_ref[0, row : row + ref.shape[0], :channels] = ref[...].astype(jnp.float32)
    first_ref[high, :, model_width : model_width + lanes] = filled(
        widened(x_weight_ref[...], 0) + rows_ref[0].T[:channels]
    )
    pl.semaphore_wait(barrier, greeted)

    @pl.when((low == split - 1) & (high < split - 1))
    def _():
        for l in range(split):
            edge_copy(l).start()

    hidden_count = c_ref.shape[0]
    c_src = c_ref.at[pl.ds(0, early_hidden)]
    d_src = c_ref.at[pl.ds(early_hidden, hidden_count - early_hidden)]
    a_ref, b_ref, g_ref = first_ref.at[high], gate_ref.at[high], routed_ref.at[low]

    def a_dst(at):
        return first_ref.at[at]

    def b_dst(at):
        return gate_ref.at[at]

    def c_dst(at):
        return hidden_ref.at[at, pl.ds(0, early_hidden)]

    def d_dst(at):
        return hidden_ref.at[at, pl.ds(early_hidden, hidden_count - early_hidden)]

    token_copies = plane_copies(lambda to, k: normed_ref.at[low], normed_ref, token_sems, True)
    a_copies = line_copies(a_ref, a_dst, a_sems)
    b_copies = line_copies(b_ref, b_dst, b_sems)
    c_copies = line_copies(c_src, c_dst, c_sems)
    d_copies = line_copies(d_src, d_dst, d_sems)
    route_copies = plane_copies(lambda to, k: g_ref, routed_ref, route_sems, True)
    relays = [line_relay(a_dst, a_sems), line_relay(b_dst, b_sems)]
    relays += [line_relay(c_dst, c_sems), line_relay(d_dst, d_sems)]
    for copy in token_copies + a_copies:
        copy.start()

    def relay_from_end(i):
        @pl.when(at_ends())
        def _():
            relays[i].start()

    def relay_inside(i):
        @pl.when(jnp.logical_not(at_ends()))
        def _():
            relays[i].start()

    def arrived(src, dst_of, sems, core_sems, ks):
        for k in ks:
            line_arrived(src, dst_of, sems, k)
            copy = core_copy(dst_of, core_sems, k)
            copy.start()
            core_copies.append(copy)

    relay_from_end(0)
    core_copies = [core_copy(a_dst, a_core, 0)]
    core_copies[0].start()
    routed_ref[low, :, :model_width] = low_bits(grad_ref[...])
    routes = jnp.broadcast_to(routes_ref[...].astype(jnp.float32), (own_rows, own_rows)).T
    routed_ref[low, :, model_width:] = low_bits(routes)
    gate_ref[high, :channel_rows] = filled(in_weight_ref[1])
    gate_ref[high, channel_rows:] = filled(out_weight_ref[...])
    hidden = expert_in_ref.shape[1]
    for part in range(hidden_count // hidden):
        source = expert_out_ref if part % 2 else expert_in_ref
        c_ref[part * hidden : (part + 1) * hidden] = source[part // 2]
    local = pltpu.make_async_copy(c_ref, hidden_ref.at[high], local_sem)
    local.start()
    core_copies.append(core_copy(b_dst, b_core, 0))
    for copy in core_copies[1:] + route_copies:
        copy.start()

    first_len = lengths_ref[0, 0]

    def offsets(at, rows):
        place = high * row_count + at + lax.broadcasted_iota(jnp.int32, (rows, lanes), 0)
        return jnp.where(place < first_len, place, place - first_len)

    @pl.when(high == 0)
    def _():
        edge_ref[...] = jnp.zeros_like(edge_ref)

    arrived(a_ref, a_dst, a_sems, a_core, (1, 3))
    relay_inside(0)
    for copy in b_copies + c_copies:
        copy.start()
    local.wait()
    relay_from_end(1)
    relay_from_end(2)
    for copy in (core_copy(c_dst, c_core, 0), core_copy(d_dst, d_core, 0)):
        copy.start()
        core_copies.append(copy)
    for copy in token_copies:
        copy.wait()
    arrived(a_ref, a_dst, a_sems, a_core, (2,))

    @pl.when(high > 0)
    def _():
        edge_copy(0).wait_recv()

    @pl.when((low == split - 1) & (high < split - 1))
    def _():
        for l in range(split):
            edge_copy(l).wait_send()

    for k in range(split):
        core_copy(a_dst, a_core, k).wait_recv()

    weights = first_ref[:, :, :model_width].reshape(width, model_width)
    input_ref[:edge, :] = low_bits(matmul_nt(edge_ref[...], weights)).astype(jnp.float32)
    for l in range(split):
        block = low_bits(matmul_nt(normed_ref[l], weights)).astype(jnp.float32)
        input_ref[edge + l * own_rows : edge + (l + 1) * own_rows, :] = block
    store(first_ref, first_out)
    store(normed_ref, normed_out)
    store(input_ref, input_out)
    small = first_ref[:, :, model_width : model_width + lanes].reshape(width, lanes)
    small = small.astype(jnp.float32)
    for j in range(tiles):
        rows_ref[j] = small[j * lanes : (j + 1) * lanes].T

    store(rows_ref, rows_out)

    def convolve(at):
        offset = offsets(at, 32)
        for j in range(tiles):
            span = input_ref[pl.ds(at, 32 + edge), j * lanes : (j + 1) * lanes]
            conv_sum = jnp.zeros((32, lanes), jnp.float32)
            for k in range(tap_count):
                shift = edge - (tap_count - 1) + k
                term = rows_ref[j, tap_row + k : tap_row + k + 1, :] * span[shift : shift + 32]
                conv_sum = conv_sum + jnp.where(offset >= tap_count - 1 - k, term, 0.0)
            mixed_ref[pl.ds(at, 32), j * lanes : (j + 1) * lanes] = low_bits(
                conv_sum * sigmoid_of(conv_sum)
            )

    row_loop(row_count, 32, convolve)

    x_full = first_ref[:, :, model_width : model_width + lanes].reshape(width, lanes)
    part = matmul(mixed_ref[...], x_full)
    coef_ref[...] = part
    coef_send_ref[...] = low_bits(part)
    coef_copies = plane_copies(lambda to, k: coef_send_ref, coef_arrive_ref, coef_sems, False)
    for copy in coef_copies:
        copy.start()
    for copy in coef_copies:
        copy.wait()
    arrived(b_ref, b_dst, b_sems, b_core, (1, 3))
    relay_inside(1)
    total = coef_ref[...]
    for k in range(1, split):
        total = total + coef_arrive_ref[k - 1].astype(jnp.float32)
    coef_ref[...] = total
    dt_full = first_ref[:, :, model_width + lanes : model_width + 2 * lanes].reshape(width, lanes)

    def step_sizes(chunk):
        at = pl.multiple_of(chunk * steps, steps)
        pre = matmul_nt(low_bits(coef_ref[pl.ds(at, steps), :]), dt_full)
        reset = jnp.where(offsets(at, steps) == 0, 1e30, 0.0)
        rows = pl.ds(chunk, steps, stride=subs)
        for j in range(tiles):
            cols = slice(j * lanes, (j + 1) * lanes)
            step = softplus_of(pre[:, cols] + rows_ref[j, bias_row : bias_row + 1, :])
            step_ref[j, rows, :] = step + reset
            drive_ref[j, rows, :] = step * mixed_ref[pl.ds(at, steps), cols].astype(jnp.float32)

    lax.fori_loop(0, subs, lambda chunk, _: (step_sizes(chunk), 0)[1], 0)
    store(drive_ref, drive_out)
    store(coef_ref, coef_out)
    store(step_ref, step_out)
    spread(coef_ref, first_b, in_ref, steps, states)
    store(in_ref, in_out)

    def rates_of(j):
        values = -jnp.exp(rows_ref[j, alog_row : alog_row + states, :]) * log2e
        return [jnp.broadcast_to(values[n : n + 1, :], (subs, lanes)) for n in range(states)]

    def ends_of(j, _):
        found = scan_one_way(
            j,
            False,
            states,
            steps,
            step_ref,
            lambda s: drive_ref[j, step_rows(s), :],
            in_ref,
            rates_of(j),
        )
        for n, (grow, state) in enumerate(found):
            grow_ref[j, n] = grow
            state_ref[j, n] = state
            send_ref[j, n : n + 1] = grow[subs - 1 :]
            send_ref[j, states + n : states + n + 1] = state[subs - 1 :]
        for copy in ends_copies(send_ref, ends_ref, ends_sems, j, False):
            copy.start()
        return 0

    lax.fori_loop(0, tiles, ends_of, 0)
    arrived(c_src, c_dst, c_sems, c_core, (1, 3))
    relay_inside(2)
    for copy in d_copies:
        copy.start()
    relay_from_end(3)
    spread(coef_ref, first_c, out_ref, steps, states)
    store(out_ref, out_out)
    arrived(b_ref, b_dst, b_sems, b_core, (2,))
    row = lax.broadcasted_iota(jnp.int32, (subs, lanes), 0)

    def forward_of(j, _):
        for copy in ends_copies(send_ref, ends_ref, ends_sems, j, False):
            copy.wait()
        enter = chain_enter(ends_ref, j, states, False)
        rates = rates_of(j)
        held = []
        for n in range(states):
            near_grow = jnp.where(row >= 1, pltpu.roll(grow_ref[j, n], 1, 0), 1.0)
            near_state = jnp.where(row >= 1, pltpu.roll(state_ref[j, n], 1, 0), 0.0)
            start = near_state + near_grow * jnp.broadcast_to(enter[n : n + 1, :], (subs, lanes))
            start_ref[j, n] = start
            held.append(start)

        def one(s, held):
            step = step_ref[j, step_rows(s), :]
            drive = drive_ref[j, step_rows(s), :]
            now_all = []
            y = jnp.zeros((subs, lanes), jnp.float32)
            for n in range(states):
                now = jnp.exp2(step * rates[n]) * held[n] + in_ref[s, n] * drive
                y = y + out_ref[s, n] * now
                now_all.append(now)
            y_ref[j, pl.ds(s, subs, stride=steps), :] = y
            return tuple(now_all)

        lax.fori_loop(0, steps, one, tuple(held), unroll=2)
        return 0

    lax.fori_loop(0, tiles, forward_of, 0)

    for k in range(split):
        core_copy(b_dst, b_core, k).wait_recv()
    store(gate_ref, gate_out)
    store(start_ref, start_out)
    second_in = gate_ref[:, :channel_rows].reshape(width, model_width)
    for l in range(split):
        z_block = matmul_nt(normed_ref[l], second_in)
        rows = slice(l * own_rows, (l + 1) * own_rows)
        for j in range(tiles):
            z_ref[j, rows, :] = z_block[:, j * lanes : (j + 1) * lanes]

    def gate(at):
        for j in range(tiles):
            cols = slice(j * lanes, (j + 1) * lanes)
            mixed = mixed_ref[pl.ds(at, 32), cols].astype(jnp.float32)
            y = y_ref[j, pl.ds(at, 32), :] + rows_ref[j, skip_row : skip_row + 1, :] * mixed
            y_ref[j, pl.ds(at, 32), :] = y
            z = z_ref[j, pl.ds(at, 32), :]
            gated_ref[pl.ds(at, 32), cols] = low_bits(y * z * sigmoid_of(z))

    row_loop(row_count, 32, gate)
    store(z_ref, z_out)
    store(y_ref, y_out)
    store(gated_ref, gated_out)
    out_full = gate_ref[:, channel_rows:].reshape(width, model_width)

    def out_block(l):
        at = pl.multiple_of(l * own_rows, own_rows)
        return matmul(gated_ref[pl.ds(at, own_rows), :], out_full)

    sum_copies = plane_copies(lambda to, k: partial_ref.at[k - 1], arrive_ref, sum_sems, False)
    for k in range(1, split):
        partial_ref[k - 1] = low_bits(out_block(lax.rem(low + k, split)))
        sum_copies[k - 1].start()
    resid = tokens_ref[...].astype(jnp.float32) + out_block(low)
    arrived(c_src, c_dst, c_sems, c_core, (2,))
    for copy in route_copies:
        copy.wait()
    store(routed_ref, routed_out)
    for k in range(1, split):
        sum_copies[k - 1].wait()
        resid = resid + arrive_ref[k - 1].astype(jnp.float32)
    resid_ref[...] = resid
    second_ref[low] = low_bits(norm_rows(resid, gains_ref[1:2, :]))
    second_copies = plane_copies(lambda to, k: second_ref.at[low], second_ref, second_sems, True)
    for copy in second_copies:
        copy.start()
    arrived(d_src, d_dst, d_sems, d_core, (1, 3))
    relay_inside(3)
    arrived(d_src, d_dst, d_sems, d_core, (2,))
    for copy in second_copies:
        copy.wait()
    store(second_ref, second_out)
    for copy in a_copies + b_copies + c_copies + d_copies + relays + core_copies:
        copy.wait_send()
    for dst_of, sems in ((c_dst, c_core), (d_dst, d_core)):
        for k in range(split):
            core_copy(dst_of, sems, k).wait_recv()
    for copy in stores:
        copy.wait()


def run_mixer(
    tokens, gains, lengths, in_weight, conv_weight, x_weight, dt_weight, dt_bias, a_log, skip_gain,
    out_weight, expert_in, expert_out, grad_out, routes,
):
    own_rows, model_width = tokens.shape
    tap_count, channels = conv_weight.shape
    dt_rank, states = dt_weight.shape[1], a_log.shape[0]
    expert_count, hidden, _ = expert_in.shape
    row_count = own_rows * split
    steps = row_count // subs
    blocks = 2 * split
    channel_rows = -(-channels // 16) * 16
    width = blocks * channel_rows
    tiles = width // lanes
    vmem = pl.BlockSpec(memory_space=pltpu.VMEM)
    anywhere = pl.BlockSpec(memory_space=pl.ANY)
    f32, bf16 = jnp.float32, jnp.bfloat16
    tiled = (tiles, row_count, lanes)
    hidden_part = ((2 * expert_count - 1) * hidden, model_width)
    first = ((blocks, channel_rows, model_width + 2 * lanes), bf16)
    gate = ((blocks, 2 * channel_rows, model_width), bf16)
    normed = ((split, own_rows, model_width), bf16)
    edge = ((16, model_width), bf16)
    routed = ((split, own_rows, model_width + lanes), bf16)
    inputs = ((row_count + 16, width), f32)
    coef = ((row_count, lanes), f32)
    gated = ((row_count, width), bf16)
    start = ((tiles, states, subs, lanes), f32)
    resid = ((own_rows, model_width), f32)
    rows = ((tiles, lanes, lanes), f32)
    kept = [first, gate, normed, edge, routed, inputs, coef, (tiled, f32), (tiled, f32)]
    kept += [(tiled, f32), gated, start, normed, rows, (hidden_part, bf16)]
    outs = [first, gate, ((blocks,) + hidden_part, bf16), normed, routed, inputs, coef]
    spread_out = ((steps, states, subs, lanes), f32)
    outs += [(tiled, f32)] * 3 + [gated, start, resid, normed, rows, spread_out, spread_out, (tiled, f32)]
    spreads = pltpu.VMEM((steps, states, subs, lanes), f32)
    dma = pltpu.SemaphoreType.DMA
    others = split - 1
    return pl.pallas_call(
        functools.partial(mixer_kernel, dt_rank, states, tap_count),
        in_specs=[pl.BlockSpec(memory_space=pltpu.SMEM) if i == 2 else vmem for i in range(15)],
        out_specs=[vmem if i == 12 else anywhere for i in range(len(outs))],
        out_shape=[jax.ShapeDtypeStruct(shape, kind) for shape, kind in outs],
        scratch_shapes=[pltpu.VMEM(shape, kind) for shape, kind in kept]
        + [dma((len(outs),))]
        + [
            spreads,
            spreads,
            pltpu.VMEM(tiled, f32),
            pltpu.VMEM((row_count, width), bf16),
            pltpu.VMEM((others, own_rows, model_width), bf16),
            pltpu.VMEM((others, own_rows, model_width), bf16),
            pltpu.VMEM((row_count, lanes), bf16),
            pltpu.VMEM((others, row_count, lanes), bf16),
            pltpu.VMEM((tiles, 2 * states, lanes), f32),
            pltpu.VMEM((others, tiles, 2 * states, lanes), f32),
            pltpu.VMEM((tiles, states, subs, lanes), f32),
            pltpu.VMEM((tiles, states, subs, lanes), f32),
        ]
        + [dma((2, others))] * 4
        + [dma((2, split))] * 4
        + [dma((2, others))] * 5
        + [dma((split,)), dma, dma((2, others, tiles)), dma],
        compiler_params=pltpu.CompilerParams(
            collective_id=3, has_side_effects=True, vmem_limit_bytes=60 << 20
        ),
        cost_estimate=pl.CostEstimate(flops=1000, bytes_accessed=1000, transcendentals=0),
    )(
        tokens, gains, lengths, in_weight, conv_weight, x_weight, dt_weight, dt_bias, a_log, skip_gain,
        out_weight, expert_in, expert_out, grad_out, routes,
    )


def norm_back(values, gain_row, grads):
    scale = lax.rsqrt(jnp.mean(values * values, -1, keepdims=True) + eps_norm)
    unit = values * scale
    inner = grads * gain_row
    return scale * (inner - unit * jnp.mean(inner * unit, -1, keepdims=True)), grads * unit


def route_probs(rows, router, route_lanes, expert_count):
    logits = matmul_nt(rows, router)
    lane = lax.broadcasted_iota(jnp.int32, logits.shape, 1)
    logits = jnp.where(lane < expert_count, logits, -1e30)
    powers = jnp.exp(logits - jnp.max(logits, -1, keepdims=True))
    probs = powers / jnp.sum(powers, -1, keepdims=True)
    chosen = jnp.where(lane.astype(jnp.float32) == route_lanes, 1.0, 0.0)
    return probs, chosen, jnp.sum(probs * chosen, -1, keepdims=True)


class LineScatter:
    def __init__(self, src_of, arrive_ref, sems):
        core, high, low = kernel_place()
        self.src_of, self.arrive, self.high = src_of, arrive_ref, high
        relay = split

        def send(src, to, slot, index):
            return remote(src, arrive_ref.at[slot], sems.at[0, index], sems.at[1, slot], core, to, low)

        def slot_at(to, sender):
            return lax.rem(to - sender + split, split) - 1

        way = 1 - 2 * (high // (split - 1))
        near, mid, far = high + way, high + 2 * way, high + 3 * way
        self.end_sends = [
            send(src_of(far), near, relay, 0),
            send(src_of(mid), mid, slot_at(mid, high), 1),
            send(src_of(near), near, slot_at(near, high), 2),
        ]
        self.empty_slot = slot_at(high, far)
        self.end_slots = [slot_at(high, near), slot_at(high, mid)]
        beside, other = (split - 1) * (high - 1), split - 1 - high
        self.far_end = split - 1 - beside
        self.inner_sends = [
            send(src_of(other), other, slot_at(other, high), 1),
            send(src_of(beside), beside, slot_at(beside, high), 2),
        ]
        self.relay_send = send(arrive_ref.at[relay], self.far_end, slot_at(self.far_end, high), 0)
        self.inner_slots = [0, 1, 2]
        self.relay = relay
        self.sems = sems

    def landed(self, slot):
        core, high, low = kernel_place()
        remote(
            self.arrive.at[slot], self.arrive.at[slot], self.sems.at[0, 0], self.sems.at[1, slot],
            core, high, low,
        ).wait_recv()

    def start(self):
        @pl.when(at_ends())
        def _():
            for copy in self.end_sends:
                copy.start()
            self.arrive[self.empty_slot] = jnp.zeros(self.arrive.shape[1:], self.arrive.dtype)

        @pl.when(jnp.logical_not(at_ends()))
        def _():
            for copy in self.inner_sends:
                copy.start()

    def pass_on(self):
        @pl.when(jnp.logical_not(at_ends()))
        def _():
            self.landed(self.relay)
            own = self.src_of(self.far_end)
            rows = self.arrive.shape[1]

            def add(at):
                here = pl.ds(at, 16)
                total = self.arrive[self.relay, here].astype(jnp.float32)
                total = total + own[here, :].astype(jnp.float32)
                self.arrive[self.relay, here] = low_bits(total)

            row_loop(rows, 16, add)
            self.relay_send.start()

    def finish(self, out_ref):
        @pl.when(at_ends())
        def _():
            for copy in self.end_sends:
                copy.wait_send()
            for slot in self.end_slots:
                self.landed(slot)

        @pl.when(jnp.logical_not(at_ends()))
        def _():
            for copy in self.inner_sends + [self.relay_send]:
                copy.wait_send()
            for slot in self.inner_slots:
                self.landed(slot)

        own = self.src_of(self.high)

        def one(at):
            rows = pl.ds(at, 16)
            total = own[rows, :].astype(jnp.float32)
            for k in range(split - 1):
                total = total + self.arrive[k, rows].astype(jnp.float32)
            out_ref[rows, :] = total

        row_loop(out_ref.shape[0], 16, one)


def half_copy(src, dst, sems, h):
    core, high, low = kernel_place()
    return remote(src, dst, sems.at[0, h], sems.at[1, h], 1 - core, high, low)


def turn_kernel(
    states, expert_count,
    second_ref, routed_ref, hidden_hbm, weights_ref, router_ref, resid_ref, grad_ref, gains_ref,
    gate_hbm, normed_hbm, out_hbm, step_hbm, z_hbm, y_hbm, gated_hbm, rows_hbm,
    mixed_out_ref, d_resid_ref, small_ref, dy_out, gz_out, later_ref, mine_out, early_ref,
    gate_mine_ref, mid_ref,
    hidden_ref, gate_ref, normed_ref, out_ref, step_ref, z_ref, y_ref, gated_ref, rows_ref, dy_ref,
    gz_ref, load_sems, store_sems,
    grads_ref, half_ref, y_sum_ref, d_sum_ref, dg_sum_ref, gates_ref, scaled_ref, act_ref, pre_ref,
    part_ref, arrive_ref, y_arrive_ref, branch_ref, send_ref,
    ends_ref, early_arrive_ref, gate_half_ref, down_ref, growth_ref,
    mid_arrive_ref,
    half_sems, sum_sems, y_sems, branch_sems, early_sems, ends_sems, gate_half_sems, last_sems,
    last_core, mid_sems,
):
    core, high, low = kernel_place()
    _, own_rows, model_width = second_ref.shape
    row_count = own_rows * split
    steps = row_count // subs
    tiles = step_ref.shape[0]
    width = tiles * lanes
    loads = [
        pltpu.make_async_copy(source, target, load_sems.at[i])
        for i, (source, target) in enumerate(
            (
                (hidden_hbm, hidden_ref),
                (gate_hbm, gate_ref),
                (z_hbm, z_ref),
                (y_hbm, y_ref),
                (step_hbm, step_ref),
                (rows_hbm, rows_ref),
                (out_hbm, out_ref),
                (normed_hbm, normed_ref),
                (gated_hbm, gated_ref),
            )
        )
    ]
    for copy in loads:
        copy.start()
    hidden = weights_ref.shape[1]
    stores = [
        pltpu.make_async_copy(source, target, store_sems.at[i])
        for i, (source, target) in enumerate(
            (
                (dy_ref, dy_out),
                (gz_ref, gz_out),
                (half_ref.at[:, pl.ds(3 * hidden, hidden)], mine_out),
            )
        )
    ]
    last_ref = weights_ref.at[expert_count - 1]
    hidden_rows = 2 * expert_count * hidden
    channel_rows = width // (2 * split)
    greeted = greet_all()
    at = lax.broadcasted_iota(jnp.int32, (lanes, expert_count), 0)
    to = lax.broadcasted_iota(jnp.int32, (lanes, expert_count), 1)
    router = low_bits(
        matmul(jnp.where(at == to, 1.0, 0.0).astype(jnp.bfloat16), router_ref[...])
    )

    for l in range(split):
        rows = slice(l * own_rows, (l + 1) * own_rows)
        route_lanes = routed_ref[l, :, model_width:].astype(jnp.float32)
        _, _, gate = route_probs(second_ref[l], router, route_lanes, expert_count)
        gates_ref[rows, :] = jnp.broadcast_to(gate, (own_rows, lanes))
        scaled_ref[rows, :] = low_bits(gate * routed_ref[l, :, :model_width].astype(jnp.float32))
    y_sum_ref[...] = jnp.zeros_like(y_sum_ref)
    d_sum_ref[...] = jnp.zeros_like(d_sum_ref)
    dg_sum_ref[...] = jnp.zeros_like(dg_sum_ref)
    span = split * hidden

    pl.semaphore_wait(pltpu.get_barrier_semaphore(), greeted)

    loads[0].wait()

    def down_at(at):
        return down_ref.at[at]

    down_ref[high] = last_ref[...]
    last_copies = line_copies(last_ref, down_at, last_sems)
    last_relay = line_relay(down_at, last_sems)
    own_copy = core_copy(down_at, last_core, 0)
    for copy in last_copies + [own_copy]:
        copy.start()
    last_copies.append(own_copy)

    @pl.when(at_ends())
    def _():
        last_relay.start()

    def last_arrived(ks):
        for k in ks:
            line_arrived(last_ref, down_at, last_sems, k)
            copy = core_copy(down_at, last_core, k)
            copy.start()
            last_copies.append(copy)

    def halves_of(e, first):
        up = hidden_ref[first : first + split, 2 * e * hidden : (2 * e + 1) * hidden]
        up = up.reshape(span, model_width)
        if e < expert_count - 1:
            down = hidden_ref[first : first + split, (2 * e + 1) * hidden : (2 * e + 2) * hidden]
        else:
            down = down_ref[first : first + split]
        return up, down.reshape(span, model_width)

    def token_block(e, first, l):
        up, down = halves_of(e, first)
        cols = slice(0, span) if first else slice(span, 2 * span)
        rows = pl.ds(pl.multiple_of(l * own_rows, own_rows), own_rows)
        pre = matmul_nt(second_ref[l], up)
        picked = routed_ref[l, :, model_width : model_width + 1].astype(jnp.float32) == e
        half = 0.5 + 0.5 * lax.erf(pre * (0.5**0.5))
        bell = jnp.exp(-0.5 * pre * pre) * (1.0 / (2.0 * math.pi) ** 0.5)
        act = low_bits(jnp.where(picked, pre * half, 0.0))
        d_raw = matmul_nt(routed_ref[l, :, :model_width], down)
        weighted = act.astype(jnp.float32) * d_raw
        dg_sum_ref[rows, :] += sum(weighted[:, c : c + lanes] for c in range(0, span, lanes))
        d_pre = jnp.where(picked, gates_ref[rows, :1] * d_raw * (half + pre * bell), 0.0)
        d_pre = low_bits(d_pre)
        y_sum_ref[rows, :] += matmul(act, down)
        d_sum_ref[rows, :] += matmul(d_pre, up)
        act_ref[rows, cols] = act
        pre_ref[rows, cols] = d_pre

    def weight_grads(e, first):
        cols = slice(0, span) if first else slice(span, 2 * span)
        second = second_ref[...].reshape(row_count, model_width)
        up_grad = low_bits(matmul_tn(pre_ref[:, cols], second))
        down_grad = low_bits(matmul_tn(act_ref[:, cols], scaled_ref[...]))
        for b in range(split):
            piece = slice(b * hidden, (b + 1) * hidden)
            to = 2 * e * hidden
            grads_ref[first + b, to : to + hidden] = up_grad[piece]
            grads_ref[first + b, to + hidden : to + 2 * hidden] = down_grad[piece]

    def part_of(e):
        return pl.ds(2 * e * hidden, 2 * hidden)

    half_copies = {}

    def send_half(e):
        half_copies[e] = [
            half_copy(
                grads_ref.at[split + h, part_of(e)],
                half_ref.at[h, part_of(e)],
                half_sems.at[e],
                h,
            )
            for h in range(split)
        ]
        for copy in half_copies[e]:
            copy.start()

    def add_half(e):
        for copy in half_copies[e]:
            copy.wait()

        def one(i, _):
            h, at = i // (2 * hidden // 32), lax.rem(i, 2 * hidden // 32) * 32
            rows = pl.ds(2 * e * hidden + at, 32)
            half_ref[h, rows] = low_bits(
                grads_ref[h, rows].astype(jnp.float32) + half_ref[h, rows].astype(jnp.float32)
            )
            return 0

        lax.fori_loop(0, split * (2 * hidden // 32), one, 0)

    mid = LineScatter(
        lambda to: half_ref.at[to, pl.ds(2 * hidden, hidden)], mid_arrive_ref, mid_sems
    )
    early = LineScatter(lambda to: half_ref.at[to, part_of(0)], early_arrive_ref, early_sems)
    final = expert_count - 1
    for e in range(final):
        for first in (split, 0):
            lax.fori_loop(0, split, lambda l, _: (token_block(e, first, l), 0)[1], 0)
            weight_grads(e, first)
            if first:
                send_half(e)
                if e == 0:
                    last_arrived((1, 3))

                    @pl.when(jnp.logical_not(at_ends()))
                    def _():
                        last_relay.start()

    last_arrived((2,))
    for e in range(final):
        add_half(e)
    early.start()
    for k in range(split):
        core_copy(down_at, last_core, k).wait_recv()

    def sum_copy(index):
        to = lax.rem(low + 1 + index, split)
        return remote(
            part_ref.at[index], arrive_ref.at[index], sum_sems.at[0, index], sum_sems.at[1, index],
            core, high, to,
        )

    def last_block(index, _):
        l = lax.rem(low + 1 + index, split)
        token_block(final, split, l)
        token_block(final, 0, l)

        @pl.when(index < split - 1)
        def _():
            rows = pl.ds(pl.multiple_of(l * own_rows, own_rows), own_rows)
            part_ref[index, :, :model_width] = low_bits(d_sum_ref[rows, :])
            part_ref[index, :, model_width:] = low_bits(dg_sum_ref[rows, :])
            sum_copy(index).start()

        return 0

    lax.fori_loop(0, split, last_block, 0)
    weight_grads(final, split)
    send_half(final)
    weight_grads(final, 0)
    early.pass_on()
    for copy in last_copies + [last_relay]:
        copy.wait_send()

    y_copies = plane_copies(
        lambda to, k: part_ref.at[k - 1, :, pl.ds(0, model_width)], y_arrive_ref, y_sems, False
    )
    own = pl.ds(pl.multiple_of(low * own_rows, own_rows), own_rows)
    d_second, dg_lanes = d_sum_ref[own, :], dg_sum_ref[own, :]
    for k in range(1, split):
        sum_copy(k - 1).wait()
        d_second = d_second + arrive_ref[k - 1, :, :model_width].astype(jnp.float32)
        dg_lanes = dg_lanes + arrive_ref[k - 1, :, model_width:].astype(jnp.float32)
    d_gate = jnp.sum(dg_lanes, -1, keepdims=True)
    second_own = second_ref[low]
    route_lanes = routed_ref[low, :, model_width:].astype(jnp.float32)
    probs, chosen, gate = route_probs(second_own, router, route_lanes, expert_count)
    d_logits = low_bits(probs * (d_gate * (chosen - gate)))
    d_second = d_second + matmul(d_logits, router)
    d_rows, d_gain = norm_back(resid_ref[...], gains_ref[1:2, :], d_second)
    d_resid = grad_ref[...] + d_rows
    d_resid_ref[...] = d_resid
    branch_ref[low] = low_bits(d_resid)
    branch_copies = plane_copies(lambda to, k: branch_ref.at[low], branch_ref, branch_sems, True)
    for copy in branch_copies:
        copy.start()
    for k in range(1, split):
        to = pl.ds(pl.multiple_of(lax.rem(low + k, split) * own_rows, own_rows), own_rows)
        part_ref[k - 1, :, :model_width] = low_bits(y_sum_ref[to, :])
        y_copies[k - 1].start()
    small_ref[...] = jnp.zeros_like(small_ref)
    small_ref[1:2, :] = jnp.sum(d_gain, 0, keepdims=True)
    small_ref[2 : 2 + expert_count, :] = matmul_tn(d_logits, second_own)[:expert_count]

    add_half(final)
    mid.start()
    stores[2].start()
    for copy in loads[1:]:
        copy.wait()
    out_full = gate_ref[:, channel_rows:].reshape(width, model_width)
    for copy in branch_copies:
        copy.wait()
    for l in range(split):
        d_gated = matmul_nt(branch_ref[l], out_full)
        rows = slice(l * own_rows, (l + 1) * own_rows)
        for j in range(tiles):
            cols = slice(j * lanes, (j + 1) * lanes)
            z = z_ref[j, rows, :]
            sig = sigmoid_of(z)
            d_tile = d_gated[:, cols]
            dy_ref[j, rows, :] = d_tile * (z * sig)
            d_z = d_tile * y_ref[j, rows, :] * (sig * (1.0 + z * (1.0 - sig)))
            gz_ref[rows, cols] = low_bits(d_z)

    def rates_of(j):
        values = -jnp.exp(rows_ref[j, alog_row : alog_row + states, :]) * log2e
        return [jnp.broadcast_to(values[n : n + 1, :], (subs, lanes)) for n in range(states)]

    def ends_of(j, _):
        found = scan_one_way(
            j,
            True,
            states,
            steps,
            step_ref,
            lambda s: dy_ref[j, pl.ds(s, subs, stride=steps), :],
            out_ref,
            rates_of(j),
        )
        row = lax.broadcasted_iota(jnp.int32, (subs, lanes), 0)
        for n, (grow, state) in enumerate(found):
            send_ref[j, n : n + 1] = grow[:1]
            send_ref[j, states + n : states + n + 1] = state[:1]
            has = row < subs - 1
            growth_ref[j, n] = jnp.where(has, pltpu.roll(grow, subs - 1, 0), 1.0)
            later_ref[j, n] = jnp.where(has, pltpu.roll(state, subs - 1, 0), 0.0)
        for copy in ends_copies(send_ref, ends_ref, ends_sems, j, True):
            copy.start()
        return 0

    stores[0].start()
    stores[1].start()
    mid.pass_on()
    lax.fori_loop(0, tiles, ends_of, 0)

    normed = normed_ref[...].reshape(row_count, model_width)
    branch = branch_ref[...].reshape(row_count, model_width)
    for part, (first_op, second_op) in enumerate(((gz_ref, normed), (gated_ref, branch))):
        half_width = width // 2
        for at in (half_width, 0):
            grad = low_bits(matmul_tn(first_op[:, at : at + half_width], second_op))
            for b in range(split):
                piece = grad[b * channel_rows : (b + 1) * channel_rows]
                to = part * channel_rows
                grads_ref[at // channel_rows + b, to : to + channel_rows] = piece
    gate_rows = 2 * channel_rows
    gate_copies = [
        half_copy(
            grads_ref.at[split + h, pl.ds(0, gate_rows)], gate_half_ref.at[h], gate_half_sems, h
        )
        for h in range(split)
    ]
    for copy in gate_copies:
        copy.start()

    def settle(j, _):
        for copy in ends_copies(send_ref, ends_ref, ends_sems, j, True):
            copy.wait()
        enter = chain_enter(ends_ref, j, states, True)
        for n in range(states):
            entered = jnp.broadcast_to(enter[n : n + 1, :], (subs, lanes))
            later_ref[j, n] += growth_ref[j, n] * entered
        return 0

    lax.fori_loop(0, tiles, settle, 0)
    y = y_sum_ref[own, :]
    for k in range(1, split):
        y_copies[k - 1].wait()
        y = y + y_arrive_ref[k - 1].astype(jnp.float32)
    mixed_out_ref[...] = low_bits(resid_ref[...] + gates_ref[own, :1] * y)
    for h in range(split):
        gate_copies[h].wait()

        def add_gate(at, h=h):
            rows = pl.ds(at, 16)
            total = grads_ref[h, rows].astype(jnp.float32) + gate_half_ref[h, rows].astype(jnp.float32)
            gate_mine_ref[h, rows] = low_bits(total)

        row_loop(gate_rows, 16, add_gate)
    early.finish(early_ref)
    mid.finish(mid_ref)
    for copy in stores:
        copy.wait()


def run_turn(
    second, routed, hidden_full, last_part, router_lanes, resid, grad_out, gains, gate_full, normed,
    spread_out, step, z, y, gated, rows, states, expert_count,
):
    _, own_rows, model_width = second.shape
    row_count = own_rows * split
    steps = row_count // subs
    tiles = step.shape[0]
    width = tiles * lanes
    hidden = last_part.shape[1]
    hidden_rows = 2 * expert_count * hidden
    cut = 2 * hidden
    gate_rows = gate_full.shape[1]
    others = split - 1
    vmem = pl.BlockSpec(memory_space=pltpu.VMEM)
    f32, bf16 = jnp.float32, jnp.bfloat16
    dma = pltpu.SemaphoreType.DMA
    outs = [
        ((own_rows, model_width), bf16),
        ((own_rows, model_width), f32),
        ((8, model_width), f32),
        ((tiles, row_count, lanes), f32),
        ((row_count, width), bf16),
        ((tiles, states, subs, lanes), f32),
        ((split, hidden, model_width), bf16),
        ((cut, model_width), f32),
        ((split, gate_rows, model_width), bf16),
        ((hidden, model_width), f32),
    ]
    span = split * hidden
    anywhere = pl.BlockSpec(memory_space=pl.ANY)
    specs = [anywhere if i == 2 or i > 7 else vmem for i in range(16)]
    loaded = [hidden_full, gate_full, normed, spread_out, step, z, y, gated, rows]
    return pl.pallas_call(
        functools.partial(turn_kernel, states, expert_count),
        in_specs=specs,
        out_specs=[anywhere if i in (3, 4, 6) else vmem for i in range(len(outs))],
        out_shape=[jax.ShapeDtypeStruct(shape, kind) for shape, kind in outs],
        scratch_shapes=[pltpu.VMEM(value.shape, value.dtype) for value in loaded]
        + [pltpu.VMEM(*outs[i]) for i in (3, 4)]
        + [dma((len(loaded),)), dma((3,))]
        + [
            pltpu.VMEM((2 * split, hidden_rows, model_width), bf16),
            pltpu.VMEM((split, hidden_rows, model_width), bf16),
            pltpu.VMEM((row_count, model_width), f32),
            pltpu.VMEM((row_count, model_width), f32),
            pltpu.VMEM((row_count, lanes), f32),
            pltpu.VMEM((row_count, lanes), f32),
            pltpu.VMEM((row_count, model_width), bf16),
            pltpu.VMEM((row_count, 2 * span), bf16),
            pltpu.VMEM((row_count, 2 * span), bf16),
            pltpu.VMEM((others, own_rows, model_width + lanes), bf16),
            pltpu.VMEM((others, own_rows, model_width + lanes), bf16),
            pltpu.VMEM((others, own_rows, model_width), bf16),
            pltpu.VMEM((split, own_rows, model_width), bf16),
            pltpu.VMEM((tiles, 2 * states, lanes), f32),
            pltpu.VMEM((others, tiles, 2 * states, lanes), f32),
            pltpu.VMEM((split + 1, cut, model_width), bf16),
            pltpu.VMEM((split, gate_rows, model_width), bf16),
            pltpu.VMEM((2 * split, hidden, model_width), bf16),
            pltpu.VMEM((tiles, states, subs, lanes), f32),
            pltpu.VMEM((split + 1, hidden, model_width), bf16),
            dma((expert_count, 2, split)),
            dma((2, others)),
            dma((2, others)),
            dma((2, others)),
            dma((2, split + 1)),
            dma((2, others, tiles)),
            dma((2, split)),
            dma((2, others)),
            dma((2, split)),
            dma((2, split + 1)),
        ],
        compiler_params=pltpu.CompilerParams(
            collective_id=4, has_side_effects=True, vmem_limit_bytes=63 << 20
        ),
        cost_estimate=pl.CostEstimate(flops=1000, bytes_accessed=1000, transcendentals=0),
    )(
        second, routed, hidden_full, last_part, router_lanes, resid, grad_out, gains, gate_full, normed,
        spread_out, step, z, y, gated, rows,
    )


def back_kernel(
    dt_rank, states, tap_count,
    dy_hbm, gz_hbm, later_hbm, mine_ref, gate_mine_hbm, first_hbm, gate_hbm, normed_hbm, input_ref,
    coef_ref, step_hbm, start_hbm, rows_ref, d_resid_ref, tokens_ref, gains_ref, small_ref,
    lengths_ref, in_hbm, out_hbm, drive_hbm,
    grad_tokens_ref, total_ref, late_ref, second_own_ref, out_own_ref, first_own_ref,
    dy_ref, gz_ref, later_ref, gate_mine_ref, first_ref, gate_ref, normed_ref, step_ref, start_ref,
    in_ref, out_ref, drive_ref, load_sems,
    hist_ref, acc_in_ref, acc_out_ref, conv_ref, q_ref, r_ref,
    gdt_ref, gin_ref, halo_ref, part_ref, arrive_ref, fold_ref, coef_send_ref,
    coef_arrive_ref, gcoef_ref, misc_ref, select_ref, payload_ref, half_ref, mine_first_ref,
    late_arrive_ref, second_arrive_ref, out_arrive_ref, first_arrive_ref, core_slots, plane_slots, line_slots,
    late_sems, second_sems, out_sems, first_sems, half_sems, halo_sems, coef_sems, sum_sems, core_sems,
    plane_sems, line_sems,
):
    core, high, low = kernel_place()
    _, own_rows, model_width = normed_ref.shape
    row_count = own_rows * split
    steps = row_count // subs
    tiles = step_ref.shape[0]
    loads = [
        pltpu.make_async_copy(source, target, load_sems.at[i])
        for i, (source, target) in enumerate(
            (
                (step_hbm, step_ref),
                (start_hbm, start_ref),
                (gate_mine_hbm, gate_mine_ref),
                (in_hbm, in_ref),
                (drive_hbm, drive_ref),
                (dy_hbm, dy_ref),
                (later_hbm, later_ref),
                (out_hbm, out_ref),
                (first_hbm, first_ref),
                (gate_hbm, gate_ref),
                (gz_hbm, gz_ref),
                (normed_hbm, normed_ref),
            )
        )
    ]
    for copy in loads:
        copy.start()
    width = tiles * lanes
    channel_rows = width // (2 * split)
    edge = input_ref.shape[0] - row_count
    greeted = greet_all()
    first_len = lengths_ref[0, 0]

    def offsets(at, rows):
        place = high * row_count + at + lax.broadcasted_iota(jnp.int32, (rows, lanes), 0)
        return jnp.where(place < first_len, place, place - first_len)

    late = LineScatter(lambda to: mine_ref.at[to], late_arrive_ref, late_sems)
    gate_parts = [
        LineScatter(
            lambda to: gate_mine_ref.at[to, pl.ds(0, channel_rows)], second_arrive_ref, second_sems
        ),
        LineScatter(
            lambda to: gate_mine_ref.at[to, pl.ds(channel_rows, channel_rows)], out_arrive_ref, out_sems
        ),
    ]
    def convolve(at):
        offset = offsets(at, 32)
        for j in range(tiles):
            span = input_ref[pl.ds(at, 32 + edge), j * lanes : (j + 1) * lanes]
            conv_sum = jnp.zeros((32, lanes), jnp.float32)
            for k in range(tap_count):
                shift = edge - (tap_count - 1) + k
                term = rows_ref[j, tap_row + k : tap_row + k + 1, :] * span[shift : shift + 32]
                conv_sum = conv_sum + jnp.where(offset >= tap_count - 1 - k, term, 0.0)
            conv_ref[j, pl.ds(at, 32), :] = conv_sum

    row_loop(row_count, 32, convolve)
    pl.semaphore_wait(pltpu.get_barrier_semaphore(), greeted)
    late.start()
    for copy in loads[:8]:
        copy.wait()
    acc_in_ref[...] = jnp.zeros_like(acc_in_ref)
    acc_out_ref[...] = jnp.zeros_like(acc_out_ref)
    misc_ref[...] = jnp.zeros_like(misc_ref)

    def back_of(j, _):
        @pl.when(j == 2)
        def _():
            late.pass_on()
            for part in gate_parts:
                part.start()

        values = -jnp.exp(rows_ref[j, alog_row : alog_row + states, :]) * log2e
        rates = [jnp.broadcast_to(values[n : n + 1, :], (subs, lanes)) for n in range(states)]

        def forward(s, held):
            step = step_ref[j, step_rows(s), :]
            drive = drive_ref[j, step_rows(s), :]
            now_all = []
            for n in range(states):
                now = jnp.exp2(step * rates[n]) * held[n] + in_ref[s, n] * drive
                hist_ref[s + 1, n] = now
                now_all.append(now)
            return tuple(now_all)

        held = []
        for n in range(states):
            hist_ref[0, n] = start_ref[j, n]
            held.append(start_ref[j, n])
        lax.fori_loop(0, steps, forward, tuple(held), unroll=2)

        def backward(turn, carry):
            s = steps - 1 - turn
            later, sums = carry
            step = step_ref[j, step_rows(s), :]
            drive = drive_ref[j, step_rows(s), :]
            dy = dy_ref[j, pl.ds(s, subs, stride=steps), :]
            rows = step_rows(s)
            q = jnp.zeros((subs, lanes), jnp.float32)
            r = jnp.zeros((subs, lanes), jnp.float32)
            later_next, sums_next = [], []
            for n in range(states):
                cols = slice(n * lanes, (n + 1) * lanes)
                d_state = out_ref[s, n] * dy + later[n]
                back = jnp.exp2(step * rates[n]) * d_state
                scaled = back * hist_ref[s, n]
                sums_next.append(sums[n] + scaled * step)
                q = q + scaled * rates[n]
                r = r + d_state * in_ref[s, n]
                acc_in_ref[rows, cols] += d_state * drive
                acc_out_ref[rows, cols] += hist_ref[s + 1, n] * dy
                later_next.append(back)
            q_ref[j, pl.ds(s, subs, stride=steps), :] = q * (1.0 / log2e)
            r_ref[j, pl.ds(s, subs, stride=steps), :] = r
            return tuple(later_next), tuple(sums_next)

        zero = jnp.zeros((subs, lanes), jnp.float32)
        later = tuple(later_ref[j, n] for n in range(states))
        _, sums = lax.fori_loop(0, steps, backward, (later, (zero,) * states))
        for n in range(states):
            total = jnp.sum(sums[n] * rates[n], 0, keepdims=True) * (1.0 / log2e)
            misc_ref[j, alog_row + n : alog_row + n + 1, :] = total
        return 0

    lax.fori_loop(0, tiles, back_of, 0)

    for copy in loads[8:]:
        copy.wait()

    source = lax.broadcasted_iota(jnp.int32, select_ref.shape, 0) // lanes
    target = lax.broadcasted_iota(jnp.int32, select_ref.shape, 1)

    def fold(acc_ref, first, fresh):
        select_ref[...] = jnp.where(target == first + source, 1.0, 0.0).astype(jnp.bfloat16)

        def one(at):
            values = acc_ref[pl.ds(at, 128), :]
            coarse = low_bits(values)
            fine = low_bits(values - coarse.astype(jnp.float32))
            found = matmul(coarse, select_ref[...]) + matmul(fine, select_ref[...])
            for i in range(128 // subs):
                rows = pl.ds(at // subs + i, subs, stride=steps)
                piece = found[i * subs : (i + 1) * subs]
                fold_ref[rows, :] = piece if fresh else fold_ref[rows, :] + piece

        row_loop(row_count, 128, one)

    fold(acc_in_ref, dt_rank, True)
    fold(acc_out_ref, dt_rank + states, False)
    dt_full = first_ref[:, :, model_width + lanes : model_width + 2 * lanes].reshape(width, lanes)

    def mixed_of(j, rows):
        conv = conv_ref[j, rows, :]
        return low_bits(conv * sigmoid_of(conv)).astype(jnp.float32)

    def step_grads(at):
        rows = pl.ds(at, 128)
        pre = matmul_nt(low_bits(coef_ref[rows, :]), dt_full)
        for j in range(tiles):
            cols = slice(j * lanes, (j + 1) * lanes)
            mixed = mixed_of(j, rows)
            in_sum = r_ref[j, rows, :]
            d_step = q_ref[j, rows, :] + in_sum * mixed
            biased = pre[:, cols] + rows_ref[j, bias_row : bias_row + 1, :]
            r_ref[j, rows, :] = in_sum * softplus_of(biased)
            d_dt = d_step * sigmoid_of(biased)
            gdt_ref[rows, cols] = low_bits(d_dt)
            misc_ref[j, bias_row : bias_row + 1, :] += jnp.sum(d_dt, 0, keepdims=True)
            misc_ref[j, skip_row : skip_row + 1, :] += jnp.sum(
                dy_ref[j, rows, :] * mixed, 0, keepdims=True
            )
        part = fold_ref[rows, :] + matmul(gdt_ref[rows, :], dt_full)
        fold_ref[rows, :] = part
        coef_send_ref[rows, :] = low_bits(part)

    row_loop(row_count, 128, step_grads)
    coef_copies = plane_copies(lambda to, k: coef_send_ref, coef_arrive_ref, coef_sems, False)
    for copy in coef_copies:
        copy.start()
    low_coef = low_bits(coef_ref[...])
    for j in range(tiles):
        rows = slice(j * lanes, (j + 1) * lanes)
        payload_ref[rows, model_width + lanes : model_width + 2 * lanes] = low_bits(
            matmul_tn(gdt_ref[:, rows], low_coef)
        )
    for copy in coef_copies:
        copy.wait()
    total = fold_ref[...]
    for k in range(1, split):
        total = total + coef_arrive_ref[k - 1].astype(jnp.float32)
    gcoef_ref[...] = low_bits(total)
    x_full = first_ref[:, :, model_width : model_width + lanes].reshape(width, lanes)

    def conv_grads(at):
        rows = pl.ds(at, 128)
        from_coef = matmul_nt(gcoef_ref[rows, :], x_full)
        for j in range(tiles):
            cols = slice(j * lanes, (j + 1) * lanes)
            d_mixed = rows_ref[j, skip_row : skip_row + 1, :] * dy_ref[j, rows, :]
            d_mixed = d_mixed + r_ref[j, rows, :] + from_coef[:, cols]
            conv = conv_ref[j, rows, :]
            sig = sigmoid_of(conv)
            q_ref[j, rows, :] = d_mixed * (sig * (1.0 + conv * (1.0 - sig)))

    row_loop(row_count, 128, conv_grads)

    def halo_copy():
        return remote(
            q_ref.at[:, pl.ds(0, subs)], halo_ref, halo_sems.at[0], halo_sems.at[1],
            core, lax.rem(high + split - 1, split), low,
        )

    for part in gate_parts:
        part.pass_on()

    @pl.when(high > 0)
    def _():
        halo_copy().start()

    def tap_grads(at):
        offset = offsets(at, 32)
        for j in range(tiles):
            cols = slice(j * lanes, (j + 1) * lanes)
            span = input_ref[pl.ds(at, 32 + edge), cols]
            d_conv = q_ref[j, pl.ds(at, 32), :]
            for k in range(tap_count):
                shift = edge - (tap_count - 1) + k
                term = jnp.where(offset >= tap_count - 1 - k, d_conv * span[shift : shift + 32], 0.0)
                misc_ref[j, tap_row + k : tap_row + k + 1, :] += jnp.sum(term, 0, keepdims=True)

    row_loop(row_count, 32, tap_grads)

    @pl.when(high < split - 1)
    def _():
        halo_copy().wait_recv()
        q_ref[:, row_count:, :] = halo_ref[...]

    @pl.when(high == split - 1)
    def _():
        q_ref[:, row_count:, :] = jnp.zeros_like(halo_ref)

    def input_grads(at):
        masks = [offsets(at + m, 32) >= m for m in range(tap_count)]
        for j in range(tiles):
            cols = slice(j * lanes, (j + 1) * lanes)
            span = q_ref[j, pl.ds(at, 32 + subs), :]
            d_input = jnp.zeros((32, lanes), jnp.float32)
            for m in range(tap_count):
                k = tap_count - 1 - m
                term = rows_ref[j, tap_row + k : tap_row + k + 1, :] * span[m : m + 32]
                d_input = d_input + jnp.where(masks[m], term, 0.0)
            gin_ref[pl.ds(at, 32), cols] = low_bits(d_input)

    row_loop(row_count, 32, input_grads)

    first_in = first_ref[:, :, :model_width].reshape(width, model_width)
    second_in = gate_ref[:, :channel_rows].reshape(width, model_width)

    def normed_block(l):
        rows = pl.ds(pl.multiple_of(l * own_rows, own_rows), own_rows)
        return matmul(gin_ref[rows, :], first_in) + matmul(gz_ref[rows, :], second_in)

    normed = normed_ref[...].reshape(row_count, model_width)
    for j in range(tiles):
        rows = slice(j * lanes, (j + 1) * lanes)
        grad_x = matmul_tn(low_bits(mixed_of(j, slice(0, row_count))), gcoef_ref[...])
        payload_ref[rows, model_width : model_width + lanes] = low_bits(grad_x + misc_ref[j].T)
    half_width = width // 2
    half = remote(
        payload_ref.at[pl.ds(half_width, half_width)], half_ref, half_sems.at[0], half_sems.at[1],
        1 - core, high, low,
    )

    def first_half(at):
        payload_ref[at : at + half_width, :model_width] = low_bits(
            matmul_tn(gin_ref[:, at : at + half_width], normed)
        )

    first_half(half_width)
    half.start()
    sum_copies = plane_copies(lambda to, k: part_ref.at[k - 1], arrive_ref, sum_sems, False)
    gain = jnp.zeros((1, model_width), jnp.float32)
    for k in range(1, split + 1):
        l = lax.rem(low + k, split)
        block = normed_block(l)
        gain = gain + jnp.sum(block * normed_ref[l].astype(jnp.float32), 0, keepdims=True)
        if k < split:
            part_ref[k - 1] = low_bits(block)
            sum_copies[k - 1].start()
        else:
            grad_tokens_ref[...] = block

    line_slots[high] = small_ref[...]
    line_slots[high, 0:1, :] = gain / gains_ref[0:1, :]
    line = line_copies(line_slots.at[high], lambda at: line_slots.at[at], line_sems, True)
    for copy in line:
        copy.start()
    first_half(0)
    half.wait()

    def add_half(at):
        rows = pl.ds(at, 64)
        both = payload_ref[rows, :].astype(jnp.float32) + half_ref[rows, :].astype(jnp.float32)
        mine_first_ref[rows, :] = low_bits(both)

    row_loop(half_width, 64, add_half)
    first = LineScatter(
        lambda to: mine_first_ref.at[pl.ds(pl.multiple_of(to * channel_rows, 16), channel_rows)],
        first_arrive_ref,
        first_sems,
    )
    first.start()
    for k in range(1, split):
        line_arrived(line_slots.at[high], lambda at: line_slots.at[at], line_sems, k)
    core_slots[core] = (line_slots[0] + line_slots[1]) + (line_slots[2] + line_slots[3])
    hop = remote(
        core_slots.at[core], core_slots.at[core], core_sems.at[0], core_sems.at[1], 1 - core, high, low
    )
    hop.start()
    late.finish(late_ref)
    hop.wait()
    plane_slots[low] = core_slots[0] + core_slots[1]
    plane = plane_copies(lambda to, k: plane_slots.at[low], plane_slots, plane_sems, True)
    for copy in plane:
        copy.start()
    first.pass_on()
    gate_parts[0].finish(second_own_ref)
    gate_parts[1].finish(out_own_ref)
    d_normed = grad_tokens_ref[...]
    for k in range(1, split):
        sum_copies[k - 1].wait()
        d_normed = d_normed + arrive_ref[k - 1].astype(jnp.float32)
    tokens = tokens_ref[...].astype(jnp.float32)
    d_rows, _ = norm_back(tokens, gains_ref[0:1, :], d_normed)
    grad_tokens_ref[...] = d_resid_ref[...] + d_rows
    for copy in plane:
        copy.wait()
    for copy in line:
        copy.wait_send()
    total_ref[...] = (plane_slots[0] + plane_slots[1]) + (plane_slots[2] + plane_slots[3])
    first.finish(first_own_ref)

    @pl.when(high > 0)
    def _():
        halo_copy().wait_send()


def run_back(
    dy, gz, later, mine, gate_mine, first_full, gate_full, normed, input_all, coef, step, start, rows,
    d_resid, tokens, gains, small, lengths, spread_in, spread_out, drive, dt_rank, states,
    tap_count,
):
    _, own_rows, model_width = normed.shape
    row_count = own_rows * split
    steps = row_count // subs
    tiles = step.shape[0]
    width = tiles * lanes
    channel_rows = width // (2 * split)
    others = split - 1
    late_rows = mine.shape[1]
    first_columns = first_full.shape[2]
    vmem = pl.BlockSpec(memory_space=pltpu.VMEM)
    specs = [pl.BlockSpec(memory_space=pl.ANY) if i in (0, 1, 2, 4, 5, 6, 7, 10, 11) else vmem for i in range(17)]
    loaded = [dy, gz, later, gate_mine, first_full, gate_full, normed, step, start]
    loaded += [spread_in, spread_out, drive]
    specs.append(pl.BlockSpec(memory_space=pltpu.SMEM))
    specs += [pl.BlockSpec(memory_space=pl.ANY)] * 3
    f32, bf16 = jnp.float32, jnp.bfloat16
    dma = pltpu.SemaphoreType.DMA
    outs = [
        (own_rows, model_width),
        (8, model_width),
        (late_rows, model_width),
        (channel_rows, model_width),
        (channel_rows, model_width),
        (channel_rows, first_columns),
    ]
    tiled = pltpu.VMEM((tiles, row_count, lanes), f32)
    summed = pltpu.VMEM((row_count, states * lanes), f32)
    return pl.pallas_call(
        functools.partial(back_kernel, dt_rank, states, tap_count),
        in_specs=specs,
        out_specs=[vmem] * len(outs),
        out_shape=[jax.ShapeDtypeStruct(shape, f32) for shape in outs],
        scratch_shapes=[pltpu.VMEM(value.shape, value.dtype) for value in loaded]
        + [dma((len(loaded),))]
        + [
            pltpu.VMEM((steps + 1, states, subs, lanes), f32),
            summed,
            summed,
            tiled,
            pltpu.VMEM((tiles, row_count + subs, lanes), f32),
            tiled,
            pltpu.VMEM((row_count, width), bf16),
            pltpu.VMEM((row_count, width), bf16),
            pltpu.VMEM((tiles, subs, lanes), f32),
            pltpu.VMEM((others, own_rows, model_width), bf16),
            pltpu.VMEM((others, own_rows, model_width), bf16),
            pltpu.VMEM((row_count, lanes), f32),
            pltpu.VMEM((row_count, lanes), bf16),
            pltpu.VMEM((others, row_count, lanes), bf16),
            pltpu.VMEM((row_count, lanes), bf16),
            pltpu.VMEM((tiles, lanes, lanes), f32),
            pltpu.VMEM((states * lanes, lanes), bf16),
            pltpu.VMEM((width, first_columns), bf16),
            pltpu.VMEM((width // 2, first_columns), bf16),
            pltpu.VMEM((width // 2, first_columns), bf16),
            pltpu.VMEM((split + 1, late_rows, model_width), bf16),
            pltpu.VMEM((split + 1, channel_rows, model_width), bf16),
            pltpu.VMEM((split + 1, channel_rows, model_width), bf16),
            pltpu.VMEM((split + 1, channel_rows, first_columns), bf16),
            pltpu.VMEM((2, 8, model_width), f32),
            pltpu.VMEM((split, 8, model_width), f32),
            pltpu.VMEM((split, 8, model_width), f32),
        ]
        + [dma((2, split + 1))] * 4
        + [dma((2,)), dma((2,)), dma((2, others)), dma((2, others)), dma((2,))]
        + [dma((2, others)), dma((2, others))],
        compiler_params=pltpu.CompilerParams(
            collective_id=5, has_side_effects=True, vmem_limit_bytes=63 << 20
        ),
        cost_estimate=pl.CostEstimate(flops=1000, bytes_accessed=1000, transcendentals=0),
    )(
        dy, gz, later, mine, gate_mine, first_full, gate_full, normed, input_all, coef, step, start,
        rows, d_resid, tokens, gains, small, lengths, spread_in, spread_out, drive,
    )


def results_kernel(
    tap_count, states, coef_count, dt_rank, expert_count,
    mixed_ref, tokens_ref, total_ref, early_ref, mid_ref, late_ref, second_ref, out_ref, first_ref,
    mixed_out, tokens_out, gains_out, router_out, in_out, conv_out, x_out, dt_out, bias_out, alog_out,
    skip_out, out_out, up_out, down_out,
):
    channels, model_width = out_out.shape
    hidden = up_out.shape[1]
    mixed_out[...] = mixed_ref[...]
    tokens_out[...] = tokens_ref[...]
    gains_out[...] = total_ref[:2]
    router_out[...] = total_ref[2 : 2 + expert_count]
    in_out[0] = first_ref[:channels, :model_width]
    in_out[1] = second_ref[:channels]
    out_out[...] = out_ref[:channels]
    at = model_width
    x_out[...] = first_ref[:channels, at : at + lanes][:, :coef_count]
    dt_out[...] = first_ref[:channels, at + lanes : at + 2 * lanes][:, :dt_rank]
    misc = first_ref[:, at : at + lanes]
    rows = misc.T
    conv_out[...] = rows[tap_row : tap_row + tap_count, :channels]
    alog_out[...] = rows[alog_row : alog_row + states, :channels]
    bias_out[...] = rows[bias_row : bias_row + 1, :channels]
    skip_out[...] = rows[skip_row : skip_row + 1, :channels]
    up_out[0], down_out[0] = early_ref[:hidden], early_ref[hidden:]
    up_out[1], down_out[1] = mid_ref[...], late_ref[...]


def run_results(parts, channels, tap_count, states, coef_count, dt_rank, expert_count, hidden):
    own_rows, model_width = parts[0].shape
    f32 = jnp.float32
    shapes = [
        (own_rows, model_width),
        (2, model_width),
        (expert_count, model_width),
        (2, channels, model_width),
        (tap_count, channels),
        (channels, coef_count),
        (channels, dt_rank),
        (1, channels),
        (states, channels),
        (1, channels),
        (channels, model_width),
        (expert_count, hidden, model_width),
        (expert_count, hidden, model_width),
    ]
    vmem = pl.BlockSpec(memory_space=pltpu.VMEM)
    return pl.pallas_call(
        functools.partial(results_kernel, tap_count, states, coef_count, dt_rank, expert_count),
        in_specs=[vmem] * len(parts),
        out_specs=[vmem] * (len(shapes) + 1),
        out_shape=[jax.ShapeDtypeStruct((own_rows, model_width), jnp.bfloat16)]
        + [jax.ShapeDtypeStruct(shape, f32) for shape in shapes],
        compiler_params=pltpu.CompilerParams(vmem_limit_bytes=62 << 20),
        cost_estimate=pl.CostEstimate(flops=1000, bytes_accessed=1000, transcendentals=0),
    )(*parts)


def norm_rows(values, gain_row):
    return values * lax.rsqrt(jnp.mean(values * values, -1, keepdims=True) + eps_norm) * gain_row


def matmul(first_op, second_op):
    return jnp.dot(first_op, second_op, preferred_element_type=jnp.float32)


def matmul_nt(first_op, second_op):
    return lax.dot_general(
        first_op, second_op, (((1,), (1,)), ((), ())), preferred_element_type=jnp.float32
    )


def matmul_tn(first_op, second_op):
    return lax.dot_general(
        first_op, second_op, (((0,), (0,)), ((), ())), preferred_element_type=jnp.float32
    )


def low_bits(value):
    return value.astype(jnp.bfloat16)


def swap_low(value, k):
    count = lax.axis_size("seq")
    return lax.ppermute(value, "seq", [(s, s ^ k) for s in range(count)])


def turn_high(value, k):
    count = lax.axis_size("seq")
    return lax.ppermute(value, "seq", [(s, (s + split * k) % count) for s in range(count)])


def from_high(value, k):
    count = lax.axis_size("seq")
    pairs = [(s, s + split * k) for s in range(count) if 0 <= s + split * k < count]
    return lax.ppermute(value, "seq", pairs)


def swap_core(value):
    return lax.ppermute(value, "grp", [(0, 1), (1, 0)])


def high_groups():
    count = lax.axis_size("seq")
    return [[h * split + l for h in range(count // split)] for l in range(split)]


def gather_low(value):
    low = lax.axis_index("seq") % split
    first_bit, second_bit = low % 2 == 1, low // 2 == 1
    own, one, two, three = [value] + [swap_low(value, k) for k in range(1, split)]
    a, b = jnp.where(first_bit, one, own), jnp.where(first_bit, own, one)
    c, d = jnp.where(first_bit, three, two), jnp.where(first_bit, two, three)
    pieces = [
        jnp.where(second_bit, c, a),
        jnp.where(second_bit, d, b),
        jnp.where(second_bit, a, c),
        jnp.where(second_bit, b, d),
    ]
    return jnp.concatenate(pieces, 0)


def scatter_low(partial):
    low = lax.axis_index("seq") % split
    rows = partial.shape[0] // split

    def block(at):
        return lax.dynamic_slice_in_dim(partial, at * rows, rows, 0)

    arrived = [swap_low(low_bits(block(low ^ k)), k) for k in range(1, split)]
    return sum(a.astype(jnp.float32) for a in [block(low)] + arrived)


def sum_low(partial):
    low_partial = low_bits(partial)
    arrived = [swap_low(low_partial, k) for k in range(1, split)]
    return partial + sum(a.astype(jnp.float32) for a in arrived)


def gather_high(value):
    high_count = lax.axis_size("seq") // split
    if high_count > 4:
        return lax.all_gather(value, "seq", axis_index_groups=high_groups())
    high = lax.axis_index("seq") // split
    turned = [turn_high(value, k) for k in range(1, high_count)]
    line = turned[::-1] + [value] + turned[::-1]
    return lax.dynamic_slice_in_dim(jnp.stack(line), high_count - 1 - high, high_count, 0)


def gather_core(own):
    full = jnp.stack([own, swap_core(own)])
    return full.reshape((-1,) + own.shape[1:])


def after(value, *others):
    return lax.optimization_barrier((value,) + others)[0]


def pad_rows(value, rows):
    return jnp.pad(value, ((0, rows - value.shape[0]), (0, 0)))


def fold_core(partial, rows):
    high_count = lax.axis_size("seq") // split
    blocks = partial.reshape(2, high_count, rows, partial.shape[-1])
    arrived = swap_core(low_bits(blocks[1]))
    return low_bits(blocks[0].astype(jnp.float32) + arrived.astype(jnp.float32))


def fold_high(mine):
    high_count = lax.axis_size("seq") // split
    if high_count > 4:
        return lax.psum_scatter(
            mine.astype(jnp.float32), "seq", scatter_dimension=0, axis_index_groups=high_groups()
        )
    high = lax.axis_index("seq") // split

    def block(at):
        return lax.dynamic_index_in_dim(mine, at % high_count, 0, False)

    arrived = [turn_high(block(high + k), k) for k in range(1, high_count)]
    return sum(a.astype(jnp.float32) for a in [block(high)] + arrived)


def sum_all(partial):
    high_count = lax.axis_size("seq") // split
    total = partial + swap_core(partial)
    step = 1
    while step < high_count * split:
        total = total + swap_low(total, step)
        step *= 2
    return total


def entering_state(grow, state, reverse):
    high_count = lax.axis_size("seq") // split
    packed = jnp.concatenate([grow, state], 0)
    states = grow.shape[0]
    if high_count > 4:
        high = lax.axis_index("seq") // split
        every = lax.all_gather(packed, "seq", axis_index_groups=high_groups())

        def one(turn, total):
            source = high_count - 1 - turn if reverse else turn
            piece = lax.dynamic_index_in_dim(every, source, 0, False)
            return piece[states:] + piece[:states] * total

        ahead = high_count - 1 - high if reverse else high
        return lax.fori_loop(0, ahead, one, jnp.zeros_like(state))
    total = jnp.zeros_like(state)
    near = [from_high(packed, -k if reverse else k) for k in range(1, high_count)]
    for piece in near[::-1]:
        total = piece[states:] + piece[:states] * total
    return total


def shards_general(
    tokens,
    routes,
    lengths,
    grad_out,
    norm_gains,
    router,
    in_weight,
    conv_weight,
    x_weight,
    dt_weight,
    dt_bias,
    a_log,
    skip_gain,
    out_weight,
    expert_in,
    expert_out,
):
    channels, tap_count = conv_weight.shape
    dt_rank = dt_weight.shape[1]
    states = a_log.shape[1]
    expert_count, hidden, model_width = expert_in.shape
    own_rows = tokens.shape[0]
    row_count = own_rows * split
    high_count = lax.axis_size("seq") // split
    low = lax.axis_index("seq") % split
    high = lax.axis_index("seq") // split
    coef_count = dt_rank + 2 * states
    channel_rows = -(-channels // 16) * 16
    width = 2 * high_count * channel_rows
    hidden_rows = expert_count * hidden
    small_width = -(-(coef_count + dt_rank + tap_count + 2 + states) // lanes) * lanes

    small = jnp.concatenate(
        [x_weight, dt_weight, conv_weight, dt_bias[:, None], a_log, skip_gain[:, None]], 1
    )
    small = jnp.pad(small, ((0, 0), (0, small_width - small.shape[1])))
    inputs = tokens.astype(jnp.float32)
    edge = 16
    halo = from_high(tokens[own_rows - edge :], 1).astype(jnp.float32)
    normed_own = low_bits(norm_rows(jnp.concatenate([inputs, halo], 0), norm_gains[0]))
    payload = pad_rows(jnp.concatenate([in_weight[0], small], 1), channel_rows)
    first_full = gather_core(gather_high(payload)).reshape(width, -1)
    normed = gather_low(normed_own).reshape(split, own_rows + edge, model_width)
    normed_edge = normed[split - 1, own_rows:]
    normed = normed[:, :own_rows].reshape(row_count, model_width)
    first_in, small_full = first_full[:, :model_width], first_full[:, model_width:]
    x_full = small_full[:, :coef_count]
    at = coef_count
    dt_full = small_full[:, at : at + dt_rank]
    at = at + dt_rank
    conv_taps = small_full[:, at : at + tap_count].astype(jnp.float32)
    at = at + tap_count
    bias_vals = small_full[:, at].astype(jnp.float32)
    at = at + 1
    decay_rate = -jnp.exp(small_full[:, at : at + states].astype(jnp.float32)).T
    at = at + states
    skip_vals = small_full[:, at].astype(jnp.float32)
    rate = decay_rate * log2e

    early_part = jnp.concatenate(
        [
            pad_rows(in_weight[1], channel_rows),
            pad_rows(out_weight, channel_rows),
            expert_in[0],
        ],
        0,
    )
    early_part = gather_high(after(early_part, first_full))
    routed_part = jnp.concatenate(
        [grad_out, routes[:, None].astype(jnp.float32) * jnp.ones((1, lanes), jnp.float32)], 1
    )
    routed_part = gather_low(after(low_bits(routed_part), normed))
    grad_rows = routed_part[:, :model_width]
    routes_all = routed_part[:, model_width : model_width + 1].astype(jnp.int32)
    late_part = jnp.concatenate(
        [expert_in[1:].reshape(-1, model_width), expert_out.reshape(-1, model_width)], 0
    )

    place = high * row_count + jnp.arange(row_count, dtype=jnp.int32)
    first_len = lengths[0, 0]
    offset = jnp.where(place < first_len, place, place - first_len)
    reset = jnp.where(offset[:, None] == 0, 1e30, 0.0) * jnp.ones((1, lanes), jnp.float32)
    valid_rows = [
        (offset >= tap_count - 1 - k).astype(jnp.float32)[:, None] for k in range(tap_count)
    ]

    all_input = low_bits(matmul_nt(jnp.concatenate([normed_edge, normed], 0), first_in))
    conv_input = all_input[edge:]
    window = all_input[edge - (tap_count - 1) :].astype(jnp.float32)
    conv_sum = sum(
        conv_taps[:, k] * window[k : k + row_count] * valid_rows[k] for k in range(tap_count)
    )
    mixed_in = low_bits(jax.nn.silu(conv_sum))
    mixed_val = mixed_in.astype(jnp.float32)
    coef_pad = jnp.pad(x_full, ((0, 0), (0, lanes - coef_count)))
    coef_rows = sum_low(matmul(mixed_in, coef_pad))
    dt_low = low_bits(coef_rows[:, :dt_rank])
    dt_pre = matmul_nt(dt_low, dt_full) + bias_vals
    step_size = jax.nn.softplus(dt_pre)
    drive = step_size * mixed_val
    first_b, first_c = dt_rank, dt_rank + states
    peers = high_count - 1 if high_count <= 4 else 0
    grow, state, enter = scan_ends(
        step_size, reset, drive, coef_rows, rate, first_b, False, peers
    )
    slice_grow = grow[:, subs - 1]
    if not peers:
        enter = entering_state(slice_grow, state[:, subs - 1], False)
    enter, early_part, late_part = lax.optimization_barrier((enter, early_part, late_part))
    early_full = gather_core(early_part)
    late_part = gather_high(late_part)
    y_scan, start, hist = scan_forward(
        step_size, reset, drive, coef_rows, rate, grow, state, enter, first_b, first_c
    )
    y_scan, early_full = lax.optimization_barrier((y_scan, early_full))
    second_in = early_full[:, :channel_rows].reshape(width, model_width)
    out_full = early_full[:, channel_rows : 2 * channel_rows].reshape(width, model_width)
    z_gate = matmul_nt(normed, second_in)
    y_value = y_scan + skip_vals * mixed_val
    gate_z = jax.nn.silu(z_gate)
    gated = low_bits(y_value * gate_z)
    resid = inputs + scatter_low(matmul(gated, out_full))

    resid, late_part = lax.optimization_barrier((resid, late_part))
    late_full = gather_core(late_part)
    second_own = low_bits(norm_rows(resid, norm_gains[1]))
    second = gather_low(second_own)

    def gate_of(rows, row_routes):
        logits = matmul(rows, router)
        chosen = row_routes == jnp.arange(expert_count, dtype=jnp.int32)[None, :]
        chosen = chosen.astype(jnp.float32)
        probs = jax.nn.softmax(logits, -1)
        return logits, chosen, jnp.sum(probs * chosen, -1, keepdims=True)

    gate_rows = gate_of(second, routes_all)[2]
    routed = low_bits(gate_rows * grad_rows.astype(jnp.float32))
    parts = [(early_full[:, 2 * channel_rows :], 0)]
    parts += [(late_full, e * hidden) for e in range(2 * expert_count - 1)]
    step_rows = hidden
    if hidden % 16:
        step_rows = 2 * high_count * hidden // 4
        parts = [
            (w[:, a : a + hidden].reshape(4, step_rows, model_width), 0) for w, a in parts
        ]
    sums, hidden_grads = run_experts(
        second, routed, routed_part[:, model_width:].astype(jnp.float32), parts, step_rows
    )
    if hidden % 16:
        pieces = hidden_grads.reshape(4, 2 * expert_count, -1, hidden, model_width)
        hidden_grads = pieces.swapaxes(1, 2).reshape(-1, 2 * hidden_rows, model_width)
    hidden_mine = fold_core(hidden_grads, 2 * hidden_rows)
    sums = scatter_low(sums)
    expert_y, d_second = sums[:, :model_width], sums[:, model_width:]
    d_second, hidden_mine = lax.optimization_barrier((d_second, hidden_mine))
    cut = hidden_rows * 2 // 3
    hidden_early = fold_high(hidden_mine[:, :cut])
    hidden_mine = hidden_mine[:, cut:]
    logits, chosen, gate_own = gate_of(second_own, routes[:, None])
    mixed_out = low_bits(resid + gate_own * expert_y)
    d_gate = jnp.sum(expert_y * grad_out, -1, keepdims=True)
    _, soft_pull = jax.vjp(lambda v: jax.nn.softmax(v, -1), logits)
    d_logits = low_bits(soft_pull(chosen * d_gate)[0])
    grad_router = matmul_tn(d_logits, second_own)
    d_second = d_second + matmul_nt(d_logits, router)
    _, norm_pull_two = jax.vjp(norm_rows, resid, norm_gains[1])
    d_resid_norm, d_gain_two = norm_pull_two(d_second)
    d_resid = grad_out + d_resid_norm

    g_branch = gather_low(low_bits(d_resid))
    d_gated = matmul_nt(g_branch, out_full)
    d_y = d_gated * gate_z
    _, silu_pull = jax.vjp(jax.nn.silu, z_gate)
    d_z = silu_pull(d_gated * y_value)[0]
    gate_grads = jnp.concatenate(
        [matmul_tn(low_bits(d_z), normed), matmul_tn(gated, g_branch)], 1
    )
    gate_mine = fold_core(gate_grads, channel_rows)
    back_grow, back_state, back_enter = scan_ends(
        step_size, reset, d_y, coef_rows, rate, first_c, True, peers
    )
    if not peers:
        back_enter = entering_state(slice_grow, back_state[:, 0], True)
    back_enter, hidden_mine = lax.optimization_barrier((back_enter, hidden_mine))
    hidden_late = fold_high(hidden_mine)
    scaled_sum, in_sum, rate_sum, d_in_coef, d_out_coef = scan_backward(
        step_size,
        reset,
        drive,
        d_y,
        coef_rows,
        rate,
        start,
        hist,
        back_grow,
        back_state,
        back_enter,
        first_b,
        first_c,
    )
    d_step = scaled_sum + in_sum * mixed_val
    d_mixed = skip_vals * d_y + in_sum * step_size
    grad_skip = jnp.sum(d_y * mixed_val, 0)
    d_dt = d_step * jax.nn.sigmoid(dt_pre)
    grad_bias = jnp.sum(d_dt, 0)
    g_dt = low_bits(d_dt)
    grad_dt = matmul_tn(g_dt, dt_low)
    part_coef = jnp.concatenate([matmul(g_dt, dt_full), d_in_coef, d_out_coef], 1)
    part_coef = jnp.pad(part_coef, ((0, 0), (0, lanes - coef_count)))
    g_coef = low_bits(sum_low(part_coef)[:, :coef_count])
    grad_x = matmul_tn(mixed_in, g_coef)
    d_mixed = d_mixed + matmul_nt(g_coef, x_full)
    _, conv_pull = jax.vjp(jax.nn.silu, conv_sum)
    d_conv = conv_pull(d_mixed)[0]
    grad_conv = jnp.stack(
        [jnp.sum(d_conv * valid_rows[k] * window[k : k + row_count], 0) for k in range(tap_count)],
        1,
    )
    d_window = sum(
        jnp.pad(conv_taps[:, k] * d_conv * valid_rows[k], ((k, tap_count - 1 - k), (0, 0)))
        for k in range(tap_count)
    )
    from_next = from_high(d_window[: tap_count - 1], -1)
    d_input = d_window[tap_count - 1 :] + jnp.pad(
        from_next, ((row_count - (tap_count - 1), 0), (0, 0))
    )
    g_in = low_bits(d_input)
    g_in, hidden_late, gate_mine = lax.optimization_barrier((g_in, hidden_late, gate_mine))
    hidden_own = jnp.concatenate([hidden_early, hidden_late], 0)
    gate_own_grads = fold_high(gate_mine)
    g_z = low_bits(d_z)
    d_normed = scatter_low(matmul(g_in, first_in) + matmul(g_z, second_in))
    _, norm_pull_one = jax.vjp(norm_rows, inputs, norm_gains[0])
    d_inputs, d_gain_one = norm_pull_one(d_normed)
    grad_tokens = d_resid + d_inputs

    rest = jnp.concatenate(
        [grad_x, grad_dt, grad_conv, grad_bias[:, None], rate_sum.T, grad_skip[:, None]], 1
    )
    rest = jnp.pad(rest, ((0, 0), (0, small_width - rest.shape[1])))
    first_own = fold_high(
        fold_core(jnp.concatenate([matmul_tn(g_in, normed), rest], 1), channel_rows)
    )[:channels]
    rest_own = first_own[:, model_width:]
    gate_own_grads = gate_own_grads[:channels]
    sums = sum_all(jnp.concatenate([jnp.stack([d_gain_one, d_gain_two]), grad_router], 0))
    ends = [0]
    for count in (coef_count, dt_rank, tap_count, 1, states, 1):
        ends.append(ends[-1] + count)
    grad_x, grad_dt, grad_conv, grad_bias, grad_alog, grad_skip = (
        rest_own[:, a:b] for a, b in zip(ends[:-1], ends[1:], strict=True)
    )
    return (
        mixed_out,
        grad_tokens,
        sums[:2],
        sums[2:].T,
        jnp.stack([first_own[:, :model_width], gate_own_grads[:, :model_width]]),
        grad_conv,
        grad_x,
        grad_dt,
        grad_bias[:, 0],
        grad_alog,
        grad_skip[:, 0],
        gate_own_grads[:, model_width:],
        hidden_own[:hidden_rows].reshape(expert_count, hidden, model_width),
        hidden_own[hidden_rows:].reshape(expert_count, hidden, model_width),
    )


def shards_plane(
    tokens,
    routes,
    lengths,
    grad_out,
    norm_gains,
    router,
    in_weight,
    conv_weight,
    x_weight,
    dt_weight,
    dt_bias,
    a_log,
    skip_gain,
    out_weight,
    expert_in,
    expert_out,
):
    channels, tap_count = conv_weight.shape
    dt_rank, states = dt_weight.shape[1], a_log.shape[1]
    expert_count, hidden, _ = expert_in.shape
    coef_count = dt_rank + 2 * states
    (
        first_full, gate_full, hidden_full, normed, routed, input_all, coef, step, z, y, gated, start,
        resid, second, rows, spread_in, spread_out, drive,
    ) = run_mixer(
        tokens, norm_gains, lengths, in_weight, conv_weight.T, x_weight, dt_weight, dt_bias[None], a_log.T,
        skip_gain[None], out_weight, expert_in, expert_out, grad_out, routes[None],
    )
    mixed_out, d_resid, small_sums, dy, gz, later, mine, early, gate_mine, mid = run_turn(
        second, routed, hidden_full, expert_out, router.T, resid, grad_out, norm_gains,
        gate_full, normed, spread_out, step, z, y, gated, rows, states, expert_count,
    )
    grad_tokens, sums, late, second_own, out_own, first_own = run_back(
        dy, gz, later, mine, gate_mine, first_full, gate_full, normed, input_all, coef, step, start,
        rows, d_resid, tokens, norm_gains, small_sums, lengths, spread_in, spread_out, drive, dt_rank,
        states, tap_count,
    )
    (
        mixed_out, grad_tokens, grad_gains, grad_router, grad_in, grad_conv, grad_x, grad_dt, grad_bias,
        grad_alog, grad_skip, grad_out_w, grad_up, grad_down,
    ) = run_results(
        (mixed_out, grad_tokens, sums, early, mid, late, second_own, out_own, first_own),
        channels, tap_count, states, coef_count, dt_rank, expert_count, hidden,
    )
    return (
        mixed_out,
        grad_tokens,
        grad_gains,
        grad_router.T,
        grad_in,
        grad_conv.T,
        grad_x,
        grad_dt,
        grad_bias[0],
        grad_alog.T,
        grad_skip[0],
        grad_out_w,
        grad_up,
        grad_down,
    )


def solution(mesh):
    both = ("grp", "seq")
    in_specs = (
        P(both, None),
        P(both),
        P("grp", None),
        P(both, None),
        P(),
        P(),
        P(None, both, None),
        P(both, None),
        P(both, None),
        P(both, None),
        P(both),
        P(both, None),
        P(both),
        P(both, None),
        P(None, both, None),
        P(None, both, None),
    )
    out_specs = (
        P(both, None),
        P(both, None),
        P(),
        P(),
        P(None, both, None),
        P(both, None),
        P(both, None),
        P(both, None),
        P(both),
        P(both, None),
        P(both),
        P(both, None),
        P(None, both, None),
        P(None, both, None),
    )
    shards = shards_plane if mesh.shape["seq"] == split * split else shards_general
    return jax.shard_map(shards, mesh=mesh, in_specs=in_specs, out_specs=out_specs, check_vma=False)
```
